32 devices in a mesh: section: 2 (over core), dp: 4 (over y, x), tensor: 4 (over z).
Axes of the slice: x: 2, y: 2, z: 4, core: 2. Of those that a mesh axis runs over, the one named last changes fastest.
Arguments:
- tokens: bfloat16 [16, 1024, 512], P('dp', 'tensor'), may hold values from -6 to 6
- lengths: int32 [16, 8], P('dp'), may hold values from 1 to 896, 1024 in all within a row
- cotangent: bfloat16 [16, 1024, 512], P('dp', 'tensor'), may hold values from -6 to 6
- ln_one_gain: float32 [2, 512], P('section'), may hold values from 0.5 to 1.5
- ln_one_bias: float32 [2, 512], P('section'), may hold values from -1.75 to 1.75
- qkv_weight: bfloat16 [2, 512, 3, 512], P('section', None, None, 'tensor'), may hold values from -0.25 to 0.25
- out_weight: bfloat16 [2, 512, 512], P('section', 'tensor'), may hold values from -1.5 to 1.5
- out_bias: float32 [2, 512], P('section'), may hold values from -3 to 3
- ln_two_gain: float32 [2, 512], P('section'), may hold values from 0.5 to 1.5
- ln_two_bias: float32 [2, 512], P('section'), may hold values from -1.75 to 1.75
- up_weight: bfloat16 [2, 512, 2048], P('section', None, 'tensor'), may hold values from -0.25 to 0.25
- up_bias: float32 [2, 2048], P('section', 'tensor'), may hold values from -3 to 3
- down_weight: bfloat16 [2, 2048, 512], P('section', 'tensor'), may hold values from -0.125 to 0.125
- down_bias: float32 [2, 512], P('section'), may hold values from -3 to 3
Outputs:
- block_outputs: bfloat16 [2, 16, 1024, 512], P('section', 'dp', 'tensor')
- input_grads: float32 [2, 16, 1024, 512], P('section', 'dp', 'tensor')
- grad_ln_one_gain: float32 [2, 512], P('section', ('dp', 'tensor'))
- grad_ln_one_bias: float32 [2, 512], P('section', ('dp', 'tensor'))
- grad_qkv_weight: float32 [2, 512, 3, 512], P('section', 'dp', None, 'tensor')
- grad_out_weight: float32 [2, 512, 512], P('section', 'tensor', 'dp')
- grad_out_bias: float32 [2, 512], P('section', ('dp', 'tensor'))
- grad_ln_two_gain: float32 [2, 512], P('section', ('dp', 'tensor'))
- grad_ln_two_bias: float32 [2, 512], P('section', ('dp', 'tensor'))
- grad_up_weight: float32 [2, 512, 2048], P('section', 'dp', 'tensor')
- grad_up_bias: float32 [2, 4, 512], P('section', 'tensor', 'dp')
- grad_down_weight: float32 [2, 2048, 512], P('section', 'tensor', 'dp')
- grad_down_bias: float32 [2, 512], P('section', ('dp', 'tensor'))
The draws below stay inside these ranges and needn't reach their ends.
Inputs may be any that keep to these rules, and one draw needn't show every extreme that they name: Each row holds 8 lengths that fill 1024 rows exactly; the largest of each row is 896.
All inputs are finite; a program needn't handle non-finite values.
Results may differ from the reference program's by a relative error of at most 0.025.
Values may be sent and summed in bfloat16 or wider, within the bound.
A program may use at most 192 MiB of HBM per device.

```python
import math
import jax
import jax.numpy as jnp
import numpy as np
from jax import lax

D = 512
HEADS = 8
HEAD = 64
FF = 2048
ROWS = 1024
SEQS = 8
LONGEST = 896
BLOCK = 512
MBATCHES = 16
N_TENSOR = 4


def levels(key, extent, cuts, smallest, high):
    gain = 1.0
    for dim, shards_of in cuts:
        heights = jax.random.uniform(jax.random.fold_in(jax.random.fold_in(key, 6), dim), (shards_of,), jnp.float32, smallest / len(cuts), high / len(cuts))
        gain = gain * jnp.repeat(jnp.exp(heights), extent[dim] // shards_of).reshape((-1,) + (1,) * (len(extent) - 1 - dim))
    return gain


def length_profile(number_of, total, most, lean):
    portions = [(1 << 20) // math.isqrt(rank ** lean) + 1 for rank in range(2, number_of + 1)]
    spare, holding = total - most - (number_of - 1), [1] * (number_of - 1)
    while spare > 0:
        free = [i for i in range(number_of - 1) if holding[i] < most]
        pool, remaining = sum([portions[i] for i in free]), spare
        for i in free:
            more = min(most - holding[i], max(1, remaining * portions[i] // pool), spare)
            holding[i] = holding[i] + more
            spare = spare - more
    return np.array([most] + holding)


def ragged_sizes(own_key, count, total, bound, skew):
    if count == 2:
        one = jax.random.randint(own_key, (), max(1, total - bound), min(bound, total - 1) + 1)
        return jnp.stack([one, total - one])
    sizes = jnp.asarray(length_profile(count, total, bound, skew), jnp.int32)
    twos = (count - 1) // 2
    donor, sink = sizes[1:1 + 2 * twos:2], sizes[2:2 + 2 * twos:2]
    room = jnp.minimum(donor - 1, bound - sink)
    moved = jax.random.randint(jax.random.fold_in(own_key, 1), (twos,), 0, 1 << 20) % (room + 1)
    sizes = sizes.at[1:1 + 2 * twos:2].set(donor - moved).at[2:2 + 2 * twos:2].set(sink + moved)
    return sizes[jax.random.permutation(jax.random.fold_in(own_key, 2), count)]


def gaussian(rng, dims, scale, most, split=(), kind=jnp.bfloat16):
    result = jax.random.normal(rng, dims, jnp.float32) * scale
    if len(split) > 0:
        result = levels(rng, dims, split, -0.22, 0.18) * result
    return jnp.clip(result, min=-most, max=most).astype(kind)


def setup_inputs(seed: int = 0) -> dict:
    key_list = jax.random.split(jax.random.key(seed), 15)
    tokens = gaussian(key_list[0], (MBATCHES, ROWS, D), 1.0, 6.0, ((0, 4), (1, 4)))
    lengths = jax.vmap(lambda own: ragged_sizes(own, SEQS, ROWS, LONGEST, 2))(jax.random.split(key_list[1], MBATCHES)).reshape((MBATCHES, SEQS)).astype(jnp.int32)
    cotangent = gaussian(key_list[2], (MBATCHES, ROWS, D), 1.0, 6.0, ((0, 4), (1, 4)))
    ln_one_gain = jnp.clip(1.0 + 0.1 * jax.random.normal(key_list[3], (2, D), jnp.float32), 0.5, 1.5)
    ln_one_bias = gaussian(key_list[4], (2, D), 0.3, 1.75, ((0, 2),), jnp.float32)
    qkv_weight = gaussian(key_list[5], (2, D, 3, D), D ** -0.5, 0.25, ((0, 2), (3, 4)))
    out_weight = gaussian(key_list[6], (2, D, D), (D // 32) ** -0.5, 1.5, ((0, 2), (1, 4)))
    out_bias = gaussian(key_list[7], (2, D), 0.5, 3.0, ((0, 2),), jnp.float32)
    ln_two_gain = jnp.clip(1.0 + 0.1 * jax.random.normal(key_list[8], (2, D), jnp.float32), 0.5, 1.5)
    ln_two_bias = gaussian(key_list[9], (2, D), 0.3, 1.75, ((0, 2),), jnp.float32)
    up_weight = gaussian(key_list[10], (2, D, FF), D ** -0.5, 0.25, ((0, 2), (2, 4)))
    up_bias = gaussian(key_list[11], (2, FF), 0.5, 3.0, ((0, 2), (1, 4)), jnp.float32)
    down_weight = gaussian(key_list[12], (2, FF, D), FF ** -0.5, 0.125, ((0, 2), (1, 4)))
    down_bias = gaussian(key_list[13], (2, D), 0.5, 3.0, ((0, 2),), jnp.float32)
    return {"tokens": tokens, "lengths": lengths, "cotangent": cotangent, "ln_one_gain": ln_one_gain, "ln_one_bias": ln_one_bias, "qkv_weight": qkv_weight, "out_weight": out_weight, "out_bias": out_bias, "ln_two_gain": ln_two_gain, "ln_two_bias": ln_two_bias, "up_weight": up_weight, "up_bias": up_bias, "down_weight": down_weight, "down_bias": down_bias}


@jax.custom_vjp
def low(v):
    return lax.optimization_barrier(v.astype(jnp.bfloat16)).astype(jnp.float32)

@jax.custom_vjp
def low_back(v):
    return v

def low_keep(v):
    return (low(v), None)

def low_pass(kept, grad):
    return (grad,)

def back_keep(v):
    return (v, None)

def back_low(kept, grad):
    return (low(grad),)
low.defvjp(low_keep, low_pass)
low_back.defvjp(back_keep, back_low)

def normalize(values, gain_vec, bias_vec):
    centre = values - lax.optimization_barrier(jnp.mean(values, axis=-1, keepdims=True))
    spread = lax.optimization_barrier(jnp.mean(centre * centre, axis=-1, keepdims=True))
    return centre * lax.rsqrt(spread + 1e-05) * gain_vec + bias_vec

def document_ids(seq_lens, row_count):
    bounds = jnp.cumsum(seq_lens.astype(jnp.int32)).astype(jnp.int32)
    places = jnp.arange(row_count, dtype=jnp.int32)
    return lax.optimization_barrier(jnp.sum((places[:, None] >= bounds[None, :]).astype(jnp.int32), axis=1)).astype(jnp.int32)

def block_layer(inputs, seq_lens, params, signed):
    gain_one, bias_one, qkv_weight, out_weight, out_bias, gain_two, bias_two, up_weight, up_bias, down_weight, down_bias = params
    highest = lax.Precision.HIGHEST
    normed_one = low(normalize(inputs, gain_one, bias_one))
    projected = jnp.dot(normed_one, qkv_weight.reshape(D, 3 * D), precision=highest)
    projected = low(low_back(projected)).reshape(ROWS, 3, HEADS, HEAD)
    queries = projected[:, 0]
    key_rows = projected[:, 1]
    values = projected[:, 2]
    doc_rows = document_ids(seq_lens, ROWS)
    places = jnp.arange(ROWS, dtype=jnp.int32)
    scale = 1.0 / math.sqrt(HEAD)

    def one_block(block_index):
        first_row = (block_index * BLOCK).astype(jnp.int32)
        query_rows = lax.dynamic_slice_in_dim(queries, first_row, BLOCK, 0)
        query_docs = lax.dynamic_slice_in_dim(doc_rows, first_row, BLOCK, 0)
        query_places = first_row + jnp.arange(BLOCK, dtype=jnp.int32)
        scores = low_back(jnp.einsum('qhe,khe->hqk', query_rows, key_rows, precision=highest) * scale)
        allowed = ((query_docs[:, None] == doc_rows[None, :]) & (query_places[:, None] >= places[None, :]))[None]
        if signed:
            modulus = jnp.sqrt(scores * scores + 1.0)
            logits = modulus
            factor = scores / modulus
        else:
            logits = scores
            factor = jnp.ones_like(scores)
        masked = jnp.where(allowed, logits, -1e+30)
        row_max = lax.optimization_barrier(jnp.max(masked, axis=-1, keepdims=True))
        exponent = jnp.where(allowed, jnp.exp(masked - row_max), 0.0)
        weights = low(factor * exponent / lax.optimization_barrier(jnp.sum(exponent, axis=-1, keepdims=True)))
        return jnp.einsum('hqk,khe->qhe', weights, values, precision=highest)
    attended = lax.map(jax.checkpoint(one_block), jnp.arange(ROWS // BLOCK, dtype=jnp.int32))
    attended = low(low_back(attended.reshape(ROWS, D)))
    branch_terms = jnp.einsum('rgc,gcd->grd', attended.reshape(ROWS, N_TENSOR, D // N_TENSOR), out_weight.reshape(N_TENSOR, D // N_TENSOR, D), precision=highest)
    hidden_one = inputs + low_back(lax.optimization_barrier(jnp.sum(low(branch_terms), axis=0))) + out_bias
    normed_two = low(normalize(hidden_one, gain_two, bias_two))
    up_values = low_back(jnp.dot(normed_two, up_weight, precision=highest) + up_bias)
    activated = low(jax.nn.gelu(up_values, approximate=False))
    feed_terms = jnp.einsum('rgf,gfd->grd', activated.reshape(ROWS, N_TENSOR, FF // N_TENSOR), down_weight.reshape(N_TENSOR, FF // N_TENSOR, D), precision=highest)
    return hidden_one + low_back(lax.optimization_barrier(jnp.sum(low(feed_terms), axis=0))) + down_bias

def stack_layer(inputs, lengths, params, signed):

    def one_batch(batch_pair):
        return block_layer(batch_pair[0], batch_pair[1], params, signed)
    return lax.map(jax.checkpoint(one_batch), (inputs, lengths))

def reference(tokens, lengths, cotangent, ln_one_gain, ln_one_bias, qkv_weight, out_weight, out_bias, ln_two_gain, ln_two_bias, up_weight, up_bias, down_weight, down_bias):
    weight_list = (ln_one_gain, ln_one_bias, qkv_weight, out_weight, out_bias, ln_two_gain, ln_two_bias, up_weight, up_bias, down_weight, down_bias)
    first_params = tuple((array_item[0].astype(jnp.float32) for array_item in weight_list))
    second_params = tuple((array_item[1].astype(jnp.float32) for array_item in weight_list))
    inputs = tokens.astype(jnp.float32)
    hidden, back_one = jax.vjp(lambda layer_in, layer_params: stack_layer(layer_in, lengths, layer_params, True), inputs, first_params)
    hidden = low(hidden)
    outputs, back_two = jax.vjp(lambda layer_in, layer_params: stack_layer(layer_in, lengths, layer_params, False), hidden, second_params)
    grad_hidden, grads_two = back_two(cotangent.astype(jnp.float32))
    grad_inputs, grads_one = back_one(grad_hidden)
    stacked = [jnp.stack([grad_first, grad_second]) for grad_first, grad_second in zip(grads_one, grads_two)]
    return (jnp.stack([hidden, outputs]).astype(jnp.bfloat16), jnp.stack([grad_inputs, grad_hidden]), stacked[0], stacked[1], stacked[2], stacked[3], stacked[4], stacked[5], stacked[6], stacked[7], stacked[8].reshape(2, N_TENSOR, FF // N_TENSOR), stacked[9], stacked[10])
```

```python
from functools import partial
import math

import jax
import jax.numpy as jnp
from jax import lax
from jax.experimental import pallas as pl
from jax.experimental.pallas import tpu as pltpu
from jax.sharding import PartitionSpec as P

HEAD = 64
FF = 2048


def passed_along(block, axis, distance):
    devices = range(lax.axis_size(axis))
    route = [(i - distance, i) for i in devices if i - distance in devices]
    return lax.ppermute(block, axis, route)


def normalize(values, gain_vec, bias_vec):
    centre = values - jnp.mean(values, axis=-1, keepdims=True)
    spread = jnp.mean(centre * centre, axis=-1, keepdims=True)
    return centre * lax.rsqrt(spread + 1e-05) * gain_vec + bias_vec


def document_ids(seq_lens, row_count):
    bounds = jnp.cumsum(seq_lens)
    places = jnp.arange(row_count, dtype=jnp.int32)
    return jnp.sum((places[:, None] >= bounds[None, :]).astype(jnp.int32), axis=1)


def first_key_block(doc_number, seq_lens, block):
    starts = jnp.cumsum(seq_lens) - seq_lens
    numbers = jnp.arange(seq_lens.shape[0], dtype=jnp.int32)
    return jnp.sum(jnp.where(numbers == doc_number, starts, 0)) // block


def grouped_sum(left, right, groups):
    row_count, inner = left.shape
    terms = jnp.einsum(
        "rgc,gcd->grd",
        left.reshape(row_count, groups, inner // groups),
        right.reshape(groups, inner // groups, right.shape[-1]),
        preferred_element_type=jnp.float32,
    )
    return jnp.sum(lax.optimization_barrier(terms.astype(jnp.bfloat16)).astype(jnp.float32), axis=0)


def branch_total(left, right):
    return grouped_sum(left, right, lax.axis_size("tensor"))


def key_scores(query_rows, key_part, query_docs, key_docs, query_first, key_first, signed):
    scale = 1.0 / math.sqrt(query_rows.shape[-1])
    scores = (
        jnp.einsum("qhe,khe->hqk", query_rows, key_part, preferred_element_type=jnp.float32) * scale
    )
    query_places = query_first + jnp.arange(query_rows.shape[0], dtype=jnp.int32)
    key_places = key_first + jnp.arange(key_part.shape[0], dtype=jnp.int32)
    allowed = (query_docs[:, None] == key_docs[None, :]) & (
        query_places[:, None] >= key_places[None, :]
    )
    modulus = jnp.sqrt(scores * scores + 1.0)
    logits = jnp.where(signed, modulus, scores)
    factor = jnp.where(signed, scores / modulus, 1.0)
    return (modulus, logits, factor, allowed[None])


def attend(queries, key_rows, values, doc_rows, seq_lens, signed, offset):
    query_count, heads_here, head_size = queries.shape
    key_count = key_rows.shape[0]
    query_block = min(512, query_count)
    key_block = min(512, key_count)
    query_first = offset + 0
    query_docs = lax.dynamic_slice_in_dim(doc_rows, query_first, query_block, 0)
    lowest = first_key_block(query_docs[0], seq_lens, key_block)
    upper = (query_first + query_block - 1) // key_block + 1

    def block_scores(key_index):
        key_first = key_index * key_block
        return key_scores(
            queries,
            lax.dynamic_slice_in_dim(key_rows, key_first, key_block, 0),
            query_docs,
            lax.dynamic_slice_in_dim(doc_rows, key_first, key_block, 0),
            query_first,
            key_first,
            signed,
        )

    def measure(key_index, carry):
        running_max, running_sum = carry
        modulus, logits, factor, allowed = block_scores(key_index)
        masked = jnp.where(allowed, logits, -1e30)
        new_max = jnp.maximum(running_max, jnp.max(masked, axis=-1))
        added = jnp.sum(jnp.where(allowed, jnp.exp(masked - new_max[:, :, None]), 0.0), axis=-1)
        return (new_max, running_sum * jnp.exp(running_max - new_max) + added)

    start_max = jnp.full((heads_here, query_block), -1e30, jnp.float32)
    start_sum = jnp.zeros((heads_here, query_block), jnp.float32)
    row_max, row_sum = lax.fori_loop(lowest, upper, measure, (start_max, start_sum))
    log_total = row_max + jnp.log(row_sum)

    def accumulate(key_index, partial_out):
        modulus, logits, factor, allowed = block_scores(key_index)
        probs = jnp.where(allowed, jnp.exp(logits - log_total[:, :, None]), 0.0)
        weights = (factor * probs).astype(jnp.bfloat16)
        value_rows = lax.dynamic_slice_in_dim(values, key_index * key_block, key_block, 0)
        return partial_out + jnp.einsum(
            "hqk,khe->qhe", weights, value_rows, preferred_element_type=jnp.float32
        )

    outputs_list = lax.fori_loop(
        lowest, upper, accumulate, jnp.zeros((query_block, heads_here, head_size), jnp.float32)
    )
    return (outputs_list, log_total)


def attend_back(
    queries,
    key_rows,
    values,
    doc_rows,
    seq_lens,
    signed,
    attended,
    log_totals,
    grad_attended,
    offset,
):
    query_count, heads_here, head_size = queries.shape
    key_count = key_rows.shape[0]
    query_block = min(512, query_count)
    key_block = min(512, key_count)
    scale = 1.0 / math.sqrt(head_size)
    centre_terms = jnp.sum(grad_attended.astype(jnp.float32) * attended, axis=-1).T
    grad_keys = jnp.zeros(key_rows.shape, jnp.float32)
    grad_values = jnp.zeros(key_rows.shape, jnp.float32)
    query_first = offset + 0
    query_docs = lax.dynamic_slice_in_dim(doc_rows, query_first, query_block, 0)
    lowest = first_key_block(query_docs[0], seq_lens, key_block)
    upper = (query_first + query_block - 1) // key_block + 1

    def backward_step(key_index, carry):
        grad_query, keys_total, values_total = carry
        key_first = key_index * key_block
        key_part = lax.dynamic_slice_in_dim(key_rows, key_first, key_block, 0)
        value_rows = lax.dynamic_slice_in_dim(values, key_first, key_block, 0)
        modulus, logits, factor, allowed = key_scores(
            queries,
            key_part,
            query_docs,
            lax.dynamic_slice_in_dim(doc_rows, key_first, key_block, 0),
            query_first,
            key_first,
            signed,
        )
        probs = jnp.where(allowed, jnp.exp(logits - log_totals[:, :, None]), 0.0)
        weights = (factor * probs).astype(jnp.bfloat16)
        grad_weights = jnp.einsum(
            "qhe,khe->hqk", grad_attended, value_rows, preferred_element_type=jnp.float32
        )
        grad_scores = factor * probs * (factor * grad_weights - centre_terms[:, :, None])
        grad_scores = grad_scores + jnp.where(
            signed, probs * grad_weights / (modulus * modulus * modulus), 0.0
        )
        grad_low = grad_scores.astype(jnp.bfloat16)
        grad_query = (
            grad_query
            + jnp.einsum("hqk,khe->qhe", grad_low, key_part, preferred_element_type=jnp.float32)
            * scale
        )
        key_term = (
            jnp.einsum("hqk,qhe->khe", grad_low, queries, preferred_element_type=jnp.float32)
            * scale
        )
        value_term = jnp.einsum(
            "hqk,qhe->khe", weights, grad_attended, preferred_element_type=jnp.float32
        )
        keys_total = lax.dynamic_update_slice_in_dim(
            keys_total,
            lax.dynamic_slice_in_dim(keys_total, key_first, key_block, 0) + key_term,
            key_first,
            0,
        )
        values_total = lax.dynamic_update_slice_in_dim(
            values_total,
            lax.dynamic_slice_in_dim(values_total, key_first, key_block, 0) + value_term,
            key_first,
            0,
        )
        return (grad_query, keys_total, values_total)

    start_query = jnp.zeros((query_block, heads_here, head_size), jnp.float32)
    grad_query, grad_keys, grad_values = lax.fori_loop(
        lowest, upper, backward_step, (start_query, grad_keys, grad_values)
    )
    return (grad_query, grad_keys, grad_values)


def forward_layer(inputs, seq_lens, params, signed, finish):
    (
        gain_one,
        bias_one,
        qkv_weight,
        out_weight,
        out_bias,
        gain_two,
        bias_two,
        up_weight,
        up_bias,
        down_weight,
        down_bias,
    ) = params
    normed_one = normalize(inputs, gain_one, bias_one).astype(jnp.bfloat16)
    offset = lax.axis_index("tensor") * normed_one.shape[0]
    row_count = normed_one.shape[0]
    width = qkv_weight.shape[-1]
    projected = jnp.dot(
        normed_one,
        qkv_weight.reshape(qkv_weight.shape[0], 3 * width),
        preferred_element_type=jnp.float32,
    ).astype(jnp.bfloat16)
    head_shape = (row_count, width // HEAD, HEAD)
    queries = projected[:, :width].reshape(head_shape)
    key_rows = projected[:, width : 2 * width].reshape(head_shape)
    values = projected[:, 2 * width :].reshape(head_shape)
    key_all, value_all = (
        lax.all_gather(key_rows, "tensor", axis=0, tiled=True),
        lax.all_gather(values, "tensor", axis=0, tiled=True),
    )
    doc_rows = document_ids(seq_lens, key_all.shape[0])
    attended, log_totals = attend(queries, key_all, value_all, doc_rows, seq_lens, signed, offset)
    attended_low = attended.reshape(row_count, width).astype(jnp.bfloat16)
    hidden_one = inputs + branch_total(attended_low, out_weight) + out_bias
    normed_two = normalize(hidden_one, gain_two, bias_two).astype(jnp.bfloat16)
    up_values = jnp.dot(normed_two, up_weight, preferred_element_type=jnp.float32) + up_bias
    activated = jax.nn.gelu(up_values, approximate=False).astype(jnp.bfloat16)
    if finish:
        outputs = hidden_one + branch_total(activated, down_weight) + down_bias
    else:
        outputs = hidden_one
    saved = (
        normed_one,
        queries,
        key_all,
        value_all,
        doc_rows,
        attended,
        attended_low,
        log_totals,
        hidden_one,
        normed_two,
        up_values,
        activated,
        offset,
    )
    return (outputs, saved)


def backward_layer(inputs, seq_lens, params, signed, grad_outputs):
    (
        gain_one,
        bias_one,
        qkv_weight,
        out_weight,
        out_bias,
        gain_two,
        bias_two,
        up_weight,
        up_bias,
        down_weight,
        down_bias,
    ) = params
    unused_out, saved = forward_layer(inputs, seq_lens, params, signed, False)
    (
        rows_one,
        queries,
        key_all,
        value_all,
        doc_rows,
        attended,
        attended_low,
        log_totals,
        hidden_one,
        rows_two,
        up_values,
        activated,
        offset,
    ) = saved
    row_count, width = attended_low.shape
    grad_low = grad_outputs.astype(jnp.bfloat16)
    grad_down = jnp.einsum("rf,rd->fd", activated, grad_low, preferred_element_type=jnp.float32)
    grad_act = jnp.einsum("rd,fd->rf", grad_low, down_weight, preferred_element_type=jnp.float32)
    gelu_value, gelu_back = jax.vjp(partial(jax.nn.gelu, approximate=False), up_values)
    grad_up_values = gelu_back(grad_act)[0].astype(jnp.bfloat16)
    grad_up_bias = jnp.sum(grad_up_values.astype(jnp.float32), axis=0)
    grad_up = jnp.einsum("rd,rf->df", rows_two, grad_up_values, preferred_element_type=jnp.float32)
    normed_two_terms = jnp.einsum(
        "rf,df->rd", grad_up_values, up_weight, preferred_element_type=jnp.float32
    )
    norm_value, norm_back = jax.vjp(normalize, hidden_one, gain_two, bias_two)
    grad_hidden, grad_gain_two, grad_bias_two = norm_back(normed_two_terms)
    grad_hidden = grad_hidden + grad_outputs
    hidden_low = grad_hidden.astype(jnp.bfloat16)
    grad_out = jnp.einsum("rc,rd->cd", attended_low, hidden_low, preferred_element_type=jnp.float32)
    grad_attended = (
        jnp.einsum("rd,cd->rc", hidden_low, out_weight, preferred_element_type=jnp.float32)
        .astype(jnp.bfloat16)
        .reshape(queries.shape)
    )
    grad_queries, grad_keys, grad_values = attend_back(
        queries,
        key_all,
        value_all,
        doc_rows,
        seq_lens,
        signed,
        attended,
        log_totals,
        grad_attended,
        offset,
    )
    grad_keys, grad_values = (
        lax.psum_scatter(
            grad_keys.astype(jnp.bfloat16), "tensor", scatter_dimension=0, tiled=True
        ).astype(jnp.float32),
        lax.psum_scatter(
            grad_values.astype(jnp.bfloat16), "tensor", scatter_dimension=0, tiled=True
        ).astype(jnp.float32),
    )
    grad_projected = jnp.concatenate(
        [
            grad_queries.reshape(row_count, width),
            grad_keys.reshape(row_count, width),
            grad_values.reshape(row_count, width),
        ],
        axis=1,
    ).astype(jnp.bfloat16)
    grad_qkv = jnp.einsum(
        "rd,rc->dc", rows_one, grad_projected, preferred_element_type=jnp.float32
    ).reshape(qkv_weight.shape)
    normed_one_terms = jnp.einsum(
        "rc,dc->rd",
        grad_projected,
        qkv_weight.reshape(qkv_weight.shape[0], 3 * width),
        preferred_element_type=jnp.float32,
    )
    norm_value_one, norm_back_one = jax.vjp(normalize, inputs, gain_one, bias_one)
    grad_inputs, grad_gain_one, grad_bias_one = norm_back_one(normed_one_terms)
    grad_inputs = grad_inputs + grad_hidden
    matrices = (
        grad_qkv[None],
        grad_out[None],
        grad_up[None],
        grad_up_bias.reshape(1, -1, FF // lax.axis_size("tensor")),
        grad_down[None],
    )
    vectors = (
        grad_gain_one[None],
        grad_bias_one[None],
        jnp.sum(grad_hidden, axis=0)[None],
        grad_gain_two[None],
        grad_bias_two[None],
        jnp.sum(grad_outputs, axis=0)[None],
    )
    return (grad_inputs, matrices, vectors)


def on_device(
    tokens,
    lengths,
    cotangent,
    ln_one_gain,
    ln_one_bias,
    qkv_weight,
    out_weight,
    out_bias,
    ln_two_gain,
    ln_two_bias,
    up_weight,
    up_bias,
    down_weight,
    down_bias,
):
    signed = lax.axis_index("section") == 0
    params = tuple(
        (
            array_item[0]
            for array_item in (
                ln_one_gain,
                ln_one_bias,
                qkv_weight,
                out_weight,
                out_bias,
                ln_two_gain,
                ln_two_bias,
                up_weight,
                up_bias,
                down_weight,
                down_bias,
            )
        )
    )
    whole = (
        lax.all_gather(qkv_weight, "tensor", axis=3, tiled=True),
        lax.all_gather(out_weight, "tensor", axis=1, tiled=True),
        lax.all_gather(up_weight, "tensor", axis=2, tiled=True),
        lax.all_gather(down_weight, "tensor", axis=1, tiled=True),
    )
    bias_whole = lax.all_gather(up_bias, "tensor", axis=1, tiled=True)
    params = (
        params[0],
        params[1],
        whole[0][0],
        whole[1][0],
        params[4],
        params[5],
        params[6],
        whole[2][0],
        bias_whole[0],
        whole[3][0],
        params[10],
    )
    batches = tokens.shape[0]
    arrived = jnp.zeros(tokens.shape[1:], jnp.bfloat16)
    produced_all = jnp.zeros(tokens.shape, jnp.bfloat16)
    received_all = jnp.zeros(tokens.shape, jnp.bfloat16)
    for tick in range(batches + 1):
        own_index = min(tick, batches - 1)
        prior_index = max(tick - 1, 0)
        inputs_now = jnp.where(signed, tokens[own_index], arrived).astype(jnp.float32)
        lens_now = jnp.where(signed, lengths[own_index], lengths[prior_index])
        produced = forward_layer(inputs_now, lens_now, params, signed, True)[0].astype(jnp.bfloat16)
        if tick < batches:
            produced_all = produced_all.at[tick].set(
                jnp.where(signed, produced, produced_all[tick])
            )
        if tick > 0:
            produced_all = produced_all.at[tick - 1].set(
                jnp.where(signed, produced_all[tick - 1], produced)
            )
            received_all = received_all.at[tick - 1].set(arrived)
        if tick < batches:
            arrived = passed_along(produced, "section", 1)
    block_inputs = jnp.where(signed, tokens, received_all)
    returned = jnp.zeros(tokens.shape[1:], jnp.float32)
    grad_inputs_all = jnp.zeros(tokens.shape, jnp.float32)
    matrix_total = None
    vector_total = None
    for tick in range(batches + 1):
        later_index = batches - 1 - tick if tick < batches else 0
        earlier_index = batches - tick if tick > 0 else 0
        index_now = jnp.where(signed, earlier_index, later_index)
        live_now = jnp.where(signed, tick > 0, tick < batches)
        grad_now = jnp.where(signed, returned, cotangent[later_index].astype(jnp.float32))
        grad_now = jnp.where(live_now, grad_now, 0.0)
        inputs_now = block_inputs[index_now].astype(jnp.float32)
        grad_back, matrices, vectors = backward_layer(
            inputs_now, lengths[index_now], params, signed, grad_now
        )
        if tick == 0:
            matrix_total = tuple(matrices)
            vector_total = tuple(vectors)
        else:
            matrix_total = tuple(
                (
                    jnp.add(total_item, new_item)
                    for total_item, new_item in zip(matrix_total, matrices)
                )
            )
            vector_total = tuple(
                (
                    jnp.add(total_item, new_item)
                    for total_item, new_item in zip(vector_total, vectors)
                )
            )
        if tick > 0:
            grad_inputs_all = grad_inputs_all.at[earlier_index].set(
                jnp.where(signed, grad_back, grad_inputs_all[earlier_index])
            )
        if tick < batches:
            grad_inputs_all = grad_inputs_all.at[later_index].set(
                jnp.where(signed, grad_inputs_all[later_index], grad_back)
            )
            returned = passed_along(grad_back.astype(jnp.bfloat16), "section", -1).astype(
                grad_back.dtype
            )
    matrix_final = (
        lax.psum_scatter(
            matrix_total[0].astype(jnp.bfloat16), "dp", scatter_dimension=1, tiled=True
        ).astype(jnp.float32),
        lax.psum_scatter(
            matrix_total[1].astype(jnp.bfloat16), "dp", scatter_dimension=2, tiled=True
        ).astype(jnp.float32),
        lax.psum_scatter(
            matrix_total[2].astype(jnp.bfloat16), "dp", scatter_dimension=1, tiled=True
        ).astype(jnp.float32),
        lax.psum_scatter(
            matrix_total[3].astype(jnp.bfloat16), "dp", scatter_dimension=2, tiled=True
        ).astype(jnp.float32),
        lax.psum_scatter(
            matrix_total[4].astype(jnp.bfloat16), "dp", scatter_dimension=2, tiled=True
        ).astype(jnp.float32),
    )
    vector_final = (
        lax.psum_scatter(vector_total[0], ("dp", "tensor"), scatter_dimension=1, tiled=True),
        lax.psum_scatter(vector_total[1], ("dp", "tensor"), scatter_dimension=1, tiled=True),
        lax.psum_scatter(vector_total[2], ("dp", "tensor"), scatter_dimension=1, tiled=True),
        lax.psum_scatter(vector_total[3], ("dp", "tensor"), scatter_dimension=1, tiled=True),
        lax.psum_scatter(vector_total[4], ("dp", "tensor"), scatter_dimension=1, tiled=True),
        lax.psum_scatter(vector_total[5], ("dp", "tensor"), scatter_dimension=1, tiled=True),
    )
    matrix_final = (
        lax.psum_scatter(
            matrix_final[0].astype(jnp.bfloat16), "tensor", scatter_dimension=3, tiled=True
        ).astype(jnp.float32),
        lax.psum_scatter(
            matrix_final[1].astype(jnp.bfloat16), "tensor", scatter_dimension=1, tiled=True
        ).astype(jnp.float32),
        lax.psum_scatter(
            matrix_final[2].astype(jnp.bfloat16), "tensor", scatter_dimension=2, tiled=True
        ).astype(jnp.float32),
        lax.psum_scatter(
            matrix_final[3].astype(jnp.bfloat16), "tensor", scatter_dimension=1, tiled=True
        ).astype(jnp.float32),
        lax.psum_scatter(
            matrix_final[4].astype(jnp.bfloat16), "tensor", scatter_dimension=1, tiled=True
        ).astype(jnp.float32),
    )
    grad_qkv, grad_out, grad_up, grad_up_bias, grad_down = matrix_final
    grad_gain_one, grad_bias_one, grad_out_bias, grad_gain_two, grad_bias_two, grad_down_bias = (
        vector_final
    )
    return (
        produced_all[None],
        grad_inputs_all[None],
        grad_gain_one,
        grad_bias_one,
        grad_qkv,
        grad_out,
        grad_out_bias,
        grad_gain_two,
        grad_bias_two,
        grad_up,
        grad_up_bias,
        grad_down,
        grad_down_bias,
    )


MESH = pl.DeviceIdType.MESH
PARTS = 4
BLOCK = 256
OWN = 512
WIDTH = 512
PAIRS = 4
TASKS = 5
NEGATIVE = -1e30
LEFT = (((1,), (0,)), ((), ()))
BOTH_LAST = (((1,), (1,)), ((), ()))
BOTH_FIRST = (((0,), (0,)), ((), ()))


def whole_batch_fits(mesh):
    shape = dict(mesh.shape)
    return shape["tensor"] == PARTS and shape["dp"] == PARTS and shape["section"] == 2


def dot(left, right, dims=LEFT):
    return lax.dot_general(left, right, dims, preferred_element_type=jnp.float32)


def place():
    return lax.axis_index("section"), lax.axis_index("dp"), lax.axis_index("tensor")


def blocks_of(core):
    return (core, 3 - core)


def tile_rows(start, count):
    return pl.ds(pl.multiple_of(start, count), count)


def standard(values):
    centre = values - jnp.mean(values, axis=-1, keepdims=True)
    spread = jnp.mean(centre * centre, axis=-1, keepdims=True)
    inverse = lax.rsqrt(spread + 1e-05)
    return centre * inverse, inverse


def standard_back(grads, gain, units, inverse):
    scaled = grads * gain
    inner = jnp.mean(scaled * units, axis=-1, keepdims=True)
    return inverse * (scaled - jnp.mean(scaled, axis=-1, keepdims=True) - units * inner)


def column_sum(values):
    return jnp.sum(values, axis=0, keepdims=True)


def keep_head(values, parity):
    lane = lax.broadcasted_iota(jnp.int32, values.shape, 1)
    return jnp.where((lane < HEAD) == (parity == 0), values, 0.0)


def project(x_ref, vec_ref, weight_ref, normed_t_ref, query_ref, kv_ref, normed_ref):
    gain, bias = vec_ref[0, 0:1, :], vec_ref[0, 1:2, :]

    def norm_rows(index, carry):
        rows = tile_rows(index * 128, 128)
        units, _ = standard(x_ref[rows, :].astype(jnp.float32))
        normed_ref[rows, :] = (units * gain + bias).astype(jnp.bfloat16)
        return carry

    lax.fori_loop(0, OWN // 128, norm_rows, 0)
    normed_t_ref[...] = normed_ref[...].T

    def pair_step(pair, carry):
        out = dot(normed_ref[...], weight_ref[pair])
        queries = out[:, :128] * 0.125
        for parity in range(2):
            query_ref[pair, parity] = keep_head(queries, parity).astype(jnp.bfloat16)
        kv_ref[0, pair] = out[:, 128:256].astype(jnp.bfloat16)
        kv_ref[1, pair] = out[:, 256:].astype(jnp.bfloat16)
        return carry

    lax.fori_loop(0, PAIRS, pair_step, 0)


def task_plan(core):
    first = core == 0
    slots = (0, jnp.where(first, 1, 0), 1, 1, 1)
    keys = (0, jnp.where(first, 0, 1), jnp.where(first, 1, 0), jnp.where(first, 2, 1), jnp.where(first, 3, 2))
    return slots, keys


def attend_rows(signed, query_ref, kv_ref, bias_ref, attended_ref, attended_t_ref, log_ref, logit_ref, factor_ref, stat_ref):
    core = lax.axis_index("section")
    slots, keys = task_plan(core)
    middle_late = core == 0
    lane = lax.broadcasted_iota(jnp.int32, (BLOCK, 128), 1)

    def pair_step(pair, carry):
        outs = [[None, None], [None, None]]
        for parity in range(2):
            tops = []
            for task in range(TASKS):
                rows = tile_rows(slots[task] * BLOCK, BLOCK)
                key_rows = tile_rows(keys[task] * BLOCK, BLOCK)
                scores = dot(query_ref[pair, parity, rows, :], kv_ref[0, pair, key_rows, :], BOTH_LAST)
                if signed:
                    raised = scores * scores + 1.0
                    inverse = lax.rsqrt(raised)
                    factor_ref[task] = scores * inverse
                    scores = raised * inverse
                logits = scores + bias_ref[task]
                logit_ref[task] = logits
                tops.append(jnp.maximum(logits[:, :128], logits[:, 128:]))
            low = jnp.full((BLOCK, 128), NEGATIVE, jnp.float32)
            top_early = jnp.maximum(tops[0], jnp.where(middle_late, low, tops[1]))
            top_late = jnp.maximum(jnp.maximum(tops[2], tops[3]), jnp.maximum(tops[4], jnp.where(middle_late, tops[1], low)))
            max_early = jnp.max(top_early, axis=-1, keepdims=True)
            max_late = jnp.max(top_late, axis=-1, keepdims=True)
            max_middle = jnp.where(middle_late, max_late, max_early)
            shifts = (max_early, max_middle, max_late, max_late, max_late)
            sums, terms = [], []
            for task in range(TASKS):
                key_rows = tile_rows(keys[task] * BLOCK, BLOCK)
                powers = jnp.exp(logit_ref[task] - shifts[task])
                sums.append(powers[:, :128] + powers[:, 128:])
                if signed:
                    powers = powers * factor_ref[task]
                terms.append(dot(powers.astype(jnp.bfloat16), kv_ref[1, pair, key_rows, :]))
            early = jnp.where(middle_late, 0.0, 1.0)
            late = 1.0 - early
            totals = (sums[0] + sums[1] * early, sums[2] + sums[3] + sums[4] + sums[1] * late)
            values = (terms[0] + terms[1] * early, terms[2] + terms[3] + terms[4] + terms[1] * late)
            for slot, top in enumerate((max_early, max_late)):
                total = jnp.sum(totals[slot], axis=-1, keepdims=True)
                outs[slot][parity] = values[slot] / total
                head = pair * 2 + parity
                stat_ref[slot] = jnp.where(lane == head, top + jnp.log(total), stat_ref[slot])
        for slot in range(2):
            merged = jnp.where(lane < HEAD, outs[slot][0], outs[slot][1])
            attended_ref[pair, slot * BLOCK : (slot + 1) * BLOCK, :] = merged
            attended_t_ref[pair, :, slot * BLOCK : (slot + 1) * BLOCK] = merged.T.astype(jnp.bfloat16)
        return carry

    stat_ref[...] = jnp.zeros_like(stat_ref)
    lax.fori_loop(0, PAIRS, pair_step, 0)
    for slot in range(2):
        log_ref[slot] = stat_ref[slot].T[:8, :]


def gelu_both(values):
    lower = 0.5 * (1.0 + lax.erf(values * math.sqrt(0.5)))
    density = jnp.exp(-0.5 * values * values) * (1.0 / math.sqrt(2.0 * math.pi))
    return values * lower, lower + values * density


def feed(x_ref, attended_ref, vec_ref, out_ref, up_ref, down_ref, hidden_ref, normed_t_ref, act_ref, slope_ref, y_ref, normed_ref, wide_ref, sum_ref):
    out_bias = vec_ref[0, 2:3, :]
    gain, bias = vec_ref[0, 3:4, :], vec_ref[0, 4:5, :]
    down_bias = vec_ref[0, 5:6, :]
    sum_ref[...] = jnp.zeros_like(sum_ref)

    def out_step(pair, carry):
        sum_ref[...] += dot(attended_ref[pair].astype(jnp.bfloat16), out_ref[pair])
        return carry

    lax.fori_loop(0, PAIRS, out_step, 0)

    def norm_rows(index, carry):
        rows = tile_rows(index * 128, 128)
        hidden = x_ref[rows, :].astype(jnp.float32) + sum_ref[rows, :] + out_bias
        hidden_ref[rows, :] = hidden
        units, _ = standard(hidden)
        normed_ref[rows, :] = (units * gain + bias).astype(jnp.bfloat16)
        sum_ref[rows, :] = hidden + down_bias
        return carry

    lax.fori_loop(0, OWN // 128, norm_rows, 0)
    normed_t_ref[...] = normed_ref[...].T

    def chunk_step(chunk, carry):
        wide_ref[...] = dot(normed_ref[...], up_ref[chunk])
        up_bias = vec_ref[chunk, 6:7, :]

        def gelu_rows(index, inner):
            rows = tile_rows(index * 32, 32)
            act, slope = gelu_both(wide_ref[rows, :] + up_bias)
            act_ref[chunk, rows, :] = act.astype(jnp.bfloat16)
            slope_ref[chunk, rows, :] = slope.astype(jnp.bfloat16)
            return inner

        lax.fori_loop(0, OWN // 32, gelu_rows, 0)
        sum_ref[...] += dot(act_ref[chunk], down_ref[chunk])
        return carry

    lax.fori_loop(0, PARTS, chunk_step, 0)
    y_ref[...] = sum_ref[...].astype(jnp.bfloat16)


def feed_back(dy_ref, act_ref, slope_ref, down_ref, up_ref, hidden_ref, normed_t_ref, vec_ref, out_ref, attended_ref, attended_t_ref, grad_hidden_ref, grad_att_ref, centre_ref, grads_ref, vec_grad_ref, low_ref, low_t_ref, chunk_ref, sum_ref):
    gain = vec_ref[0, 3:4, :]
    low_ref[...] = dy_ref[...].astype(jnp.bfloat16)
    low_t_ref[...] = low_ref[...].T
    vec_grad_ref[...] = jnp.zeros_like(vec_grad_ref)
    sum_ref[...] = jnp.zeros_like(sum_ref)

    def chunk_step(chunk, carry):
        grad_act = dot(low_ref[...], down_ref[chunk], BOTH_LAST)
        grad_up = (grad_act * slope_ref[chunk].astype(jnp.float32)).astype(jnp.bfloat16)
        chunk_ref[...] = grad_up
        vec_grad_ref[pl.ds(6 + chunk, 1), :] = column_sum(grad_up.astype(jnp.float32))
        down_term = dot(low_t_ref[...], act_ref[chunk]).astype(jnp.bfloat16)
        up_term = dot(normed_t_ref[...], chunk_ref[...]).astype(jnp.bfloat16)
        for part in range(PARTS):
            grads_ref[part, chunk, :, 0:512] = down_term[part * 128 : (part + 1) * 128, :]
            grads_ref[part, chunk, :, 512:1024] = up_term[part * 128 : (part + 1) * 128, :]
        sum_ref[...] += dot(chunk_ref[...], up_ref[chunk], BOTH_LAST)
        return carry

    lax.fori_loop(0, PARTS, chunk_step, 0)

    def norm_rows(index, carry):
        rows = tile_rows(index * 128, 128)
        grads, dy = sum_ref[rows, :], dy_ref[rows, :]
        units, inverse = standard(hidden_ref[rows, :])
        grad_hidden = dy + standard_back(grads, gain, units, inverse)
        grad_hidden_ref[rows, :] = grad_hidden
        low_ref[rows, :] = grad_hidden.astype(jnp.bfloat16)
        vec_grad_ref[2:3, :] += column_sum(grad_hidden)
        vec_grad_ref[3:4, :] += column_sum(grads * units)
        vec_grad_ref[4:5, :] += column_sum(grads)
        vec_grad_ref[5:6, :] += column_sum(dy)
        return carry

    lax.fori_loop(0, OWN // 128, norm_rows, 0)
    row = lax.broadcasted_iota(jnp.int32, (8, 128), 0)
    lane = lax.broadcasted_iota(jnp.int32, (8, 128), 1)
    picks = jnp.where((row < 2) & ((lane < HEAD) == (row == 0)), 1.0, 0.0)

    def pair_step(pair, carry):
        out_term = dot(attended_t_ref[pair], low_ref[...]).astype(jnp.bfloat16)
        for part in range(PARTS):
            grads_ref[part, pair, :, 1024:1152] = out_term[:, part * 128 : (part + 1) * 128]
        grad_att = dot(low_ref[...], out_ref[pair], BOTH_LAST).astype(jnp.bfloat16)
        wide = grad_att.astype(jnp.float32)
        for parity in range(2):
            grad_att_ref[pair, parity] = keep_head(wide, parity).astype(jnp.bfloat16)
        centres = lax.dot_general(picks, wide * attended_ref[pair], BOTH_LAST, precision=lax.Precision.HIGHEST, preferred_element_type=jnp.float32)
        centre_ref[pair] = centres
        return carry

    lax.fori_loop(0, PAIRS, pair_step, 0)


def attend_rows_back(signed, query_ref, kv_ref, grad_att_ref, bias_ref, log_ref, centre_ref, grad_query_ref, grad_kv_ref, grad_kv_low_ref):
    core = lax.axis_index("section")
    slots, keys = task_plan(core)
    early = jnp.where(core == 0, 0.0, 1.0)
    lane = lax.broadcasted_iota(jnp.int32, (BLOCK, 128), 1)
    grad_kv_ref[...] = jnp.zeros_like(grad_kv_ref)

    def pair_step(pair, carry):
        parts = [[None] * TASKS, [None] * TASKS]
        for task in range(TASKS):
            rows = tile_rows(slots[task] * BLOCK, BLOCK)
            key_rows = tile_rows(keys[task] * BLOCK, BLOCK)
            key_part, value_part = kv_ref[0, pair, key_rows, :], kv_ref[1, pair, key_rows, :]
            key_term, value_term = None, None
            for parity in range(2):
                queries = query_ref[pair, parity, rows, :]
                grad_att = grad_att_ref[pair, parity, rows, :]
                scores = dot(key_part, queries, BOTH_LAST)
                grad_weights = dot(value_part, grad_att, BOTH_LAST)
                log_row = log_ref[slots[task], pl.ds(pair * 2 + parity, 1), :]
                centre = centre_ref[pair, parity : parity + 1, rows]
                if signed:
                    raised = scores * scores + 1.0
                    inverse = lax.rsqrt(raised)
                    factor = scores * inverse
                    probs = jnp.exp(raised * inverse + bias_ref[task] - log_row)
                    weights = factor * probs
                    grad_scores = weights * (factor * grad_weights - centre)
                    grad_scores = grad_scores + probs * grad_weights * (inverse * inverse * inverse)
                else:
                    weights = jnp.exp(scores + bias_ref[task] - log_row)
                    grad_scores = weights * (grad_weights - centre)
                grad_low = grad_scores.astype(jnp.bfloat16)
                new_key = dot(grad_low, queries)
                new_value = dot(weights.astype(jnp.bfloat16), grad_att)
                key_term = new_key if parity == 0 else key_term + new_key
                value_term = new_value if parity == 0 else value_term + new_value
                parts[parity][task] = dot(grad_low, key_part, BOTH_FIRST)
            grad_kv_ref[0, pair, key_rows, :] += key_term
            grad_kv_ref[1, pair, key_rows, :] += value_term
        merged = []
        for task in range(TASKS):
            merged.append(jnp.where(lane < HEAD, parts[0][task], parts[1][task]))
        grad_query_ref[pair, :BLOCK, :] = ((merged[0] + merged[1] * early) * 0.125).astype(jnp.bfloat16)
        grad_query_ref[pair, BLOCK:, :] = ((merged[1] * (1.0 - early) + merged[2] + merged[3] + merged[4]) * 0.125).astype(jnp.bfloat16)
        grad_kv_low_ref[0, pair] = grad_kv_ref[0, pair].astype(jnp.bfloat16)
        grad_kv_low_ref[1, pair] = grad_kv_ref[1, pair].astype(jnp.bfloat16)
        return carry

    lax.fori_loop(0, PAIRS, pair_step, 0)


def project_back(grad_query_ref, grad_kv_ref, other_ref, x_ref, grad_hidden_ref, normed_t_ref, weight_ref, vec_ref, grad_x_ref, grads_ref, vec_grad_ref, sum_ref):
    core = lax.axis_index("section")
    gain = vec_ref[0, 0:1, :]
    sum_ref[...] = jnp.zeros_like(sum_ref)
    vec_grad_ref[...] = jnp.zeros_like(vec_grad_ref)

    def pair_step(pair, carry):
        parts = [grad_query_ref[pair]]
        for kind in range(2):
            halves = []
            for slot, block in enumerate(blocks_of(core)):
                own = grad_kv_ref[kind, pair, tile_rows(block * BLOCK, BLOCK), :]
                halves.append(own + other_ref[kind, pair, slot * BLOCK : (slot + 1) * BLOCK, :].astype(jnp.float32))
            parts.append(jnp.concatenate(halves, axis=0).astype(jnp.bfloat16))
        grads = jnp.concatenate(parts, axis=1)
        term = dot(normed_t_ref[...], grads).astype(jnp.bfloat16)
        for part in range(PARTS):
            grads_ref[part, pair] = term[part * 128 : (part + 1) * 128, :]
        sum_ref[...] += dot(grads, weight_ref[pair], BOTH_LAST)
        return carry

    lax.fori_loop(0, PAIRS, pair_step, 0)

    def norm_rows(index, carry):
        rows = tile_rows(index * 128, 128)
        grads = sum_ref[rows, :]
        units, inverse = standard(x_ref[rows, :].astype(jnp.float32))
        grad_x_ref[rows, :] = grad_hidden_ref[rows, :] + standard_back(grads, gain, units, inverse)
        vec_grad_ref[0:1, :] += column_sum(grads * units)
        vec_grad_ref[1:2, :] += column_sum(grads)
        return carry

    lax.fori_loop(0, OWN // 128, norm_rows, 0)


def greet(partners):
    barrier = pltpu.get_barrier_semaphore()
    for partner in partners:
        pl.semaphore_signal(barrier, inc=1, device_id=partner, device_id_type=MESH)
    pl.semaphore_wait(barrier, len(partners))


def along_tensor(step):
    core, rep, part = place()
    return (core, rep, lax.rem(part + step, PARTS))


def along_dp(step):
    core, rep, part = place()
    return (core, lax.bitwise_xor(rep, step), part)


def sibling():
    core, rep, part = place()
    return (1 - core, rep, part)


def all_partners():
    return [along_tensor(step) for step in (1, 2, 3)] + [along_dp(step) for step in (1, 2, 3)] + [sibling()]


def remote(source, target, send, receive, device):
    return pltpu.make_async_remote_copy(src_ref=source, dst_ref=target, send_sem=send, recv_sem=receive, device_id=device, device_id_type=MESH)


def gather_kernel(tokens, cotangent, qkv, out, up, down, vec, x_ref, dy_ref, qkv_all, out_all, up_all, down_all, vec_all, tok_send, tok_recv, z_send, z_recv, xy_send, xy_recv, sib_send, sib_recv, local):
    core, rep, part = place()
    greet(all_partners())
    owner = jnp.where((part == 0) | (part == 3), 0, 1)
    slot = jnp.where(part < 2, 0, 1)
    shards = (qkv, out, up, down, vec)
    wholes = (qkv_all, out_all, up_all, down_all, vec_all)

    def row_copies(array, source, target, batch):
        there = remote(source.at[batch], target.at[slot], tok_send.at[array, batch], tok_recv.at[array, slot], (core, rep, batch))
        here = pltpu.make_async_copy(source.at[batch], target.at[slot], tok_send.at[array, batch])
        return there, here

    def each_row_copy(act):
        for array, (source, target) in enumerate(((tokens, x_ref), (cotangent, dy_ref))):
            for batch in range(PARTS):
                there, here = row_copies(array, source, target, batch)

                @pl.when((core == owner) & (part != batch))
                def _():
                    if act == "start":
                        there.start()
                    else:
                        there.wait_send()

                @pl.when((core == owner) & (part == batch))
                def _():
                    if act == "start":
                        here.start()
                    else:
                        here.wait()

    each_row_copy("start")

    def quarter(index, which):
        count = shards[index].shape[0] // PARTS
        return pl.ds(pl.multiple_of(which * count, count), count)

    z_copies = []
    for index in range(5):
        own = pltpu.make_async_copy(shards[index], wholes[index].at[core, part], local.at[index])
        own.start()
        row = []
        for step in (1, 2, 3):
            if index < 4:
                rows = quarter(index, rep)
                copy = remote(shards[index].at[rows], wholes[index].at[core, part, rows], z_send.at[index, step - 1], z_recv.at[index, step - 1], along_tensor(step))
            else:
                copy = remote(shards[index], wholes[index].at[core, part], z_send.at[index, step - 1], z_recv.at[index, step - 1], along_tensor(step))
            copy.start()
            row.append(copy)
        z_copies.append(row)
    xy_copies = []
    for index in range(5):
        pltpu.make_async_copy(shards[index], wholes[index].at[core, part], local.at[index]).wait()
        for copy in z_copies[index]:
            copy.wait_recv()
        row = []
        if index < 4:
            rows = quarter(index, rep)
            for step in (1, 2, 3):
                for far in (1, 2, 3):
                    other = lax.rem(part + far, PARTS)
                    view = wholes[index].at[core, other, rows]
                    copy = remote(view, view, xy_send.at[index, step - 1, far - 1], xy_recv.at[index, step - 1, far - 1], along_dp(step))
                    copy.start()
                    row.append(copy)
        xy_copies.append(row)
    sib_copies = []
    for index in range(5):
        for copy in xy_copies[index]:
            copy.wait_recv()
        view = wholes[index].at[core]
        copy = remote(view, view, sib_send.at[index], sib_recv.at[index], sibling())
        copy.start()
        sib_copies.append(copy)
    for array, (source, target) in enumerate(((tokens, x_ref), (cotangent, dy_ref))):
        for place_of, block in enumerate(blocks_of(core)):

            @pl.when(block != part)
            def _():
                remote(source.at[0], target.at[place_of], tok_send.at[array, 0], tok_recv.at[array, place_of], sibling()).wait_recv()

    each_row_copy("wait")
    for row in z_copies:
        for copy in row:
            copy.wait_send()
    for row in xy_copies:
        for copy in row:
            copy.wait_send()
    for copy in sib_copies:
        copy.wait_send()
        copy.wait_recv()


def exchange_kernel(own_ref, all_ref, send, receive, local):
    core = lax.axis_index("section")
    greet([sibling()])
    copies = []
    for slot, block in enumerate(blocks_of(core)):
        source = own_ref.at[:, :, slot * BLOCK : (slot + 1) * BLOCK, :]
        target = all_ref.at[:, :, tile_rows(block * BLOCK, BLOCK), :]
        copies.append(remote(source, target, send.at[slot], receive.at[slot], sibling()))
        copies.append(pltpu.make_async_copy(source, target, local.at[slot]))
    for copy in copies:
        copy.start()
    for copy in copies:
        copy.wait()


def return_kernel(all_ref, got_ref, send, receive):
    core = lax.axis_index("section")
    greet([sibling()])
    copies = []
    for slot, block in enumerate(blocks_of(1 - core)):
        source = all_ref.at[:, :, tile_rows(block * BLOCK, BLOCK), :]
        target = got_ref.at[:, :, slot * BLOCK : (slot + 1) * BLOCK, :]
        copies.append(remote(source, target, send.at[slot], receive.at[slot], sibling()))
    for copy in copies:
        copy.start()
    for copy in copies:
        copy.wait()


GRAD_COLUMNS = ((0, 1152), (1152, 1536))


def reduce_kernel(early_one, early_two, late_one, late_two, vec_ref, out_ref, vec_out_ref, got_core, chip, got_dp, part_sum, got_part, final, vec_core, vec_chip, vec_dp, vec_rep, vec_part, core_send, core_recv, dp_send, dp_recv, part_send, part_recv, vec_send, vec_recv, last_send, last_recv):
    core, rep, part = place()
    greet(all_partners())
    grads = ((early_one, late_one), (early_two, late_two))
    mine, theirs = tile_rows(core * 64, 64), tile_rows((1 - core) * 64, 64)
    vec_copy = remote(vec_ref.at[1 - core], vec_core, vec_send.at[0], vec_recv.at[0], sibling())
    vec_copy.start()
    copies = {}
    for layer in (1, 0):
        for kind, (first, last) in enumerate(GRAD_COLUMNS):
            copy = remote(grads[layer][kind].at[:, :, theirs, :], got_core.at[layer, :, :, :, first:last], core_send.at[layer, kind], core_recv.at[layer, kind], sibling())
            copy.start()
            copies["core", layer, kind] = copy
    for layer in (1, 0):
        for kind, (first, last) in enumerate(GRAD_COLUMNS):
            copies["core", layer, kind].wait_recv()

            def add_core(index, carry):
                major, minor = index // PARTS, lax.rem(index, PARTS)
                own = grads[layer][kind][major, minor, mine, :].astype(jnp.float32)
                total = own + got_core[layer, major, minor, :, first:last].astype(jnp.float32)
                chip[layer, major, minor, :, first:last] = total.astype(jnp.bfloat16)
                return carry

            lax.fori_loop(0, PARTS * PARTS, add_core, 0)
        for step in (1, 2, 3):
            copy = remote(chip.at[layer, lax.bitwise_xor(rep, step)], got_dp.at[layer, step - 1], dp_send.at[layer, step - 1], dp_recv.at[layer, step - 1], along_dp(step))
            copy.start()
            copies["dp", layer, step] = copy
    vec_copy.wait()
    vec_chip[...] = vec_ref[core] + vec_core[...]
    vec_copies = [remote(vec_chip, vec_dp.at[step - 1], vec_send.at[step], vec_recv.at[step], along_dp(step)) for step in (1, 2, 3)]
    for copy in vec_copies:
        copy.start()
    for layer in (1, 0):
        for step in (1, 2, 3):
            copies["dp", layer, step].wait_recv()
        for minor in range(PARTS):
            total = chip[layer, rep, minor].astype(jnp.float32)
            for step in (1, 2, 3):
                total = total + got_dp[layer, step - 1, minor].astype(jnp.float32)
            part_sum[layer, minor] = total.astype(jnp.bfloat16)
        for step in (1, 2, 3):
            copy = remote(part_sum.at[layer, lax.rem(part + step, PARTS)], got_part.at[layer, step - 1], part_send.at[layer, step - 1], part_recv.at[layer, step - 1], along_tensor(step))
            copy.start()
            copies["part", layer, step] = copy
    for copy in vec_copies:
        copy.wait()
    vec_rep[...] = vec_chip[...] + vec_dp[0] + vec_dp[1] + vec_dp[2]
    vec_copies = [remote(vec_rep, vec_part.at[step - 1], vec_send.at[3 + step], vec_recv.at[3 + step], along_tensor(step)) for step in (1, 2, 3)]
    for copy in vec_copies:
        copy.start()
    for layer in (1, 0):
        for step in (1, 2, 3):
            copies["part", layer, step].wait_recv()
        total = part_sum[layer, part].astype(jnp.float32)
        for step in (1, 2, 3):
            total = total + got_part[layer, step - 1].astype(jnp.float32)
        final[layer] = total
    last_copy = remote(final.at[1 - core], out_ref.at[mine], last_send, last_recv, sibling())
    last_copy.start()
    out_ref[mine, :] = final[core]
    for copy in vec_copies:
        copy.wait()
    vec_out_ref[...] = vec_rep[...] + vec_part[0] + vec_part[1] + vec_part[2]
    for copy in copies.values():
        copy.wait_send()
    last_copy.wait()


def deliver_kernel(first_y, second_y, second_grad, first_grad, y_ref, grad_ref, send, receive):
    core, rep, part = place()
    greet([along_tensor(step) for step in (1, 2, 3)] + [(1 - core, rep, lax.rem(part + step, PARTS)) for step in range(4)])
    sources = ((first_y, second_y), (first_grad, second_grad))
    targets = (y_ref, grad_ref)

    def each(act):
        for kind in range(2):
            for layer in range(2):
                for slot, block in enumerate(blocks_of(core)):
                    source = sources[kind][layer].at[slot * BLOCK : (slot + 1) * BLOCK]
                    target = targets[kind].at[part]
                    semaphore = send.at[kind, layer, slot]
                    stays = (core == layer) & (block == part)

                    @pl.when(stays)
                    def _():
                        copy = pltpu.make_async_copy(source, target, semaphore)
                        copy.start() if act == "start" else copy.wait()

                    @pl.when(jnp.logical_not(stays))
                    def _():
                        copy = remote(source, target, semaphore, receive.at[kind, part], (layer, rep, block))
                        copy.start() if act == "start" else copy.wait_send()

    each("start")
    owner = jnp.where((part == 0) | (part == 3), 0, 1)
    for kind in range(2):
        for batch in range(PARTS):

            @pl.when((core != owner) | (part != batch))
            def _():
                remote(sources[kind][0].at[:BLOCK], targets[kind].at[batch], send.at[kind, 0, 0], receive.at[kind, batch], sibling()).wait_recv()

    each("wait")


def call(body, name, ins, outs, scratch=(), collective=None, space=pltpu.VMEM):
    dma = pltpu.SemaphoreType.DMA
    shapes = [dma(item) if isinstance(item, tuple) else item for item in scratch]
    params = dict(vmem_limit_bytes=56 * 2**20)
    if collective is not None:
        params.update(collective_id=collective, has_side_effects=True)
    return pl.pallas_call(
        body,
        out_shape=[jax.ShapeDtypeStruct(shape, kind) for shape, kind in outs],
        in_specs=[pl.BlockSpec(memory_space=space)] * len(ins),
        out_specs=[pl.BlockSpec(memory_space=space)] * len(outs),
        scratch_shapes=shapes,
        compiler_params=pltpu.CompilerParams(**params),
        name=name,
    )(*ins)


def mask_terms(lens, core):
    bounds = jnp.cumsum(lens)
    first = core == 0
    slots = jnp.where(first, jnp.array([0, 1, 1, 1, 1]), jnp.array([0, 0, 1, 1, 1]))
    keys = jnp.where(first, jnp.array([0, 0, 1, 2, 3]), jnp.array([0, 1, 0, 1, 2]))
    blocks = jnp.where(slots == 0, core, 3 - core)
    places = jnp.arange(BLOCK, dtype=jnp.int32)
    query = blocks[:, None] * BLOCK + places[None, :]
    key = keys[:, None] * BLOCK + places[None, :]
    starts = jnp.max(jnp.where(bounds[None, None, :] <= query[:, :, None], bounds[None, None, :], 0), axis=-1)
    straight = (key[:, None, :] >= starts[:, :, None]) & (key[:, None, :] <= query[:, :, None])
    turned = (key[:, :, None] >= starts[:, None, :]) & (key[:, :, None] <= query[:, None, :])
    return jnp.where(straight, 0.0, NEGATIVE), jnp.where(turned, 0.0, NEGATIVE)


def on_device_whole(
    tokens,
    lengths,
    cotangent,
    ln_one_gain,
    ln_one_bias,
    qkv_weight,
    out_weight,
    out_bias,
    ln_two_gain,
    ln_two_bias,
    up_weight,
    up_bias,
    down_weight,
    down_bias,
):
    f32, low = jnp.float32, jnp.bfloat16
    vmem = pltpu.VMEM
    core, rep, part = place()
    vec = jnp.concatenate([ln_one_gain, ln_one_bias, out_bias, ln_two_gain, ln_two_bias, down_bias, up_bias, jnp.zeros_like(up_bias)])
    lens = lax.dynamic_index_in_dim(lengths, part, 0, keepdims=False)
    bias, bias_turned = mask_terms(lens, core)
    x_rows, dy_rows, qkv_all, out_all, up_all, down_all, vec_all = call(
        gather_kernel,
        "gather",
        (tokens, cotangent, qkv_weight.reshape(WIDTH, 384), out_weight[0], up_weight[0], down_weight[0], vec),
        (
            ((2, BLOCK, WIDTH), low),
            ((2, BLOCK, WIDTH), low),
            ((2, PARTS, 512, 384), low),
            ((2, PARTS, 128, 512), low),
            ((2, PARTS, 512, 512), low),
            ((2, PARTS, 512, 512), low),
            ((2, PARTS, 8, 512), f32),
        ),
        ((2, 4), (2, 2), (5, 3), (5, 3), (4, 3, 3), (4, 3, 3), (5,), (5,), (5,)),
        collective=0,
        space=pl.ANY,
    )
    inputs = x_rows.reshape(OWN, WIDTH)
    saved, produced = [], []
    for layer in range(2):
        signed = layer == 0
        qkv, out, up, down, vecs = qkv_all[layer], out_all[layer], up_all[layer], down_all[layer], vec_all[layer]
        normed_one_t, queries, kv = call(
            project,
            f"project{layer}",
            (inputs, vecs, qkv),
            (((WIDTH, OWN), low), ((PAIRS, 2, OWN, 128), low), ((2, PAIRS, OWN, 128), low)),
            (vmem((OWN, WIDTH), low),),
        )
        (kv_all,) = call(
            exchange_kernel, f"exchange{layer}", (kv,), (((2, PAIRS, 1024, 128), low),), ((2,), (2,), (2,)), collective=1 + layer, space=pl.ANY
        )
        attended, attended_t, logs = call(
            partial(attend_rows, signed),
            f"attend{layer}",
            (queries, kv_all, bias),
            (((PAIRS, OWN, 128), f32), ((PAIRS, 128, OWN), low), ((2, 8, BLOCK), f32)),
            (vmem((TASKS, BLOCK, BLOCK), f32), vmem((TASKS, BLOCK, BLOCK), f32), vmem((2, BLOCK, 128), f32)),
        )
        hidden, normed_two_t, act, slope, y = call(
            feed,
            f"feed{layer}",
            (inputs, attended, vecs, out, up, down),
            (((OWN, WIDTH), f32), ((WIDTH, OWN), low), ((PARTS, OWN, 512), low), ((PARTS, OWN, 512), low), ((OWN, WIDTH), low)),
            (vmem((OWN, WIDTH), low), vmem((OWN, 512), f32), vmem((OWN, WIDTH), f32)),
        )
        saved.append((inputs, normed_one_t, queries, kv_all, attended, attended_t, logs, hidden, normed_two_t, act, slope))
        produced.append(y)
        inputs = y
    dy = dy_rows.reshape(OWN, WIDTH).astype(f32)
    early, late, vec_grads, input_grads = [None, None], [None, None], [None, None], [None, None]
    for layer in (1, 0):
        signed = layer == 0
        qkv, out, up, down, vecs = qkv_all[layer], out_all[layer], up_all[layer], down_all[layer], vec_all[layer]
        inputs, normed_one_t, queries, kv_all, attended, attended_t, logs, hidden, normed_two_t, act, slope = saved[layer]
        grad_hidden, grad_att, centres, early[layer], vec_one = call(
            feed_back,
            f"feed_back{layer}",
            (dy, act, slope, down, up, hidden, normed_two_t, vecs, out, attended, attended_t),
            (((OWN, WIDTH), f32), ((PAIRS, 2, OWN, 128), low), ((PAIRS, 8, OWN), f32), ((PARTS, PARTS, 128, 1152), low), ((16, 512), f32)),
            (vmem((OWN, WIDTH), low), vmem((WIDTH, OWN), low), vmem((OWN, 512), low), vmem((OWN, WIDTH), f32)),
        )
        grad_query, grad_kv, grad_kv_low = call(
            partial(attend_rows_back, signed),
            f"attend_back{layer}",
            (queries, kv_all, grad_att, bias_turned, logs, centres),
            (((PAIRS, OWN, 128), low), ((2, PAIRS, 1024, 128), f32), ((2, PAIRS, 1024, 128), low)),
        )
        (other,) = call(
            return_kernel, f"return{layer}", (grad_kv_low,), (((2, PAIRS, OWN, 128), low),), ((2,), (2,)), collective=3 + layer, space=pl.ANY
        )
        dy, late[layer], vec_two = call(
            project_back,
            f"project_back{layer}",
            (grad_query, grad_kv, other, inputs, grad_hidden, normed_one_t, qkv, vecs),
            (((OWN, WIDTH), f32), ((PARTS, PARTS, 128, 384), low), ((16, 512), f32)),
            (vmem((OWN, WIDTH), f32),),
        )
        vec_grads[layer] = vec_one + vec_two
        input_grads[layer] = dy.astype(low)
    grads, vec_sum = call(
        reduce_kernel,
        "reduce",
        (early[0], early[1], late[0], late[1], jnp.stack(vec_grads)),
        (((128, 1536), f32), ((16, 512), f32)),
        (
            vmem((2, PARTS, PARTS, 64, 1536), low),
            vmem((2, PARTS, PARTS, 64, 1536), low),
            vmem((2, 3, PARTS, 64, 1536), low),
            vmem((2, PARTS, 64, 1536), low),
            vmem((2, 3, 64, 1536), low),
            vmem((2, 64, 1536), f32),
            vmem((16, 512), f32),
            vmem((16, 512), f32),
            vmem((3, 16, 512), f32),
            vmem((16, 512), f32),
            vmem((3, 16, 512), f32),
            (2, 2),
            (2, 2),
            (2, 3),
            (2, 3),
            (2, 3),
            (2, 3),
            (7,),
            (7,),
            pltpu.SemaphoreType.DMA,
            pltpu.SemaphoreType.DMA,
        ),
        collective=5,
    )
    block_outputs, grad_inputs = call(
        deliver_kernel,
        "deliver",
        (produced[0], produced[1], input_grads[1], input_grads[0]),
        (((PARTS, BLOCK, WIDTH), low), ((PARTS, BLOCK, WIDTH), low)),
        ((2, 2, 2), (2, 4)),
        collective=6,
        space=pl.ANY,
    )
    spread = lax.dynamic_slice_in_dim(vec_sum, (rep * PARTS + part) * 32, 32, 1)
    up_bias_grad = lax.dynamic_slice(vec_sum, (6 + part, rep * 128), (1, 128))
    return (
        block_outputs[None],
        grad_inputs.astype(f32)[None],
        spread[0:1],
        spread[1:2],
        grads[:, 1152:].reshape(1, 128, 3, 128),
        grads[None, :, 1024:1152],
        spread[2:3],
        spread[3:4],
        spread[4:5],
        grads[None, :, 512:1024],
        up_bias_grad[None],
        grads[:, :512].T[None],
        spread[5:6],
    )


def solution(mesh):
    return jax.shard_map(
        on_device_whole if whole_batch_fits(mesh) else on_device,
        mesh=mesh,
        in_specs=(
            P("dp", "tensor", None),
            P("dp", None),
            P("dp", "tensor", None),
            P("section", None),
            P("section", None),
            P("section", None, None, "tensor"),
            P("section", "tensor", None),
            P("section", None),
            P("section", None),
            P("section", None),
            P("section", None, "tensor"),
            P("section", "tensor"),
            P("section", "tensor", None),
            P("section", None),
        ),
        out_specs=(
            P("section", "dp", "tensor", None),
            P("section", "dp", "tensor", None),
            P("section", ("dp", "tensor")),
            P("section", ("dp", "tensor")),
            P("section", "dp", None, "tensor"),
            P("section", "tensor", "dp"),
            P("section", ("dp", "tensor")),
            P("section", ("dp", "tensor")),
            P("section", ("dp", "tensor")),
            P("section", "dp", "tensor"),
            P("section", "tensor", "dp"),
            P("section", "tensor", "dp"),
            P("section", ("dp", "tensor")),
        ),
        check_vma=False,
    )
```

```python
from functools import partial
import math

import jax
import jax.numpy as jnp
from jax import lax
from jax.experimental import pallas as pl
from jax.experimental.pallas import tpu as pltpu
from jax.sharding import PartitionSpec as P

HEAD = 64
FF = 2048


def passed_along(block, axis, distance):
    devices = range(lax.axis_size(axis))
    route = [(i - distance, i) for i in devices if i - distance in devices]
    return lax.ppermute(block, axis, route)


def normalize(values, gain_vec, bias_vec):
    centre = values - jnp.mean(values, axis=-1, keepdims=True)
    spread = jnp.mean(centre * centre, axis=-1, keepdims=True)
    return centre * lax.rsqrt(spread + 1e-05) * gain_vec + bias_vec


def document_ids(seq_lens, row_count):
    bounds = jnp.cumsum(seq_lens)
    places = jnp.arange(row_count, dtype=jnp.int32)
    return jnp.sum((places[:, None] >= bounds[None, :]).astype(jnp.int32), axis=1)


def first_key_block(doc_number, seq_lens, block):
    starts = jnp.cumsum(seq_lens) - seq_lens
    numbers = jnp.arange(seq_lens.shape[0], dtype=jnp.int32)
    return jnp.sum(jnp.where(numbers == doc_number, starts, 0)) // block


def grouped_sum(left, right, groups):
    row_count, inner = left.shape
    terms = jnp.einsum(
        "rgc,gcd->grd",
        left.reshape(row_count, groups, inner // groups),
        right.reshape(groups, inner // groups, right.shape[-1]),
        preferred_element_type=jnp.float32,
    )
    return jnp.sum(lax.optimization_barrier(terms.astype(jnp.bfloat16)).astype(jnp.float32), axis=0)


def branch_total(left, right):
    return grouped_sum(left, right, lax.axis_size("tensor"))


def key_scores(query_rows, key_part, query_docs, key_docs, query_first, key_first, signed):
    scale = 1.0 / math.sqrt(query_rows.shape[-1])
    scores = (
        jnp.einsum("qhe,khe->hqk", query_rows, key_part, preferred_element_type=jnp.float32) * scale
    )
    query_places = query_first + jnp.arange(query_rows.shape[0], dtype=jnp.int32)
    key_places = key_first + jnp.arange(key_part.shape[0], dtype=jnp.int32)
    allowed = (query_docs[:, None] == key_docs[None, :]) & (
        query_places[:, None] >= key_places[None, :]
    )
    modulus = jnp.sqrt(scores * scores + 1.0)
    logits = jnp.where(signed, modulus, scores)
    factor = jnp.where(signed, scores / modulus, 1.0)
    return (modulus, logits, factor, allowed[None])


def attend(queries, key_rows, values, doc_rows, seq_lens, signed, offset):
    query_count, heads_here, head_size = queries.shape
    key_count = key_rows.shape[0]
    query_block = min(512, query_count)
    key_block = min(512, key_count)
    query_first = offset + 0
    query_docs = lax.dynamic_slice_in_dim(doc_rows, query_first, query_block, 0)
    lowest = first_key_block(query_docs[0], seq_lens, key_block)
    upper = (query_first + query_block - 1) // key_block + 1

    def block_scores(key_index):
        key_first = key_index * key_block
        return key_scores(
            queries,
            lax.dynamic_slice_in_dim(key_rows, key_first, key_block, 0),
            query_docs,
            lax.dynamic_slice_in_dim(doc_rows, key_first, key_block, 0),
            query_first,
            key_first,
            signed,
        )

    def measure(key_index, carry):
        running_max, running_sum = carry
        modulus, logits, factor, allowed = block_scores(key_index)
        masked = jnp.where(allowed, logits, -1e30)
        new_max = jnp.maximum(running_max, jnp.max(masked, axis=-1))
        added = jnp.sum(jnp.where(allowed, jnp.exp(masked - new_max[:, :, None]), 0.0), axis=-1)
        return (new_max, running_sum * jnp.exp(running_max - new_max) + added)

    start_max = jnp.full((heads_here, query_block), -1e30, jnp.float32)
    start_sum = jnp.zeros((heads_here, query_block), jnp.float32)
    row_max, row_sum = lax.fori_loop(lowest, upper, measure, (start_max, start_sum))
    log_total = row_max + jnp.log(row_sum)

    def accumulate(key_index, partial_out):
        modulus, logits, factor, allowed = block_scores(key_index)
        probs = jnp.where(allowed, jnp.exp(logits - log_total[:, :, None]), 0.0)
        weights = (factor * probs).astype(jnp.bfloat16)
        value_rows = lax.dynamic_slice_in_dim(values, key_index * key_block, key_block, 0)
        return partial_out + jnp.einsum(
            "hqk,khe->qhe", weights, value_rows, preferred_element_type=jnp.float32
        )

    outputs_list = lax.fori_loop(
        lowest, upper, accumulate, jnp.zeros((query_block, heads_here, head_size), jnp.float32)
    )
    return (outputs_list, log_total)


def attend_back(
    queries,
    key_rows,
    values,
    doc_rows,
    seq_lens,
    signed,
    attended,
    log_totals,
    grad_attended,
    offset,
):
    query_count, heads_here, head_size = queries.shape
    key_count = key_rows.shape[0]
    query_block = min(512, query_count)
    key_block = min(512, key_count)
    scale = 1.0 / math.sqrt(head_size)
    centre_terms = jnp.sum(grad_attended.astype(jnp.float32) * attended, axis=-1).T
    grad_keys = jnp.zeros(key_rows.shape, jnp.float32)
    grad_values = jnp.zeros(key_rows.shape, jnp.float32)
    query_first = offset + 0
    query_docs = lax.dynamic_slice_in_dim(doc_rows, query_first, query_block, 0)
    lowest = first_key_block(query_docs[0], seq_lens, key_block)
    upper = (query_first + query_block - 1) // key_block + 1

    def backward_step(key_index, carry):
        grad_query, keys_total, values_total = carry
        key_first = key_index * key_block
        key_part = lax.dynamic_slice_in_dim(key_rows, key_first, key_block, 0)
        value_rows = lax.dynamic_slice_in_dim(values, key_first, key_block, 0)
        modulus, logits, factor, allowed = key_scores(
            queries,
            key_part,
            query_docs,
            lax.dynamic_slice_in_dim(doc_rows, key_first, key_block, 0),
            query_first,
            key_first,
            signed,
        )
        probs = jnp.where(allowed, jnp.exp(logits - log_totals[:, :, None]), 0.0)
        weights = (factor * probs).astype(jnp.bfloat16)
        grad_weights = jnp.einsum(
            "qhe,khe->hqk", grad_attended, value_rows, preferred_element_type=jnp.float32
        )
        grad_scores = factor * probs * (factor * grad_weights - centre_terms[:, :, None])
        grad_scores = grad_scores + jnp.where(
            signed, probs * grad_weights / (modulus * modulus * modulus), 0.0
        )
        grad_low = grad_scores.astype(jnp.bfloat16)
        grad_query = (
            grad_query
            + jnp.einsum("hqk,khe->qhe", grad_low, key_part, preferred_element_type=jnp.float32)
            * scale
        )
        key_term = (
            jnp.einsum("hqk,qhe->khe", grad_low, queries, preferred_element_type=jnp.float32)
            * scale
        )
        value_term = jnp.einsum(
            "hqk,qhe->khe", weights, grad_attended, preferred_element_type=jnp.float32
        )
        keys_total = lax.dynamic_update_slice_in_dim(
            keys_total,
            lax.dynamic_slice_in_dim(keys_total, key_first, key_block, 0) + key_term,
            key_first,
            0,
        )
        values_total = lax.dynamic_update_slice_in_dim(
            values_total,
            lax.dynamic_slice_in_dim(values_total, key_first, key_block, 0) + value_term,
            key_first,
            0,
        )
        return (grad_query, keys_total, values_total)

    start_query = jnp.zeros((query_block, heads_here, head_size), jnp.float32)
    grad_query, grad_keys, grad_values = lax.fori_loop(
        lowest, upper, backward_step, (start_query, grad_keys, grad_values)
    )
    return (grad_query, grad_keys, grad_values)


def forward_layer(inputs, seq_lens, params, signed, finish):
    (
        gain_one,
        bias_one,
        qkv_weight,
        out_weight,
        out_bias,
        gain_two,
        bias_two,
        up_weight,
        up_bias,
        down_weight,
        down_bias,
    ) = params
    normed_one = normalize(inputs, gain_one, bias_one).astype(jnp.bfloat16)
    offset = lax.axis_index("tensor") * normed_one.shape[0]
    row_count = normed_one.shape[0]
    width = qkv_weight.shape[-1]
    projected = jnp.dot(
        normed_one,
        qkv_weight.reshape(qkv_weight.shape[0], 3 * width),
        preferred_element_type=jnp.float32,
    ).astype(jnp.bfloat16)
    head_shape = (row_count, width // HEAD, HEAD)
    queries = projected[:, :width].reshape(head_shape)
    key_rows = projected[:, width : 2 * width].reshape(head_shape)
    values = projected[:, 2 * width :].reshape(head_shape)
    key_all, value_all = (
        lax.all_gather(key_rows, "tensor", axis=0, tiled=True),
        lax.all_gather(values, "tensor", axis=0, tiled=True),
    )
    doc_rows = document_ids(seq_lens, key_all.shape[0])
    attended, log_totals = attend(queries, key_all, value_all, doc_rows, seq_lens, signed, offset)
    attended_low = attended.reshape(row_count, width).astype(jnp.bfloat16)
    hidden_one = inputs + branch_total(attended_low, out_weight) + out_bias
    normed_two = normalize(hidden_one, gain_two, bias_two).astype(jnp.bfloat16)
    up_values = jnp.dot(normed_two, up_weight, preferred_element_type=jnp.float32) + up_bias
    activated = jax.nn.gelu(up_values, approximate=False).astype(jnp.bfloat16)
    if finish:
        outputs = hidden_one + branch_total(activated, down_weight) + down_bias
    else:
        outputs = hidden_one
    saved = (
        normed_one,
        queries,
        key_all,
        value_all,
        doc_rows,
        attended,
        attended_low,
        log_totals,
        hidden_one,
        normed_two,
        up_values,
        activated,
        offset,
    )
    return (outputs, saved)


def backward_layer(inputs, seq_lens, params, signed, grad_outputs):
    (
        gain_one,
        bias_one,
        qkv_weight,
        out_weight,
        out_bias,
        gain_two,
        bias_two,
        up_weight,
        up_bias,
        down_weight,
        down_bias,
    ) = params
    unused_out, saved = forward_layer(inputs, seq_lens, params, signed, False)
    (
        rows_one,
        queries,
        key_all,
        value_all,
        doc_rows,
        attended,
        attended_low,
        log_totals,
        hidden_one,
        rows_two,
        up_values,
        activated,
        offset,
    ) = saved
    row_count, width = attended_low.shape
    grad_low = grad_outputs.astype(jnp.bfloat16)
    grad_down = jnp.einsum("rf,rd->fd", activated, grad_low, preferred_element_type=jnp.float32)
    grad_act = jnp.einsum("rd,fd->rf", grad_low, down_weight, preferred_element_type=jnp.float32)
    gelu_value, gelu_back = jax.vjp(partial(jax.nn.gelu, approximate=False), up_values)
    grad_up_values = gelu_back(grad_act)[0].astype(jnp.bfloat16)
    grad_up_bias = jnp.sum(grad_up_values.astype(jnp.float32), axis=0)
    grad_up = jnp.einsum("rd,rf->df", rows_two, grad_up_values, preferred_element_type=jnp.float32)
    normed_two_terms = jnp.einsum(
        "rf,df->rd", grad_up_values, up_weight, preferred_element_type=jnp.float32
    )
    norm_value, norm_back = jax.vjp(normalize, hidden_one, gain_two, bias_two)
    grad_hidden, grad_gain_two, grad_bias_two = norm_back(normed_two_terms)
    grad_hidden = grad_hidden + grad_outputs
    hidden_low = grad_hidden.astype(jnp.bfloat16)
    grad_out = jnp.einsum("rc,rd->cd", attended_low, hidden_low, preferred_element_type=jnp.float32)
    grad_attended = (
        jnp.einsum("rd,cd->rc", hidden_low, out_weight, preferred_element_type=jnp.float32)
        .astype(jnp.bfloat16)
        .reshape(queries.shape)
    )
    grad_queries, grad_keys, grad_values = attend_back(
        queries,
        key_all,
        value_all,
        doc_rows,
        seq_lens,
        signed,
        attended,
        log_totals,
        grad_attended,
        offset,
    )
    grad_keys, grad_values = (
        lax.psum_scatter(
            grad_keys.astype(jnp.bfloat16), "tensor", scatter_dimension=0, tiled=True
        ).astype(jnp.float32),
        lax.psum_scatter(
            grad_values.astype(jnp.bfloat16), "tensor", scatter_dimension=0, tiled=True
        ).astype(jnp.float32),
    )
    grad_projected = jnp.concatenate(
        [
            grad_queries.reshape(row_count, width),
            grad_keys.reshape(row_count, width),
            grad_values.reshape(row_count, width),
        ],
        axis=1,
    ).astype(jnp.bfloat16)
    grad_qkv = jnp.einsum(
        "rd,rc->dc", rows_one, grad_projected, preferred_element_type=jnp.float32
    ).reshape(qkv_weight.shape)
    normed_one_terms = jnp.einsum(
        "rc,dc->rd",
        grad_projected,
        qkv_weight.reshape(qkv_weight.shape[0], 3 * width),
        preferred_element_type=jnp.float32,
    )
    norm_value_one, norm_back_one = jax.vjp(normalize, inputs, gain_one, bias_one)
    grad_inputs, grad_gain_one, grad_bias_one = norm_back_one(normed_one_terms)
    grad_inputs = grad_inputs + grad_hidden
    matrices = (
        grad_qkv[None],
        grad_out[None],
        grad_up[None],
        grad_up_bias.reshape(1, -1, FF // lax.axis_size("tensor")),
        grad_down[None],
    )
    vectors = (
        grad_gain_one[None],
        grad_bias_one[None],
        jnp.sum(grad_hidden, axis=0)[None],
        grad_gain_two[None],
        grad_bias_two[None],
        jnp.sum(grad_outputs, axis=0)[None],
    )
    return (grad_inputs, matrices, vectors)


def on_device(
    tokens,
    lengths,
    cotangent,
    ln_one_gain,
    ln_one_bias,
    qkv_weight,
    out_weight,
    out_bias,
    ln_two_gain,
    ln_two_bias,
    up_weight,
    up_bias,
    down_weight,
    down_bias,
):
    signed = lax.axis_index("section") == 0
    params = tuple(
        (
            array_item[0]
            for array_item in (
                ln_one_gain,
                ln_one_bias,
                qkv_weight,
                out_weight,
                out_bias,
                ln_two_gain,
                ln_two_bias,
                up_weight,
                up_bias,
                down_weight,
                down_bias,
            )
        )
    )
    whole = (
        lax.all_gather(qkv_weight, "tensor", axis=3, tiled=True),
        lax.all_gather(out_weight, "tensor", axis=1, tiled=True),
        lax.all_gather(up_weight, "tensor", axis=2, tiled=True),
        lax.all_gather(down_weight, "tensor", axis=1, tiled=True),
    )
    bias_whole = lax.all_gather(up_bias, "tensor", axis=1, tiled=True)
    params = (
        params[0],
        params[1],
        whole[0][0],
        whole[1][0],
        params[4],
        params[5],
        params[6],
        whole[2][0],
        bias_whole[0],
        whole[3][0],
        params[10],
    )
    batches = tokens.shape[0]
    arrived = jnp.zeros(tokens.shape[1:], jnp.bfloat16)
    produced_all = jnp.zeros(tokens.shape, jnp.bfloat16)
    received_all = jnp.zeros(tokens.shape, jnp.bfloat16)
    for tick in range(batches + 1):
        own_index = min(tick, batches - 1)
        prior_index = max(tick - 1, 0)
        inputs_now = jnp.where(signed, tokens[own_index], arrived).astype(jnp.float32)
        lens_now = jnp.where(signed, lengths[own_index], lengths[prior_index])
        produced = forward_layer(inputs_now, lens_now, params, signed, True)[0].astype(jnp.bfloat16)
        if tick < batches:
            produced_all = produced_all.at[tick].set(
                jnp.where(signed, produced, produced_all[tick])
            )
        if tick > 0:
            produced_all = produced_all.at[tick - 1].set(
                jnp.where(signed, produced_all[tick - 1], produced)
            )
            received_all = received_all.at[tick - 1].set(arrived)
        if tick < batches:
            arrived = passed_along(produced, "section", 1)
    block_inputs = jnp.where(signed, tokens, received_all)
    returned = jnp.zeros(tokens.shape[1:], jnp.float32)
    grad_inputs_all = jnp.zeros(tokens.shape, jnp.float32)
    matrix_total = None
    vector_total = None
    for tick in range(batches + 1):
        later_index = batches - 1 - tick if tick < batches else 0
        earlier_index = batches - tick if tick > 0 else 0
        index_now = jnp.where(signed, earlier_index, later_index)
        live_now = jnp.where(signed, tick > 0, tick < batches)
        grad_now = jnp.where(signed, returned, cotangent[later_index].astype(jnp.float32))
        grad_now = jnp.where(live_now, grad_now, 0.0)
        inputs_now = block_inputs[index_now].astype(jnp.float32)
        grad_back, matrices, vectors = backward_layer(
            inputs_now, lengths[index_now], params, signed, grad_now
        )
        if tick == 0:
            matrix_total = tuple(matrices)
            vector_total = tuple(vectors)
        else:
            matrix_total = tuple(
                (
                    jnp.add(total_item, new_item)
                    for total_item, new_item in zip(matrix_total, matrices)
                )
            )
            vector_total = tuple(
                (
                    jnp.add(total_item, new_item)
                    for total_item, new_item in zip(vector_total, vectors)
                )
            )
        if tick > 0:
            grad_inputs_all = grad_inputs_all.at[earlier_index].set(
                jnp.where(signed, grad_back, grad_inputs_all[earlier_index])
            )
        if tick < batches:
            grad_inputs_all = grad_inputs_all.at[later_index].set(
                jnp.where(signed, grad_inputs_all[later_index], grad_back)
            )
            returned = passed_along(grad_back.astype(jnp.bfloat16), "section", -1).astype(
                grad_back.dtype
            )
    matrix_final = (
        lax.psum_scatter(
            matrix_total[0].astype(jnp.bfloat16), "dp", scatter_dimension=1, tiled=True
        ).astype(jnp.float32),
        lax.psum_scatter(
            matrix_total[1].astype(jnp.bfloat16), "dp", scatter_dimension=2, tiled=True
        ).astype(jnp.float32),
        lax.psum_scatter(
            matrix_total[2].astype(jnp.bfloat16), "dp", scatter_dimension=1, tiled=True
        ).astype(jnp.float32),
        lax.psum_scatter(
            matrix_total[3].astype(jnp.bfloat16), "dp", scatter_dimension=2, tiled=True
        ).astype(jnp.float32),
        lax.psum_scatter(
            matrix_total[4].astype(jnp.bfloat16), "dp", scatter_dimension=2, tiled=True
        ).astype(jnp.float32),
    )
    vector_final = (
        lax.psum_scatter(vector_total[0], ("dp", "tensor"), scatter_dimension=1, tiled=True),
        lax.psum_scatter(vector_total[1], ("dp", "tensor"), scatter_dimension=1, tiled=True),
        lax.psum_scatter(vector_total[2], ("dp", "tensor"), scatter_dimension=1, tiled=True),
        lax.psum_scatter(vector_total[3], ("dp", "tensor"), scatter_dimension=1, tiled=True),
        lax.psum_scatter(vector_total[4], ("dp", "tensor"), scatter_dimension=1, tiled=True),
        lax.psum_scatter(vector_total[5], ("dp", "tensor"), scatter_dimension=1, tiled=True),
    )
    matrix_final = (
        lax.psum_scatter(
            matrix_final[0].astype(jnp.bfloat16), "tensor", scatter_dimension=3, tiled=True
        ).astype(jnp.float32),
        lax.psum_scatter(
            matrix_final[1].astype(jnp.bfloat16), "tensor", scatter_dimension=1, tiled=True
        ).astype(jnp.float32),
        lax.psum_scatter(
            matrix_final[2].astype(jnp.bfloat16), "tensor", scatter_dimension=2, tiled=True
        ).astype(jnp.float32),
        lax.psum_scatter(
            matrix_final[3].astype(jnp.bfloat16), "tensor", scatter_dimension=1, tiled=True
        ).astype(jnp.float32),
        lax.psum_scatter(
            matrix_final[4].astype(jnp.bfloat16), "tensor", scatter_dimension=1, tiled=True
        ).astype(jnp.float32),
    )
    grad_qkv, grad_out, grad_up, grad_up_bias, grad_down = matrix_final
    grad_gain_one, grad_bias_one, grad_out_bias, grad_gain_two, grad_bias_two, grad_down_bias = (
        vector_final
    )
    return (
        produced_all[None],
        grad_inputs_all[None],
        grad_gain_one,
        grad_bias_one,
        grad_qkv,
        grad_out,
        grad_out_bias,
        grad_gain_two,
        grad_bias_two,
        grad_up,
        grad_up_bias,
        grad_down,
        grad_down_bias,
    )


MESH = pl.DeviceIdType.MESH
PARTS = 4
BLOCK = 256
OWN = 512
WIDTH = 512
PAIRS = 4
TASKS = 5
NEGATIVE = -1e30
LEFT = (((1,), (0,)), ((), ()))
BOTH_LAST = (((1,), (1,)), ((), ()))
BOTH_FIRST = (((0,), (0,)), ((), ()))


def whole_batch_fits(mesh):
    shape = dict(mesh.shape)
    return shape["tensor"] == PARTS and shape["dp"] == PARTS and shape["section"] == 2


def dot(left, right, dims=LEFT):
    return lax.dot_general(left, right, dims, preferred_element_type=jnp.float32)


def place():
    return lax.axis_index("section"), lax.axis_index("dp"), lax.axis_index("tensor")


def blocks_of(core):
    return (core, 3 - core)


def tile_rows(start, count):
    return pl.ds(pl.multiple_of(start, count), count)


def standard(values):
    centre = values - jnp.mean(values, axis=-1, keepdims=True)
    spread = jnp.mean(centre * centre, axis=-1, keepdims=True)
    inverse = lax.rsqrt(spread + 1e-05)
    return centre * inverse, inverse


def standard_back(grads, gain, units, inverse):
    scaled = grads * gain
    inner = jnp.mean(scaled * units, axis=-1, keepdims=True)
    return inverse * (scaled - jnp.mean(scaled, axis=-1, keepdims=True) - units * inner)


def column_sum(values):
    return jnp.sum(values, axis=0, keepdims=True)


def keep_head(values, parity):
    lane = lax.broadcasted_iota(jnp.int32, values.shape, 1)
    return jnp.where((lane < HEAD) == (parity == 0), values, 0.0)


def project(x_ref, vec_ref, weight_ref, normed_t_ref, query_ref, kv_ref, normed_ref, between, after_pair):
    core = lax.axis_index("section")
    gain, bias = vec_ref[0, 0:1, :], vec_ref[0, 1:2, :]

    def norm_rows(index, carry):
        rows = tile_rows(index * 128, 128)
        units, _ = standard(x_ref[rows, :].astype(jnp.float32))
        normed_ref[rows, :] = (units * gain + bias).astype(jnp.bfloat16)
        return carry

    lax.fori_loop(0, OWN // 128, norm_rows, 0)
    normed_t_ref[...] = normed_ref[...].T
    between()

    def pair_step(pair, carry):
        out = dot(normed_ref[...], weight_ref[pair])
        queries = out[:, :128] * 0.125
        for parity in range(2):
            query_ref[pair, parity] = keep_head(queries, parity).astype(jnp.bfloat16)
        for slot, block in enumerate(blocks_of(core)):
            part = out[slot * BLOCK : (slot + 1) * BLOCK, :]
            kv_ref[0, pair, tile_rows(block * BLOCK, BLOCK), :] = part[:, 128:256].astype(jnp.bfloat16)
            kv_ref[1, pair, tile_rows(block * BLOCK, BLOCK), :] = part[:, 256:].astype(jnp.bfloat16)
        after_pair(pair)
        return carry

    lax.fori_loop(0, PAIRS, pair_step, 0)


def task_plan(core):
    first = core == 0
    slots = (0, jnp.where(first, 1, 0), 1, 1, 1)
    keys = (0, jnp.where(first, 0, 1), jnp.where(first, 1, 0), jnp.where(first, 2, 1), jnp.where(first, 3, 2))
    return slots, keys


def attend_rows(signed, query_ref, kv_ref, bias_ref, attended_ref, attended_t_ref, log_ref, logit_ref, factor_ref, stat_ref, before_pair):
    core = lax.axis_index("section")
    slots, keys = task_plan(core)
    middle_late = core == 0
    lane = lax.broadcasted_iota(jnp.int32, (BLOCK, 128), 1)

    def pair_step(pair, carry):
        before_pair(pair)
        outs = [[None, None], [None, None]]
        for parity in range(2):
            tops = []
            for task in range(TASKS):
                rows = tile_rows(slots[task] * BLOCK, BLOCK)
                key_rows = tile_rows(keys[task] * BLOCK, BLOCK)
                scores = dot(query_ref[pair, parity, rows, :], kv_ref[0, pair, key_rows, :], BOTH_LAST)
                if signed:
                    raised = scores * scores + 1.0
                    inverse = lax.rsqrt(raised)
                    factor_ref[task] = scores * inverse
                    scores = raised * inverse
                logits = scores + bias_ref[task]
                logit_ref[task] = logits
                tops.append(jnp.maximum(logits[:, :128], logits[:, 128:]))
            low = jnp.full((BLOCK, 128), NEGATIVE, jnp.float32)
            top_early = jnp.maximum(tops[0], jnp.where(middle_late, low, tops[1]))
            top_late = jnp.maximum(jnp.maximum(tops[2], tops[3]), jnp.maximum(tops[4], jnp.where(middle_late, tops[1], low)))
            max_early = jnp.max(top_early, axis=-1, keepdims=True)
            max_late = jnp.max(top_late, axis=-1, keepdims=True)
            max_middle = jnp.where(middle_late, max_late, max_early)
            shifts = (max_early, max_middle, max_late, max_late, max_late)
            sums, terms = [], []
            for task in range(TASKS):
                key_rows = tile_rows(keys[task] * BLOCK, BLOCK)
                powers = jnp.exp(logit_ref[task] - shifts[task])
                sums.append(powers[:, :128] + powers[:, 128:])
                if signed:
                    powers = powers * factor_ref[task]
                terms.append(dot(powers.astype(jnp.bfloat16), kv_ref[1, pair, key_rows, :]))
            early = jnp.where(middle_late, 0.0, 1.0)
            late = 1.0 - early
            totals = (sums[0] + sums[1] * early, sums[2] + sums[3] + sums[4] + sums[1] * late)
            values = (terms[0] + terms[1] * early, terms[2] + terms[3] + terms[4] + terms[1] * late)
            for slot, top in enumerate((max_early, max_late)):
                total = jnp.sum(totals[slot], axis=-1, keepdims=True)
                outs[slot][parity] = values[slot] / total
                head = pair * 2 + parity
                stat_ref[slot] = jnp.where(lane == head, top + jnp.log(total), stat_ref[slot])
        for slot in range(2):
            merged = jnp.where(lane < HEAD, outs[slot][0], outs[slot][1])
            attended_ref[pair, slot * BLOCK : (slot + 1) * BLOCK, :] = merged
            attended_t_ref[pair, :, slot * BLOCK : (slot + 1) * BLOCK] = merged.T.astype(jnp.bfloat16)
        return carry

    stat_ref[...] = jnp.zeros_like(stat_ref)
    lax.fori_loop(0, PAIRS, pair_step, 0)
    for slot in range(2):
        log_ref[slot] = stat_ref[slot].T[:8, :]


def gelu_both(values):
    lower = 0.5 * (1.0 + lax.erf(values * math.sqrt(0.5)))
    density = jnp.exp(-0.5 * values * values) * (1.0 / math.sqrt(2.0 * math.pi))
    return values * lower, lower + values * density


def feed(x_ref, attended_ref, vec_ref, out_ref, up_ref, down_ref, hidden_ref, normed_t_ref, act_ref, slope_ref, y_ref, normed_ref, wide_ref, sum_ref, between):
    out_bias = vec_ref[0, 2:3, :]
    gain, bias = vec_ref[0, 3:4, :], vec_ref[0, 4:5, :]
    down_bias = vec_ref[0, 5:6, :]
    sum_ref[...] = jnp.zeros_like(sum_ref)

    def out_step(pair, carry):
        sum_ref[...] += dot(attended_ref[pair].astype(jnp.bfloat16), out_ref[pair])
        return carry

    lax.fori_loop(0, PAIRS, out_step, 0)

    def norm_rows(index, carry):
        rows = tile_rows(index * 128, 128)
        hidden = x_ref[rows, :].astype(jnp.float32) + sum_ref[rows, :] + out_bias
        hidden_ref[rows, :] = hidden
        units, _ = standard(hidden)
        normed_ref[rows, :] = (units * gain + bias).astype(jnp.bfloat16)
        sum_ref[rows, :] = hidden + down_bias
        return carry

    lax.fori_loop(0, OWN // 128, norm_rows, 0)
    normed_t_ref[...] = normed_ref[...].T
    between()

    def chunk_step(chunk, carry):
        wide_ref[...] = dot(normed_ref[...], up_ref[chunk])
        up_bias = vec_ref[chunk, 6:7, :]

        def gelu_rows(index, inner):
            rows = tile_rows(index * 32, 32)
            act, slope = gelu_both(wide_ref[rows, :] + up_bias)
            act_ref[chunk, rows, :] = act.astype(jnp.bfloat16)
            slope_ref[chunk, rows, :] = slope.astype(jnp.bfloat16)
            return inner

        lax.fori_loop(0, OWN // 32, gelu_rows, 0)
        sum_ref[...] += dot(act_ref[chunk], down_ref[chunk])
        return carry

    lax.fori_loop(0, PARTS, chunk_step, 0)
    y_ref[...] = sum_ref[...].astype(jnp.bfloat16)


def feed_back(dy_ref, act_ref, slope_ref, down_ref, up_ref, hidden_ref, normed_t_ref, vec_ref, out_ref, attended_ref, attended_t_ref, grad_hidden_ref, grad_att_ref, centre_ref, grads_ref, vec_grad_ref, low_ref, low_t_ref, chunk_ref, sum_ref):
    gain = vec_ref[0, 3:4, :]
    low_ref[...] = dy_ref[...].astype(jnp.bfloat16)
    low_t_ref[...] = low_ref[...].T
    vec_grad_ref[...] = jnp.zeros_like(vec_grad_ref)
    sum_ref[...] = jnp.zeros_like(sum_ref)

    def chunk_step(chunk, carry):
        grad_act = dot(low_ref[...], down_ref[chunk], BOTH_LAST)
        grad_up = (grad_act * slope_ref[chunk].astype(jnp.float32)).astype(jnp.bfloat16)
        chunk_ref[...] = grad_up
        vec_grad_ref[pl.ds(6 + chunk, 1), :] = column_sum(grad_up.astype(jnp.float32))
        down_term = dot(low_t_ref[...], act_ref[chunk]).astype(jnp.bfloat16)
        up_term = dot(normed_t_ref[...], chunk_ref[...]).astype(jnp.bfloat16)
        for part in range(PARTS):
            grads_ref[part, chunk, :, 0:512] = down_term[part * 128 : (part + 1) * 128, :]
            grads_ref[part, chunk, :, 512:1024] = up_term[part * 128 : (part + 1) * 128, :]
        sum_ref[...] += dot(chunk_ref[...], up_ref[chunk], BOTH_LAST)
        return carry

    lax.fori_loop(0, PARTS, chunk_step, 0)

    def norm_rows(index, carry):
        rows = tile_rows(index * 128, 128)
        grads, dy = sum_ref[rows, :], dy_ref[rows, :]
        units, inverse = standard(hidden_ref[rows, :])
        grad_hidden = dy + standard_back(grads, gain, units, inverse)
        grad_hidden_ref[rows, :] = grad_hidden
        low_ref[rows, :] = grad_hidden.astype(jnp.bfloat16)
        vec_grad_ref[2:3, :] += column_sum(grad_hidden)
        vec_grad_ref[3:4, :] += column_sum(grads * units)
        vec_grad_ref[4:5, :] += column_sum(grads)
        vec_grad_ref[5:6, :] += column_sum(dy)
        return carry

    lax.fori_loop(0, OWN // 128, norm_rows, 0)
    row = lax.broadcasted_iota(jnp.int32, (8, 128), 0)
    lane = lax.broadcasted_iota(jnp.int32, (8, 128), 1)
    picks = jnp.where((row < 2) & ((lane < HEAD) == (row == 0)), 1.0, 0.0)

    def pair_step(pair, carry):
        out_term = dot(attended_t_ref[pair], low_ref[...]).astype(jnp.bfloat16)
        for part in range(PARTS):
            grads_ref[part, pair, :, 1024:1152] = out_term[:, part * 128 : (part + 1) * 128]
        grad_att = dot(low_ref[...], out_ref[pair], BOTH_LAST).astype(jnp.bfloat16)
        wide = grad_att.astype(jnp.float32)
        for parity in range(2):
            grad_att_ref[pair, parity] = keep_head(wide, parity).astype(jnp.bfloat16)
        centres = lax.dot_general(picks, wide * attended_ref[pair], BOTH_LAST, precision=lax.Precision.HIGHEST, preferred_element_type=jnp.float32)
        centre_ref[pair] = centres
        return carry

    lax.fori_loop(0, PAIRS, pair_step, 0)


def attend_rows_back(signed, query_ref, kv_ref, grad_att_ref, bias_ref, log_ref, centre_ref, grad_query_ref, grad_kv_ref, send_ref, before_pair, after_pair):
    core = lax.axis_index("section")
    slots, keys = task_plan(core)
    early = jnp.where(core == 0, 0.0, 1.0)
    lane = lax.broadcasted_iota(jnp.int32, (BLOCK, 128), 1)
    grad_kv_ref[...] = jnp.zeros_like(grad_kv_ref)

    def pair_step(pair, carry):
        before_pair(pair)
        parts = [[None] * TASKS, [None] * TASKS]
        for task in range(TASKS):
            rows = tile_rows(slots[task] * BLOCK, BLOCK)
            key_rows = tile_rows(keys[task] * BLOCK, BLOCK)
            key_part, value_part = kv_ref[0, pair, key_rows, :], kv_ref[1, pair, key_rows, :]
            key_term, value_term = None, None
            for parity in range(2):
                queries = query_ref[pair, parity, rows, :]
                grad_att = grad_att_ref[pair, parity, rows, :]
                scores = dot(key_part, queries, BOTH_LAST)
                grad_weights = dot(value_part, grad_att, BOTH_LAST)
                log_row = log_ref[slots[task], pl.ds(pair * 2 + parity, 1), :]
                centre = centre_ref[pair, parity : parity + 1, rows]
                if signed:
                    raised = scores * scores + 1.0
                    inverse = lax.rsqrt(raised)
                    factor = scores * inverse
                    probs = jnp.exp(raised * inverse + bias_ref[task] - log_row)
                    weights = factor * probs
                    grad_scores = weights * (factor * grad_weights - centre)
                    grad_scores = grad_scores + probs * grad_weights * (inverse * inverse * inverse)
                else:
                    weights = jnp.exp(scores + bias_ref[task] - log_row)
                    grad_scores = weights * (grad_weights - centre)
                grad_low = grad_scores.astype(jnp.bfloat16)
                new_key = dot(grad_low, queries)
                new_value = dot(weights.astype(jnp.bfloat16), grad_att)
                key_term = new_key if parity == 0 else key_term + new_key
                value_term = new_value if parity == 0 else value_term + new_value
                parts[parity][task] = dot(grad_low, key_part, BOTH_FIRST)
            grad_kv_ref[0, pair, key_rows, :] += key_term
            grad_kv_ref[1, pair, key_rows, :] += value_term
        merged = []
        for task in range(TASKS):
            merged.append(jnp.where(lane < HEAD, parts[0][task], parts[1][task]))
        grad_query_ref[pair, :BLOCK, :] = ((merged[0] + merged[1] * early) * 0.125).astype(jnp.bfloat16)
        grad_query_ref[pair, BLOCK:, :] = ((merged[1] * (1.0 - early) + merged[2] + merged[3] + merged[4]) * 0.125).astype(jnp.bfloat16)
        for slot, block in enumerate(blocks_of(1 - core)):
            for kind in range(2):
                rows = grad_kv_ref[kind, pair, tile_rows(block * BLOCK, BLOCK), :]
                send_ref[kind, pair, slot * BLOCK : (slot + 1) * BLOCK, :] = rows.astype(jnp.bfloat16)
        after_pair(pair)
        return carry

    lax.fori_loop(0, PAIRS, pair_step, 0)


def project_back(grad_query_ref, grad_kv_ref, other_ref, x_ref, grad_hidden_ref, normed_t_ref, weight_ref, vec_ref, grad_x_ref, grad_x_low_ref, grads_ref, vec_grad_ref, sum_ref, before_pair, after_pair, between):
    core = lax.axis_index("section")
    gain = vec_ref[0, 0:1, :]
    sum_ref[...] = jnp.zeros_like(sum_ref)

    def pair_step(pair, carry):
        before_pair(pair)
        parts = [grad_query_ref[pair]]
        for kind in range(2):
            halves = []
            for slot, block in enumerate(blocks_of(core)):
                own = grad_kv_ref[kind, pair, tile_rows(block * BLOCK, BLOCK), :]
                halves.append(own + other_ref[kind, pair, slot * BLOCK : (slot + 1) * BLOCK, :].astype(jnp.float32))
            parts.append(jnp.concatenate(halves, axis=0).astype(jnp.bfloat16))
        grads = jnp.concatenate(parts, axis=1)
        term = dot(normed_t_ref[...], grads).astype(jnp.bfloat16)
        for part in range(PARTS):
            grads_ref[part, pair, :, 1152:1536] = term[part * 128 : (part + 1) * 128, :]
        after_pair(pair)
        sum_ref[...] += dot(grads, weight_ref[pair], BOTH_LAST)
        return carry

    lax.fori_loop(0, PAIRS, pair_step, 0)
    between()

    def norm_rows(index, carry):
        rows = tile_rows(index * 128, 128)
        grads = sum_ref[rows, :]
        units, inverse = standard(x_ref[rows, :].astype(jnp.float32))
        grad_x = grad_hidden_ref[rows, :] + standard_back(grads, gain, units, inverse)
        grad_x_ref[rows, :] = grad_x
        grad_x_low_ref[rows, :] = grad_x.astype(jnp.bfloat16)
        vec_grad_ref[0:1, :] += column_sum(grads * units)
        vec_grad_ref[1:2, :] += column_sum(grads)
        return carry

    lax.fori_loop(0, OWN // 128, norm_rows, 0)


def greet(partners):
    barrier = pltpu.get_barrier_semaphore()
    for partner in partners:
        pl.semaphore_signal(barrier, inc=1, device_id=partner, device_id_type=MESH)
    pl.semaphore_wait(barrier, len(partners))


def along_tensor(step):
    core, rep, part = place()
    return (core, rep, lax.rem(part + step, PARTS))


def along_dp(step):
    core, rep, part = place()
    return (core, lax.bitwise_xor(rep, step), part)


def sibling():
    core, rep, part = place()
    return (1 - core, rep, part)


def all_partners():
    return [along_tensor(step) for step in (1, 2, 3)] + [along_dp(step) for step in (1, 2, 3)] + [sibling()]


def remote(source, target, send, receive, device):
    return pltpu.make_async_remote_copy(src_ref=source, dst_ref=target, send_sem=send, recv_sem=receive, device_id=device, device_id_type=MESH)


def fill_masks(lens_ref, bias_ref, turned):
    core, rep, part = place()
    slots, keys = task_plan(core)
    bounds, bound = [], 0
    for index in range(lens_ref.shape[1]):
        bound = bound + lens_ref[part, index]
        bounds.append(bound)
    for task in range(TASKS):
        block = jnp.where(slots[task] == 0, core, 3 - core)
        shape = (1, BLOCK) if turned else (BLOCK, 1)
        query = block * BLOCK + lax.broadcasted_iota(jnp.int32, shape, 1 if turned else 0)
        start = jnp.zeros(shape, jnp.int32)
        for bound in bounds:
            start = jnp.where(query >= bound, bound, start)
        key = keys[task] * BLOCK + lax.broadcasted_iota(jnp.int32, (BLOCK, BLOCK), 0 if turned else 1)
        bias_ref[task] = jnp.where((key >= start) & (key <= query), 0.0, NEGATIVE)


def quarter_rows(array, which):
    count = array.shape[0] // PARTS
    return tile_rows(which * count, count)


SAVED = (
    ((OWN, WIDTH), jnp.bfloat16),
    ((WIDTH, OWN), jnp.bfloat16),
    ((PAIRS, 2, OWN, 128), jnp.bfloat16),
    ((2, PAIRS, 1024, 128), jnp.bfloat16),
    ((PAIRS, OWN, 128), jnp.float32),
    ((PAIRS, 128, OWN), jnp.bfloat16),
    ((2, 8, BLOCK), jnp.float32),
    ((OWN, WIDTH), jnp.float32),
    ((WIDTH, OWN), jnp.bfloat16),
    ((PARTS, OWN, 512), jnp.bfloat16),
    ((PARTS, OWN, 512), jnp.bfloat16),
)
WEIGHTS = (
    ((PARTS, 512, 384), jnp.bfloat16),
    ((PARTS, 128, 512), jnp.bfloat16),
    ((PARTS, 512, 512), jnp.bfloat16),
    ((PARTS, 512, 512), jnp.bfloat16),
    ((PARTS, 8, 512), jnp.float32),
)
QKV, OUT, UP, DOWN, VEC = range(5)


def forward_kernel(lens_ref, tokens, cotangent, *refs):
    shards, refs = refs[:5], refs[5:]
    dy_out, y_out, saved_out, weights_out, refs = refs[0], refs[1], refs[2:13], refs[13:18], refs[18:]
    saved, weights, refs = refs[:11], refs[11:16], refs[16:]
    y_ref, bias_ref, normed, logit, factor, stat, wide, total, refs = *refs[:8], refs[8:]
    row_send, row_recv, row_local, z_send, z_recv, xy_send, xy_recv, sib_send, sib_recv, local, kv_send, kv_recv, save_sem = refs
    core, rep, part = place()
    greet(all_partners())

    def z_copy(index, step):
        slot = (index, step - 1)
        if index == VEC:
            return remote(shards[index], weights[index].at[core, part], z_send.at[slot], z_recv.at[slot], along_tensor(step))
        rows = quarter_rows(shards[index], rep)
        return remote(shards[index].at[rows], weights[index].at[core, part, rows], z_send.at[slot], z_recv.at[slot], along_tensor(step))

    def own_copy(index):
        return pltpu.make_async_copy(shards[index], weights[index].at[core, part], local.at[index])

    def xy_copy(index, step, far):
        slot = (index, step - 1, far - 1)
        view = weights[index].at[core, lax.rem(part + far, PARTS), quarter_rows(shards[index], rep)]
        return remote(view, view, xy_send.at[slot], xy_recv.at[slot], along_dp(step))

    def sib_copy(index):
        view = weights[index].at[core]
        return remote(view, view, sib_send.at[index], sib_recv.at[index], sibling())

    steps = (1, 2, 3)

    def z_start(*which):
        for index in which:
            own_copy(index).start()
            for step in steps:
                z_copy(index, step).start()

    def xy_start(*which):
        for index in which:
            for step in steps:
                z_copy(index, step).wait_recv()
            for step in steps:
                for far in steps:
                    xy_copy(index, step, far).start()

    def sib_start(*which):
        for index in which:
            own_copy(index).wait()
            for step in steps:
                for far in steps:
                    xy_copy(index, step, far).wait_recv()
            sib_copy(index).start()

    def need(layer, *which):
        @pl.when(core != layer)
        def _():
            for index in which:
                sib_copy(index).wait_recv()

    owner = jnp.where((part == 0) | (part == 3), 0, 1)
    place_here = jnp.where(part < 2, 0, 1)
    row_pairs = ((tokens, saved[0].at[0]), (cotangent, dy_out))

    def row_targets(array, batch):
        source, target = row_pairs[array]
        rows = target.at[tile_rows(place_here * BLOCK, BLOCK)]
        there = remote(source.at[batch], rows, row_send.at[array, batch], row_recv.at[array, place_here], (core, rep, batch))
        here = pltpu.make_async_copy(source.at[batch], rows, row_local.at[array])
        return there, here

    def rows_each(array, act):
        for batch in range(PARTS):
            there, here = row_targets(array, batch)

            @pl.when((core == owner) & (part != batch))
            def _():
                there.start() if act == "start" else there.wait_send()

            @pl.when((core == owner) & (part == batch))
            def _():
                here.start() if act == "start" else here.wait()

    def rows_arrived(array):
        for slot, block in enumerate(blocks_of(core)):

            @pl.when(block != part)
            def _():
                source, target = row_pairs[array]
                rows = target.at[slot * BLOCK : (slot + 1) * BLOCK]
                remote(source.at[0], rows, row_send.at[array, 0], row_recv.at[array, slot], sibling()).wait_recv()

    def save(layer, *which):
        for index in which:
            pltpu.make_async_copy(saved[index].at[layer], saved_out[index].at[layer], save_sem.at[layer, index]).start()

    def kv_copies(layer, pair, receiving):
        copies = []
        for slot, block in enumerate(blocks_of(1 - core if receiving else core)):
            view = saved[3].at[layer, :, pair, tile_rows(block * BLOCK, BLOCK), :]
            copies.append(remote(view, view, kv_send.at[layer, pair, slot], kv_recv.at[layer, pair, slot], sibling()))
        return copies

    def on(layer, action, *which):
        @pl.when(core == layer)
        def _():
            action(*which)

    on(0, z_start, QKV)
    for step in steps:
        z_copy(VEC, step).start()
    own_copy(VEC).start()
    rows_each(0, "start")
    on(0, z_start, OUT, UP, DOWN)
    fill_masks(lens_ref, bias_ref, False)
    on(0, xy_start, QKV)
    own_copy(VEC).wait()
    for step in steps:
        z_copy(VEC, step).wait_recv()
    sib_copy(VEC).start()
    rows_each(0, "wait")
    rows_arrived(0)
    sib_copy(VEC).wait_recv()
    for layer in range(2):
        signed = layer == 0
        held = [item.at[layer] for item in saved]
        qkv, out, up, down, vec = [item.at[layer] for item in weights]
        x_ref, normed_one_t, queries, kv, attended, attended_t, logs, hidden, normed_two_t, act, slope = held

        def before_project():
            on(layer, sib_start, QKV)
            need(layer, QKV)
            if layer == 1:
                rows_each(1, "start")

        def push_kv(pair):
            for copy in kv_copies(layer, pair, False):
                copy.start()

        def before_attend(pair):
            for copy in kv_copies(layer, pair, True):
                copy.wait_recv()
            if layer == 0:

                @pl.when((pair == 2) & (core == 0))
                def _():
                    sib_start(OUT)

                @pl.when((pair == 2) & (core == 1))
                def _():
                    xy_start(QKV)

            else:

                @pl.when((pair == 2) & (core == 1))
                def _():
                    sib_start(UP, DOWN)

        project(x_ref, vec, qkv, normed_one_t, queries, kv, normed, before_project, push_kv)
        save(layer, 0, 1, 2)
        if layer == 0:
            on(0, xy_start, OUT, UP, DOWN)
            on(1, z_start, QKV, OUT, UP, DOWN)
        else:
            on(1, sib_start, OUT)
        attend_rows(signed, queries, kv, bias_ref, attended, attended_t, logs, logit, factor, stat, before_attend)
        save(layer, 3, 4, 5, 6)
        if layer == 0:
            on(0, sib_start, UP, DOWN)
            on(1, xy_start, OUT, UP, DOWN)
        need(layer, OUT)

        def before_feed():
            need(layer, UP, DOWN)

        target = saved[0].at[1] if layer == 0 else y_ref
        feed(x_ref, attended, vec, out, up, down, hidden, normed_two_t, act, slope, target, normed, wide, total, before_feed)
        save(layer, 7, 8, 9, 10)
    y_copy = pltpu.make_async_copy(y_ref, y_out, row_local.at[0])
    y_copy.start()
    weight_copies = [pltpu.make_async_copy(weights[index], weights_out[index], local.at[index]) for index in range(5)]
    for copy in weight_copies:
        copy.start()
    rows_each(1, "wait")
    rows_arrived(1)
    for index in range(5):
        for step in steps:
            z_copy(index, step).wait_send()
            if index != VEC:
                for far in steps:
                    xy_copy(index, step, far).wait_send()
        sib_copy(index).wait_send()
    for layer in range(2):
        for pair in range(PAIRS):
            for copy in kv_copies(layer, pair, False):
                copy.wait_send()
        for index in range(11):
            pltpu.make_async_copy(saved[index].at[layer], saved_out[index].at[layer], save_sem.at[layer, index]).wait()
    y_copy.wait()
    for copy in weight_copies:
        copy.wait()


GROUPS = ((0, 1152), (1152, 1536))


def backward_kernel(lens_ref, dy_in, y_in, *refs):
    saved_in, weights_in, refs = refs[:11], refs[11:16], refs[16:]
    grads_out, vec_out, blocks_out, rows_out, refs = *refs[:4], refs[4:]
    held, weights, refs = refs[:11], refs[11:16], refs[16:]
    dy_low, dy_ref, bias_ref, grads_ref, vec_grad, low, low_t, chunk, total, grad_hidden, grad_att, centres, grad_query, grad_kv, kv_out, kv_got, grad_low, refs = *refs[:17], refs[17:]
    got_core, got_dp, part_sum, got_part, final, vec_core, vec_chip, vec_dp, vec_rep, vec_part, refs = *refs[:10], refs[10:]
    load_sem, weight_sem, dy_sem, y_send, y_recv, row_send, row_recv, kv_send, kv_recv, core_send, core_recv, dp_send, dp_recv, part_send, part_recv, vec_send, vec_recv, last_send, last_recv = refs
    core, rep, part = place()
    steps = (1, 2, 3)
    mine, theirs = tile_rows(core * 64, 64), tile_rows((1 - core) * 64, 64)

    def load(layer, which=(), matrices=()):
        copies = [pltpu.make_async_copy(saved_in[index].at[layer], held[index], load_sem.at[index]) for index in which]
        return copies + [pltpu.make_async_copy(weights_in[index].at[layer], weights[index], weight_sem.at[index]) for index in matrices]

    def start(copies):
        for copy in copies:
            copy.start()

    def wait(copies):
        for copy in copies:
            copy.wait()

    feed_set = ((9, 10, 7, 8, 4, 5), (DOWN, UP, VEC, OUT))
    attend_set = ((2, 3, 6), ())
    project_set = ((0, 1), (QKV,))
    dy_copy = pltpu.make_async_copy(dy_in, dy_low, dy_sem.at[0])
    dy_copy.start()
    for group in (feed_set, attend_set, project_set):
        start(load(1, *group))
    greet(all_partners() + [(1 - core, rep, lax.rem(part + step, PARTS)) for step in steps])

    owner = jnp.where((part == 0) | (part == 3), 0, 1)

    def deliver(source, layer, target, send, receive, act):
        for slot, block in enumerate(blocks_of(core)):
            rows = source.at[slot * BLOCK : (slot + 1) * BLOCK]
            stays = (core == layer) & (block == part)

            @pl.when(stays)
            def _():
                copy = pltpu.make_async_copy(rows, target.at[part], send.at[layer, slot])
                copy.start() if act == "start" else copy.wait()

            @pl.when(jnp.logical_not(stays))
            def _():
                copy = remote(rows, target.at[part], send.at[layer, slot], receive.at[part], (layer, rep, block))
                copy.start() if act == "start" else copy.wait_send()

    def delivered(target, source, send, receive):
        for batch in range(PARTS):

            @pl.when((core != owner) | (part != batch))
            def _():
                remote(source.at[:BLOCK], target.at[batch], send.at[0, 0], receive.at[batch], sibling()).wait_recv()

    deliver(saved_in[0].at[1], 0, blocks_out, y_send, y_recv, "start")
    deliver(y_in, 1, blocks_out, y_send, y_recv, "start")

    def core_copy(layer, group):
        first, last = GROUPS[group]
        return remote(grads_ref.at[:, :, theirs, first:last], got_core.at[layer, :, :, :, first:last], core_send.at[layer, group], core_recv.at[layer, group], sibling())

    def dp_copy(layer, group, step):
        first, last = GROUPS[group]
        slot = (layer, group, step - 1)
        return remote(got_core.at[layer, lax.bitwise_xor(rep, step), :, :, first:last], got_dp.at[layer, step - 1, :, :, first:last], dp_send.at[slot], dp_recv.at[slot], along_dp(step))

    def part_copy(layer, group, step):
        first, last = GROUPS[group]
        slot = (layer, group, step - 1)
        return remote(part_sum.at[layer, lax.rem(part + step, PARTS), :, first:last], got_part.at[layer, step - 1, :, first:last], part_send.at[slot], part_recv.at[slot], along_tensor(step))

    def dp_start(layer, group):
        first, last = GROUPS[group]
        core_copy(layer, group).wait()

        def add(index, carry):
            major, minor = index // PARTS, lax.rem(index, PARTS)
            own = grads_ref[major, minor, mine, first:last].astype(jnp.float32)
            sum_here = own + got_core[layer, major, minor, :, first:last].astype(jnp.float32)
            got_core[layer, major, minor, :, first:last] = sum_here.astype(jnp.bfloat16)
            return carry

        lax.fori_loop(0, PARTS * PARTS, add, 0)
        start(dp_copy(layer, group, step) for step in steps)

    def part_start(layer, group):
        first, last = GROUPS[group]
        for step in steps:
            dp_copy(layer, group, step).wait()

        def add(minor, carry):
            sum_here = got_core[layer, rep, minor, :, first:last].astype(jnp.float32)
            for step in steps:
                sum_here = sum_here + got_dp[layer, step - 1, minor, :, first:last].astype(jnp.float32)
            part_sum[layer, minor, :, first:last] = sum_here.astype(jnp.bfloat16)
            return carry

        lax.fori_loop(0, PARTS, add, 0)
        start(part_copy(layer, group, step) for step in steps)

    def finish(layer, group):
        first, last = GROUPS[group]
        for step in steps:
            part_copy(layer, group, step).wait()
        sum_here = part_sum[layer, part, :, first:last].astype(jnp.float32)
        for step in steps:
            sum_here = sum_here + got_part[layer, step - 1, :, first:last].astype(jnp.float32)
        final[layer, :, first:last] = sum_here

    def last_copy(layer):
        return remote(final.at[layer], grads_out.at[mine], last_send.at[0], last_recv.at[0], sibling())

    def hand_over(layer):
        @pl.when(core == layer)
        def _():
            grads_out[mine, :] = final[layer]

        @pl.when(core != layer)
        def _():
            last_copy(layer).start()

    def kv_copy(layer, pair):
        return remote(kv_out.at[:, pair], kv_got.at[layer, :, pair], kv_send.at[layer, pair], kv_recv.at[layer, pair], sibling())

    fill_masks(lens_ref, bias_ref, True)
    for layer in (1, 0):
        signed = layer == 0
        x_ref, normed_one_t, queries, kv, attended, attended_t, logs, hidden, normed_two_t, act, slope = held
        qkv, out, up, down, vec = weights
        if layer == 1:
            dy_copy.wait()
            dy_ref[...] = dy_low[...].astype(jnp.float32)
        wait(load(layer, *feed_set))
        feed_back(dy_ref, act, slope, down, up, hidden, normed_two_t, vec, out, attended, attended_t, grad_hidden, grad_att, centres, grads_ref, vec_grad.at[layer], low, low_t, chunk, total)
        core_copy(layer, 0).start()
        if layer == 1:
            start(load(0, (9, 10, 7, 8, 4, 5), (DOWN, UP, OUT)))
        else:
            part_start(1, 0)
            part_start(1, 1)
        wait(load(layer, *attend_set))

        def before_attend(pair):
            @pl.when(pair == 2)
            def _():
                dp_start(layer, 0)
                if layer == 0:
                    finish(1, 0)
                    finish(1, 1)
                    hand_over(1)

        def push_kv(pair):
            kv_copy(layer, pair).start()

        attend_rows_back(signed, queries, kv, grad_att, bias_ref, logs, centres, grad_query, grad_kv, kv_out, before_attend, push_kv)
        if layer == 1:
            start(load(0, *attend_set))
        wait(load(layer, *project_set))

        def before_project(pair):
            kv_copy(layer, pair).wait()

        def between():
            core_copy(layer, 1).start()

        project_back(grad_query, grad_kv, kv_got.at[layer], x_ref, grad_hidden, normed_one_t, qkv, vec, dy_ref, grad_low.at[layer], grads_ref, vec_grad.at[layer], total, before_project, lambda pair: None, between)
        if layer == 1:
            start(load(0, (0, 1), (QKV, VEC)))
        deliver(grad_low.at[layer], layer, rows_out, row_send, row_recv, "start")
        dp_start(layer, 1)
    vec_copy = remote(vec_grad.at[1 - core], vec_core, vec_send.at[0], vec_recv.at[0], sibling())
    vec_copy.start()
    part_start(0, 0)
    vec_copy.wait()
    vec_chip[...] = vec_grad[core] + vec_core[...]
    vec_copies = [remote(vec_chip, vec_dp.at[step - 1], vec_send.at[step], vec_recv.at[step], along_dp(step)) for step in steps]
    start(vec_copies)
    part_start(0, 1)
    wait(vec_copies)
    vec_rep[...] = vec_chip[...] + vec_dp[0] + vec_dp[1] + vec_dp[2]
    vec_copies = [remote(vec_rep, vec_part.at[step - 1], vec_send.at[3 + step], vec_recv.at[3 + step], along_tensor(step)) for step in steps]
    start(vec_copies)
    finish(0, 0)
    finish(0, 1)
    hand_over(0)
    wait(vec_copies)
    vec_out[...] = vec_rep[...] + vec_part[0] + vec_part[1] + vec_part[2]
    deliver(saved_in[0].at[1], 0, blocks_out, y_send, y_recv, "wait")
    deliver(y_in, 1, blocks_out, y_send, y_recv, "wait")
    delivered(blocks_out, y_in, y_send, y_recv)
    for layer in range(2):
        deliver(grad_low.at[layer], layer, rows_out, row_send, row_recv, "wait")
    delivered(rows_out, grad_low.at[0], row_send, row_recv)
    last_copy(0).wait_recv()
    last_copy(0).wait_send()


def specs(space, count):
    return [pl.BlockSpec(memory_space=space)] * count


def kernel_call(body, name, ins, in_specs, outs, out_specs, scratch, collective):
    dma = pltpu.SemaphoreType.DMA
    return pl.pallas_call(
        body,
        out_shape=[jax.ShapeDtypeStruct(shape, kind) for shape, kind in outs],
        in_specs=in_specs,
        out_specs=out_specs,
        scratch_shapes=[pltpu.VMEM(*item) if len(item) == 2 and isinstance(item[0], tuple) else dma(item) for item in scratch],
        compiler_params=pltpu.CompilerParams(collective_id=collective, has_side_effects=True, vmem_limit_bytes=60 * 2**20),
        name=name,
    )(*ins)


def twice(items):
    return tuple(((2, *shape), kind) for shape, kind in items)


def on_device_whole(
    tokens,
    lengths,
    cotangent,
    ln_one_gain,
    ln_one_bias,
    qkv_weight,
    out_weight,
    out_bias,
    ln_two_gain,
    ln_two_bias,
    up_weight,
    up_bias,
    down_weight,
    down_bias,
):
    f32, low = jnp.float32, jnp.bfloat16
    core, rep, part = place()
    vec = jnp.concatenate([ln_one_gain, ln_one_bias, out_bias, ln_two_gain, ln_two_bias, down_bias, up_bias, jnp.zeros_like(up_bias)])
    rows, rows_low = ((OWN, WIDTH), f32), ((OWN, WIDTH), low)
    square = ((BLOCK, BLOCK), f32)
    results = kernel_call(
        forward_kernel,
        "forward",
        (lengths, tokens, cotangent, qkv_weight.reshape(WIDTH, 384), out_weight[0], up_weight[0], down_weight[0], vec),
        specs(pltpu.SMEM, 1) + specs(pl.ANY, 7),
        (rows_low, rows_low, *twice(SAVED), *twice(WEIGHTS)),
        specs(pl.ANY, 18),
        (
            *twice(SAVED),
            *twice(WEIGHTS),
            rows_low,
            ((TASKS, BLOCK, BLOCK), f32),
            rows_low,
            ((TASKS, BLOCK, BLOCK), f32),
            ((TASKS, BLOCK, BLOCK), f32),
            ((2, BLOCK, 128), f32),
            rows,
            rows,
            (2, 4),
            (2, 2),
            (2,),
            (5, 3),
            (5, 3),
            (4, 3, 3),
            (4, 3, 3),
            (5,),
            (5,),
            (5,),
            (2, PAIRS, 2),
            (2, PAIRS, 2),
            (2, 11),
        ),
        0,
    )
    grads, vec_sum, block_outputs, grad_rows = kernel_call(
        backward_kernel,
        "backward",
        (lengths, *results),
        specs(pltpu.SMEM, 1) + specs(pl.ANY, 18),
        (((128, 1536), f32), ((16, 512), f32), ((PARTS, BLOCK, WIDTH), low), ((PARTS, BLOCK, WIDTH), low)),
        specs(pltpu.VMEM, 2) + specs(pl.ANY, 2),
        (
            *SAVED,
            *WEIGHTS,
            rows_low,
            rows,
            ((TASKS, BLOCK, BLOCK), f32),
            ((PARTS, PARTS, 128, 1536), low),
            ((2, 16, 512), f32),
            rows_low,
            ((WIDTH, OWN), low),
            ((OWN, 512), low),
            rows,
            rows,
            ((PAIRS, 2, OWN, 128), low),
            ((PAIRS, 8, OWN), f32),
            ((PAIRS, OWN, 128), low),
            ((2, PAIRS, 1024, 128), f32),
            ((2, PAIRS, OWN, 128), low),
            ((2, 2, PAIRS, OWN, 128), low),
            ((2, OWN, WIDTH), low),
            ((2, PARTS, PARTS, 64, 1536), low),
            ((2, 3, PARTS, 64, 1536), low),
            ((2, PARTS, 64, 1536), low),
            ((2, 3, 64, 1536), low),
            ((2, 64, 1536), f32),
            ((16, 512), f32),
            ((16, 512), f32),
            ((3, 16, 512), f32),
            ((16, 512), f32),
            ((3, 16, 512), f32),
            (11,),
            (5,),
            (1,),
            (2, 2),
            (PARTS,),
            (2, 2),
            (PARTS,),
            (2, PAIRS),
            (2, PAIRS),
            (2, 2),
            (2, 2),
            (2, 2, 3),
            (2, 2, 3),
            (2, 2, 3),
            (2, 2, 3),
            (7,),
            (7,),
            (1,),
            (1,),
        ),
        1,
    )
    spread = lax.dynamic_slice_in_dim(vec_sum, (rep * PARTS + part) * 32, 32, 1)
    up_bias_grad = lax.dynamic_slice(vec_sum, (6 + part, rep * 128), (1, 128))
    return (
        block_outputs[None],
        grad_rows.astype(f32)[None],
        spread[0:1],
        spread[1:2],
        grads[:, 1152:].reshape(1, 128, 3, 128),
        grads[None, :, 1024:1152],
        spread[2:3],
        spread[3:4],
        spread[4:5],
        grads[None, :, 512:1024],
        up_bias_grad[None],
        grads[:, :512].T[None],
        spread[5:6],
    )


def solution(mesh):
    return jax.shard_map(
        on_device_whole if whole_batch_fits(mesh) else on_device,
        mesh=mesh,
        in_specs=(
            P("dp", "tensor", None),
            P("dp", None),
            P("dp", "tensor", None),
            P("section", None),
            P("section", None),
            P("section", None, None, "tensor"),
            P("section", "tensor", None),
            P("section", None),
            P("section", None),
            P("section", None),
            P("section", None, "tensor"),
            P("section", "tensor"),
            P("section", "tensor", None),
            P("section", None),
        ),
        out_specs=(
            P("section", "dp", "tensor", None),
            P("section", "dp", "tensor", None),
            P("section", ("dp", "tensor")),
            P("section", ("dp", "tensor")),
            P("section", "dp", None, "tensor"),
            P("section", "tensor", "dp"),
            P("section", ("dp", "tensor")),
            P("section", ("dp", "tensor")),
            P("section", ("dp", "tensor")),
            P("section", "dp", "tensor"),
            P("section", "tensor", "dp"),
            P("section", "tensor", "dp"),
            P("section", ("dp", "tensor")),
        ),
        check_vma=False,
    )
```

```python
from functools import partial
import math

import jax
import jax.numpy as jnp
from jax import lax
from jax.experimental import pallas as pl
from jax.experimental.pallas import tpu as pltpu
from jax.sharding import PartitionSpec as P

HEAD = 64
FF = 2048


def passed_along(block, axis, distance):
    devices = range(lax.axis_size(axis))
    route = [(i - distance, i) for i in devices if i - distance in devices]
    return lax.ppermute(block, axis, route)


def normalize(values, gain_vec, bias_vec):
    centre = values - jnp.mean(values, axis=-1, keepdims=True)
    spread = jnp.mean(centre * centre, axis=-1, keepdims=True)
    return centre * lax.rsqrt(spread + 1e-05) * gain_vec + bias_vec


def document_ids(seq_lens, row_count):
    bounds = jnp.cumsum(seq_lens)
    places = jnp.arange(row_count, dtype=jnp.int32)
    return jnp.sum((places[:, None] >= bounds[None, :]).astype(jnp.int32), axis=1)


def first_key_block(doc_number, seq_lens, block):
    starts = jnp.cumsum(seq_lens) - seq_lens
    numbers = jnp.arange(seq_lens.shape[0], dtype=jnp.int32)
    return jnp.sum(jnp.where(numbers == doc_number, starts, 0)) // block


def grouped_sum(left, right, groups):
    row_count, inner = left.shape
    terms = jnp.einsum(
        "rgc,gcd->grd",
        left.reshape(row_count, groups, inner // groups),
        right.reshape(groups, inner // groups, right.shape[-1]),
        preferred_element_type=jnp.float32,
    )
    return jnp.sum(lax.optimization_barrier(terms.astype(jnp.bfloat16)).astype(jnp.float32), axis=0)


def branch_total(left, right):
    return grouped_sum(left, right, lax.axis_size("tensor"))


def key_scores(query_rows, key_part, query_docs, key_docs, query_first, key_first, signed):
    scale = 1.0 / math.sqrt(query_rows.shape[-1])
    scores = (
        jnp.einsum("qhe,khe->hqk", query_rows, key_part, preferred_element_type=jnp.float32) * scale
    )
    query_places = query_first + jnp.arange(query_rows.shape[0], dtype=jnp.int32)
    key_places = key_first + jnp.arange(key_part.shape[0], dtype=jnp.int32)
    allowed = (query_docs[:, None] == key_docs[None, :]) & (
        query_places[:, None] >= key_places[None, :]
    )
    modulus = jnp.sqrt(scores * scores + 1.0)
    logits = jnp.where(signed, modulus, scores)
    factor = jnp.where(signed, scores / modulus, 1.0)
    return (modulus, logits, factor, allowed[None])


def attend(queries, key_rows, values, doc_rows, seq_lens, signed, offset):
    query_count, heads_here, head_size = queries.shape
    key_count = key_rows.shape[0]
    query_block = min(512, query_count)
    key_block = min(512, key_count)
    query_first = offset + 0
    query_docs = lax.dynamic_slice_in_dim(doc_rows, query_first, query_block, 0)
    lowest = first_key_block(query_docs[0], seq_lens, key_block)
    upper = (query_first + query_block - 1) // key_block + 1

    def block_scores(key_index):
        key_first = key_index * key_block
        return key_scores(
            queries,
            lax.dynamic_slice_in_dim(key_rows, key_first, key_block, 0),
            query_docs,
            lax.dynamic_slice_in_dim(doc_rows, key_first, key_block, 0),
            query_first,
            key_first,
            signed,
        )

    def measure(key_index, carry):
        running_max, running_sum = carry
        modulus, logits, factor, allowed = block_scores(key_index)
        masked = jnp.where(allowed, logits, -1e30)
        new_max = jnp.maximum(running_max, jnp.max(masked, axis=-1))
        added = jnp.sum(jnp.where(allowed, jnp.exp(masked - new_max[:, :, None]), 0.0), axis=-1)
        return (new_max, running_sum * jnp.exp(running_max - new_max) + added)

    start_max = jnp.full((heads_here, query_block), -1e30, jnp.float32)
    start_sum = jnp.zeros((heads_here, query_block), jnp.float32)
    row_max, row_sum = lax.fori_loop(lowest, upper, measure, (start_max, start_sum))
    log_total = row_max + jnp.log(row_sum)

    def accumulate(key_index, partial_out):
        modulus, logits, factor, allowed = block_scores(key_index)
        probs = jnp.where(allowed, jnp.exp(logits - log_total[:, :, None]), 0.0)
        weights = (factor * probs).astype(jnp.bfloat16)
        value_rows = lax.dynamic_slice_in_dim(values, key_index * key_block, key_block, 0)
        return partial_out + jnp.einsum(
            "hqk,khe->qhe", weights, value_rows, preferred_element_type=jnp.float32
        )

    outputs_list = lax.fori_loop(
        lowest, upper, accumulate, jnp.zeros((query_block, heads_here, head_size), jnp.float32)
    )
    return (outputs_list, log_total)


def attend_back(
    queries,
    key_rows,
    values,
    doc_rows,
    seq_lens,
    signed,
    attended,
    log_totals,
    grad_attended,
    offset,
):
    query_count, heads_here, head_size = queries.shape
    key_count = key_rows.shape[0]
    query_block = min(512, query_count)
    key_block = min(512, key_count)
    scale = 1.0 / math.sqrt(head_size)
    centre_terms = jnp.sum(grad_attended.astype(jnp.float32) * attended, axis=-1).T
    grad_keys = jnp.zeros(key_rows.shape, jnp.float32)
    grad_values = jnp.zeros(key_rows.shape, jnp.float32)
    query_first = offset + 0
    query_docs = lax.dynamic_slice_in_dim(doc_rows, query_first, query_block, 0)
    lowest = first_key_block(query_docs[0], seq_lens, key_block)
    upper = (query_first + query_block - 1) // key_block + 1

    def backward_step(key_index, carry):
        grad_query, keys_total, values_total = carry
        key_first = key_index * key_block
        key_part = lax.dynamic_slice_in_dim(key_rows, key_first, key_block, 0)
        value_rows = lax.dynamic_slice_in_dim(values, key_first, key_block, 0)
        modulus, logits, factor, allowed = key_scores(
            queries,
            key_part,
            query_docs,
            lax.dynamic_slice_in_dim(doc_rows, key_first, key_block, 0),
            query_first,
            key_first,
            signed,
        )
        probs = jnp.where(allowed, jnp.exp(logits - log_totals[:, :, None]), 0.0)
        weights = (factor * probs).astype(jnp.bfloat16)
        grad_weights = jnp.einsum(
            "qhe,khe->hqk", grad_attended, value_rows, preferred_element_type=jnp.float32
        )
        grad_scores = factor * probs * (factor * grad_weights - centre_terms[:, :, None])
        grad_scores = grad_scores + jnp.where(
            signed, probs * grad_weights / (modulus * modulus * modulus), 0.0
        )
        grad_low = grad_scores.astype(jnp.bfloat16)
        grad_query = (
            grad_query
            + jnp.einsum("hqk,khe->qhe", grad_low, key_part, preferred_element_type=jnp.float32)
            * scale
        )
        key_term = (
            jnp.einsum("hqk,qhe->khe", grad_low, queries, preferred_element_type=jnp.float32)
            * scale
        )
        value_term = jnp.einsum(
            "hqk,qhe->khe", weights, grad_attended, preferred_element_type=jnp.float32
        )
        keys_total = lax.dynamic_update_slice_in_dim(
            keys_total,
            lax.dynamic_slice_in_dim(keys_total, key_first, key_block, 0) + key_term,
            key_first,
            0,
        )
        values_total = lax.dynamic_update_slice_in_dim(
            values_total,
            lax.dynamic_slice_in_dim(values_total, key_first, key_block, 0) + value_term,
            key_first,
            0,
        )
        return (grad_query, keys_total, values_total)

    start_query = jnp.zeros((query_block, heads_here, head_size), jnp.float32)
    grad_query, grad_keys, grad_values = lax.fori_loop(
        lowest, upper, backward_step, (start_query, grad_keys, grad_values)
    )
    return (grad_query, grad_keys, grad_values)


def forward_layer(inputs, seq_lens, params, signed, finish):
    (
        gain_one,
        bias_one,
        qkv_weight,
        out_weight,
        out_bias,
        gain_two,
        bias_two,
        up_weight,
        up_bias,
        down_weight,
        down_bias,
    ) = params
    normed_one = normalize(inputs, gain_one, bias_one).astype(jnp.bfloat16)
    offset = lax.axis_index("tensor") * normed_one.shape[0]
    row_count = normed_one.shape[0]
    width = qkv_weight.shape[-1]
    projected = jnp.dot(
        normed_one,
        qkv_weight.reshape(qkv_weight.shape[0], 3 * width),
        preferred_element_type=jnp.float32,
    ).astype(jnp.bfloat16)
    head_shape = (row_count, width // HEAD, HEAD)
    queries = projected[:, :width].reshape(head_shape)
    key_rows = projected[:, width : 2 * width].reshape(head_shape)
    values = projected[:, 2 * width :].reshape(head_shape)
    key_all, value_all = (
        lax.all_gather(key_rows, "tensor", axis=0, tiled=True),
        lax.all_gather(values, "tensor", axis=0, tiled=True),
    )
    doc_rows = document_ids(seq_lens, key_all.shape[0])
    attended, log_totals = attend(queries, key_all, value_all, doc_rows, seq_lens, signed, offset)
    attended_low = attended.reshape(row_count, width).astype(jnp.bfloat16)
    hidden_one = inputs + branch_total(attended_low, out_weight) + out_bias
    normed_two = normalize(hidden_one, gain_two, bias_two).astype(jnp.bfloat16)
    up_values = jnp.dot(normed_two, up_weight, preferred_element_type=jnp.float32) + up_bias
    activated = jax.nn.gelu(up_values, approximate=False).astype(jnp.bfloat16)
    if finish:
        outputs = hidden_one + branch_total(activated, down_weight) + down_bias
    else:
        outputs = hidden_one
    saved = (
        normed_one,
        queries,
        key_all,
        value_all,
        doc_rows,
        attended,
        attended_low,
        log_totals,
        hidden_one,
        normed_two,
        up_values,
        activated,
        offset,
    )
    return (outputs, saved)


def backward_layer(inputs, seq_lens, params, signed, grad_outputs):
    (
        gain_one,
        bias_one,
        qkv_weight,
        out_weight,
        out_bias,
        gain_two,
        bias_two,
        up_weight,
        up_bias,
        down_weight,
        down_bias,
    ) = params
    unused_out, saved = forward_layer(inputs, seq_lens, params, signed, False)
    (
        rows_one,
        queries,
        key_all,
        value_all,
        doc_rows,
        attended,
        attended_low,
        log_totals,
        hidden_one,
        rows_two,
        up_values,
        activated,
        offset,
    ) = saved
    row_count, width = attended_low.shape
    grad_low = grad_outputs.astype(jnp.bfloat16)
    grad_down = jnp.einsum("rf,rd->fd", activated, grad_low, preferred_element_type=jnp.float32)
    grad_act = jnp.einsum("rd,fd->rf", grad_low, down_weight, preferred_element_type=jnp.float32)
    gelu_value, gelu_back = jax.vjp(partial(jax.nn.gelu, approximate=False), up_values)
    grad_up_values = gelu_back(grad_act)[0].astype(jnp.bfloat16)
    grad_up_bias = jnp.sum(grad_up_values.astype(jnp.float32), axis=0)
    grad_up = jnp.einsum("rd,rf->df", rows_two, grad_up_values, preferred_element_type=jnp.float32)
    normed_two_terms = jnp.einsum(
        "rf,df->rd", grad_up_values, up_weight, preferred_element_type=jnp.float32
    )
    norm_value, norm_back = jax.vjp(normalize, hidden_one, gain_two, bias_two)
    grad_hidden, grad_gain_two, grad_bias_two = norm_back(normed_two_terms)
    grad_hidden = grad_hidden + grad_outputs
    hidden_low = grad_hidden.astype(jnp.bfloat16)
    grad_out = jnp.einsum("rc,rd->cd", attended_low, hidden_low, preferred_element_type=jnp.float32)
    grad_attended = (
        jnp.einsum("rd,cd->rc", hidden_low, out_weight, preferred_element_type=jnp.float32)
        .astype(jnp.bfloat16)
        .reshape(queries.shape)
    )
    grad_queries, grad_keys, grad_values = attend_back(
        queries,
        key_all,
        value_all,
        doc_rows,
        seq_lens,
        signed,
        attended,
        log_totals,
        grad_attended,
        offset,
    )
    grad_keys, grad_values = (
        lax.psum_scatter(
            grad_keys.astype(jnp.bfloat16), "tensor", scatter_dimension=0, tiled=True
        ).astype(jnp.float32),
        lax.psum_scatter(
            grad_values.astype(jnp.bfloat16), "tensor", scatter_dimension=0, tiled=True
        ).astype(jnp.float32),
    )
    grad_projected = jnp.concatenate(
        [
            grad_queries.reshape(row_count, width),
            grad_keys.reshape(row_count, width),
            grad_values.reshape(row_count, width),
        ],
        axis=1,
    ).astype(jnp.bfloat16)
    grad_qkv = jnp.einsum(
        "rd,rc->dc", rows_one, grad_projected, preferred_element_type=jnp.float32
    ).reshape(qkv_weight.shape)
    normed_one_terms = jnp.einsum(
        "rc,dc->rd",
        grad_projected,
        qkv_weight.reshape(qkv_weight.shape[0], 3 * width),
        preferred_element_type=jnp.float32,
    )
    norm_value_one, norm_back_one = jax.vjp(normalize, inputs, gain_one, bias_one)
    grad_inputs, grad_gain_one, grad_bias_one = norm_back_one(normed_one_terms)
    grad_inputs = grad_inputs + grad_hidden
    matrices = (
        grad_qkv[None],
        grad_out[None],
        grad_up[None],
        grad_up_bias.reshape(1, -1, FF // lax.axis_size("tensor")),
        grad_down[None],
    )
    vectors = (
        grad_gain_one[None],
        grad_bias_one[None],
        jnp.sum(grad_hidden, axis=0)[None],
        grad_gain_two[None],
        grad_bias_two[None],
        jnp.sum(grad_outputs, axis=0)[None],
    )
    return (grad_inputs, matrices, vectors)


def on_device(
    tokens,
    lengths,
    cotangent,
    ln_one_gain,
    ln_one_bias,
    qkv_weight,
    out_weight,
    out_bias,
    ln_two_gain,
    ln_two_bias,
    up_weight,
    up_bias,
    down_weight,
    down_bias,
):
    signed = lax.axis_index("section") == 0
    params = tuple(
        (
            array_item[0]
            for array_item in (
                ln_one_gain,
                ln_one_bias,
                qkv_weight,
                out_weight,
                out_bias,
                ln_two_gain,
                ln_two_bias,
                up_weight,
                up_bias,
                down_weight,
                down_bias,
            )
        )
    )
    whole = (
        lax.all_gather(qkv_weight, "tensor", axis=3, tiled=True),
        lax.all_gather(out_weight, "tensor", axis=1, tiled=True),
        lax.all_gather(up_weight, "tensor", axis=2, tiled=True),
        lax.all_gather(down_weight, "tensor", axis=1, tiled=True),
    )
    bias_whole = lax.all_gather(up_bias, "tensor", axis=1, tiled=True)
    params = (
        params[0],
        params[1],
        whole[0][0],
        whole[1][0],
        params[4],
        params[5],
        params[6],
        whole[2][0],
        bias_whole[0],
        whole[3][0],
        params[10],
    )
    batches = tokens.shape[0]
    arrived = jnp.zeros(tokens.shape[1:], jnp.bfloat16)
    produced_all = jnp.zeros(tokens.shape, jnp.bfloat16)
    received_all = jnp.zeros(tokens.shape, jnp.bfloat16)
    for tick in range(batches + 1):
        own_index = min(tick, batches - 1)
        prior_index = max(tick - 1, 0)
        inputs_now = jnp.where(signed, tokens[own_index], arrived).astype(jnp.float32)
        lens_now = jnp.where(signed, lengths[own_index], lengths[prior_index])
        produced = forward_layer(inputs_now, lens_now, params, signed, True)[0].astype(jnp.bfloat16)
        if tick < batches:
            produced_all = produced_all.at[tick].set(
                jnp.where(signed, produced, produced_all[tick])
            )
        if tick > 0:
            produced_all = produced_all.at[tick - 1].set(
                jnp.where(signed, produced_all[tick - 1], produced)
            )
            received_all = received_all.at[tick - 1].set(arrived)
        if tick < batches:
            arrived = passed_along(produced, "section", 1)
    block_inputs = jnp.where(signed, tokens, received_all)
    returned = jnp.zeros(tokens.shape[1:], jnp.float32)
    grad_inputs_all = jnp.zeros(tokens.shape, jnp.float32)
    matrix_total = None
    vector_total = None
    for tick in range(batches + 1):
        later_index = batches - 1 - tick if tick < batches else 0
        earlier_index = batches - tick if tick > 0 else 0
        index_now = jnp.where(signed, earlier_index, later_index)
        live_now = jnp.where(signed, tick > 0, tick < batches)
        grad_now = jnp.where(signed, returned, cotangent[later_index].astype(jnp.float32))
        grad_now = jnp.where(live_now, grad_now, 0.0)
        inputs_now = block_inputs[index_now].astype(jnp.float32)
        grad_back, matrices, vectors = backward_layer(
            inputs_now, lengths[index_now], params, signed, grad_now
        )
        if tick == 0:
            matrix_total = tuple(matrices)
            vector_total = tuple(vectors)
        else:
            matrix_total = tuple(
                (
                    jnp.add(total_item, new_item)
                    for total_item, new_item in zip(matrix_total, matrices)
                )
            )
            vector_total = tuple(
                (
                    jnp.add(total_item, new_item)
                    for total_item, new_item in zip(vector_total, vectors)
                )
            )
        if tick > 0:
            grad_inputs_all = grad_inputs_all.at[earlier_index].set(
                jnp.where(signed, grad_back, grad_inputs_all[earlier_index])
            )
        if tick < batches:
            grad_inputs_all = grad_inputs_all.at[later_index].set(
                jnp.where(signed, grad_inputs_all[later_index], grad_back)
            )
            returned = passed_along(grad_back.astype(jnp.bfloat16), "section", -1).astype(
                grad_back.dtype
            )
    matrix_final = (
        lax.psum_scatter(
            matrix_total[0].astype(jnp.bfloat16), "dp", scatter_dimension=1, tiled=True
        ).astype(jnp.float32),
        lax.psum_scatter(
            matrix_total[1].astype(jnp.bfloat16), "dp", scatter_dimension=2, tiled=True
        ).astype(jnp.float32),
        lax.psum_scatter(
            matrix_total[2].astype(jnp.bfloat16), "dp", scatter_dimension=1, tiled=True
        ).astype(jnp.float32),
        lax.psum_scatter(
            matrix_total[3].astype(jnp.bfloat16), "dp", scatter_dimension=2, tiled=True
        ).astype(jnp.float32),
        lax.psum_scatter(
            matrix_total[4].astype(jnp.bfloat16), "dp", scatter_dimension=2, tiled=True
        ).astype(jnp.float32),
    )
    vector_final = (
        lax.psum_scatter(vector_total[0], ("dp", "tensor"), scatter_dimension=1, tiled=True),
        lax.psum_scatter(vector_total[1], ("dp", "tensor"), scatter_dimension=1, tiled=True),
        lax.psum_scatter(vector_total[2], ("dp", "tensor"), scatter_dimension=1, tiled=True),
        lax.psum_scatter(vector_total[3], ("dp", "tensor"), scatter_dimension=1, tiled=True),
        lax.psum_scatter(vector_total[4], ("dp", "tensor"), scatter_dimension=1, tiled=True),
        lax.psum_scatter(vector_total[5], ("dp", "tensor"), scatter_dimension=1, tiled=True),
    )
    matrix_final = (
        lax.psum_scatter(
            matrix_final[0].astype(jnp.bfloat16), "tensor", scatter_dimension=3, tiled=True
        ).astype(jnp.float32),
        lax.psum_scatter(
            matrix_final[1].astype(jnp.bfloat16), "tensor", scatter_dimension=1, tiled=True
        ).astype(jnp.float32),
        lax.psum_scatter(
            matrix_final[2].astype(jnp.bfloat16), "tensor", scatter_dimension=2, tiled=True
        ).astype(jnp.float32),
        lax.psum_scatter(
            matrix_final[3].astype(jnp.bfloat16), "tensor", scatter_dimension=1, tiled=True
        ).astype(jnp.float32),
        lax.psum_scatter(
            matrix_final[4].astype(jnp.bfloat16), "tensor", scatter_dimension=1, tiled=True
        ).astype(jnp.float32),
    )
    grad_qkv, grad_out, grad_up, grad_up_bias, grad_down = matrix_final
    grad_gain_one, grad_bias_one, grad_out_bias, grad_gain_two, grad_bias_two, grad_down_bias = (
        vector_final
    )
    return (
        produced_all[None],
        grad_inputs_all[None],
        grad_gain_one,
        grad_bias_one,
        grad_qkv,
        grad_out,
        grad_out_bias,
        grad_gain_two,
        grad_bias_two,
        grad_up,
        grad_up_bias,
        grad_down,
        grad_down_bias,
    )


MESH = pl.DeviceIdType.MESH
PARTS = 4
BLOCK = 256
OWN = 512
WIDTH = 512
PAIRS = 4
TASKS = 5
NEGATIVE = -1e30
LEFT = (((1,), (0,)), ((), ()))
BOTH_LAST = (((1,), (1,)), ((), ()))
BOTH_FIRST = (((0,), (0,)), ((), ()))


def whole_batch_fits(mesh):
    shape = dict(mesh.shape)
    return shape["tensor"] == PARTS and shape["dp"] == PARTS and shape["section"] == 2


def dot(left, right, dims=LEFT):
    return lax.dot_general(left, right, dims, preferred_element_type=jnp.float32)


def place():
    return lax.axis_index("section"), lax.axis_index("dp"), lax.axis_index("tensor")


def blocks_of(core):
    return (core, 3 - core)


def turn_part(turn):
    return lax.rem(lax.axis_index("tensor") + turn, PARTS)


def tile_rows(start, count):
    return pl.ds(pl.multiple_of(start, count), count)


def standard(values):
    centre = values - jnp.mean(values, axis=-1, keepdims=True)
    spread = jnp.mean(centre * centre, axis=-1, keepdims=True)
    inverse = lax.rsqrt(spread + 1e-05)
    return centre * inverse, inverse


def standard_back(grads, gain, units, inverse):
    scaled = grads * gain
    inner = jnp.mean(scaled * units, axis=-1, keepdims=True)
    return inverse * (scaled - jnp.mean(scaled, axis=-1, keepdims=True) - units * inner)


def column_sum(values):
    return jnp.sum(values, axis=0, keepdims=True)


def keep_head(values, parity):
    lane = lax.broadcasted_iota(jnp.int32, values.shape, 1)
    return jnp.where((lane < HEAD) == (parity == 0), values, 0.0)


def project(x_ref, vec_ref, weight_ref, normed_t_ref, query_ref, kv_ref, normed_ref, between, before_pair, after_pair):
    core = lax.axis_index("section")
    gain, bias = vec_ref[0, 0:1, :], vec_ref[0, 1:2, :]

    def norm_rows(index, carry):
        rows = tile_rows(index * 128, 128)
        units, _ = standard(x_ref[rows, :].astype(jnp.float32))
        normed_ref[rows, :] = (units * gain + bias).astype(jnp.bfloat16)
        return carry

    lax.fori_loop(0, OWN // 128, norm_rows, 0)
    normed_t_ref[...] = normed_ref[...].T
    between()

    def pair_step(turn, carry):
        pair = turn_part(turn)
        before_pair(turn)
        out = dot(normed_ref[...], weight_ref[pair])
        queries = out[:, :128] * 0.125
        for parity in range(2):
            query_ref[pair, parity] = keep_head(queries, parity).astype(jnp.bfloat16)
        for slot, block in enumerate(blocks_of(core)):
            part = out[slot * BLOCK : (slot + 1) * BLOCK, :]
            kv_ref[0, pair, tile_rows(block * BLOCK, BLOCK), :] = part[:, 128:256].astype(jnp.bfloat16)
            kv_ref[1, pair, tile_rows(block * BLOCK, BLOCK), :] = part[:, 256:].astype(jnp.bfloat16)
        after_pair(turn, pair)
        return carry

    lax.fori_loop(0, PAIRS, pair_step, 0)


def task_plan(core):
    first = core == 0
    slots = (0, jnp.where(first, 1, 0), 1, 1, 1)
    keys = (0, jnp.where(first, 0, 1), jnp.where(first, 1, 0), jnp.where(first, 2, 1), jnp.where(first, 3, 2))
    return slots, keys


def attend_rows(signed, query_ref, kv_ref, bias_ref, attended_ref, attended_t_ref, log_ref, logit_ref, factor_ref, stat_ref, before_pair):
    core = lax.axis_index("section")
    slots, keys = task_plan(core)
    middle_late = core == 0
    lane = lax.broadcasted_iota(jnp.int32, (BLOCK, 128), 1)

    def pair_step(turn, carry):
        pair = turn_part(turn)
        before_pair(turn, pair)
        outs = [[None, None], [None, None]]
        for parity in range(2):
            tops = []
            for task in range(TASKS):
                rows = tile_rows(slots[task] * BLOCK, BLOCK)
                key_rows = tile_rows(keys[task] * BLOCK, BLOCK)
                scores = dot(query_ref[pair, parity, rows, :], kv_ref[0, pair, key_rows, :], BOTH_LAST)
                if signed:
                    raised = scores * scores + 1.0
                    inverse = lax.rsqrt(raised)
                    factor_ref[task] = scores * inverse
                    scores = raised * inverse
                logits = scores + bias_ref[task]
                logit_ref[task] = logits
                tops.append(jnp.maximum(logits[:, :128], logits[:, 128:]))
            low = jnp.full((BLOCK, 128), NEGATIVE, jnp.float32)
            top_early = jnp.maximum(tops[0], jnp.where(middle_late, low, tops[1]))
            top_late = jnp.maximum(jnp.maximum(tops[2], tops[3]), jnp.maximum(tops[4], jnp.where(middle_late, tops[1], low)))
            max_early = jnp.max(top_early, axis=-1, keepdims=True)
            max_late = jnp.max(top_late, axis=-1, keepdims=True)
            max_middle = jnp.where(middle_late, max_late, max_early)
            shifts = (max_early, max_middle, max_late, max_late, max_late)
            sums, terms = [], []
            for task in range(TASKS):
                key_rows = tile_rows(keys[task] * BLOCK, BLOCK)
                powers = jnp.exp(logit_ref[task] - shifts[task])
                sums.append(powers[:, :128] + powers[:, 128:])
                if signed:
                    powers = powers * factor_ref[task]
                terms.append(dot(powers.astype(jnp.bfloat16), kv_ref[1, pair, key_rows, :]))
            early = jnp.where(middle_late, 0.0, 1.0)
            late = 1.0 - early
            totals = (sums[0] + sums[1] * early, sums[2] + sums[3] + sums[4] + sums[1] * late)
            values = (terms[0] + terms[1] * early, terms[2] + terms[3] + terms[4] + terms[1] * late)
            for slot, top in enumerate((max_early, max_late)):
                total = jnp.sum(totals[slot], axis=-1, keepdims=True)
                outs[slot][parity] = values[slot] / total
                head = pair * 2 + parity
                stat_ref[slot] = jnp.where(lane == head, top + jnp.log(total), stat_ref[slot])
        for slot in range(2):
            merged = jnp.where(lane < HEAD, outs[slot][0], outs[slot][1])
            attended_ref[pair, slot * BLOCK : (slot + 1) * BLOCK, :] = merged
            attended_t_ref[pair, :, slot * BLOCK : (slot + 1) * BLOCK] = merged.T.astype(jnp.bfloat16)
        return carry

    stat_ref[...] = jnp.zeros_like(stat_ref)
    lax.fori_loop(0, PAIRS, pair_step, 0)
    for slot in range(2):
        log_ref[slot] = stat_ref[slot].T[:8, :]


def gelu_both(values):
    lower = 0.5 * (1.0 + lax.erf(values * math.sqrt(0.5)))
    density = jnp.exp(-0.5 * values * values) * (1.0 / math.sqrt(2.0 * math.pi))
    return values * lower, lower + values * density


def feed(x_ref, attended_ref, vec_ref, out_ref, up_ref, down_ref, hidden_ref, normed_t_ref, act_ref, slope_ref, y_ref, normed_ref, wide_ref, sum_ref, before_out, between, before_chunk, during_chunk):
    out_bias = vec_ref[0, 2:3, :]
    gain, bias = vec_ref[0, 3:4, :], vec_ref[0, 4:5, :]
    down_bias = vec_ref[0, 5:6, :]
    sum_ref[...] = jnp.zeros_like(sum_ref)

    def out_step(turn, carry):
        pair = turn_part(turn)
        before_out(turn)
        sum_ref[...] += dot(attended_ref[pair].astype(jnp.bfloat16), out_ref[pair])
        return carry

    lax.fori_loop(0, PAIRS, out_step, 0)

    def norm_rows(index, carry):
        rows = tile_rows(index * 128, 128)
        hidden = x_ref[rows, :].astype(jnp.float32) + sum_ref[rows, :] + out_bias
        hidden_ref[rows, :] = hidden
        units, _ = standard(hidden)
        normed_ref[rows, :] = (units * gain + bias).astype(jnp.bfloat16)
        sum_ref[rows, :] = hidden + down_bias
        return carry

    lax.fori_loop(0, OWN // 128, norm_rows, 0)
    normed_t_ref[...] = normed_ref[...].T
    between()

    def chunk_step(turn, carry):
        chunk = turn_part(turn)
        before_chunk(turn)
        wide_ref[...] = dot(normed_ref[...], up_ref[chunk])
        up_bias = vec_ref[chunk, 6:7, :]

        def gelu_rows(index, inner):
            rows = tile_rows(index * 32, 32)
            act, slope = gelu_both(wide_ref[rows, :] + up_bias)
            act_ref[chunk, rows, :] = act.astype(jnp.bfloat16)
            slope_ref[chunk, rows, :] = slope.astype(jnp.bfloat16)
            return inner

        lax.fori_loop(0, OWN // 32, gelu_rows, 0)
        during_chunk(turn)
        sum_ref[...] += dot(act_ref[chunk], down_ref[chunk])
        return carry

    lax.fori_loop(0, PARTS, chunk_step, 0)
    y_ref[...] = sum_ref[...].astype(jnp.bfloat16)


def feed_back(dy_ref, act_ref, slope_ref, down_ref, up_ref, hidden_ref, normed_t_ref, vec_ref, out_ref, attended_ref, attended_t_ref, grad_hidden_ref, grad_att_ref, centre_ref, grads_ref, vec_grad_ref, low_ref, low_t_ref, chunk_ref, sum_ref, during_chunk, after_chunk, before_norm, between):
    low_ref[...] = dy_ref[...].astype(jnp.bfloat16)
    low_t_ref[...] = low_ref[...].T
    vec_grad_ref[...] = jnp.zeros_like(vec_grad_ref)
    sum_ref[...] = jnp.zeros_like(sum_ref)

    def chunk_step(turn, carry):
        chunk = turn_part(turn + 1)
        grad_act = dot(low_ref[...], down_ref[chunk], BOTH_LAST)
        grad_up = (grad_act * slope_ref[chunk].astype(jnp.float32)).astype(jnp.bfloat16)
        chunk_ref[...] = grad_up
        vec_grad_ref[pl.ds(6 + chunk, 1), :] = column_sum(grad_up.astype(jnp.float32))
        down_term = dot(low_t_ref[...], act_ref[chunk]).astype(jnp.bfloat16)
        up_term = dot(normed_t_ref[...], chunk_ref[...]).astype(jnp.bfloat16)
        for part in range(PARTS):
            grads_ref[part, chunk, :, 0:512] = down_term[part * 128 : (part + 1) * 128, :]
            grads_ref[part, chunk, :, 512:1024] = up_term[part * 128 : (part + 1) * 128, :]
        after_chunk(turn, chunk)
        sum_ref[...] += dot(chunk_ref[...], up_ref[chunk], BOTH_LAST)
        during_chunk(turn)
        return carry

    lax.fori_loop(0, PARTS, chunk_step, 0)
    before_norm()
    gain = vec_ref[0, 3:4, :]

    def norm_rows(index, carry):
        rows = tile_rows(index * 128, 128)
        grads, dy = sum_ref[rows, :], dy_ref[rows, :]
        units, inverse = standard(hidden_ref[rows, :])
        grad_hidden = dy + standard_back(grads, gain, units, inverse)
        grad_hidden_ref[rows, :] = grad_hidden
        low_ref[rows, :] = grad_hidden.astype(jnp.bfloat16)
        vec_grad_ref[2:3, :] += column_sum(grad_hidden)
        vec_grad_ref[3:4, :] += column_sum(grads * units)
        vec_grad_ref[4:5, :] += column_sum(grads)
        vec_grad_ref[5:6, :] += column_sum(dy)
        return carry

    lax.fori_loop(0, OWN // 128, norm_rows, 0)
    between()
    row = lax.broadcasted_iota(jnp.int32, (8, 128), 0)
    lane = lax.broadcasted_iota(jnp.int32, (8, 128), 1)
    picks = jnp.where((row < 2) & ((lane < HEAD) == (row == 0)), 1.0, 0.0)

    def pair_step(pair, carry):
        out_term = dot(attended_t_ref[pair], low_ref[...]).astype(jnp.bfloat16)
        for part in range(PARTS):
            grads_ref[part, pair, :, 1024:1152] = out_term[:, part * 128 : (part + 1) * 128]
        grad_att = dot(low_ref[...], out_ref[pair], BOTH_LAST).astype(jnp.bfloat16)
        wide = grad_att.astype(jnp.float32)
        for parity in range(2):
            grad_att_ref[pair, parity] = keep_head(wide, parity).astype(jnp.bfloat16)
        centres = lax.dot_general(picks, wide * attended_ref[pair], BOTH_LAST, precision=lax.Precision.HIGHEST, preferred_element_type=jnp.float32)
        centre_ref[pair] = centres
        return carry

    lax.fori_loop(0, PAIRS, pair_step, 0)


def attend_rows_back(signed, query_ref, kv_ref, grad_att_ref, bias_ref, log_ref, centre_ref, grad_query_ref, grad_kv_ref, send_ref, before_pair, after_pair):
    core = lax.axis_index("section")
    slots, keys = task_plan(core)
    early = jnp.where(core == 0, 0.0, 1.0)
    lane = lax.broadcasted_iota(jnp.int32, (BLOCK, 128), 1)
    grad_kv_ref[...] = jnp.zeros_like(grad_kv_ref)

    def pair_step(turn, carry):
        pair = turn_part(turn + 1)
        before_pair(turn)
        parts = [[None] * TASKS, [None] * TASKS]
        for task in range(TASKS):
            rows = tile_rows(slots[task] * BLOCK, BLOCK)
            key_rows = tile_rows(keys[task] * BLOCK, BLOCK)
            key_part, value_part = kv_ref[0, pair, key_rows, :], kv_ref[1, pair, key_rows, :]
            key_term, value_term = None, None
            for parity in range(2):
                queries = query_ref[pair, parity, rows, :]
                grad_att = grad_att_ref[pair, parity, rows, :]
                scores = dot(key_part, queries, BOTH_LAST)
                grad_weights = dot(value_part, grad_att, BOTH_LAST)
                log_row = log_ref[slots[task], pl.ds(pair * 2 + parity, 1), :]
                centre = centre_ref[pair, parity : parity + 1, rows]
                if signed:
                    raised = scores * scores + 1.0
                    inverse = lax.rsqrt(raised)
                    factor = scores * inverse
                    probs = jnp.exp(raised * inverse + bias_ref[task] - log_row)
                    weights = factor * probs
                    grad_scores = weights * (factor * grad_weights - centre)
                    grad_scores = grad_scores + probs * grad_weights * (inverse * inverse * inverse)
                else:
                    weights = jnp.exp(scores + bias_ref[task] - log_row)
                    grad_scores = weights * (grad_weights - centre)
                grad_low = grad_scores.astype(jnp.bfloat16)
                new_key = dot(grad_low, queries)
                new_value = dot(weights.astype(jnp.bfloat16), grad_att)
                key_term = new_key if parity == 0 else key_term + new_key
                value_term = new_value if parity == 0 else value_term + new_value
                parts[parity][task] = dot(grad_low, key_part, BOTH_FIRST)
            grad_kv_ref[0, pair, key_rows, :] += key_term
            grad_kv_ref[1, pair, key_rows, :] += value_term
        merged = []
        for task in range(TASKS):
            merged.append(jnp.where(lane < HEAD, parts[0][task], parts[1][task]))
        grad_query_ref[pair, :BLOCK, :] = ((merged[0] + merged[1] * early) * 0.125).astype(jnp.bfloat16)
        grad_query_ref[pair, BLOCK:, :] = ((merged[1] * (1.0 - early) + merged[2] + merged[3] + merged[4]) * 0.125).astype(jnp.bfloat16)
        for slot, block in enumerate(blocks_of(1 - core)):
            for kind in range(2):
                rows = grad_kv_ref[kind, pair, tile_rows(block * BLOCK, BLOCK), :]
                send_ref[kind, pair, slot * BLOCK : (slot + 1) * BLOCK, :] = rows.astype(jnp.bfloat16)
        after_pair(turn, pair)
        return carry

    lax.fori_loop(0, PAIRS, pair_step, 0)


def project_back_pair(pair, grad_query_ref, grad_kv_ref, other_ref, normed_t_ref, weight_ref, grads_ref, sum_ref, send):
    parts = [grad_query_ref[pair]]
    for kind in range(2):
        halves = []
        for slot, block in enumerate(blocks_of(lax.axis_index("section"))):
            own = grad_kv_ref[kind, pair, tile_rows(block * BLOCK, BLOCK), :]
            halves.append(own + other_ref[kind, pair, slot * BLOCK : (slot + 1) * BLOCK, :].astype(jnp.float32))
        parts.append(jnp.concatenate(halves, axis=0).astype(jnp.bfloat16))
    grads = jnp.concatenate(parts, axis=1)
    term = dot(normed_t_ref[...], grads).astype(jnp.bfloat16)
    for part in range(PARTS):
        grads_ref[part, pair, :, 1152:1536] = term[part * 128 : (part + 1) * 128, :]
    send()
    sum_ref[...] += dot(grads, weight_ref[pair], BOTH_LAST)


def project_back_norm(x_ref, grad_hidden_ref, vec_ref, grad_x_ref, grad_x_low_ref, vec_grad_ref, sum_ref):
    gain = vec_ref[0, 0:1, :]

    def norm_rows(index, carry):
        rows = tile_rows(index * 128, 128)
        grads = sum_ref[rows, :]
        units, inverse = standard(x_ref[rows, :].astype(jnp.float32))
        grad_x = grad_hidden_ref[rows, :] + standard_back(grads, gain, units, inverse)
        grad_x_ref[rows, :] = grad_x
        grad_x_low_ref[rows, :] = grad_x.astype(jnp.bfloat16)
        vec_grad_ref[0:1, :] += column_sum(grads * units)
        vec_grad_ref[1:2, :] += column_sum(grads)
        return carry

    lax.fori_loop(0, OWN // 128, norm_rows, 0)


def greet(partners):
    barrier = pltpu.get_barrier_semaphore()
    for partner in partners:
        pl.semaphore_signal(barrier, inc=1, device_id=partner, device_id_type=MESH)
    pl.semaphore_wait(barrier, len(partners))


def along_tensor(step):
    core, rep, part = place()
    return (core, rep, lax.rem(part + step, PARTS))


def along_dp(step):
    core, rep, part = place()
    return (core, lax.bitwise_xor(rep, step), part)


def sibling():
    core, rep, part = place()
    return (1 - core, rep, part)


def all_partners():
    return [along_tensor(step) for step in (1, 2, 3)] + [along_dp(step) for step in (1, 2, 3)] + [sibling()]


def remote(source, target, send, receive, device):
    return pltpu.make_async_remote_copy(src_ref=source, dst_ref=target, send_sem=send, recv_sem=receive, device_id=device, device_id_type=MESH)


def fill_masks(lens_ref, bias_ref, turned):
    core, rep, part = place()
    slots, keys = task_plan(core)
    bounds, bound = [], 0
    for index in range(lens_ref.shape[1]):
        bound = bound + lens_ref[part, index]
        bounds.append(bound)
    for task in range(TASKS):
        block = jnp.where(slots[task] == 0, core, 3 - core)
        shape = (1, BLOCK) if turned else (BLOCK, 1)
        query = block * BLOCK + lax.broadcasted_iota(jnp.int32, shape, 1 if turned else 0)
        start = jnp.zeros(shape, jnp.int32)
        for bound in bounds:
            start = jnp.where(query >= bound, bound, start)
        key = keys[task] * BLOCK + lax.broadcasted_iota(jnp.int32, (BLOCK, BLOCK), 0 if turned else 1)
        bias_ref[task] = jnp.where((key >= start) & (key <= query), 0.0, NEGATIVE)


def quarter_rows(array, which):
    count = array.shape[0] // PARTS
    return tile_rows(which * count, count)


SAVED = (
    ((OWN, WIDTH), jnp.bfloat16),
    ((WIDTH, OWN), jnp.bfloat16),
    ((PAIRS, 2, OWN, 128), jnp.bfloat16),
    ((2, PAIRS, 1024, 128), jnp.bfloat16),
    ((PAIRS, OWN, 128), jnp.float32),
    ((PAIRS, 128, OWN), jnp.bfloat16),
    ((2, 8, BLOCK), jnp.float32),
    ((OWN, WIDTH), jnp.float32),
    ((WIDTH, OWN), jnp.bfloat16),
    ((PARTS, OWN, 512), jnp.bfloat16),
    ((PARTS, OWN, 512), jnp.bfloat16),
)
WEIGHTS = (
    ((PARTS, 512, 384), jnp.bfloat16),
    ((PARTS, 128, 512), jnp.bfloat16),
    ((PARTS, 512, 512), jnp.bfloat16),
    ((PARTS, 512, 512), jnp.bfloat16),
    ((PARTS, 8, 512), jnp.float32),
)
QKV, OUT, UP, DOWN, VEC = range(5)


ALL = (1, 2, 3)
FORWARD_PLAN = (
    ("masks", None, 0, "near", ALL, (QKV,)),
    ("masks", None, 0, "z", ALL, (OUT,)),
    ("masks", None, 0, "z", (1,), (UP, DOWN)),
    ("masks", None, 0, "own", None, (QKV, OUT, UP, DOWN)),
    ("vec", None, 0, "far", ALL, (QKV,)),
    ("vec", None, 0, "z", (2,), (UP, DOWN)),
    ("rows", None, 0, "z", (3,), (UP, DOWN)),
    ("norm0", None, 0, "sib", ALL, (QKV,)),
    ("norm0", None, 1, "own", None, (QKV, OUT, UP, DOWN)),
    ("project0", 0, 0, "near", ALL, (OUT,)),
    ("project0", 1, 0, "near", (1,), (UP, DOWN)),
    ("project0", 3, 0, "far", ALL, (OUT,)),
    ("project0", 3, 0, "near", (2,), (UP, DOWN)),
    ("attend0", 0, 0, "far", (1,), (UP, DOWN)),
    ("attend0", 1, 0, "sib", ALL, (OUT,)),
    ("attend0", 1, 0, "near", (3,), (UP, DOWN)),
    ("attend0", 2, 0, "far", (2,), (UP, DOWN)),
    ("attend0", 2, 0, "sib", (1,), (UP, DOWN)),
    ("attend0", 2, 1, "z", ALL, (QKV,)),
    ("attend0", 3, 0, "far", (3,), (UP, DOWN)),
    ("attended0", None, 0, "sib", (2,), (UP, DOWN)),
    ("attended0", None, 1, "z", ALL, (OUT, UP, DOWN)),
    ("second0", None, 0, "sib", (3,), (UP, DOWN)),
    ("chunk0", 0, 1, "near", ALL, (QKV,)),
    ("chunk0", 2, 1, "far", ALL, (QKV,)),
    ("chunk0", 3, 1, "sib", ALL, (QKV,)),
    ("project1", 0, 1, "near", ALL, (OUT,)),
    ("project1", 1, 1, "near", (1,), (UP, DOWN)),
    ("project1", 2, 1, "near", (2,), (UP, DOWN)),
    ("project1", 3, 1, "near", (3,), (UP, DOWN)),
    ("attend1", 1, None, "rows", None, ()),
    ("attend1", 1, 1, "far", ALL, (OUT,)),
    ("attend1", 2, 1, "far", (1, 2), (UP, DOWN)),
    ("attend1", 3, 1, "far", (3,), (UP, DOWN)),
    ("attend1", 3, 1, "sib", ALL, (OUT,)),
    ("attended1", None, 1, "sib", (1, 2), (UP, DOWN)),
    ("chunk1", 0, 1, "sib", (3,), (UP, DOWN)),
)


def forward_kernel(lens_ref, tokens, cotangent, *refs):
    shards, refs = refs[:5], refs[5:]
    dy_out, y_out, saved_out, weights_out, refs = refs[0], refs[1], refs[2:13], refs[13:18], refs[18:]
    saved, weights, refs = refs[:11], refs[11:16], refs[16:]
    y_ref, bias_ref, normed, logit, factor, stat, wide, total, refs = *refs[:8], refs[8:]
    row_send, row_recv, row_local, z_send, z_recv, xy_send, xy_recv, sib_send, sib_recv, local, kv_send, kv_recv, save_sem, keep_sem = refs
    core, rep, part = place()
    greet(all_partners())

    steps = (1, 2, 3)

    def z_copy(index, step):
        slot = (index, step - 1)
        if index == VEC:
            return remote(shards[index], weights[index].at[core, part], z_send.at[slot], z_recv.at[slot], along_tensor(step))
        rows = quarter_rows(shards[index], rep)
        return remote(shards[index].at[rows], weights[index].at[core, part, rows], z_send.at[slot], z_recv.at[slot], along_tensor(step))

    def own_copy(index):
        return pltpu.make_async_copy(shards[index], weights[index].at[core, part], local.at[index])

    def near_copy(index, step, far):
        slot = (index, far - 1, step - 1)
        view = weights[index].at[core, turn_part(far), quarter_rows(shards[index], rep)]
        return remote(view, view, xy_send.at[slot], xy_recv.at[slot], along_dp(step))

    def far_copy(index, step, far):
        slot = (index, far - 1, step + 1)
        count = shards[index].shape[0] // PARTS
        rows = tile_rows(lax.bitwise_xor(rep, 3 - step) * count + (2 - step) * (count // 2), count // 2)
        view = weights[index].at[core, turn_part(far), rows]
        return remote(view, view, xy_send.at[slot], xy_recv.at[slot], along_dp(step))

    def sib_copy(index, far):
        target = weights[index].at[core, turn_part(far)]
        source = target if far else shards[index]
        return remote(source, target, sib_send.at[index, far], sib_recv.at[index, far], sibling())

    def vec_copy():
        view = weights[VEC].at[core]
        return remote(view, view, sib_send.at[VEC, 0], sib_recv.at[VEC, 0], sibling())

    def own_start(*which):
        for index in which:
            own_copy(index).start()
            sib_copy(index, 0).start()

    def z_start(far, *which):
        for index in which:
            z_copy(index, PARTS - far).start()

    def xy_start(far, *which):
        for index in which:
            z_copy(index, PARTS - far).wait_recv()
            for step in (1, 2):
                near_copy(index, step, far).start()

    def far_start(far, *which):
        for index in which:
            for step in (2, 1):
                near_copy(index, 3 - step, far).wait_recv()
                far_copy(index, step, far).start()

    def sib_start(far, *which):
        for index in which:
            for step in (1, 2):
                far_copy(index, step, far).wait_recv()
            sib_copy(index, far).start()

    def need(layer, far, *which):
        @pl.when(core != layer)
        def _():
            for index in which:
                sib_copy(index, far).wait_recv()

        if far == 0:

            @pl.when(core == layer)
            def _():
                for index in which:
                    own_copy(index).wait()

    def need_turn(layer, turn, *which):
        for far in range(PARTS):
            pl.when(turn == far)(partial(need, layer, far, *which))

    def keep_copy(layer, index):
        return pltpu.make_async_copy(weights[index].at[layer], weights_out[index].at[layer], keep_sem.at[layer, index])

    def keep(layer, *which):
        for index in which:
            keep_copy(layer, index).start()

    def on(layer, action, *which):
        pl.when(core == layer)(partial(action, *which))

    def at(layer, turn, when, action, *which):
        pl.when((core == layer) & (turn == when))(partial(action, *which))

    owner = jnp.where((part == 0) | (part == 3), 0, 1)
    place_here = jnp.where(part < 2, 0, 1)
    row_pairs = ((tokens, saved[0].at[0]), (cotangent, dy_out))

    def row_targets(array, batch):
        source, target = row_pairs[array]
        rows = target.at[tile_rows(place_here * BLOCK, BLOCK)]
        there = remote(source.at[batch], rows, row_send.at[array, batch], row_recv.at[array, place_here], (core, rep, batch))
        here = pltpu.make_async_copy(source.at[batch], rows, row_local.at[array])
        return there, here

    def rows_each(array, act):
        for batch in range(PARTS):
            there, here = row_targets(array, batch)

            @pl.when((core == owner) & (part != batch))
            def _():
                there.start() if act == "start" else there.wait_send()

            @pl.when((core == owner) & (part == batch))
            def _():
                here.start() if act == "start" else here.wait()

    def rows_arrived(array):
        for slot, block in enumerate(blocks_of(core)):

            @pl.when(block != part)
            def _():
                source, target = row_pairs[array]
                rows = target.at[slot * BLOCK : (slot + 1) * BLOCK]
                remote(source.at[0], rows, row_send.at[array, 0], row_recv.at[array, slot], sibling()).wait_recv()

    def save(layer, *which):
        for index in which:
            pltpu.make_async_copy(saved[index].at[layer], saved_out[index].at[layer], save_sem.at[layer, index]).start()

    def kv_copies(layer, pair, receiving):
        copies = []
        for slot, block in enumerate(blocks_of(1 - core if receiving else core)):
            view = saved[3].at[layer, :, pair, tile_rows(block * BLOCK, BLOCK), :]
            copies.append(remote(view, view, kv_send.at[layer, pair, slot], kv_recv.at[layer, pair, slot], sibling()))
        return copies

    actions = {"own": own_start, "z": z_start, "near": xy_start, "far": far_start, "sib": sib_start}

    def run(point, turn=None):
        for where, when, owner_core, name, fars, which in FORWARD_PLAN:
            if where != point:
                continue

            def act():
                if name == "own":
                    own_start(*which)
                elif name == "rows":
                    rows_each(1, "start")
                else:
                    for far in fars:
                        actions[name](far, *which)

            here = core == owner_core if owner_core is not None else None
            if turn is not None:
                here = turn == when if here is None else here & (turn == when)
            act() if here is None else pl.when(here)(act)

    for far in steps:
        on(0, z_start, far, QKV)
        z_start(far, VEC)
    own_copy(VEC).start()
    rows_each(0, "start")
    fill_masks(lens_ref, bias_ref, False)
    run("masks")
    own_copy(VEC).wait()
    for step in steps:
        z_copy(VEC, step).wait_recv()
    vec_copy().start()
    run("vec")
    rows_each(0, "wait")
    rows_arrived(0)
    vec_copy().wait_recv()
    run("rows")
    for layer in range(2):
        signed = layer == 0
        held = [item.at[layer] for item in saved]
        qkv, out, up, down, vec = [item.at[layer] for item in weights]
        x_ref, normed_one_t, queries, kv, attended, attended_t, logs, hidden, normed_two_t, act, slope = held

        def after_norm():
            run(f"norm{layer}")

        def before_project(turn):
            run(f"project{layer}", turn)
            need_turn(layer, turn, QKV)

        def push_kv(turn, pair):
            for copy in kv_copies(layer, pair, False):
                copy.start()

        def before_attend(turn, pair):
            run(f"attend{layer}", turn)
            for copy in kv_copies(layer, pair, True):
                copy.wait_recv()

        def before_out(turn):
            need_turn(layer, turn, OUT)

        def before_feed():
            run(f"second{layer}")

        def before_chunk(turn):
            need_turn(layer, turn, UP, DOWN)
            if layer == 1:
                pl.when(turn == PARTS - 1)(partial(keep, 1, OUT, UP, DOWN))

        def during_chunk(turn):
            run(f"chunk{layer}", turn)

        project(x_ref, vec, qkv, normed_one_t, queries, kv, normed, after_norm, before_project, push_kv)
        save(layer, 0, 1, 2)
        keep(layer, QKV, VEC)
        attend_rows(signed, queries, kv, bias_ref, attended, attended_t, logs, logit, factor, stat, before_attend)
        save(layer, 3, 4, 5, 6)
        run(f"attended{layer}")
        target = saved[0].at[1] if layer == 0 else y_ref
        feed(x_ref, attended, vec, out, up, down, hidden, normed_two_t, act, slope, target, normed, wide, total, before_out, before_feed, before_chunk, during_chunk)
        save(layer, 7, 8, 9, 10)
        if layer == 0:
            keep(0, OUT, UP, DOWN)
    y_copy = pltpu.make_async_copy(y_ref, y_out, row_local.at[0])
    y_copy.start()
    rows_each(1, "wait")
    rows_arrived(1)
    for index in range(5):
        for step in steps:
            z_copy(index, step).wait_send()
            if index != VEC:
                for way in (1, 2):
                    near_copy(index, way, step).wait_send()
                    far_copy(index, way, step).wait_send()
                sib_copy(index, step).wait_send()
        sib_copy(index, 0).wait_send() if index != VEC else vec_copy().wait_send()
    for layer in range(2):
        for pair in range(PAIRS):
            for copy in kv_copies(layer, pair, False):
                copy.wait_send()
        for index in range(11):
            pltpu.make_async_copy(saved[index].at[layer], saved_out[index].at[layer], save_sem.at[layer, index]).wait()
    y_copy.wait()
    for layer in range(2):
        for index in range(5):
            keep_copy(layer, index).wait()


FEED, ATTEND = 0, 1
GROUPS = ((0, 1024), (1024, 1536))


def backward_kernel(lens_ref, dy_in, y_in, *refs):
    saved_in, weights_in, refs = refs[:11], refs[11:16], refs[16:]
    grads_out, vec_out, blocks_out, rows_out, refs = *refs[:4], refs[4:]
    held, weights, refs = refs[:11], refs[11:16], refs[16:]
    dy_low, dy_ref, bias_ref, grads_ref, vec_grad, low, low_t, chunk, total, grad_hidden, grad_att, centres, grad_query, grad_kv, kv_out, kv_got, grad_low, refs = *refs[:17], refs[17:]
    got_core, got_first, got_second, part_sum, got_part, final, vec_core, vec_chip, vec_dp, vec_rep, vec_part, refs = *refs[:11], refs[11:]
    load_sem, weight_sem, dy_sem, y_send, y_recv, row_send, row_recv, kv_send, kv_recv, core_send, core_recv, first_send, first_recv, second_send, second_recv, part_send, part_recv, vec_send, vec_recv, last_send, last_recv = refs
    core, rep, part = place()
    steps = (1, 2, 3)
    mine, theirs = tile_rows(core * 64, 64), tile_rows((1 - core) * 64, 64)

    def load(layer, which=(), matrices=()):
        copies = [pltpu.make_async_copy(saved_in[index].at[layer], held[index], load_sem.at[index]) for index in which]
        return copies + [pltpu.make_async_copy(weights_in[index].at[layer], weights[index], weight_sem.at[index]) for index in matrices]

    def start(copies):
        for copy in copies:
            copy.start()

    def wait(copies):
        for copy in copies:
            copy.wait()

    chunk_set = ((10, 9, 8), (DOWN, UP))
    norm_set = ((7, 5, 4), (VEC, OUT))
    attend_set = ((2, 3, 6), ())
    project_set = ((0, 1), (QKV,))
    dy_copy = pltpu.make_async_copy(dy_in, dy_low, dy_sem.at[0])
    dy_copy.start()
    for group in (chunk_set, norm_set, attend_set, project_set):
        start(load(1, *group))
    greet(all_partners() + [(1 - core, rep, lax.rem(part + step, PARTS)) for step in steps])

    owner = jnp.where((part == 0) | (part == 3), 0, 1)

    def deliver(source, layer, target, send, receive, act):
        for slot, block in enumerate(blocks_of(core)):
            rows = source.at[slot * BLOCK : (slot + 1) * BLOCK]
            stays = (core == layer) & (block == part)

            @pl.when(stays)
            def _():
                copy = pltpu.make_async_copy(rows, target.at[part], send.at[layer, slot])
                copy.start() if act == "start" else copy.wait()

            @pl.when(jnp.logical_not(stays))
            def _():
                copy = remote(rows, target.at[part], send.at[layer, slot], receive.at[part], (layer, rep, block))
                copy.start() if act == "start" else copy.wait_send()

    def delivered(target, source, send, receive):
        for batch in range(PARTS):

            @pl.when((core != owner) | (part != batch))
            def _():
                remote(source.at[:BLOCK], target.at[batch], send.at[0, 0], receive.at[batch], sibling()).wait_recv()

    deliver(saved_in[0].at[1], 0, blocks_out, y_send, y_recv, "start")
    deliver(y_in, 1, blocks_out, y_send, y_recv, "start")

    def core_copy(layer, group, turn):
        first, last = GROUPS[group]
        other, slot = turn_part(turn + 1), (layer, group, turn)
        return remote(grads_ref.at[:, other, theirs, first:last], got_core.at[layer, :, other, :, first:last], core_send.at[slot], core_recv.at[slot], sibling())

    def halves(way):
        return pl.ds(0, 32) if way == 1 else pl.ds(32, 32)

    def first_copy(layer, group, turn, way, piece):
        first, last = GROUPS[group]
        other, slot = turn_part(turn + 1), (layer, group, turn, way - 1, piece)
        source = got_core.at[layer, lax.bitwise_xor(rep, 3 if piece else way), other, halves(way), first:last]
        return remote(source, got_first.at[layer, way - 1, piece, other, :, first:last], first_send.at[slot], first_recv.at[slot], along_dp(way))

    def second_copy(layer, group, turn, way):
        first, last = GROUPS[group]
        other, slot = turn_part(turn + 1), (layer, group, turn, way - 1)
        source = got_core.at[layer, lax.bitwise_xor(rep, 3 - way), other, halves(way), first:last]
        return remote(source, got_second.at[layer, way - 1, other, :, first:last], second_send.at[slot], second_recv.at[slot], along_dp(3 - way))

    def part_copy(layer, group, turn):
        first, last = GROUPS[group]
        slot = (layer, group, turn)
        return remote(part_sum.at[layer, turn, :, first:last], got_part.at[layer, turn, :, first:last], part_send.at[slot], part_recv.at[slot], along_tensor(turn + 1))

    def dp_start(layer, group, turn):
        first, last = GROUPS[group]
        core_copy(layer, group, turn).wait()
        other = turn_part(turn + 1)

        def add(major, carry):
            own = grads_ref[major, other, mine, first:last].astype(jnp.float32)
            sum_here = own + got_core[layer, major, other, :, first:last].astype(jnp.float32)
            got_core[layer, major, other, :, first:last] = sum_here.astype(jnp.bfloat16)
            return carry

        lax.fori_loop(0, PARTS, add, 0)
        start(first_copy(layer, group, turn, way, piece) for way in (1, 2) for piece in range(2))

    def dp_next(layer, group, turn):
        first, last = GROUPS[group]
        other = turn_part(turn + 1)
        for way in (1, 2):
            for piece in (1, 0):
                first_copy(layer, group, turn, way, piece).wait()
                major = lax.bitwise_xor(rep, 3 - way) if piece else rep
                own = got_core[layer, major, other, halves(way), first:last].astype(jnp.float32)
                sum_here = own + got_first[layer, way - 1, piece, other, :, first:last].astype(jnp.float32)
                got_core[layer, major, other, halves(way), first:last] = sum_here.astype(jnp.bfloat16)
                if piece:
                    second_copy(layer, group, turn, way).start()

    def part_start(layer, group, turn):
        first, last = GROUPS[group]
        other = turn_part(turn + 1)
        for way in (1, 2):
            second_copy(layer, group, turn, way).wait()
            own = got_core[layer, rep, other, halves(way), first:last].astype(jnp.float32)
            sum_here = own + got_second[layer, way - 1, other, :, first:last].astype(jnp.float32)
            part_sum[layer, turn, halves(way), first:last] = sum_here.astype(jnp.bfloat16)
        if turn < PARTS - 1:
            part_copy(layer, group, turn).start()

    def finish(layer, group):
        first, last = GROUPS[group]
        sum_here = part_sum[layer, PARTS - 1, :, first:last].astype(jnp.float32)
        for turn in range(PARTS - 1):
            part_copy(layer, group, turn).wait()
            sum_here = sum_here + got_part[layer, turn, :, first:last].astype(jnp.float32)
        final[layer, :, first:last] = sum_here

    def last_copy(layer):
        return remote(final.at[layer], grads_out.at[mine], last_send.at[0], last_recv.at[0], sibling())

    def hand_over(layer):
        @pl.when(core == layer)
        def _():
            grads_out[mine, :] = final[layer]

        @pl.when(core != layer)
        def _():
            last_copy(layer).start()

    def kv_copy(layer, pair):
        return remote(kv_out.at[:, pair], kv_got.at[layer, :, pair], kv_send.at[layer, pair], kv_recv.at[layer, pair], sibling())

    fill_masks(lens_ref, bias_ref, True)
    for layer in (1, 0):
        signed = layer == 0
        x_ref, normed_one_t, queries, kv, attended, attended_t, logs, hidden, normed_two_t, act, slope = held
        qkv, out, up, down, vec = weights
        if layer == 1:
            dy_copy.wait()
            dy_ref[...] = dy_low[...].astype(jnp.float32)
        wait(load(layer, *chunk_set))

        def at(turn, when, action, *which):
            pl.when(turn == when)(partial(action, *which))

        def during_chunk(turn):
            pl.when(turn > 0)(lambda: dp_start(layer, FEED, turn - 1))
            at(turn, 3, dp_next, layer, FEED, 0)
            if layer == 0:
                at(turn, 0, dp_next, 1, ATTEND, 1)
                at(turn, 0, dp_next, 1, ATTEND, 2)
                at(turn, 1, dp_next, 1, ATTEND, 3)
                at(turn, 1, part_start, 1, ATTEND, 0)
                at(turn, 2, part_start, 1, ATTEND, 1)
                at(turn, 2, part_start, 1, ATTEND, 2)
                at(turn, 2, finish, 1, FEED)
                at(turn, 3, part_start, 1, ATTEND, 3)

        def after_chunk(turn, chunk):
            core_copy(layer, FEED, turn).start()

        def before_norm():
            wait(load(layer, *norm_set))

        def after_norm():
            dp_start(layer, FEED, 3)
            dp_next(layer, FEED, 1)

        feed_back(dy_ref, act, slope, down, up, hidden, normed_two_t, vec, out, attended, attended_t, grad_hidden, grad_att, centres, grads_ref, vec_grad.at[layer], low, low_t, chunk, total, during_chunk, after_chunk, before_norm, after_norm)
        if layer == 1:
            start(load(0, (9, 10, 7, 8, 4, 5), (DOWN, UP, OUT)))
        wait(load(layer, *attend_set))

        def before_attend(turn):
            at(turn, 0, dp_next, layer, FEED, 2)
            at(turn, 1, dp_next, layer, FEED, 3)
            at(turn, 1, part_start, layer, FEED, 0)
            at(turn, 1, part_start, layer, FEED, 1)
            at(turn, 2, part_start, layer, FEED, 2)
            at(turn, 3, part_start, layer, FEED, 3)
            if layer == 0:
                at(turn, 0, finish, 1, ATTEND)
                at(turn, 0, hand_over, 1)

        def project_turn(turn):
            pair = turn_part(turn + 1)
            kv_copy(layer, pair).wait()
            project_back_pair(pair, grad_query, grad_kv, kv_got.at[layer], normed_one_t, qkv, grads_ref, total, core_copy(layer, ATTEND, turn).start)

        def after_attend(turn, pair):
            kv_copy(layer, pair).start()
            at(turn, 2, dp_start, layer, ATTEND, 0)
            at(turn, 3, dp_start, layer, ATTEND, 1)
            at(turn, 3, dp_next, layer, ATTEND, 0)
            pl.when(turn > 0)(lambda: project_turn(turn - 1))

        wait(load(layer, *project_set))
        total[...] = jnp.zeros_like(total)
        attend_rows_back(signed, queries, kv, grad_att, bias_ref, logs, centres, grad_query, grad_kv, kv_out, before_attend, after_attend)
        if layer == 1:
            start(load(0, *attend_set))
        dp_start(layer, ATTEND, 2)
        project_turn(PAIRS - 1)
        project_back_norm(x_ref, grad_hidden, vec, dy_ref, grad_low.at[layer], vec_grad.at[layer], total)
        if layer == 1:
            start(load(0, (0, 1), (QKV, VEC)))
        deliver(grad_low.at[layer], layer, rows_out, row_send, row_recv, "start")
        dp_start(layer, ATTEND, 3)
    vec_copy = remote(vec_grad.at[1 - core], vec_core, vec_send.at[0], vec_recv.at[0], sibling())
    vec_copy.start()
    dp_next(0, ATTEND, 1)
    dp_next(0, ATTEND, 2)
    finish(0, FEED)
    vec_copy.wait()
    vec_chip[...] = vec_grad[core] + vec_core[...]
    vec_copies = [remote(vec_chip, vec_dp.at[step - 1], vec_send.at[step], vec_recv.at[step], along_dp(step)) for step in steps]
    start(vec_copies)
    dp_next(0, ATTEND, 3)
    for turn in range(PARTS):
        part_start(0, ATTEND, turn)
    wait(vec_copies)
    vec_rep[...] = vec_chip[...] + vec_dp[0] + vec_dp[1] + vec_dp[2]
    vec_copies = [remote(vec_rep, vec_part.at[step - 1], vec_send.at[3 + step], vec_recv.at[3 + step], along_tensor(step)) for step in steps]
    start(vec_copies)
    finish(0, ATTEND)
    hand_over(0)
    wait(vec_copies)
    vec_out[...] = vec_rep[...] + vec_part[0] + vec_part[1] + vec_part[2]
    deliver(saved_in[0].at[1], 0, blocks_out, y_send, y_recv, "wait")
    deliver(y_in, 1, blocks_out, y_send, y_recv, "wait")
    delivered(blocks_out, y_in, y_send, y_recv)
    for layer in range(2):
        deliver(grad_low.at[layer], layer, rows_out, row_send, row_recv, "wait")
    delivered(rows_out, grad_low.at[0], row_send, row_recv)
    last_copy(0).wait_recv()
    last_copy(0).wait_send()


def specs(space, count):
    return [pl.BlockSpec(memory_space=space)] * count


def kernel_call(body, name, ins, in_specs, outs, out_specs, scratch, collective):
    dma = pltpu.SemaphoreType.DMA
    return pl.pallas_call(
        body,
        out_shape=[jax.ShapeDtypeStruct(shape, kind) for shape, kind in outs],
        in_specs=in_specs,
        out_specs=out_specs,
        scratch_shapes=[pltpu.VMEM(*item) if len(item) == 2 and isinstance(item[0], tuple) else dma(item) for item in scratch],
        compiler_params=pltpu.CompilerParams(collective_id=collective, has_side_effects=True, vmem_limit_bytes=60 * 2**20),
        name=name,
    )(*ins)


def twice(items):
    return tuple(((2, *shape), kind) for shape, kind in items)


def on_device_whole(
    tokens,
    lengths,
    cotangent,
    ln_one_gain,
    ln_one_bias,
    qkv_weight,
    out_weight,
    out_bias,
    ln_two_gain,
    ln_two_bias,
    up_weight,
    up_bias,
    down_weight,
    down_bias,
):
    f32, low = jnp.float32, jnp.bfloat16
    core, rep, part = place()
    vec = jnp.concatenate([ln_one_gain, ln_one_bias, out_bias, ln_two_gain, ln_two_bias, down_bias, up_bias, jnp.zeros_like(up_bias)])
    rows, rows_low = ((OWN, WIDTH), f32), ((OWN, WIDTH), low)
    square = ((BLOCK, BLOCK), f32)
    results = kernel_call(
        forward_kernel,
        "forward",
        (lengths, tokens, cotangent, qkv_weight.reshape(WIDTH, 384), out_weight[0], up_weight[0], down_weight[0], vec),
        specs(pltpu.SMEM, 1) + specs(pl.ANY, 7),
        (rows_low, rows_low, *twice(SAVED), *twice(WEIGHTS)),
        specs(pl.ANY, 18),
        (
            *twice(SAVED),
            *twice(WEIGHTS),
            rows_low,
            ((TASKS, BLOCK, BLOCK), f32),
            rows_low,
            ((TASKS, BLOCK, BLOCK), f32),
            ((TASKS, BLOCK, BLOCK), f32),
            ((2, BLOCK, 128), f32),
            rows,
            rows,
            (2, 4),
            (2, 2),
            (2,),
            (5, 3),
            (5, 3),
            (4, 3, 4),
            (4, 3, 4),
            (5, PARTS),
            (5, PARTS),
            (5,),
            (2, PAIRS, 2),
            (2, PAIRS, 2),
            (2, 11),
            (2, 5),
        ),
        0,
    )
    grads, vec_sum, block_outputs, grad_rows = kernel_call(
        backward_kernel,
        "backward",
        (lengths, *results),
        specs(pltpu.SMEM, 1) + specs(pl.ANY, 18),
        (((128, 1536), f32), ((16, 512), f32), ((PARTS, BLOCK, WIDTH), low), ((PARTS, BLOCK, WIDTH), low)),
        specs(pltpu.VMEM, 2) + specs(pl.ANY, 2),
        (
            *SAVED,
            *WEIGHTS,
            rows_low,
            rows,
            ((TASKS, BLOCK, BLOCK), f32),
            ((PARTS, PARTS, 128, 1536), low),
            ((2, 16, 512), f32),
            rows_low,
            ((WIDTH, OWN), low),
            ((OWN, 512), low),
            rows,
            rows,
            ((PAIRS, 2, OWN, 128), low),
            ((PAIRS, 8, OWN), f32),
            ((PAIRS, OWN, 128), low),
            ((2, PAIRS, 1024, 128), f32),
            ((2, PAIRS, OWN, 128), low),
            ((2, 2, PAIRS, OWN, 128), low),
            ((2, OWN, WIDTH), low),
            ((2, PARTS, PARTS, 64, 1536), low),
            ((2, 2, 2, PARTS, 32, 1536), low),
            ((2, 2, PARTS, 32, 1536), low),
            ((2, PARTS, 64, 1536), low),
            ((2, 3, 64, 1536), low),
            ((2, 64, 1536), f32),
            ((16, 512), f32),
            ((16, 512), f32),
            ((3, 16, 512), f32),
            ((16, 512), f32),
            ((3, 16, 512), f32),
            (11,),
            (5,),
            (1,),
            (2, 2),
            (PARTS,),
            (2, 2),
            (PARTS,),
            (2, PAIRS),
            (2, PAIRS),
            (2, 2, PARTS),
            (2, 2, PARTS),
            (2, 2, PARTS, 2, 2),
            (2, 2, PARTS, 2, 2),
            (2, 2, PARTS, 2),
            (2, 2, PARTS, 2),
            (2, 2, PARTS),
            (2, 2, PARTS),
            (7,),
            (7,),
            (1,),
            (1,),
        ),
        1,
    )
    spread = lax.dynamic_slice_in_dim(vec_sum, (rep * PARTS + part) * 32, 32, 1)
    up_bias_grad = lax.dynamic_slice(vec_sum, (6 + part, rep * 128), (1, 128))
    return (
        block_outputs[None],
        grad_rows.astype(f32)[None],
        spread[0:1],
        spread[1:2],
        grads[:, 1152:].reshape(1, 128, 3, 128),
        grads[None, :, 1024:1152],
        spread[2:3],
        spread[3:4],
        spread[4:5],
        grads[None, :, 512:1024],
        up_bias_grad[None],
        grads[:, :512].T[None],
        spread[5:6],
    )


def solution(mesh):
    return jax.shard_map(
        on_device_whole if whole_batch_fits(mesh) else on_device,
        mesh=mesh,
        in_specs=(
            P("dp", "tensor", None),
            P("dp", None),
            P("dp", "tensor", None),
            P("section", None),
            P("section", None),
            P("section", None, None, "tensor"),
            P("section", "tensor", None),
            P("section", None),
            P("section", None),
            P("section", None),
            P("section", None, "tensor"),
            P("section", "tensor"),
            P("section", "tensor", None),
            P("section", None),
        ),
        out_specs=(
            P("section", "dp", "tensor", None),
            P("section", "dp", "tensor", None),
            P("section", ("dp", "tensor")),
            P("section", ("dp", "tensor")),
            P("section", "dp", None, "tensor"),
            P("section", "tensor", "dp"),
            P("section", ("dp", "tensor")),
            P("section", ("dp", "tensor")),
            P("section", ("dp", "tensor")),
            P("section", "dp", "tensor"),
            P("section", "tensor", "dp"),
            P("section", "tensor", "dp"),
            P("section", ("dp", "tensor")),
        ),
        check_vma=False,
    )
```

```python
from functools import partial
import math

import jax
import jax.numpy as jnp
from jax import lax
from jax.experimental import pallas as pl
from jax.experimental.pallas import tpu as pltpu
from jax.sharding import PartitionSpec as P

HEAD = 64
FF = 2048


def passed_along(block, axis, distance):
    devices = range(lax.axis_size(axis))
    route = [(i - distance, i) for i in devices if i - distance in devices]
    return lax.ppermute(block, axis, route)


def normalize(values, gain_vec, bias_vec):
    centre = values - jnp.mean(values, axis=-1, keepdims=True)
    spread = jnp.mean(centre * centre, axis=-1, keepdims=True)
    return centre * lax.rsqrt(spread + 1e-05) * gain_vec + bias_vec


def document_ids(seq_lens, row_count):
    bounds = jnp.cumsum(seq_lens)
    places = jnp.arange(row_count, dtype=jnp.int32)
    return jnp.sum((places[:, None] >= bounds[None, :]).astype(jnp.int32), axis=1)


def first_key_block(doc_number, seq_lens, block):
    starts = jnp.cumsum(seq_lens) - seq_lens
    numbers = jnp.arange(seq_lens.shape[0], dtype=jnp.int32)
    return jnp.sum(jnp.where(numbers == doc_number, starts, 0)) // block


def grouped_sum(left, right, groups):
    row_count, inner = left.shape
    terms = jnp.einsum(
        "rgc,gcd->grd",
        left.reshape(row_count, groups, inner // groups),
        right.reshape(groups, inner // groups, right.shape[-1]),
        preferred_element_type=jnp.float32,
    )
    return jnp.sum(lax.optimization_barrier(terms.astype(jnp.bfloat16)).astype(jnp.float32), axis=0)


def branch_total(left, right):
    return grouped_sum(left, right, lax.axis_size("tensor"))


def key_scores(query_rows, key_part, query_docs, key_docs, query_first, key_first, signed):
    scale = 1.0 / math.sqrt(query_rows.shape[-1])
    scores = (
        jnp.einsum("qhe,khe->hqk", query_rows, key_part, preferred_element_type=jnp.float32) * scale
    )
    query_places = query_first + jnp.arange(query_rows.shape[0], dtype=jnp.int32)
    key_places = key_first + jnp.arange(key_part.shape[0], dtype=jnp.int32)
    allowed = (query_docs[:, None] == key_docs[None, :]) & (
        query_places[:, None] >= key_places[None, :]
    )
    modulus = jnp.sqrt(scores * scores + 1.0)
    logits = jnp.where(signed, modulus, scores)
    factor = jnp.where(signed, scores / modulus, 1.0)
    return (modulus, logits, factor, allowed[None])


def attend(queries, key_rows, values, doc_rows, seq_lens, signed, offset):
    query_count, heads_here, head_size = queries.shape
    key_count = key_rows.shape[0]
    query_block = min(512, query_count)
    key_block = min(512, key_count)
    query_first = offset + 0
    query_docs = lax.dynamic_slice_in_dim(doc_rows, query_first, query_block, 0)
    lowest = first_key_block(query_docs[0], seq_lens, key_block)
    upper = (query_first + query_block - 1) // key_block + 1

    def block_scores(key_index):
        key_first = key_index * key_block
        return key_scores(
            queries,
            lax.dynamic_slice_in_dim(key_rows, key_first, key_block, 0),
            query_docs,
            lax.dynamic_slice_in_dim(doc_rows, key_first, key_block, 0),
            query_first,
            key_first,
            signed,
        )

    def measure(key_index, carry):
        running_max, running_sum = carry
        modulus, logits, factor, allowed = block_scores(key_index)
        masked = jnp.where(allowed, logits, -1e30)
        new_max = jnp.maximum(running_max, jnp.max(masked, axis=-1))
        added = jnp.sum(jnp.where(allowed, jnp.exp(masked - new_max[:, :, None]), 0.0), axis=-1)
        return (new_max, running_sum * jnp.exp(running_max - new_max) + added)

    start_max = jnp.full((heads_here, query_block), -1e30, jnp.float32)
    start_sum = jnp.zeros((heads_here, query_block), jnp.float32)
    row_max, row_sum = lax.fori_loop(lowest, upper, measure, (start_max, start_sum))
    log_total = row_max + jnp.log(row_sum)

    def accumulate(key_index, partial_out):
        modulus, logits, factor, allowed = block_scores(key_index)
        probs = jnp.where(allowed, jnp.exp(logits - log_total[:, :, None]), 0.0)
        weights = (factor * probs).astype(jnp.bfloat16)
        value_rows = lax.dynamic_slice_in_dim(values, key_index * key_block, key_block, 0)
        return partial_out + jnp.einsum(
            "hqk,khe->qhe", weights, value_rows, preferred_element_type=jnp.float32
        )

    outputs_list = lax.fori_loop(
        lowest, upper, accumulate, jnp.zeros((query_block, heads_here, head_size), jnp.float32)
    )
    return (outputs_list, log_total)


def attend_back(
    queries,
    key_rows,
    values,
    doc_rows,
    seq_lens,
    signed,
    attended,
    log_totals,
    grad_attended,
    offset,
):
    query_count, heads_here, head_size = queries.shape
    key_count = key_rows.shape[0]
    query_block = min(512, query_count)
    key_block = min(512, key_count)
    scale = 1.0 / math.sqrt(head_size)
    centre_terms = jnp.sum(grad_attended.astype(jnp.float32) * attended, axis=-1).T
    grad_keys = jnp.zeros(key_rows.shape, jnp.float32)
    grad_values = jnp.zeros(key_rows.shape, jnp.float32)
    query_first = offset + 0
    query_docs = lax.dynamic_slice_in_dim(doc_rows, query_first, query_block, 0)
    lowest = first_key_block(query_docs[0], seq_lens, key_block)
    upper = (query_first + query_block - 1) // key_block + 1

    def backward_step(key_index, carry):
        grad_query, keys_total, values_total = carry
        key_first = key_index * key_block
        key_part = lax.dynamic_slice_in_dim(key_rows, key_first, key_block, 0)
        value_rows = lax.dynamic_slice_in_dim(values, key_first, key_block, 0)
        modulus, logits, factor, allowed = key_scores(
            queries,
            key_part,
            query_docs,
            lax.dynamic_slice_in_dim(doc_rows, key_first, key_block, 0),
            query_first,
            key_first,
            signed,
        )
        probs = jnp.where(allowed, jnp.exp(logits - log_totals[:, :, None]), 0.0)
        weights = (factor * probs).astype(jnp.bfloat16)
        grad_weights = jnp.einsum(
            "qhe,khe->hqk", grad_attended, value_rows, preferred_element_type=jnp.float32
        )
        grad_scores = factor * probs * (factor * grad_weights - centre_terms[:, :, None])
        grad_scores = grad_scores + jnp.where(
            signed, probs * grad_weights / (modulus * modulus * modulus), 0.0
        )
        grad_low = grad_scores.astype(jnp.bfloat16)
        grad_query = (
            grad_query
            + jnp.einsum("hqk,khe->qhe", grad_low, key_part, preferred_element_type=jnp.float32)
            * scale
        )
        key_term = (
            jnp.einsum("hqk,qhe->khe", grad_low, queries, preferred_element_type=jnp.float32)
            * scale
        )
        value_term = jnp.einsum(
            "hqk,qhe->khe", weights, grad_attended, preferred_element_type=jnp.float32
        )
        keys_total = lax.dynamic_update_slice_in_dim(
            keys_total,
            lax.dynamic_slice_in_dim(keys_total, key_first, key_block, 0) + key_term,
            key_first,
            0,
        )
        values_total = lax.dynamic_update_slice_in_dim(
            values_total,
            lax.dynamic_slice_in_dim(values_total, key_first, key_block, 0) + value_term,
            key_first,
            0,
        )
        return (grad_query, keys_total, values_total)

    start_query = jnp.zeros((query_block, heads_here, head_size), jnp.float32)
    grad_query, grad_keys, grad_values = lax.fori_loop(
        lowest, upper, backward_step, (start_query, grad_keys, grad_values)
    )
    return (grad_query, grad_keys, grad_values)


def forward_layer(inputs, seq_lens, params, signed, finish):
    (
        gain_one,
        bias_one,
        qkv_weight,
        out_weight,
        out_bias,
        gain_two,
        bias_two,
        up_weight,
        up_bias,
        down_weight,
        down_bias,
    ) = params
    normed_one = normalize(inputs, gain_one, bias_one).astype(jnp.bfloat16)
    offset = lax.axis_index("tensor") * normed_one.shape[0]
    row_count = normed_one.shape[0]
    width = qkv_weight.shape[-1]
    projected = jnp.dot(
        normed_one,
        qkv_weight.reshape(qkv_weight.shape[0], 3 * width),
        preferred_element_type=jnp.float32,
    ).astype(jnp.bfloat16)
    head_shape = (row_count, width // HEAD, HEAD)
    queries = projected[:, :width].reshape(head_shape)
    key_rows = projected[:, width : 2 * width].reshape(head_shape)
    values = projected[:, 2 * width :].reshape(head_shape)
    key_all, value_all = (
        lax.all_gather(key_rows, "tensor", axis=0, tiled=True),
        lax.all_gather(values, "tensor", axis=0, tiled=True),
    )
    doc_rows = document_ids(seq_lens, key_all.shape[0])
    attended, log_totals = attend(queries, key_all, value_all, doc_rows, seq_lens, signed, offset)
    attended_low = attended.reshape(row_count, width).astype(jnp.bfloat16)
    hidden_one = inputs + branch_total(attended_low, out_weight) + out_bias
    normed_two = normalize(hidden_one, gain_two, bias_two).astype(jnp.bfloat16)
    up_values = jnp.dot(normed_two, up_weight, preferred_element_type=jnp.float32) + up_bias
    activated = jax.nn.gelu(up_values, approximate=False).astype(jnp.bfloat16)
    if finish:
        outputs = hidden_one + branch_total(activated, down_weight) + down_bias
    else:
        outputs = hidden_one
    saved = (
        normed_one,
        queries,
        key_all,
        value_all,
        doc_rows,
        attended,
        attended_low,
        log_totals,
        hidden_one,
        normed_two,
        up_values,
        activated,
        offset,
    )
    return (outputs, saved)


def backward_layer(inputs, seq_lens, params, signed, grad_outputs):
    (
        gain_one,
        bias_one,
        qkv_weight,
        out_weight,
        out_bias,
        gain_two,
        bias_two,
        up_weight,
        up_bias,
        down_weight,
        down_bias,
    ) = params
    unused_out, saved = forward_layer(inputs, seq_lens, params, signed, False)
    (
        rows_one,
        queries,
        key_all,
        value_all,
        doc_rows,
        attended,
        attended_low,
        log_totals,
        hidden_one,
        rows_two,
        up_values,
        activated,
        offset,
    ) = saved
    row_count, width = attended_low.shape
    grad_low = grad_outputs.astype(jnp.bfloat16)
    grad_down = jnp.einsum("rf,rd->fd", activated, grad_low, preferred_element_type=jnp.float32)
    grad_act = jnp.einsum("rd,fd->rf", grad_low, down_weight, preferred_element_type=jnp.float32)
    gelu_value, gelu_back = jax.vjp(partial(jax.nn.gelu, approximate=False), up_values)
    grad_up_values = gelu_back(grad_act)[0].astype(jnp.bfloat16)
    grad_up_bias = jnp.sum(grad_up_values.astype(jnp.float32), axis=0)
    grad_up = jnp.einsum("rd,rf->df", rows_two, grad_up_values, preferred_element_type=jnp.float32)
    normed_two_terms = jnp.einsum(
        "rf,df->rd", grad_up_values, up_weight, preferred_element_type=jnp.float32
    )
    norm_value, norm_back = jax.vjp(normalize, hidden_one, gain_two, bias_two)
    grad_hidden, grad_gain_two, grad_bias_two = norm_back(normed_two_terms)
    grad_hidden = grad_hidden + grad_outputs
    hidden_low = grad_hidden.astype(jnp.bfloat16)
    grad_out = jnp.einsum("rc,rd->cd", attended_low, hidden_low, preferred_element_type=jnp.float32)
    grad_attended = (
        jnp.einsum("rd,cd->rc", hidden_low, out_weight, preferred_element_type=jnp.float32)
        .astype(jnp.bfloat16)
        .reshape(queries.shape)
    )
    grad_queries, grad_keys, grad_values = attend_back(
        queries,
        key_all,
        value_all,
        doc_rows,
        seq_lens,
        signed,
        attended,
        log_totals,
        grad_attended,
        offset,
    )
    grad_keys, grad_values = (
        lax.psum_scatter(
            grad_keys.astype(jnp.bfloat16), "tensor", scatter_dimension=0, tiled=True
        ).astype(jnp.float32),
        lax.psum_scatter(
            grad_values.astype(jnp.bfloat16), "tensor", scatter_dimension=0, tiled=True
        ).astype(jnp.float32),
    )
    grad_projected = jnp.concatenate(
        [
            grad_queries.reshape(row_count, width),
            grad_keys.reshape(row_count, width),
            grad_values.reshape(row_count, width),
        ],
        axis=1,
    ).astype(jnp.bfloat16)
    grad_qkv = jnp.einsum(
        "rd,rc->dc", rows_one, grad_projected, preferred_element_type=jnp.float32
    ).reshape(qkv_weight.shape)
    normed_one_terms = jnp.einsum(
        "rc,dc->rd",
        grad_projected,
        qkv_weight.reshape(qkv_weight.shape[0], 3 * width),
        preferred_element_type=jnp.float32,
    )
    norm_value_one, norm_back_one = jax.vjp(normalize, inputs, gain_one, bias_one)
    grad_inputs, grad_gain_one, grad_bias_one = norm_back_one(normed_one_terms)
    grad_inputs = grad_inputs + grad_hidden
    matrices = (
        grad_qkv[None],
        grad_out[None],
        grad_up[None],
        grad_up_bias.reshape(1, -1, FF // lax.axis_size("tensor")),
        grad_down[None],
    )
    vectors = (
        grad_gain_one[None],
        grad_bias_one[None],
        jnp.sum(grad_hidden, axis=0)[None],
        grad_gain_two[None],
        grad_bias_two[None],
        jnp.sum(grad_outputs, axis=0)[None],
    )
    return (grad_inputs, matrices, vectors)


def on_device(
    tokens,
    lengths,
    cotangent,
    ln_one_gain,
    ln_one_bias,
    qkv_weight,
    out_weight,
    out_bias,
    ln_two_gain,
    ln_two_bias,
    up_weight,
    up_bias,
    down_weight,
    down_bias,
):
    signed = lax.axis_index("section") == 0
    params = tuple(
        (
            array_item[0]
            for array_item in (
                ln_one_gain,
                ln_one_bias,
                qkv_weight,
                out_weight,
                out_bias,
                ln_two_gain,
                ln_two_bias,
                up_weight,
                up_bias,
                down_weight,
                down_bias,
            )
        )
    )
    whole = (
        lax.all_gather(qkv_weight, "tensor", axis=3, tiled=True),
        lax.all_gather(out_weight, "tensor", axis=1, tiled=True),
        lax.all_gather(up_weight, "tensor", axis=2, tiled=True),
        lax.all_gather(down_weight, "tensor", axis=1, tiled=True),
    )
    bias_whole = lax.all_gather(up_bias, "tensor", axis=1, tiled=True)
    params = (
        params[0],
        params[1],
        whole[0][0],
        whole[1][0],
        params[4],
        params[5],
        params[6],
        whole[2][0],
        bias_whole[0],
        whole[3][0],
        params[10],
    )
    batches = tokens.shape[0]
    arrived = jnp.zeros(tokens.shape[1:], jnp.bfloat16)
    produced_all = jnp.zeros(tokens.shape, jnp.bfloat16)
    received_all = jnp.zeros(tokens.shape, jnp.bfloat16)
    for tick in range(batches + 1):
        own_index = min(tick, batches - 1)
        prior_index = max(tick - 1, 0)
        inputs_now = jnp.where(signed, tokens[own_index], arrived).astype(jnp.float32)
        lens_now = jnp.where(signed, lengths[own_index], lengths[prior_index])
        produced = forward_layer(inputs_now, lens_now, params, signed, True)[0].astype(jnp.bfloat16)
        if tick < batches:
            produced_all = produced_all.at[tick].set(
                jnp.where(signed, produced, produced_all[tick])
            )
        if tick > 0:
            produced_all = produced_all.at[tick - 1].set(
                jnp.where(signed, produced_all[tick - 1], produced)
            )
            received_all = received_all.at[tick - 1].set(arrived)
        if tick < batches:
            arrived = passed_along(produced, "section", 1)
    block_inputs = jnp.where(signed, tokens, received_all)
    returned = jnp.zeros(tokens.shape[1:], jnp.float32)
    grad_inputs_all = jnp.zeros(tokens.shape, jnp.float32)
    matrix_total = None
    vector_total = None
    for tick in range(batches + 1):
        later_index = batches - 1 - tick if tick < batches else 0
        earlier_index = batches - tick if tick > 0 else 0
        index_now = jnp.where(signed, earlier_index, later_index)
        live_now = jnp.where(signed, tick > 0, tick < batches)
        grad_now = jnp.where(signed, returned, cotangent[later_index].astype(jnp.float32))
        grad_now = jnp.where(live_now, grad_now, 0.0)
        inputs_now = block_inputs[index_now].astype(jnp.float32)
        grad_back, matrices, vectors = backward_layer(
            inputs_now, lengths[index_now], params, signed, grad_now
        )
        if tick == 0:
            matrix_total = tuple(matrices)
            vector_total = tuple(vectors)
        else:
            matrix_total = tuple(
                (
                    jnp.add(total_item, new_item)
                    for total_item, new_item in zip(matrix_total, matrices)
                )
            )
            vector_total = tuple(
                (
                    jnp.add(total_item, new_item)
                    for total_item, new_item in zip(vector_total, vectors)
                )
            )
        if tick > 0:
            grad_inputs_all = grad_inputs_all.at[earlier_index].set(
                jnp.where(signed, grad_back, grad_inputs_all[earlier_index])
            )
        if tick < batches:
            grad_inputs_all = grad_inputs_all.at[later_index].set(
                jnp.where(signed, grad_inputs_all[later_index], grad_back)
            )
            returned = passed_along(grad_back.astype(jnp.bfloat16), "section", -1).astype(
                grad_back.dtype
            )
    matrix_final = (
        lax.psum_scatter(
            matrix_total[0].astype(jnp.bfloat16), "dp", scatter_dimension=1, tiled=True
        ).astype(jnp.float32),
        lax.psum_scatter(
            matrix_total[1].astype(jnp.bfloat16), "dp", scatter_dimension=2, tiled=True
        ).astype(jnp.float32),
        lax.psum_scatter(
            matrix_total[2].astype(jnp.bfloat16), "dp", scatter_dimension=1, tiled=True
        ).astype(jnp.float32),
        lax.psum_scatter(
            matrix_total[3].astype(jnp.bfloat16), "dp", scatter_dimension=2, tiled=True
        ).astype(jnp.float32),
        lax.psum_scatter(
            matrix_total[4].astype(jnp.bfloat16), "dp", scatter_dimension=2, tiled=True
        ).astype(jnp.float32),
    )
    vector_final = (
        lax.psum_scatter(vector_total[0], ("dp", "tensor"), scatter_dimension=1, tiled=True),
        lax.psum_scatter(vector_total[1], ("dp", "tensor"), scatter_dimension=1, tiled=True),
        lax.psum_scatter(vector_total[2], ("dp", "tensor"), scatter_dimension=1, tiled=True),
        lax.psum_scatter(vector_total[3], ("dp", "tensor"), scatter_dimension=1, tiled=True),
        lax.psum_scatter(vector_total[4], ("dp", "tensor"), scatter_dimension=1, tiled=True),
        lax.psum_scatter(vector_total[5], ("dp", "tensor"), scatter_dimension=1, tiled=True),
    )
    matrix_final = (
        lax.psum_scatter(
            matrix_final[0].astype(jnp.bfloat16), "tensor", scatter_dimension=3, tiled=True
        ).astype(jnp.float32),
        lax.psum_scatter(
            matrix_final[1].astype(jnp.bfloat16), "tensor", scatter_dimension=1, tiled=True
        ).astype(jnp.float32),
        lax.psum_scatter(
            matrix_final[2].astype(jnp.bfloat16), "tensor", scatter_dimension=2, tiled=True
        ).astype(jnp.float32),
        lax.psum_scatter(
            matrix_final[3].astype(jnp.bfloat16), "tensor", scatter_dimension=1, tiled=True
        ).astype(jnp.float32),
        lax.psum_scatter(
            matrix_final[4].astype(jnp.bfloat16), "tensor", scatter_dimension=1, tiled=True
        ).astype(jnp.float32),
    )
    grad_qkv, grad_out, grad_up, grad_up_bias, grad_down = matrix_final
    grad_gain_one, grad_bias_one, grad_out_bias, grad_gain_two, grad_bias_two, grad_down_bias = (
        vector_final
    )
    return (
        produced_all[None],
        grad_inputs_all[None],
        grad_gain_one,
        grad_bias_one,
        grad_qkv,
        grad_out,
        grad_out_bias,
        grad_gain_two,
        grad_bias_two,
        grad_up,
        grad_up_bias,
        grad_down,
        grad_down_bias,
    )


MESH = pl.DeviceIdType.MESH
PARTS = 4
BLOCK = 256
OWN = 512
WIDTH = 512
PAIRS = 4
TASKS = 5
NEGATIVE = -1e30
LEFT = (((1,), (0,)), ((), ()))
BOTH_LAST = (((1,), (1,)), ((), ()))
BOTH_FIRST = (((0,), (0,)), ((), ()))


def whole_batch_fits(mesh):
    shape = dict(mesh.shape)
    return shape["tensor"] == PARTS and shape["dp"] == PARTS and shape["section"] == 2


def dot(left, right, dims=LEFT):
    return lax.dot_general(left, right, dims, preferred_element_type=jnp.float32)


def place():
    return lax.axis_index("section"), lax.axis_index("dp"), lax.axis_index("tensor")


def blocks_of(core):
    return (core, 3 - core)


def turn_part(turn):
    return lax.bitwise_xor(lax.axis_index("tensor"), lax.rem(turn, PARTS))


def tile_rows(start, count):
    return pl.ds(pl.multiple_of(start, count), count)


def standard(values):
    centre = values - jnp.mean(values, axis=-1, keepdims=True)
    spread = jnp.mean(centre * centre, axis=-1, keepdims=True)
    inverse = lax.rsqrt(spread + 1e-05)
    return centre * inverse, inverse


def standard_back(grads, gain, units, inverse):
    scaled = grads * gain
    inner = jnp.mean(scaled * units, axis=-1, keepdims=True)
    return inverse * (scaled - jnp.mean(scaled, axis=-1, keepdims=True) - units * inner)


def column_sum(values):
    return jnp.sum(values, axis=0, keepdims=True)


def keep_head(values, parity):
    lane = lax.broadcasted_iota(jnp.int32, values.shape, 1)
    return jnp.where((lane < HEAD) == (parity == 0), values, 0.0)


def side_by_side(weight_ref, pair):
    return jnp.concatenate([weight_ref[pair, kind] for kind in range(3)], axis=1)


def project(x_ref, vec_ref, weight_ref, normed_t_ref, query_ref, kv_ref, normed_ref, between, before_pair, after_pair):
    core = lax.axis_index("section")
    gain, bias = vec_ref[0, 0:1, :], vec_ref[0, 1:2, :]

    def norm_rows(index, carry):
        rows = tile_rows(index * 128, 128)
        units, _ = standard(x_ref[rows, :].astype(jnp.float32))
        normed_ref[rows, :] = (units * gain + bias).astype(jnp.bfloat16)
        return carry

    lax.fori_loop(0, OWN // 128, norm_rows, 0)
    normed_t_ref[...] = normed_ref[...].T
    between()

    def pair_step(turn, carry):
        pair = turn_part(turn)
        before_pair(turn)
        out = dot(normed_ref[...], side_by_side(weight_ref, pair))
        queries = out[:, :128] * 0.125
        for parity in range(2):
            query_ref[pair, parity] = keep_head(queries, parity).astype(jnp.bfloat16)
        for slot, block in enumerate(blocks_of(core)):
            part = out[slot * BLOCK : (slot + 1) * BLOCK, :]
            kv_ref[0, pair, tile_rows(block * BLOCK, BLOCK), :] = part[:, 128:256].astype(jnp.bfloat16)
            kv_ref[1, pair, tile_rows(block * BLOCK, BLOCK), :] = part[:, 256:].astype(jnp.bfloat16)
        after_pair(turn, pair)
        return carry

    lax.fori_loop(0, PAIRS, pair_step, 0)


def task_plan(core):
    first = core == 0
    slots = (0, jnp.where(first, 1, 0), 1, 1, 1)
    keys = (0, jnp.where(first, 0, 1), jnp.where(first, 1, 0), jnp.where(first, 2, 1), jnp.where(first, 3, 2))
    return slots, keys


def attend_rows(signed, query_ref, kv_ref, bias_ref, attended_ref, attended_t_ref, log_ref, logit_ref, factor_ref, stat_ref, before_pair):
    core = lax.axis_index("section")
    slots, keys = task_plan(core)
    middle_late = core == 0
    lane = lax.broadcasted_iota(jnp.int32, (BLOCK, 128), 1)

    def pair_step(turn, carry):
        pair = turn_part(turn)
        before_pair(turn, pair)
        outs = [[None, None], [None, None]]
        for parity in range(2):
            tops = []
            for task in range(TASKS):
                rows = tile_rows(slots[task] * BLOCK, BLOCK)
                key_rows = tile_rows(keys[task] * BLOCK, BLOCK)
                scores = dot(query_ref[pair, parity, rows, :], kv_ref[0, pair, key_rows, :], BOTH_LAST)
                if signed:
                    raised = scores * scores + 1.0
                    inverse = lax.rsqrt(raised)
                    factor_ref[task] = scores * inverse
                    scores = raised * inverse
                logits = scores + bias_ref[task]
                logit_ref[task] = logits
                tops.append(jnp.maximum(logits[:, :128], logits[:, 128:]))
            low = jnp.full((BLOCK, 128), NEGATIVE, jnp.float32)
            top_early = jnp.maximum(tops[0], jnp.where(middle_late, low, tops[1]))
            top_late = jnp.maximum(jnp.maximum(tops[2], tops[3]), jnp.maximum(tops[4], jnp.where(middle_late, tops[1], low)))
            max_early = jnp.max(top_early, axis=-1, keepdims=True)
            max_late = jnp.max(top_late, axis=-1, keepdims=True)
            max_middle = jnp.where(middle_late, max_late, max_early)
            shifts = (max_early, max_middle, max_late, max_late, max_late)
            sums, terms = [], []
            for task in range(TASKS):
                key_rows = tile_rows(keys[task] * BLOCK, BLOCK)
                powers = jnp.exp(logit_ref[task] - shifts[task])
                sums.append(powers[:, :128] + powers[:, 128:])
                if signed:
                    powers = powers * factor_ref[task]
                terms.append(dot(powers.astype(jnp.bfloat16), kv_ref[1, pair, key_rows, :]))
            early = jnp.where(middle_late, 0.0, 1.0)
            late = 1.0 - early
            totals = (sums[0] + sums[1] * early, sums[2] + sums[3] + sums[4] + sums[1] * late)
            values = (terms[0] + terms[1] * early, terms[2] + terms[3] + terms[4] + terms[1] * late)
            for slot, top in enumerate((max_early, max_late)):
                total = jnp.sum(totals[slot], axis=-1, keepdims=True)
                outs[slot][parity] = values[slot] / total
                head = pair * 2 + parity
                stat_ref[slot] = jnp.where(lane == head, top + jnp.log(total), stat_ref[slot])
        for slot in range(2):
            merged = jnp.where(lane < HEAD, outs[slot][0], outs[slot][1])
            attended_ref[pair, slot * BLOCK : (slot + 1) * BLOCK, :] = merged
            attended_t_ref[pair, :, slot * BLOCK : (slot + 1) * BLOCK] = merged.T.astype(jnp.bfloat16)
        return carry

    stat_ref[...] = jnp.zeros_like(stat_ref)
    lax.fori_loop(0, PAIRS, pair_step, 0)
    for slot in range(2):
        log_ref[slot] = stat_ref[slot].T[:8, :]


def gelu_both(values):
    lower = 0.5 * (1.0 + lax.erf(values * math.sqrt(0.5)))
    density = jnp.exp(-0.5 * values * values) * (1.0 / math.sqrt(2.0 * math.pi))
    return values * lower, lower + values * density


def feed(x_ref, attended_ref, vec_ref, out_ref, up_ref, down_ref, hidden_ref, normed_t_ref, act_ref, slope_ref, y_ref, normed_ref, wide_ref, sum_ref, before_out, between, before_chunk, during_chunk):
    out_bias = vec_ref[0, 2:3, :]
    gain, bias = vec_ref[0, 3:4, :], vec_ref[0, 4:5, :]
    down_bias = vec_ref[0, 5:6, :]
    sum_ref[...] = jnp.zeros_like(sum_ref)

    def out_step(turn, carry):
        pair = turn_part(turn)
        before_out(turn)
        sum_ref[...] += dot(attended_ref[pair].astype(jnp.bfloat16), out_ref[pair])
        return carry

    lax.fori_loop(0, PAIRS, out_step, 0)

    def norm_rows(index, carry):
        rows = tile_rows(index * 128, 128)
        hidden = x_ref[rows, :].astype(jnp.float32) + sum_ref[rows, :] + out_bias
        hidden_ref[rows, :] = hidden
        units, _ = standard(hidden)
        normed_ref[rows, :] = (units * gain + bias).astype(jnp.bfloat16)
        sum_ref[rows, :] = hidden + down_bias
        return carry

    lax.fori_loop(0, OWN // 128, norm_rows, 0)
    normed_t_ref[...] = normed_ref[...].T
    between()

    def chunk_step(turn, carry):
        chunk = turn_part(turn)
        before_chunk(turn)
        wide_ref[...] = dot(normed_ref[...], up_ref[chunk])
        up_bias = vec_ref[chunk, 6:7, :]

        def gelu_rows(index, inner):
            rows = tile_rows(index * 32, 32)
            act, slope = gelu_both(wide_ref[rows, :] + up_bias)
            act_ref[chunk, rows, :] = act.astype(jnp.bfloat16)
            slope_ref[chunk, rows, :] = slope.astype(jnp.bfloat16)
            return inner

        lax.fori_loop(0, OWN // 32, gelu_rows, 0)
        during_chunk(turn)
        sum_ref[...] += dot(act_ref[chunk], down_ref[chunk])
        return carry

    lax.fori_loop(0, PARTS, chunk_step, 0)
    y_ref[...] = sum_ref[...].astype(jnp.bfloat16)


def feed_back(dy_ref, act_ref, slope_ref, down_ref, up_ref, hidden_ref, normed_t_ref, vec_ref, out_ref, attended_ref, attended_t_ref, grad_hidden_ref, grad_att_ref, centre_ref, grads_ref, vec_grad_ref, low_ref, low_t_ref, chunk_ref, sum_ref, during_chunk, after_chunk, before_norm, between):
    low_ref[...] = dy_ref[...].astype(jnp.bfloat16)
    low_t_ref[...] = low_ref[...].T
    vec_grad_ref[...] = jnp.zeros_like(vec_grad_ref)
    sum_ref[...] = jnp.zeros_like(sum_ref)

    def chunk_step(turn, carry):
        chunk = turn_part(turn + 1)
        grad_act = dot(low_ref[...], down_ref[chunk], BOTH_LAST)
        grad_up = (grad_act * slope_ref[chunk].astype(jnp.float32)).astype(jnp.bfloat16)
        chunk_ref[...] = grad_up
        vec_grad_ref[pl.ds(6 + chunk, 1), :] = column_sum(grad_up.astype(jnp.float32))
        down_term = dot(low_t_ref[...], act_ref[chunk]).astype(jnp.bfloat16)
        up_term = dot(normed_t_ref[...], chunk_ref[...]).astype(jnp.bfloat16)
        for part in range(PARTS):
            grads_ref[part, chunk, :, 0:512] = down_term[part * 128 : (part + 1) * 128, :]
            grads_ref[part, chunk, :, 512:1024] = up_term[part * 128 : (part + 1) * 128, :]
        after_chunk(turn, chunk)
        sum_ref[...] += dot(chunk_ref[...], up_ref[chunk], BOTH_LAST)
        during_chunk(turn)
        return carry

    lax.fori_loop(0, PARTS, chunk_step, 0)
    before_norm()
    gain = vec_ref[0, 3:4, :]

    def norm_rows(index, carry):
        rows = tile_rows(index * 128, 128)
        grads, dy = sum_ref[rows, :], dy_ref[rows, :]
        units, inverse = standard(hidden_ref[rows, :])
        grad_hidden = dy + standard_back(grads, gain, units, inverse)
        grad_hidden_ref[rows, :] = grad_hidden
        low_ref[rows, :] = grad_hidden.astype(jnp.bfloat16)
        vec_grad_ref[2:3, :] += column_sum(grad_hidden)
        vec_grad_ref[3:4, :] += column_sum(grads * units)
        vec_grad_ref[4:5, :] += column_sum(grads)
        vec_grad_ref[5:6, :] += column_sum(dy)
        return carry

    lax.fori_loop(0, OWN // 128, norm_rows, 0)
    between()
    row = lax.broadcasted_iota(jnp.int32, (8, 128), 0)
    lane = lax.broadcasted_iota(jnp.int32, (8, 128), 1)
    picks = jnp.where((row < 2) & ((lane < HEAD) == (row == 0)), 1.0, 0.0)

    def pair_step(pair, carry):
        out_term = dot(attended_t_ref[pair], low_ref[...]).astype(jnp.bfloat16)
        for part in range(PARTS):
            grads_ref[part, pair, :, 1024:1152] = out_term[:, part * 128 : (part + 1) * 128]
        grad_att = dot(low_ref[...], out_ref[pair], BOTH_LAST).astype(jnp.bfloat16)
        wide = grad_att.astype(jnp.float32)
        for parity in range(2):
            grad_att_ref[pair, parity] = keep_head(wide, parity).astype(jnp.bfloat16)
        centres = lax.dot_general(picks, wide * attended_ref[pair], BOTH_LAST, precision=lax.Precision.HIGHEST, preferred_element_type=jnp.float32)
        centre_ref[pair] = centres
        return carry

    lax.fori_loop(0, PAIRS, pair_step, 0)


def attend_rows_back(signed, query_ref, kv_ref, grad_att_ref, bias_ref, log_ref, centre_ref, grad_query_ref, grad_kv_ref, send_ref, before_pair, after_pair):
    core = lax.axis_index("section")
    slots, keys = task_plan(core)
    early = jnp.where(core == 0, 0.0, 1.0)
    lane = lax.broadcasted_iota(jnp.int32, (BLOCK, 128), 1)
    grad_kv_ref[...] = jnp.zeros_like(grad_kv_ref)

    def pair_step(turn, carry):
        pair = turn_part(turn + 1)
        before_pair(turn)
        parts = [[None] * TASKS, [None] * TASKS]
        for task in range(TASKS):
            rows = tile_rows(slots[task] * BLOCK, BLOCK)
            key_rows = tile_rows(keys[task] * BLOCK, BLOCK)
            key_part, value_part = kv_ref[0, pair, key_rows, :], kv_ref[1, pair, key_rows, :]
            key_term, value_term = None, None
            for parity in range(2):
                queries = query_ref[pair, parity, rows, :]
                grad_att = grad_att_ref[pair, parity, rows, :]
                scores = dot(key_part, queries, BOTH_LAST)
                grad_weights = dot(value_part, grad_att, BOTH_LAST)
                log_row = log_ref[slots[task], pl.ds(pair * 2 + parity, 1), :]
                centre = centre_ref[pair, parity : parity + 1, rows]
                if signed:
                    raised = scores * scores + 1.0
                    inverse = lax.rsqrt(raised)
                    factor = scores * inverse
                    probs = jnp.exp(raised * inverse + bias_ref[task] - log_row)
                    weights = factor * probs
                    grad_scores = weights * (factor * grad_weights - centre)
                    grad_scores = grad_scores + probs * grad_weights * (inverse * inverse * inverse)
                else:
                    weights = jnp.exp(scores + bias_ref[task] - log_row)
                    grad_scores = weights * (grad_weights - centre)
                grad_low = grad_scores.astype(jnp.bfloat16)
                new_key = dot(grad_low, queries)
                new_value = dot(weights.astype(jnp.bfloat16), grad_att)
                key_term = new_key if parity == 0 else key_term + new_key
                value_term = new_value if parity == 0 else value_term + new_value
                parts[parity][task] = dot(grad_low, key_part, BOTH_FIRST)
            grad_kv_ref[0, pair, key_rows, :] += key_term
            grad_kv_ref[1, pair, key_rows, :] += value_term
        merged = []
        for task in range(TASKS):
            merged.append(jnp.where(lane < HEAD, parts[0][task], parts[1][task]))
        grad_query_ref[pair, :BLOCK, :] = ((merged[0] + merged[1] * early) * 0.125).astype(jnp.bfloat16)
        grad_query_ref[pair, BLOCK:, :] = ((merged[1] * (1.0 - early) + merged[2] + merged[3] + merged[4]) * 0.125).astype(jnp.bfloat16)
        for slot, block in enumerate(blocks_of(1 - core)):
            for kind in range(2):
                rows = grad_kv_ref[kind, pair, tile_rows(block * BLOCK, BLOCK), :]
                send_ref[kind, pair, slot * BLOCK : (slot + 1) * BLOCK, :] = rows.astype(jnp.bfloat16)
        after_pair(turn, pair)
        return carry

    lax.fori_loop(0, PAIRS, pair_step, 0)


def project_back_pair(pair, grad_query_ref, grad_kv_ref, other_ref, normed_t_ref, weight_ref, grads_ref, sum_ref, send):
    parts = [grad_query_ref[pair]]
    for kind in range(2):
        halves = []
        for slot, block in enumerate(blocks_of(lax.axis_index("section"))):
            own = grad_kv_ref[kind, pair, tile_rows(block * BLOCK, BLOCK), :]
            halves.append(own + other_ref[kind, pair, slot * BLOCK : (slot + 1) * BLOCK, :].astype(jnp.float32))
        parts.append(jnp.concatenate(halves, axis=0).astype(jnp.bfloat16))
    grads = jnp.concatenate(parts, axis=1)
    term = dot(normed_t_ref[...], grads).astype(jnp.bfloat16)
    for part in range(PARTS):
        grads_ref[part, pair, :, 1152:1536] = term[part * 128 : (part + 1) * 128, :]
    send()
    sum_ref[...] += dot(grads, side_by_side(weight_ref, pair), BOTH_LAST)


def project_back_norm(x_ref, grad_hidden_ref, vec_ref, grad_x_ref, grad_x_low_ref, vec_grad_ref, sum_ref):
    gain = vec_ref[0, 0:1, :]

    def norm_rows(index, carry):
        rows = tile_rows(index * 128, 128)
        grads = sum_ref[rows, :]
        units, inverse = standard(x_ref[rows, :].astype(jnp.float32))
        grad_x = grad_hidden_ref[rows, :] + standard_back(grads, gain, units, inverse)
        grad_x_ref[rows, :] = grad_x
        grad_x_low_ref[rows, :] = grad_x.astype(jnp.bfloat16)
        vec_grad_ref[0:1, :] += column_sum(grads * units)
        vec_grad_ref[1:2, :] += column_sum(grads)
        return carry

    lax.fori_loop(0, OWN // 128, norm_rows, 0)


def greet(partners):
    barrier = pltpu.get_barrier_semaphore()
    for partner in partners:
        pl.semaphore_signal(barrier, inc=1, device_id=partner, device_id_type=MESH)
    pl.semaphore_wait(barrier, len(partners))


def along_tensor(step):
    core, rep, part = place()
    return (core, rep, lax.bitwise_xor(part, step))


def along_dp(step):
    core, rep, part = place()
    return (core, lax.bitwise_xor(rep, step), part)


def sibling():
    core, rep, part = place()
    return (1 - core, rep, part)


def all_partners():
    return [along_tensor(step) for step in (1, 2, 3)] + [along_dp(step) for step in (1, 2, 3)] + [sibling()]


def remote(source, target, send, receive, device):
    return pltpu.make_async_remote_copy(src_ref=source, dst_ref=target, send_sem=send, recv_sem=receive, device_id=device, device_id_type=MESH)


def fill_masks(lens_ref, bias_ref, turned):
    core, rep, part = place()
    slots, keys = task_plan(core)
    bounds, bound = [], 0
    for index in range(lens_ref.shape[1]):
        bound = bound + lens_ref[part, index]
        bounds.append(bound)
    for task in range(TASKS):
        block = jnp.where(slots[task] == 0, core, 3 - core)
        shape = (1, BLOCK) if turned else (BLOCK, 1)
        query = block * BLOCK + lax.broadcasted_iota(jnp.int32, shape, 1 if turned else 0)
        start = jnp.zeros(shape, jnp.int32)
        for bound in bounds:
            start = jnp.where(query >= bound, bound, start)
        key = keys[task] * BLOCK + lax.broadcasted_iota(jnp.int32, (BLOCK, BLOCK), 0 if turned else 1)
        bias_ref[task] = jnp.where((key >= start) & (key <= query), 0.0, NEGATIVE)


def rows_view(array, rows, index):
    return array.at[:, rows] if index == QKV else array.at[rows]


def quarter_rows(array, which):
    count = array.shape[-2] // PARTS
    return tile_rows(which * count, count)


SAVED = (
    ((OWN, WIDTH), jnp.bfloat16),
    ((WIDTH, OWN), jnp.bfloat16),
    ((PAIRS, 2, OWN, 128), jnp.bfloat16),
    ((2, PAIRS, 1024, 128), jnp.bfloat16),
    ((PAIRS, OWN, 128), jnp.float32),
    ((PAIRS, 128, OWN), jnp.bfloat16),
    ((2, 8, BLOCK), jnp.float32),
    ((OWN, WIDTH), jnp.float32),
    ((WIDTH, OWN), jnp.bfloat16),
    ((PARTS, OWN, 512), jnp.bfloat16),
    ((PARTS, OWN, 512), jnp.bfloat16),
)
WEIGHTS = (
    ((PARTS, 3, 512, 128), jnp.bfloat16),
    ((PARTS, 128, 512), jnp.bfloat16),
    ((PARTS, 512, 512), jnp.bfloat16),
    ((PARTS, 512, 512), jnp.bfloat16),
    ((PARTS, 8, 512), jnp.float32),
)
QKV, OUT, UP, DOWN, VEC = range(5)


ALL = (1, 2, 3)
DIRECT = (QKV,)
FORWARD_PLAN = (
    ("masks", None, 0, "near", ALL, (QKV,)),
    ("masks", None, 0, "own", None, (QKV, OUT, UP, DOWN)),
    ("vec", None, 0, "z", (1, 2), (OUT, UP, DOWN)),
    ("rows", None, 0, "z", (3,), (OUT, UP, DOWN)),
    ("norm0", None, 0, "sib", ALL, (QKV,)),
    ("norm0", None, 1, "own", None, (QKV, OUT, UP, DOWN)),
    ("project0", 0, 0, "near", (1,), (OUT, UP, DOWN)),
    ("project0", 2, 0, "near", (2,), (OUT, UP, DOWN)),
    ("attend0", 0, 0, "far", (1,), (OUT, UP, DOWN)),
    ("attend0", 1, 0, "near", (3,), (OUT, UP, DOWN)),
    ("attend0", 1, 0, "far", (2,), (OUT, UP, DOWN)),
    ("attend0", 2, 1, "z", ALL, (QKV,)),
    ("attend0", 2, 0, "sib", (1,), (OUT, UP, DOWN)),
    ("attend0", 3, 0, "far", (3,), (OUT, UP, DOWN)),
    ("attend0", 3, 0, "sib", (2,), (OUT, UP, DOWN)),
    ("attended0", None, 1, "z", (1, 2), (OUT, UP, DOWN)),
    ("second0", None, 1, "near", ALL, (QKV,)),
    ("attended0", None, 0, "sib", (3,), (OUT, UP, DOWN)),
    ("chunk0", 0, 1, "z", (3,), (OUT, UP, DOWN)),
    ("chunk0", 2, 1, "near", (1,), (OUT, UP, DOWN)),
    ("chunk0", 3, 1, "near", (2,), (OUT, UP, DOWN)),
    ("chunk0", 2, 1, "far", ALL, (QKV,)),
    ("chunk0", 2, None, "rows", None, ()),
    ("chunk0", 3, 1, "sib", ALL, (QKV,)),
    ("project1", 1, 1, "near", (3,), (OUT, UP, DOWN)),
    ("project1", 2, 1, "far", (1,), (OUT, UP, DOWN)),
    ("attend1", 0, 1, "far", (2,), (OUT, UP, DOWN)),
    ("attend1", 1, 1, "sib", (1,), (OUT, UP, DOWN)),
    ("attend1", 2, 1, "far", (3,), (OUT, UP, DOWN)),
    ("attend1", 3, 1, "sib", (2,), (OUT, UP, DOWN)),
    ("attended1", None, 1, "sib", (3,), (OUT, UP, DOWN)),
)


def forward_kernel(lens_ref, tokens, cotangent, *refs):
    shards, vectors, refs = refs[:4], refs[4:11], refs[11:]
    dy_out, y_out, saved_out, weights_out, refs = refs[0], refs[1], refs[2:13], refs[13:18], refs[18:]
    saved, weights, refs = refs[:11], refs[11:16], refs[16:]
    y_ref, bias_ref, normed, logit, factor, stat, wide, total, vec_own, refs = *refs[:9], refs[9:]
    row_send, row_recv, row_local, z_send, z_recv, xy_send, xy_recv, sib_send, sib_recv, local, kv_send, kv_recv, save_sem, keep_sem, pass_send = refs
    core, rep, part = place()
    shards = (*shards, vec_own)
    vec_own[...] = jnp.zeros_like(vec_own)
    for row, vector in enumerate(vectors):
        vec_own[row : row + 1, :] = vector[...]
    greet(all_partners())

    steps = (1, 2, 3)

    def z_copy(index, step):
        slot = (index, step - 1)
        if index == VEC:
            return remote(shards[index], weights[index].at[core, part], z_send.at[slot], z_recv.at[slot], along_tensor(step))
        rows = quarter_rows(shards[index], rep)
        return remote(rows_view(shards[index], rows, index), rows_view(weights[index].at[core, part], rows, index), z_send.at[slot], z_recv.at[slot], along_tensor(step))

    def ends():
        return (part == 0) | (part == 3)

    def pass_copy(index):
        view = rows_view(weights[index].at[core, turn_part(2)], quarter_rows(shards[index], rep), index)
        return remote(view, view, pass_send.at[index], z_recv.at[index, 2], along_tensor(1))

    def own_copy(index):
        return pltpu.make_async_copy(shards[index], weights[index].at[core, part], local.at[index])

    def near_copy(index, step, far):
        slot = (index, far - 1, step - 1)
        view = rows_view(weights[index].at[core, turn_part(far)], quarter_rows(shards[index], rep), index)
        return remote(view, view, xy_send.at[slot], xy_recv.at[slot], along_dp(step))

    def far_copy(index, step, far):
        slot = (index, far - 1, step + 1)
        count = shards[index].shape[-2] // PARTS
        rows = tile_rows(lax.bitwise_xor(rep, 3 - step) * count + (2 - step) * (count // 2), count // 2)
        view = rows_view(weights[index].at[core, turn_part(far)], rows, index)
        return remote(view, view, xy_send.at[slot], xy_recv.at[slot], along_dp(step))

    def across_copy(index, far):
        slot = (index, far - 1, 2)
        view = rows_view(weights[index].at[core, turn_part(far)], quarter_rows(shards[index], rep), index)
        return remote(view, view, xy_send.at[slot], xy_recv.at[slot], along_dp(3))

    def sib_copy(index, far):
        target = weights[index].at[core, turn_part(far)]
        source = target if far else shards[index]
        return remote(source, target, sib_send.at[index, far], sib_recv.at[index, far], sibling())

    def vec_copy():
        view = weights[VEC].at[core]
        return remote(view, view, sib_send.at[VEC, 0], sib_recv.at[VEC, 0], sibling())

    def own_start(*which):
        for index in which:
            own_copy(index).start()
            sib_copy(index, 0).start()

    def z_start(far, *which):
        for index in which:
            if far < 3 or index == VEC:
                z_copy(index, far).start()
            else:
                pl.when(jnp.logical_not(ends()))(z_copy(index, far).start)

    def near_start(far, *which):
        for index in which:
            z_copy(index, far).wait_recv()
            if far == 2:
                pl.when(jnp.logical_not(ends()))(pass_copy(index).start)
            for step in (1, 2):
                near_copy(index, step, far).start()
            if index in DIRECT:
                pl.when(core == 0)(across_copy(index, far).start)

    def far_start(far, *which):
        for index in which:
            for step in (2, 1):
                near_copy(index, 3 - step, far).wait_recv()
                far_copy(index, step, far).start()

    def sib_direct(far, *which):
        for index in which:
            for step in (1, 2):
                near_copy(index, step, far).wait_recv()
            across_copy(index, far).wait_recv()
            sib_copy(index, far).start()

    def sib_passed(far, *which):
        for index in which:
            for step in (1, 2):
                far_copy(index, step, far).wait_recv()
            sib_copy(index, far).start()

    def sib_start(far, *which):
        direct = [index for index in which if index in DIRECT]
        passed = [index for index in which if index not in DIRECT]
        pl.when(core == 0)(partial(sib_direct, far, *direct))
        pl.when(core == 0)(partial(sib_passed, far, *passed))
        pl.when(core == 1)(partial(sib_passed, far, *which))

    def need(layer, far, *which):
        @pl.when(core != layer)
        def _():
            for index in which:
                sib_copy(index, far).wait_recv()

        if far == 0:

            @pl.when(core == layer)
            def _():
                for index in which:
                    own_copy(index).wait()

    def need_turn(layer, turn, *which):
        for far in range(PARTS):
            pl.when(turn == far)(partial(need, layer, far, *which))

    def keep_copy(layer, index):
        return pltpu.make_async_copy(weights[index].at[layer], weights_out[index].at[layer], keep_sem.at[layer, index])

    def keep(layer, *which):
        for index in which:
            keep_copy(layer, index).start()

    def on(layer, action, *which):
        pl.when(core == layer)(partial(action, *which))

    def at(layer, turn, when, action, *which):
        pl.when((core == layer) & (turn == when))(partial(action, *which))

    owner = jnp.where((part == 0) | (part == 3), 0, 1)
    place_here = jnp.where(part < 2, 0, 1)
    row_pairs = ((tokens, saved[0].at[0]), (cotangent, dy_out))

    def row_targets(array, batch):
        source, target = row_pairs[array]
        rows = target.at[tile_rows(place_here * BLOCK, BLOCK)]
        there = remote(source.at[batch], rows, row_send.at[array, batch], row_recv.at[array, place_here], (core, rep, batch))
        here = pltpu.make_async_copy(source.at[batch], rows, row_local.at[array])
        return there, here

    def rows_each(array, act):
        for batch in range(PARTS):
            there, here = row_targets(array, batch)

            @pl.when((core == owner) & (part != batch))
            def _():
                there.start() if act == "start" else there.wait_send()

            @pl.when((core == owner) & (part == batch))
            def _():
                here.start() if act == "start" else here.wait()

    def rows_arrived(array):
        for slot, block in enumerate(blocks_of(core)):

            @pl.when(block != part)
            def _():
                source, target = row_pairs[array]
                rows = target.at[slot * BLOCK : (slot + 1) * BLOCK]
                remote(source.at[0], rows, row_send.at[array, 0], row_recv.at[array, slot], sibling()).wait_recv()

    def save(layer, *which):
        for index in which:
            pltpu.make_async_copy(saved[index].at[layer], saved_out[index].at[layer], save_sem.at[layer, index]).start()

    def kv_copies(layer, pair, receiving):
        copies = []
        for slot, block in enumerate(blocks_of(1 - core if receiving else core)):
            view = saved[3].at[layer, :, pair, tile_rows(block * BLOCK, BLOCK), :]
            copies.append(remote(view, view, kv_send.at[layer, pair, slot], kv_recv.at[layer, pair, slot], sibling()))
        return copies

    actions = {"own": own_start, "z": z_start, "near": near_start, "far": far_start, "sib": sib_start}

    def run(point, turn=None):
        for where, when, owner_core, name, fars, which in FORWARD_PLAN:
            if where != point:
                continue

            def act():
                if name == "own":
                    own_start(*which)
                elif name == "rows":
                    rows_each(1, "start")
                else:
                    for far in fars:
                        actions[name](far, *which)

            here = core == owner_core if owner_core is not None else None
            if turn is not None:
                here = turn == when if here is None else here & (turn == when)
            act() if here is None else pl.when(here)(act)

    for far in steps:
        on(0, z_start, far, QKV)
        z_start(far, VEC)
    own_copy(VEC).start()
    rows_each(0, "start")
    fill_masks(lens_ref, bias_ref, False)
    run("masks")
    own_copy(VEC).wait()
    for step in steps:
        z_copy(VEC, step).wait_recv()
    vec_copy().start()
    run("vec")
    rows_each(0, "wait")
    rows_arrived(0)
    vec_copy().wait_recv()
    run("rows")
    for layer in range(2):
        signed = layer == 0
        held = [item.at[layer] for item in saved]
        qkv, out, up, down, vec = [item.at[layer] for item in weights]
        x_ref, normed_one_t, queries, kv, attended, attended_t, logs, hidden, normed_two_t, act, slope = held

        def after_norm():
            run(f"norm{layer}")

        def before_project(turn):
            run(f"project{layer}", turn)
            need_turn(layer, turn, QKV)

        def push_kv(turn, pair):
            for copy in kv_copies(layer, pair, False):
                copy.start()

        def before_attend(turn, pair):
            run(f"attend{layer}", turn)
            for copy in kv_copies(layer, pair, True):
                copy.wait_recv()

        def before_out(turn):
            need_turn(layer, turn, OUT)

        def before_feed():
            run(f"second{layer}")

        def before_chunk(turn):
            need_turn(layer, turn, UP, DOWN)
            if layer == 1:
                pl.when(turn == PARTS - 1)(partial(keep, 1, OUT, UP, DOWN))

        def during_chunk(turn):
            run(f"chunk{layer}", turn)

        project(x_ref, vec, qkv, normed_one_t, queries, kv, normed, after_norm, before_project, push_kv)
        save(layer, 0, 1, 2)
        keep(layer, QKV, VEC)
        attend_rows(signed, queries, kv, bias_ref, attended, attended_t, logs, logit, factor, stat, before_attend)
        save(layer, 3, 4, 5, 6)
        run(f"attended{layer}")
        target = saved[0].at[1] if layer == 0 else y_ref
        feed(x_ref, attended, vec, out, up, down, hidden, normed_two_t, act, slope, target, normed, wide, total, before_out, before_feed, before_chunk, during_chunk)
        save(layer, 7, 8, 9, 10)
        if layer == 0:
            keep(0, OUT, UP, DOWN)
    y_copy = pltpu.make_async_copy(y_ref, y_out, row_local.at[0])
    y_copy.start()
    rows_each(1, "wait")
    rows_arrived(1)
    for index in range(5):
        for step in steps:
            if step < 3 or index == VEC:
                z_copy(index, step).wait_send()
            else:
                pl.when(jnp.logical_not(ends()))(z_copy(index, step).wait_send)
                pl.when(jnp.logical_not(ends()))(pass_copy(index).wait_send)
            if index != VEC:
                for way in (1, 2):
                    near_copy(index, way, step).wait_send()
                    if index in DIRECT:
                        pl.when(core == 1)(far_copy(index, way, step).wait_send)
                    else:
                        far_copy(index, way, step).wait_send()
                if index in DIRECT:
                    pl.when(core == 0)(across_copy(index, step).wait_send)
                sib_copy(index, step).wait_send()
        sib_copy(index, 0).wait_send() if index != VEC else vec_copy().wait_send()
    for layer in range(2):
        for pair in range(PAIRS):
            for copy in kv_copies(layer, pair, False):
                copy.wait_send()
        for index in range(11):
            pltpu.make_async_copy(saved[index].at[layer], saved_out[index].at[layer], save_sem.at[layer, index]).wait()
    y_copy.wait()
    for layer in range(2):
        for index in range(5):
            keep_copy(layer, index).wait()


FEED, ATTEND = 0, 1
GROUPS = ((0, 1024), (1024, 1536))


def backward_kernel(lens_ref, dy_in, y_in, *refs):
    saved_in, weights_in, refs = refs[:11], refs[11:16], refs[16:]
    down_out, up_out, out_out, qkv_out, vec_out, bias_out, blocks_out, rows_out, refs = *refs[:8], refs[8:]
    held, weights, refs = refs[:11], refs[11:16], refs[16:]
    dy_low, dy_ref, bias_ref, grads_ref, vec_grad, low, low_t, chunk, total, grad_hidden, grad_att, centres, grad_query, grad_kv, kv_out, kv_got, grad_low, refs = *refs[:17], refs[17:]
    got_core, got_first, got_second, part_sum, got_part, final, vec_core, vec_chip, vec_dp, vec_rep, vec_part, grads_out, vec_total, refs = *refs[:13], refs[13:]
    load_sem, weight_sem, dy_sem, y_send, y_recv, row_send, row_recv, kv_send, kv_recv, core_send, core_recv, first_send, first_recv, second_send, second_recv, part_send, part_recv, vec_send, vec_recv, last_send, last_recv = refs
    core, rep, part = place()
    steps = (1, 2, 3)
    mine, theirs = tile_rows(core * 64, 64), tile_rows((1 - core) * 64, 64)

    def load(layer, which=(), matrices=()):
        copies = [pltpu.make_async_copy(saved_in[index].at[layer], held[index], load_sem.at[index]) for index in which]
        return copies + [pltpu.make_async_copy(weights_in[index].at[layer], weights[index], weight_sem.at[index]) for index in matrices]

    def start(copies):
        for copy in copies:
            copy.start()

    def wait(copies):
        for copy in copies:
            copy.wait()

    chunk_set = ((10, 9, 8), (DOWN, UP))
    norm_set = ((7, 5, 4), (VEC, OUT))
    attend_set = ((2, 3, 6), ())
    project_set = ((0, 1), (QKV,))
    dy_copy = pltpu.make_async_copy(dy_in, dy_low, dy_sem.at[0])
    dy_copy.start()
    for group in (chunk_set, norm_set, attend_set, project_set):
        start(load(1, *group))
    greet(all_partners() + [(1 - core, rep, lax.bitwise_xor(part, step)) for step in steps])

    owner = jnp.where((part == 0) | (part == 3), 0, 1)

    def deliver(source, layer, target, send, receive, act):
        for slot, block in enumerate(blocks_of(core)):
            rows = source.at[slot * BLOCK : (slot + 1) * BLOCK]
            stays = (core == layer) & (block == part)

            @pl.when(stays)
            def _():
                copy = pltpu.make_async_copy(rows, target.at[part], send.at[layer, slot])
                copy.start() if act == "start" else copy.wait()

            @pl.when(jnp.logical_not(stays))
            def _():
                copy = remote(rows, target.at[part], send.at[layer, slot], receive.at[part], (layer, rep, block))
                copy.start() if act == "start" else copy.wait_send()

    def delivered(target, source, send, receive):
        for batch in range(PARTS):

            @pl.when((core != owner) | (part != batch))
            def _():
                remote(source.at[:BLOCK], target.at[batch], send.at[0, 0], receive.at[batch], sibling()).wait_recv()

    deliver(saved_in[0].at[1], 0, blocks_out, y_send, y_recv, "start")
    deliver(y_in, 1, blocks_out, y_send, y_recv, "start")

    def core_copy(layer, group, turn):
        first, last = GROUPS[group]
        other, slot = turn_part(turn + 1), (layer, group, turn)
        return remote(grads_ref.at[:, other, theirs, first:last], got_core.at[layer, :, other, :, first:last], core_send.at[slot], core_recv.at[slot], sibling())

    def halves(way):
        return pl.ds(0, 32) if way == 1 else pl.ds(32, 32)

    def first_copy(layer, group, turn, way, piece):
        first, last = GROUPS[group]
        other, slot = turn_part(turn + 1), (layer, group, turn, way - 1, piece)
        source = got_core.at[layer, lax.bitwise_xor(rep, 3 if piece else way), other, halves(way), first:last]
        return remote(source, got_first.at[layer, way - 1, piece, other, :, first:last], first_send.at[slot], first_recv.at[slot], along_dp(way))

    def second_copy(layer, group, turn, way):
        first, last = GROUPS[group]
        other, slot = turn_part(turn + 1), (layer, group, turn, way - 1)
        source = got_core.at[layer, lax.bitwise_xor(rep, 3 - way), other, halves(way), first:last]
        return remote(source, got_second.at[layer, way - 1, other, :, first:last], second_send.at[slot], second_recv.at[slot], along_dp(3 - way))

    def part_copy(layer, group, turn):
        first, last = GROUPS[group]
        slot = (layer, group, turn)
        return remote(part_sum.at[layer, turn, :, first:last], got_part.at[layer, turn, :, first:last], part_send.at[slot], part_recv.at[slot], along_tensor(turn + 1))

    def dp_start(layer, group, turn):
        first, last = GROUPS[group]
        core_copy(layer, group, turn).wait()
        other = turn_part(turn + 1)

        def add(major, carry):
            own = grads_ref[major, other, mine, first:last].astype(jnp.float32)
            sum_here = own + got_core[layer, major, other, :, first:last].astype(jnp.float32)
            got_core[layer, major, other, :, first:last] = sum_here.astype(jnp.bfloat16)
            return carry

        lax.fori_loop(0, PARTS, add, 0)
        start(first_copy(layer, group, turn, way, piece) for way in (1, 2) for piece in range(2))

    def dp_next(layer, group, turn):
        first, last = GROUPS[group]
        other = turn_part(turn + 1)
        for way in (1, 2):
            for piece in (1, 0):
                first_copy(layer, group, turn, way, piece).wait()
                major = lax.bitwise_xor(rep, 3 - way) if piece else rep
                own = got_core[layer, major, other, halves(way), first:last].astype(jnp.float32)
                sum_here = own + got_first[layer, way - 1, piece, other, :, first:last].astype(jnp.float32)
                got_core[layer, major, other, halves(way), first:last] = sum_here.astype(jnp.bfloat16)
                if piece:
                    second_copy(layer, group, turn, way).start()

    def part_start(layer, group, turn):
        first, last = GROUPS[group]
        other = turn_part(turn + 1)
        for way in (1, 2):
            second_copy(layer, group, turn, way).wait()
            own = got_core[layer, rep, other, halves(way), first:last].astype(jnp.float32)
            sum_here = own + got_second[layer, way - 1, other, :, first:last].astype(jnp.float32)
            part_sum[layer, turn, halves(way), first:last] = sum_here.astype(jnp.bfloat16)
        if turn < PARTS - 1:
            part_copy(layer, group, turn).start()

    def finish(layer, group):
        first, last = GROUPS[group]
        sum_here = part_sum[layer, PARTS - 1, :, first:last].astype(jnp.float32)
        for turn in range(PARTS - 1):
            part_copy(layer, group, turn).wait()
            sum_here = sum_here + got_part[layer, turn, :, first:last].astype(jnp.float32)
        final[layer, :, first:last] = sum_here

    def last_copy(layer):
        return remote(final.at[layer], grads_out.at[mine], last_send.at[0], last_recv.at[0], sibling())

    def hand_over(layer):
        @pl.when(core == layer)
        def _():
            grads_out[mine, :] = final[layer]

        @pl.when(core != layer)
        def _():
            last_copy(layer).start()

    def kv_copy(layer, pair):
        return remote(kv_out.at[:, pair], kv_got.at[layer, :, pair], kv_send.at[layer, pair], kv_recv.at[layer, pair], sibling())

    fill_masks(lens_ref, bias_ref, True)
    for layer in (1, 0):
        signed = layer == 0
        x_ref, normed_one_t, queries, kv, attended, attended_t, logs, hidden, normed_two_t, act, slope = held
        qkv, out, up, down, vec = weights
        if layer == 1:
            dy_copy.wait()
            dy_ref[...] = dy_low[...].astype(jnp.float32)
        wait(load(layer, *chunk_set))

        def at(turn, when, action, *which):
            pl.when(turn == when)(partial(action, *which))

        def during_chunk(turn):
            pl.when(turn > 0)(lambda: dp_start(layer, FEED, turn - 1))
            if layer == 0:
                at(turn, 0, dp_next, 1, ATTEND, 1)
                at(turn, 0, dp_next, 1, ATTEND, 2)
                at(turn, 1, dp_next, 1, ATTEND, 3)
                at(turn, 1, part_start, 1, ATTEND, 0)
                at(turn, 2, part_start, 1, ATTEND, 1)
                at(turn, 2, part_start, 1, ATTEND, 2)
                at(turn, 3, part_start, 1, ATTEND, 3)

        def after_chunk(turn, chunk):
            core_copy(layer, FEED, turn).start()

        def before_norm():
            wait(load(layer, *norm_set))

        def after_norm():
            dp_start(layer, FEED, 3)
            dp_next(layer, FEED, 0)

        feed_back(dy_ref, act, slope, down, up, hidden, normed_two_t, vec, out, attended, attended_t, grad_hidden, grad_att, centres, grads_ref, vec_grad.at[layer], low, low_t, chunk, total, during_chunk, after_chunk, before_norm, after_norm)
        if layer == 1:
            start(load(0, (9, 10, 7, 8, 4, 5), (DOWN, UP, OUT)))
        wait(load(layer, *attend_set))

        def before_attend(turn):
            for index in range(3):
                at(turn, index, dp_next, layer, FEED, index + 1)
                at(turn, index + 1, part_start, layer, FEED, index)
            if layer == 0:
                at(turn, 3, finish, 1, FEED)
                at(turn, 3, finish, 1, ATTEND)
                at(turn, 3, hand_over, 1)

        def project_turn(turn):
            pair = turn_part(turn + 1)
            kv_copy(layer, pair).wait()
            project_back_pair(pair, grad_query, grad_kv, kv_got.at[layer], normed_one_t, qkv, grads_ref, total, core_copy(layer, ATTEND, turn).start)

        def after_attend(turn, pair):
            kv_copy(layer, pair).start()
            at(turn, 2, dp_start, layer, ATTEND, 0)
            at(turn, 3, dp_start, layer, ATTEND, 1)
            at(turn, 3, dp_next, layer, ATTEND, 0)
            pl.when(turn > 0)(lambda: project_turn(turn - 1))

        wait(load(layer, *project_set))
        total[...] = jnp.zeros_like(total)
        attend_rows_back(signed, queries, kv, grad_att, bias_ref, logs, centres, grad_query, grad_kv, kv_out, before_attend, after_attend)
        if layer == 1:
            start(load(0, *attend_set))
        dp_start(layer, ATTEND, 2)
        part_start(layer, FEED, 3)
        project_turn(PAIRS - 1)
        project_back_norm(x_ref, grad_hidden, vec, dy_ref, grad_low.at[layer], vec_grad.at[layer], total)
        if layer == 1:
            start(load(0, (0, 1), (QKV, VEC)))
        deliver(grad_low.at[layer], layer, rows_out, row_send, row_recv, "start")
        dp_start(layer, ATTEND, 3)
    vec_copy = remote(vec_grad.at[1 - core], vec_core, vec_send.at[0], vec_recv.at[0], sibling())
    vec_copy.start()
    dp_next(0, ATTEND, 1)
    dp_next(0, ATTEND, 2)
    finish(0, FEED)
    vec_copy.wait()
    vec_chip[...] = vec_grad[core] + vec_core[...]
    vec_copies = [remote(vec_chip, vec_dp.at[step - 1], vec_send.at[step], vec_recv.at[step], along_dp(step)) for step in steps]
    start(vec_copies)
    dp_next(0, ATTEND, 3)
    for turn in range(PARTS):
        part_start(0, ATTEND, turn)
    wait(vec_copies)
    vec_rep[...] = vec_chip[...] + vec_dp[0] + vec_dp[1] + vec_dp[2]
    vec_copies = [remote(vec_rep, vec_part.at[step - 1], vec_send.at[3 + step], vec_recv.at[3 + step], along_tensor(step)) for step in steps]
    start(vec_copies)
    finish(0, ATTEND)
    hand_over(0)
    wait(vec_copies)
    vec_total[...] = vec_rep[...] + vec_part[0] + vec_part[1] + vec_part[2]
    own = rep * PARTS + part
    vec_out[...] = pltpu.roll(vec_total[:8, :], 512 - own * 32, 1)[:, :128]
    columns = vec_total[:, tile_rows(rep * 128, 128)]
    row = lax.broadcasted_iota(jnp.int32, columns.shape, 0)
    bias_out[...] = column_sum(jnp.where(row == 6 + part, columns, 0.0))
    deliver(saved_in[0].at[1], 0, blocks_out, y_send, y_recv, "wait")
    deliver(y_in, 1, blocks_out, y_send, y_recv, "wait")
    delivered(blocks_out, y_in, y_send, y_recv)
    for layer in range(2):
        deliver(grad_low.at[layer], layer, rows_out, row_send, row_recv, "wait")
    delivered(rows_out, grad_low.at[0], row_send, row_recv)
    last_copy(0).wait_recv()
    last_copy(0).wait_send()
    down_out[...] = grads_out[:, :512].T
    up_out[...] = grads_out[:, 512:1024]
    out_out[...] = grads_out[:, 1024:1152]
    for kind in range(3):
        qkv_out[kind] = grads_out[:, 1152 + kind * 128 : 1280 + kind * 128]


def specs(space, count):
    return [pl.BlockSpec(memory_space=space)] * count


def kernel_call(body, name, ins, in_specs, outs, out_specs, scratch, collective):
    dma = pltpu.SemaphoreType.DMA
    return pl.pallas_call(
        body,
        out_shape=[jax.ShapeDtypeStruct(shape, kind) for shape, kind in outs],
        in_specs=in_specs,
        out_specs=out_specs,
        scratch_shapes=[pltpu.VMEM(*item) if len(item) == 2 and isinstance(item[0], tuple) else dma(item) for item in scratch],
        compiler_params=pltpu.CompilerParams(collective_id=collective, has_side_effects=True, vmem_limit_bytes=60 * 2**20),
        name=name,
    )(*ins)


def twice(items):
    return tuple(((2, *shape), kind) for shape, kind in items)


def on_device_whole(
    tokens,
    lengths,
    cotangent,
    ln_one_gain,
    ln_one_bias,
    qkv_weight,
    out_weight,
    out_bias,
    ln_two_gain,
    ln_two_bias,
    up_weight,
    up_bias,
    down_weight,
    down_bias,
):
    f32, low = jnp.float32, jnp.bfloat16
    core, rep, part = place()
    vectors = (ln_one_gain, ln_one_bias, out_bias, ln_two_gain, ln_two_bias, down_bias, up_bias)
    rows, rows_low = ((OWN, WIDTH), f32), ((OWN, WIDTH), low)
    square = ((BLOCK, BLOCK), f32)
    results = kernel_call(
        forward_kernel,
        "forward",
        (lengths, tokens, cotangent, qkv_weight[0].transpose(1, 0, 2), out_weight[0], up_weight[0], down_weight[0], *vectors),
        specs(pltpu.SMEM, 1) + specs(pl.ANY, 6) + specs(pltpu.VMEM, 7),
        (rows_low, rows_low, *twice(SAVED), *twice(WEIGHTS)),
        specs(pl.ANY, 18),
        (
            *twice(SAVED),
            *twice(WEIGHTS),
            rows_low,
            ((TASKS, BLOCK, BLOCK), f32),
            rows_low,
            ((TASKS, BLOCK, BLOCK), f32),
            ((TASKS, BLOCK, BLOCK), f32),
            ((2, BLOCK, 128), f32),
            rows,
            rows,
            ((8, 512), f32),
            (2, 4),
            (2, 2),
            (2,),
            (5, 3),
            (5, 3),
            (4, 3, 4),
            (4, 3, 4),
            (5, PARTS),
            (5, PARTS),
            (5,),
            (2, PAIRS, 2),
            (2, PAIRS, 2),
            (2, 11),
            (2, 5),
            (4,),
        ),
        0,
    )
    down_grad, up_grad, out_grad, qkv_grad, spread, up_bias_grad, block_outputs, grad_rows = kernel_call(
        backward_kernel,
        "backward",
        (lengths, *results),
        specs(pltpu.SMEM, 1) + specs(pl.ANY, 18),
        (
            ((512, 128), f32),
            ((128, 512), f32),
            ((128, 128), f32),
            ((3, 128, 128), f32),
            ((8, 128), f32),
            ((1, 128), f32),
            ((PARTS, BLOCK, WIDTH), low),
            ((PARTS, BLOCK, WIDTH), low),
        ),
        specs(pltpu.VMEM, 6) + specs(pl.ANY, 2),
        (
            *SAVED,
            *WEIGHTS,
            rows_low,
            rows,
            ((TASKS, BLOCK, BLOCK), f32),
            ((PARTS, PARTS, 128, 1536), low),
            ((2, 16, 512), f32),
            rows_low,
            ((WIDTH, OWN), low),
            ((OWN, 512), low),
            rows,
            rows,
            ((PAIRS, 2, OWN, 128), low),
            ((PAIRS, 8, OWN), f32),
            ((PAIRS, OWN, 128), low),
            ((2, PAIRS, 1024, 128), f32),
            ((2, PAIRS, OWN, 128), low),
            ((2, 2, PAIRS, OWN, 128), low),
            ((2, OWN, WIDTH), low),
            ((2, PARTS, PARTS, 64, 1536), low),
            ((2, 2, 2, PARTS, 32, 1536), low),
            ((2, 2, PARTS, 32, 1536), low),
            ((2, PARTS, 64, 1536), low),
            ((2, 3, 64, 1536), low),
            ((2, 64, 1536), f32),
            ((16, 512), f32),
            ((16, 512), f32),
            ((3, 16, 512), f32),
            ((16, 512), f32),
            ((3, 16, 512), f32),
            ((128, 1536), f32),
            ((16, 512), f32),
            (11,),
            (5,),
            (1,),
            (2, 2),
            (PARTS,),
            (2, 2),
            (PARTS,),
            (2, PAIRS),
            (2, PAIRS),
            (2, 2, PARTS),
            (2, 2, PARTS),
            (2, 2, PARTS, 2, 2),
            (2, 2, PARTS, 2, 2),
            (2, 2, PARTS, 2),
            (2, 2, PARTS, 2),
            (2, 2, PARTS),
            (2, 2, PARTS),
            (7,),
            (7,),
            (1,),
            (1,),
        ),
        1,
    )
    vector_grads = [spread[row : row + 1, :32] for row in range(6)]
    return (
        block_outputs[None],
        grad_rows.astype(f32)[None],
        vector_grads[0],
        vector_grads[1],
        qkv_grad.transpose(1, 0, 2)[None],
        out_grad[None],
        vector_grads[2],
        vector_grads[3],
        vector_grads[4],
        up_grad[None],
        up_bias_grad[None],
        down_grad[None],
        vector_grads[5],
    )


def solution(mesh):
    return jax.shard_map(
        on_device_whole if whole_batch_fits(mesh) else on_device,
        mesh=mesh,
        in_specs=(
            P("dp", "tensor", None),
            P("dp", None),
            P("dp", "tensor", None),
            P("section", None),
            P("section", None),
            P("section", None, None, "tensor"),
            P("section", "tensor", None),
            P("section", None),
            P("section", None),
            P("section", None),
            P("section", None, "tensor"),
            P("section", "tensor"),
            P("section", "tensor", None),
            P("section", None),
        ),
        out_specs=(
            P("section", "dp", "tensor", None),
            P("section", "dp", "tensor", None),
            P("section", ("dp", "tensor")),
            P("section", ("dp", "tensor")),
            P("section", "dp", None, "tensor"),
            P("section", "tensor", "dp"),
            P("section", ("dp", "tensor")),
            P("section", ("dp", "tensor")),
            P("section", ("dp", "tensor")),
            P("section", "dp", "tensor"),
            P("section", "tensor", "dp"),
            P("section", "tensor", "dp"),
            P("section", ("dp", "tensor")),
        ),
        check_vma=False,
    )
```

```python
from functools import partial
import math

import jax
import jax.numpy as jnp
from jax import lax
from jax.experimental import pallas as pl
from jax.experimental.pallas import tpu as pltpu
from jax.sharding import PartitionSpec as P

HEAD = 64
FF = 2048


def passed_along(block, axis, distance):
    devices = range(lax.axis_size(axis))
    route = [(i - distance, i) for i in devices if i - distance in devices]
    return lax.ppermute(block, axis, route)


def normalize(values, gain_vec, bias_vec):
    centre = values - jnp.mean(values, axis=-1, keepdims=True)
    spread = jnp.mean(centre * centre, axis=-1, keepdims=True)
    return centre * lax.rsqrt(spread + 1e-05) * gain_vec + bias_vec


def document_ids(seq_lens, row_count):
    bounds = jnp.cumsum(seq_lens)
    places = jnp.arange(row_count, dtype=jnp.int32)
    return jnp.sum((places[:, None] >= bounds[None, :]).astype(jnp.int32), axis=1)


def first_key_block(doc_number, seq_lens, block):
    starts = jnp.cumsum(seq_lens) - seq_lens
    numbers = jnp.arange(seq_lens.shape[0], dtype=jnp.int32)
    return jnp.sum(jnp.where(numbers == doc_number, starts, 0)) // block


def grouped_sum(left, right, groups):
    row_count, inner = left.shape
    terms = jnp.einsum(
        "rgc,gcd->grd",
        left.reshape(row_count, groups, inner // groups),
        right.reshape(groups, inner // groups, right.shape[-1]),
        preferred_element_type=jnp.float32,
    )
    return jnp.sum(lax.optimization_barrier(terms.astype(jnp.bfloat16)).astype(jnp.float32), axis=0)


def branch_total(left, right):
    return grouped_sum(left, right, lax.axis_size("tensor"))


def key_scores(query_rows, key_part, query_docs, key_docs, query_first, key_first, signed):
    scale = 1.0 / math.sqrt(query_rows.shape[-1])
    scores = (
        jnp.einsum("qhe,khe->hqk", query_rows, key_part, preferred_element_type=jnp.float32) * scale
    )
    query_places = query_first + jnp.arange(query_rows.shape[0], dtype=jnp.int32)
    key_places = key_first + jnp.arange(key_part.shape[0], dtype=jnp.int32)
    allowed = (query_docs[:, None] == key_docs[None, :]) & (
        query_places[:, None] >= key_places[None, :]
    )
    modulus = jnp.sqrt(scores * scores + 1.0)
    logits = jnp.where(signed, modulus, scores)
    factor = jnp.where(signed, scores / modulus, 1.0)
    return (modulus, logits, factor, allowed[None])


def attend(queries, key_rows, values, doc_rows, seq_lens, signed, offset):
    query_count, heads_here, head_size = queries.shape
    key_count = key_rows.shape[0]
    query_block = min(512, query_count)
    key_block = min(512, key_count)
    query_first = offset + 0
    query_docs = lax.dynamic_slice_in_dim(doc_rows, query_first, query_block, 0)
    lowest = first_key_block(query_docs[0], seq_lens, key_block)
    upper = (query_first + query_block - 1) // key_block + 1

    def block_scores(key_index):
        key_first = key_index * key_block
        return key_scores(
            queries,
            lax.dynamic_slice_in_dim(key_rows, key_first, key_block, 0),
            query_docs,
            lax.dynamic_slice_in_dim(doc_rows, key_first, key_block, 0),
            query_first,
            key_first,
            signed,
        )

    def measure(key_index, carry):
        running_max, running_sum = carry
        modulus, logits, factor, allowed = block_scores(key_index)
        masked = jnp.where(allowed, logits, -1e30)
        new_max = jnp.maximum(running_max, jnp.max(masked, axis=-1))
        added = jnp.sum(jnp.where(allowed, jnp.exp(masked - new_max[:, :, None]), 0.0), axis=-1)
        return (new_max, running_sum * jnp.exp(running_max - new_max) + added)

    start_max = jnp.full((heads_here, query_block), -1e30, jnp.float32)
    start_sum = jnp.zeros((heads_here, query_block), jnp.float32)
    row_max, row_sum = lax.fori_loop(lowest, upper, measure, (start_max, start_sum))
    log_total = row_max + jnp.log(row_sum)

    def accumulate(key_index, partial_out):
        modulus, logits, factor, allowed = block_scores(key_index)
        probs = jnp.where(allowed, jnp.exp(logits - log_total[:, :, None]), 0.0)
        weights = (factor * probs).astype(jnp.bfloat16)
        value_rows = lax.dynamic_slice_in_dim(values, key_index * key_block, key_block, 0)
        return partial_out + jnp.einsum(
            "hqk,khe->qhe", weights, value_rows, preferred_element_type=jnp.float32
        )

    outputs_list = lax.fori_loop(
        lowest, upper, accumulate, jnp.zeros((query_block, heads_here, head_size), jnp.float32)
    )
    return (outputs_list, log_total)


def attend_back(
    queries,
    key_rows,
    values,
    doc_rows,
    seq_lens,
    signed,
    attended,
    log_totals,
    grad_attended,
    offset,
):
    query_count, heads_here, head_size = queries.shape
    key_count = key_rows.shape[0]
    query_block = min(512, query_count)
    key_block = min(512, key_count)
    scale = 1.0 / math.sqrt(head_size)
    centre_terms = jnp.sum(grad_attended.astype(jnp.float32) * attended, axis=-1).T
    grad_keys = jnp.zeros(key_rows.shape, jnp.float32)
    grad_values = jnp.zeros(key_rows.shape, jnp.float32)
    query_first = offset + 0
    query_docs = lax.dynamic_slice_in_dim(doc_rows, query_first, query_block, 0)
    lowest = first_key_block(query_docs[0], seq_lens, key_block)
    upper = (query_first + query_block - 1) // key_block + 1

    def backward_step(key_index, carry):
        grad_query, keys_total, values_total = carry
        key_first = key_index * key_block
        key_part = lax.dynamic_slice_in_dim(key_rows, key_first, key_block, 0)
        value_rows = lax.dynamic_slice_in_dim(values, key_first, key_block, 0)
        modulus, logits, factor, allowed = key_scores(
            queries,
            key_part,
            query_docs,
            lax.dynamic_slice_in_dim(doc_rows, key_first, key_block, 0),
            query_first,
            key_first,
            signed,
        )
        probs = jnp.where(allowed, jnp.exp(logits - log_totals[:, :, None]), 0.0)
        weights = (factor * probs).astype(jnp.bfloat16)
        grad_weights = jnp.einsum(
            "qhe,khe->hqk", grad_attended, value_rows, preferred_element_type=jnp.float32
        )
        grad_scores = factor * probs * (factor * grad_weights - centre_terms[:, :, None])
        grad_scores = grad_scores + jnp.where(
            signed, probs * grad_weights / (modulus * modulus * modulus), 0.0
        )
        grad_low = grad_scores.astype(jnp.bfloat16)
        grad_query = (
            grad_query
            + jnp.einsum("hqk,khe->qhe", grad_low, key_part, preferred_element_type=jnp.float32)
            * scale
        )
        key_term = (
            jnp.einsum("hqk,qhe->khe", grad_low, queries, preferred_element_type=jnp.float32)
            * scale
        )
        value_term = jnp.einsum(
            "hqk,qhe->khe", weights, grad_attended, preferred_element_type=jnp.float32
        )
        keys_total = lax.dynamic_update_slice_in_dim(
            keys_total,
            lax.dynamic_slice_in_dim(keys_total, key_first, key_block, 0) + key_term,
            key_first,
            0,
        )
        values_total = lax.dynamic_update_slice_in_dim(
            values_total,
            lax.dynamic_slice_in_dim(values_total, key_first, key_block, 0) + value_term,
            key_first,
            0,
        )
        return (grad_query, keys_total, values_total)

    start_query = jnp.zeros((query_block, heads_here, head_size), jnp.float32)
    grad_query, grad_keys, grad_values = lax.fori_loop(
        lowest, upper, backward_step, (start_query, grad_keys, grad_values)
    )
    return (grad_query, grad_keys, grad_values)


def forward_layer(inputs, seq_lens, params, signed, finish):
    (
        gain_one,
        bias_one,
        qkv_weight,
        out_weight,
        out_bias,
        gain_two,
        bias_two,
        up_weight,
        up_bias,
        down_weight,
        down_bias,
    ) = params
    normed_one = normalize(inputs, gain_one, bias_one).astype(jnp.bfloat16)
    offset = lax.axis_index("tensor") * normed_one.shape[0]
    row_count = normed_one.shape[0]
    width = qkv_weight.shape[-1]
    projected = jnp.dot(
        normed_one,
        qkv_weight.reshape(qkv_weight.shape[0], 3 * width),
        preferred_element_type=jnp.float32,
    ).astype(jnp.bfloat16)
    head_shape = (row_count, width // HEAD, HEAD)
    queries = projected[:, :width].reshape(head_shape)
    key_rows = projected[:, width : 2 * width].reshape(head_shape)
    values = projected[:, 2 * width :].reshape(head_shape)
    key_all, value_all = (
        lax.all_gather(key_rows, "tensor", axis=0, tiled=True),
        lax.all_gather(values, "tensor", axis=0, tiled=True),
    )
    doc_rows = document_ids(seq_lens, key_all.shape[0])
    attended, log_totals = attend(queries, key_all, value_all, doc_rows, seq_lens, signed, offset)
    attended_low = attended.reshape(row_count, width).astype(jnp.bfloat16)
    hidden_one = inputs + branch_total(attended_low, out_weight) + out_bias
    normed_two = normalize(hidden_one, gain_two, bias_two).astype(jnp.bfloat16)
    up_values = jnp.dot(normed_two, up_weight, preferred_element_type=jnp.float32) + up_bias
    activated = jax.nn.gelu(up_values, approximate=False).astype(jnp.bfloat16)
    if finish:
        outputs = hidden_one + branch_total(activated, down_weight) + down_bias
    else:
        outputs = hidden_one
    saved = (
        normed_one,
        queries,
        key_all,
        value_all,
        doc_rows,
        attended,
        attended_low,
        log_totals,
        hidden_one,
        normed_two,
        up_values,
        activated,
        offset,
    )
    return (outputs, saved)


def backward_layer(inputs, seq_lens, params, signed, grad_outputs):
    (
        gain_one,
        bias_one,
        qkv_weight,
        out_weight,
        out_bias,
        gain_two,
        bias_two,
        up_weight,
        up_bias,
        down_weight,
        down_bias,
    ) = params
    unused_out, saved = forward_layer(inputs, seq_lens, params, signed, False)
    (
        rows_one,
        queries,
        key_all,
        value_all,
        doc_rows,
        attended,
        attended_low,
        log_totals,
        hidden_one,
        rows_two,
        up_values,
        activated,
        offset,
    ) = saved
    row_count, width = attended_low.shape
    grad_low = grad_outputs.astype(jnp.bfloat16)
    grad_down = jnp.einsum("rf,rd->fd", activated, grad_low, preferred_element_type=jnp.float32)
    grad_act = jnp.einsum("rd,fd->rf", grad_low, down_weight, preferred_element_type=jnp.float32)
    gelu_value, gelu_back = jax.vjp(partial(jax.nn.gelu, approximate=False), up_values)
    grad_up_values = gelu_back(grad_act)[0].astype(jnp.bfloat16)
    grad_up_bias = jnp.sum(grad_up_values.astype(jnp.float32), axis=0)
    grad_up = jnp.einsum("rd,rf->df", rows_two, grad_up_values, preferred_element_type=jnp.float32)
    normed_two_terms = jnp.einsum(
        "rf,df->rd", grad_up_values, up_weight, preferred_element_type=jnp.float32
    )
    norm_value, norm_back = jax.vjp(normalize, hidden_one, gain_two, bias_two)
    grad_hidden, grad_gain_two, grad_bias_two = norm_back(normed_two_terms)
    grad_hidden = grad_hidden + grad_outputs
    hidden_low = grad_hidden.astype(jnp.bfloat16)
    grad_out = jnp.einsum("rc,rd->cd", attended_low, hidden_low, preferred_element_type=jnp.float32)
    grad_attended = (
        jnp.einsum("rd,cd->rc", hidden_low, out_weight, preferred_element_type=jnp.float32)
        .astype(jnp.bfloat16)
        .reshape(queries.shape)
    )
    grad_queries, grad_keys, grad_values = attend_back(
        queries,
        key_all,
        value_all,
        doc_rows,
        seq_lens,
        signed,
        attended,
        log_totals,
        grad_attended,
        offset,
    )
    grad_keys, grad_values = (
        lax.psum_scatter(
            grad_keys.astype(jnp.bfloat16), "tensor", scatter_dimension=0, tiled=True
        ).astype(jnp.float32),
        lax.psum_scatter(
            grad_values.astype(jnp.bfloat16), "tensor", scatter_dimension=0, tiled=True
        ).astype(jnp.float32),
    )
    grad_projected = jnp.concatenate(
        [
            grad_queries.reshape(row_count, width),
            grad_keys.reshape(row_count, width),
            grad_values.reshape(row_count, width),
        ],
        axis=1,
    ).astype(jnp.bfloat16)
    grad_qkv = jnp.einsum(
        "rd,rc->dc", rows_one, grad_projected, preferred_element_type=jnp.float32
    ).reshape(qkv_weight.shape)
    normed_one_terms = jnp.einsum(
        "rc,dc->rd",
        grad_projected,
        qkv_weight.reshape(qkv_weight.shape[0], 3 * width),
        preferred_element_type=jnp.float32,
    )
    norm_value_one, norm_back_one = jax.vjp(normalize, inputs, gain_one, bias_one)
    grad_inputs, grad_gain_one, grad_bias_one = norm_back_one(normed_one_terms)
    grad_inputs = grad_inputs + grad_hidden
    matrices = (
        grad_qkv[None],
        grad_out[None],
        grad_up[None],
        grad_up_bias.reshape(1, -1, FF // lax.axis_size("tensor")),
        grad_down[None],
    )
    vectors = (
        grad_gain_one[None],
        grad_bias_one[None],
        jnp.sum(grad_hidden, axis=0)[None],
        grad_gain_two[None],
        grad_bias_two[None],
        jnp.sum(grad_outputs, axis=0)[None],
    )
    return (grad_inputs, matrices, vectors)


def on_device(
    tokens,
    lengths,
    cotangent,
    ln_one_gain,
    ln_one_bias,
    qkv_weight,
    out_weight,
    out_bias,
    ln_two_gain,
    ln_two_bias,
    up_weight,
    up_bias,
    down_weight,
    down_bias,
):
    signed = lax.axis_index("section") == 0
    params = tuple(
        (
            array_item[0]
            for array_item in (
                ln_one_gain,
                ln_one_bias,
                qkv_weight,
                out_weight,
                out_bias,
                ln_two_gain,
                ln_two_bias,
                up_weight,
                up_bias,
                down_weight,
                down_bias,
            )
        )
    )
    whole = (
        lax.all_gather(qkv_weight, "tensor", axis=3, tiled=True),
        lax.all_gather(out_weight, "tensor", axis=1, tiled=True),
        lax.all_gather(up_weight, "tensor", axis=2, tiled=True),
        lax.all_gather(down_weight, "tensor", axis=1, tiled=True),
    )
    bias_whole = lax.all_gather(up_bias, "tensor", axis=1, tiled=True)
    params = (
        params[0],
        params[1],
        whole[0][0],
        whole[1][0],
        params[4],
        params[5],
        params[6],
        whole[2][0],
        bias_whole[0],
        whole[3][0],
        params[10],
    )
    batches = tokens.shape[0]
    arrived = jnp.zeros(tokens.shape[1:], jnp.bfloat16)
    produced_all = jnp.zeros(tokens.shape, jnp.bfloat16)
    received_all = jnp.zeros(tokens.shape, jnp.bfloat16)
    for tick in range(batches + 1):
        own_index = min(tick, batches - 1)
        prior_index = max(tick - 1, 0)
        inputs_now = jnp.where(signed, tokens[own_index], arrived).astype(jnp.float32)
        lens_now = jnp.where(signed, lengths[own_index], lengths[prior_index])
        produced = forward_layer(inputs_now, lens_now, params, signed, True)[0].astype(jnp.bfloat16)
        if tick < batches:
            produced_all = produced_all.at[tick].set(
                jnp.where(signed, produced, produced_all[tick])
            )
        if tick > 0:
            produced_all = produced_all.at[tick - 1].set(
                jnp.where(signed, produced_all[tick - 1], produced)
            )
            received_all = received_all.at[tick - 1].set(arrived)
        if tick < batches:
            arrived = passed_along(produced, "section", 1)
    block_inputs = jnp.where(signed, tokens, received_all)
    returned = jnp.zeros(tokens.shape[1:], jnp.float32)
    grad_inputs_all = jnp.zeros(tokens.shape, jnp.float32)
    matrix_total = None
    vector_total = None
    for tick in range(batches + 1):
        later_index = batches - 1 - tick if tick < batches else 0
        earlier_index = batches - tick if tick > 0 else 0
        index_now = jnp.where(signed, earlier_index, later_index)
        live_now = jnp.where(signed, tick > 0, tick < batches)
        grad_now = jnp.where(signed, returned, cotangent[later_index].astype(jnp.float32))
        grad_now = jnp.where(live_now, grad_now, 0.0)
        inputs_now = block_inputs[index_now].astype(jnp.float32)
        grad_back, matrices, vectors = backward_layer(
            inputs_now, lengths[index_now], params, signed, grad_now
        )
        if tick == 0:
            matrix_total = tuple(matrices)
            vector_total = tuple(vectors)
        else:
            matrix_total = tuple(
                (
                    jnp.add(total_item, new_item)
                    for total_item, new_item in zip(matrix_total, matrices)
                )
            )
            vector_total = tuple(
                (
                    jnp.add(total_item, new_item)
                    for total_item, new_item in zip(vector_total, vectors)
                )
            )
        if tick > 0:
            grad_inputs_all = grad_inputs_all.at[earlier_index].set(
                jnp.where(signed, grad_back, grad_inputs_all[earlier_index])
            )
        if tick < batches:
            grad_inputs_all = grad_inputs_all.at[later_index].set(
                jnp.where(signed, grad_inputs_all[later_index], grad_back)
            )
            returned = passed_along(grad_back.astype(jnp.bfloat16), "section", -1).astype(
                grad_back.dtype
            )
    matrix_final = (
        lax.psum_scatter(
            matrix_total[0].astype(jnp.bfloat16), "dp", scatter_dimension=1, tiled=True
        ).astype(jnp.float32),
        lax.psum_scatter(
            matrix_total[1].astype(jnp.bfloat16), "dp", scatter_dimension=2, tiled=True
        ).astype(jnp.float32),
        lax.psum_scatter(
            matrix_total[2].astype(jnp.bfloat16), "dp", scatter_dimension=1, tiled=True
        ).astype(jnp.float32),
        lax.psum_scatter(
            matrix_total[3].astype(jnp.bfloat16), "dp", scatter_dimension=2, tiled=True
        ).astype(jnp.float32),
        lax.psum_scatter(
            matrix_total[4].astype(jnp.bfloat16), "dp", scatter_dimension=2, tiled=True
        ).astype(jnp.float32),
    )
    vector_final = (
        lax.psum_scatter(vector_total[0], ("dp", "tensor"), scatter_dimension=1, tiled=True),
        lax.psum_scatter(vector_total[1], ("dp", "tensor"), scatter_dimension=1, tiled=True),
        lax.psum_scatter(vector_total[2], ("dp", "tensor"), scatter_dimension=1, tiled=True),
        lax.psum_scatter(vector_total[3], ("dp", "tensor"), scatter_dimension=1, tiled=True),
        lax.psum_scatter(vector_total[4], ("dp", "tensor"), scatter_dimension=1, tiled=True),
        lax.psum_scatter(vector_total[5], ("dp", "tensor"), scatter_dimension=1, tiled=True),
    )
    matrix_final = (
        lax.psum_scatter(
            matrix_final[0].astype(jnp.bfloat16), "tensor", scatter_dimension=3, tiled=True
        ).astype(jnp.float32),
        lax.psum_scatter(
            matrix_final[1].astype(jnp.bfloat16), "tensor", scatter_dimension=1, tiled=True
        ).astype(jnp.float32),
        lax.psum_scatter(
            matrix_final[2].astype(jnp.bfloat16), "tensor", scatter_dimension=2, tiled=True
        ).astype(jnp.float32),
        lax.psum_scatter(
            matrix_final[3].astype(jnp.bfloat16), "tensor", scatter_dimension=1, tiled=True
        ).astype(jnp.float32),
        lax.psum_scatter(
            matrix_final[4].astype(jnp.bfloat16), "tensor", scatter_dimension=1, tiled=True
        ).astype(jnp.float32),
    )
    grad_qkv, grad_out, grad_up, grad_up_bias, grad_down = matrix_final
    grad_gain_one, grad_bias_one, grad_out_bias, grad_gain_two, grad_bias_two, grad_down_bias = (
        vector_final
    )
    return (
        produced_all[None],
        grad_inputs_all[None],
        grad_gain_one,
        grad_bias_one,
        grad_qkv,
        grad_out,
        grad_out_bias,
        grad_gain_two,
        grad_bias_two,
        grad_up,
        grad_up_bias,
        grad_down,
        grad_down_bias,
    )


MESH = pl.DeviceIdType.MESH
PARTS = 4
BLOCK = 256
OWN = 512
WIDTH = 512
PAIRS = 4
TASKS = 5
NEGATIVE = -1e30
LEFT = (((1,), (0,)), ((), ()))
BOTH_LAST = (((1,), (1,)), ((), ()))
BOTH_FIRST = (((0,), (0,)), ((), ()))


def whole_batch_fits(mesh):
    shape = dict(mesh.shape)
    return shape["tensor"] == PARTS and shape["dp"] == PARTS and shape["section"] == 2


def dot(left, right, dims=LEFT):
    return lax.dot_general(left, right, dims, preferred_element_type=jnp.float32)


def place():
    return lax.axis_index("section"), lax.axis_index("dp"), lax.axis_index("tensor")


def blocks_of(core):
    return (core, 3 - core)


def turn_part(turn):
    return lax.bitwise_xor(lax.axis_index("tensor"), lax.rem(turn, PARTS))


def tile_rows(start, count):
    return pl.ds(pl.multiple_of(start, count), count)


def standard(values):
    centre = values - jnp.mean(values, axis=-1, keepdims=True)
    spread = jnp.mean(centre * centre, axis=-1, keepdims=True)
    inverse = lax.rsqrt(spread + 1e-05)
    return centre * inverse, inverse


def standard_back(grads, gain, units, inverse):
    scaled = grads * gain
    inner = jnp.mean(scaled * units, axis=-1, keepdims=True)
    return inverse * (scaled - jnp.mean(scaled, axis=-1, keepdims=True) - units * inner)


def column_sum(values):
    return jnp.sum(values, axis=0, keepdims=True)


def keep_head(values, parity):
    lane = lax.broadcasted_iota(jnp.int32, values.shape, 1)
    return jnp.where((lane < HEAD) == (parity == 0), values, 0.0)


def side_by_side(weight_ref, pair):
    return jnp.concatenate([weight_ref[pair, kind] for kind in range(3)], axis=1)


def project(x_ref, vec_ref, weight_ref, normed_t_ref, query_ref, kv_ref, normed_ref, between, before_pair, after_pair):
    core = lax.axis_index("section")
    gain, bias = vec_ref[0, 0:1, :], vec_ref[0, 1:2, :]

    def norm_rows(index, carry):
        rows = tile_rows(index * 128, 128)
        units, _ = standard(x_ref[rows, :].astype(jnp.float32))
        normed_ref[rows, :] = (units * gain + bias).astype(jnp.bfloat16)
        return carry

    lax.fori_loop(0, OWN // 128, norm_rows, 0)
    normed_t_ref[...] = normed_ref[...].T
    between()

    def pair_step(turn, carry):
        pair = turn_part(turn)
        before_pair(turn)
        out = dot(normed_ref[...], side_by_side(weight_ref, pair))
        queries = out[:, :128] * 0.125
        for parity in range(2):
            query_ref[pair, parity] = keep_head(queries, parity).astype(jnp.bfloat16)
        for slot, block in enumerate(blocks_of(core)):
            part = out[slot * BLOCK : (slot + 1) * BLOCK, :]
            kv_ref[0, pair, tile_rows(block * BLOCK, BLOCK), :] = part[:, 128:256].astype(jnp.bfloat16)
            kv_ref[1, pair, tile_rows(block * BLOCK, BLOCK), :] = part[:, 256:].astype(jnp.bfloat16)
        after_pair(turn, pair)
        return carry

    lax.fori_loop(0, PAIRS, pair_step, 0)


def task_plan(core):
    first = core == 0
    slots = (0, jnp.where(first, 1, 0), 1, 1, 1)
    keys = (0, jnp.where(first, 0, 1), jnp.where(first, 1, 0), jnp.where(first, 2, 1), jnp.where(first, 3, 2))
    return slots, keys


def attend_rows(signed, query_ref, kv_ref, bias_ref, attended_ref, attended_t_ref, log_ref, logit_ref, factor_ref, stat_ref, before_pair):
    core = lax.axis_index("section")
    slots, keys = task_plan(core)
    middle_late = core == 0
    lane = lax.broadcasted_iota(jnp.int32, (BLOCK, 128), 1)

    def pair_step(turn, carry):
        pair = turn_part(turn)
        before_pair(turn, pair)
        tops = []
        for task in range(TASKS):
            rows = tile_rows(slots[task] * BLOCK, BLOCK)
            key_rows = tile_rows(keys[task] * BLOCK, BLOCK)
            queries = query_ref[pair, :, rows, :].reshape(2 * BLOCK, 128)
            scores = dot(queries, kv_ref[0, pair, key_rows, :], BOTH_LAST)
            if signed:
                raised = scores * scores + 1.0
                inverse = lax.rsqrt(raised)
                factor_ref[task] = scores * inverse
                scores = raised * inverse
            logits = scores + jnp.concatenate([bias_ref[task]] * 2, axis=0)
            logit_ref[task] = logits
            tops.append(jnp.maximum(logits[:, :128], logits[:, 128:]))
        low = jnp.full((2 * BLOCK, 128), NEGATIVE, jnp.float32)
        top_early = jnp.maximum(tops[0], jnp.where(middle_late, low, tops[1]))
        top_late = jnp.maximum(jnp.maximum(tops[2], tops[3]), jnp.maximum(tops[4], jnp.where(middle_late, tops[1], low)))
        max_early = jnp.max(top_early, axis=-1, keepdims=True)
        max_late = jnp.max(top_late, axis=-1, keepdims=True)
        max_middle = jnp.where(middle_late, max_late, max_early)
        shifts = (max_early, max_middle, max_late, max_late, max_late)
        sums, terms = [], []
        for task in range(TASKS):
            key_rows = tile_rows(keys[task] * BLOCK, BLOCK)
            powers = jnp.exp(logit_ref[task] - shifts[task])
            sums.append(powers[:, :128] + powers[:, 128:])
            if signed:
                powers = powers * factor_ref[task]
            terms.append(dot(powers.astype(jnp.bfloat16), kv_ref[1, pair, key_rows, :]))
        early = jnp.where(middle_late, 0.0, 1.0)
        late = 1.0 - early
        totals = (sums[0] + sums[1] * early, sums[2] + sums[3] + sums[4] + sums[1] * late)
        values = (terms[0] + terms[1] * early, terms[2] + terms[3] + terms[4] + terms[1] * late)
        for slot, top in enumerate((max_early, max_late)):
            total = jnp.sum(totals[slot], axis=-1, keepdims=True)
            outs = values[slot] / total
            logs = top + jnp.log(total)
            for parity in range(2):
                stat_ref[slot] = jnp.where(lane == pair * 2 + parity, logs[parity * BLOCK : (parity + 1) * BLOCK], stat_ref[slot])
            merged = jnp.where(lane < HEAD, outs[:BLOCK], outs[BLOCK:])
            attended_ref[pair, slot * BLOCK : (slot + 1) * BLOCK, :] = merged
            attended_t_ref[pair, :, slot * BLOCK : (slot + 1) * BLOCK] = merged.T.astype(jnp.bfloat16)
        return carry

    stat_ref[...] = jnp.zeros_like(stat_ref)
    lax.fori_loop(0, PAIRS, pair_step, 0)
    for slot in range(2):
        log_ref[slot] = stat_ref[slot].T[:8, :]


def gelu_both(values):
    lower = 0.5 * (1.0 + lax.erf(values * math.sqrt(0.5)))
    density = jnp.exp(-0.5 * values * values) * (1.0 / math.sqrt(2.0 * math.pi))
    return values * lower, lower + values * density


def feed(x_ref, attended_ref, vec_ref, out_ref, up_ref, down_ref, hidden_ref, normed_t_ref, act_ref, slope_ref, y_ref, normed_ref, wide_ref, sum_ref, before_out, between, before_chunk, during_chunk):
    out_bias = vec_ref[0, 2:3, :]
    gain, bias = vec_ref[0, 3:4, :], vec_ref[0, 4:5, :]
    down_bias = vec_ref[0, 5:6, :]
    sum_ref[...] = jnp.zeros_like(sum_ref)

    def out_step(turn, carry):
        pair = turn_part(turn)
        before_out(turn)
        sum_ref[...] += dot(attended_ref[pair].astype(jnp.bfloat16), out_ref[pair])
        return carry

    lax.fori_loop(0, PAIRS, out_step, 0)

    def norm_rows(index, carry):
        rows = tile_rows(index * 128, 128)
        hidden = x_ref[rows, :].astype(jnp.float32) + sum_ref[rows, :] + out_bias
        hidden_ref[rows, :] = hidden
        units, _ = standard(hidden)
        normed_ref[rows, :] = (units * gain + bias).astype(jnp.bfloat16)
        sum_ref[rows, :] = hidden + down_bias
        return carry

    lax.fori_loop(0, OWN // 128, norm_rows, 0)
    normed_t_ref[...] = normed_ref[...].T
    between()

    def chunk_step(turn, carry):
        chunk = turn_part(turn)
        before_chunk(turn)
        wide_ref[...] = dot(normed_ref[...], up_ref[chunk])
        up_bias = vec_ref[chunk, 6:7, :]

        def gelu_rows(index, inner):
            rows = tile_rows(index * 32, 32)
            act, slope = gelu_both(wide_ref[rows, :] + up_bias)
            act_ref[chunk, rows, :] = act.astype(jnp.bfloat16)
            slope_ref[chunk, rows, :] = slope.astype(jnp.bfloat16)
            return inner

        lax.fori_loop(0, OWN // 32, gelu_rows, 0)
        during_chunk(turn)
        sum_ref[...] += dot(act_ref[chunk], down_ref[chunk])
        return carry

    lax.fori_loop(0, PARTS, chunk_step, 0)
    y_ref[...] = sum_ref[...].astype(jnp.bfloat16)


def feed_back(dy_ref, act_ref, slope_ref, down_ref, up_ref, hidden_ref, normed_t_ref, vec_ref, out_ref, attended_ref, attended_t_ref, grad_hidden_ref, grad_att_ref, centre_ref, grads_ref, vec_grad_ref, low_ref, low_t_ref, chunk_ref, sum_ref, during_chunk, after_chunk, before_norm, between):
    low_ref[...] = dy_ref[...].astype(jnp.bfloat16)
    low_t_ref[...] = low_ref[...].T
    vec_grad_ref[...] = jnp.zeros_like(vec_grad_ref)
    sum_ref[...] = jnp.zeros_like(sum_ref)

    def chunk_step(turn, carry):
        chunk = turn_part(turn + 1)
        grad_act = dot(low_ref[...], down_ref[chunk], BOTH_LAST)
        grad_up = (grad_act * slope_ref[chunk].astype(jnp.float32)).astype(jnp.bfloat16)
        chunk_ref[...] = grad_up
        vec_grad_ref[pl.ds(6 + chunk, 1), :] = column_sum(grad_up.astype(jnp.float32))
        down_term = dot(low_t_ref[...], act_ref[chunk]).astype(jnp.bfloat16)
        up_term = dot(normed_t_ref[...], chunk_ref[...]).astype(jnp.bfloat16)
        for part in range(PARTS):
            grads_ref[part, chunk, :, 0:512] = down_term[part * 128 : (part + 1) * 128, :]
            grads_ref[part, chunk, :, 512:1024] = up_term[part * 128 : (part + 1) * 128, :]
        after_chunk(turn, chunk)
        sum_ref[...] += dot(chunk_ref[...], up_ref[chunk], BOTH_LAST)
        during_chunk(turn)
        return carry

    lax.fori_loop(0, PARTS, chunk_step, 0)
    before_norm()
    gain = vec_ref[0, 3:4, :]

    def norm_rows(index, carry):
        rows = tile_rows(index * 128, 128)
        grads, dy = sum_ref[rows, :], dy_ref[rows, :]
        units, inverse = standard(hidden_ref[rows, :])
        grad_hidden = dy + standard_back(grads, gain, units, inverse)
        grad_hidden_ref[rows, :] = grad_hidden
        low_ref[rows, :] = grad_hidden.astype(jnp.bfloat16)
        vec_grad_ref[2:3, :] += column_sum(grad_hidden)
        vec_grad_ref[3:4, :] += column_sum(grads * units)
        vec_grad_ref[4:5, :] += column_sum(grads)
        vec_grad_ref[5:6, :] += column_sum(dy)
        return carry

    lax.fori_loop(0, OWN // 128, norm_rows, 0)
    between()
    row = lax.broadcasted_iota(jnp.int32, (8, 128), 0)
    lane = lax.broadcasted_iota(jnp.int32, (8, 128), 1)
    picks = jnp.where((row < 2) & ((lane < HEAD) == (row == 0)), 1.0, 0.0).astype(jnp.bfloat16)

    def pair_step(pair, carry):
        out_term = dot(attended_t_ref[pair], low_ref[...]).astype(jnp.bfloat16)
        for part in range(PARTS):
            grads_ref[part, pair, :, 1024:1152] = out_term[:, part * 128 : (part + 1) * 128]
        grad_att = dot(low_ref[...], out_ref[pair], BOTH_LAST).astype(jnp.bfloat16)
        wide = grad_att.astype(jnp.float32)
        for parity in range(2):
            grad_att_ref[pair, parity] = keep_head(wide, parity).astype(jnp.bfloat16)
        products = wide * attended_ref[pair]
        upper = products.astype(jnp.bfloat16)
        lower = (products - upper.astype(jnp.float32)).astype(jnp.bfloat16)
        centre_ref[pair] = dot(picks, upper, BOTH_LAST) + dot(picks, lower, BOTH_LAST)
        return carry

    lax.fori_loop(0, PAIRS, pair_step, 0)


def attend_rows_back(signed, query_ref, kv_ref, grad_att_ref, bias_ref, log_ref, centre_ref, grad_query_ref, grad_kv_ref, send_ref, before_pair, after_pair):
    core = lax.axis_index("section")
    slots, keys = task_plan(core)
    early = jnp.where(core == 0, 0.0, 1.0)
    lane = lax.broadcasted_iota(jnp.int32, (BLOCK, 128), 1)

    def pair_step(turn, carry):
        pair = turn_part(turn + 1)
        held = lax.rem(turn, 2)
        before_pair(turn)
        grad_kv_ref[held] = jnp.zeros(grad_kv_ref.shape[1:], jnp.float32)
        merged = []
        for task in range(TASKS):
            rows = tile_rows(slots[task] * BLOCK, BLOCK)
            key_rows = tile_rows(keys[task] * BLOCK, BLOCK)
            key_part, value_part = kv_ref[0, pair, key_rows, :], kv_ref[1, pair, key_rows, :]
            queries = query_ref[pair, :, rows, :].reshape(2 * BLOCK, 128)
            grad_att = grad_att_ref[pair, :, rows, :].reshape(2 * BLOCK, 128)
            scores = dot(key_part, queries, BOTH_LAST)
            grad_weights = dot(value_part, grad_att, BOTH_LAST)
            log_row = jnp.concatenate([log_ref[slots[task], pl.ds(pair * 2 + parity, 1), :] for parity in range(2)], axis=1)
            centre = jnp.concatenate([centre_ref[pair, parity : parity + 1, rows] for parity in range(2)], axis=1)
            bias = jnp.concatenate([bias_ref[task]] * 2, axis=1)
            if signed:
                raised = scores * scores + 1.0
                inverse = lax.rsqrt(raised)
                factor = scores * inverse
                probs = jnp.exp(raised * inverse + bias - log_row)
                weights = factor * probs
                grad_scores = weights * (factor * grad_weights - centre)
                grad_scores = grad_scores + probs * grad_weights * (inverse * inverse * inverse)
            else:
                weights = jnp.exp(scores + bias - log_row)
                grad_scores = weights * (grad_weights - centre)
            grad_low = grad_scores.astype(jnp.bfloat16)
            grad_kv_ref[held, 0, key_rows, :] += dot(grad_low, queries)
            grad_kv_ref[held, 1, key_rows, :] += dot(weights.astype(jnp.bfloat16), grad_att)
            grad_query = dot(grad_low, key_part, BOTH_FIRST)
            merged.append(jnp.where(lane < HEAD, grad_query[:BLOCK], grad_query[BLOCK:]))
        grad_query_ref[pair, :BLOCK, :] = ((merged[0] + merged[1] * early) * 0.125).astype(jnp.bfloat16)
        grad_query_ref[pair, BLOCK:, :] = ((merged[1] * (1.0 - early) + merged[2] + merged[3] + merged[4]) * 0.125).astype(jnp.bfloat16)
        for slot, block in enumerate(blocks_of(1 - core)):
            for kind in range(2):
                rows = grad_kv_ref[held, kind, tile_rows(block * BLOCK, BLOCK), :]
                send_ref[kind, pair, slot * BLOCK : (slot + 1) * BLOCK, :] = rows.astype(jnp.bfloat16)
        after_pair(turn, pair)
        return carry

    lax.fori_loop(0, PAIRS, pair_step, 0)


def project_back_pair(pair, held, grad_query_ref, grad_kv_ref, other_ref, normed_t_ref, weight_ref, grads_ref, sum_ref, send):
    parts = [grad_query_ref[pair]]
    for kind in range(2):
        halves = []
        for slot, block in enumerate(blocks_of(lax.axis_index("section"))):
            own = grad_kv_ref[held, kind, tile_rows(block * BLOCK, BLOCK), :]
            halves.append(own + other_ref[kind, pair, slot * BLOCK : (slot + 1) * BLOCK, :].astype(jnp.float32))
        parts.append(jnp.concatenate(halves, axis=0).astype(jnp.bfloat16))
    grads = jnp.concatenate(parts, axis=1)
    term = dot(normed_t_ref[...], grads).astype(jnp.bfloat16)
    for part in range(PARTS):
        grads_ref[part, pair, :, 1152:1536] = term[part * 128 : (part + 1) * 128, :]
    send()
    sum_ref[...] += dot(grads, side_by_side(weight_ref, pair), BOTH_LAST)


def project_back_norm(x_ref, grad_hidden_ref, vec_ref, grad_x_ref, grad_x_low_ref, vec_grad_ref, sum_ref):
    gain = vec_ref[0, 0:1, :]

    def norm_rows(index, carry):
        rows = tile_rows(index * 128, 128)
        grads = sum_ref[rows, :]
        units, inverse = standard(x_ref[rows, :].astype(jnp.float32))
        grad_x = grad_hidden_ref[rows, :] + standard_back(grads, gain, units, inverse)
        grad_x_ref[rows, :] = grad_x
        grad_x_low_ref[rows, :] = grad_x.astype(jnp.bfloat16)
        vec_grad_ref[0:1, :] += column_sum(grads * units)
        vec_grad_ref[1:2, :] += column_sum(grads)
        return carry

    lax.fori_loop(0, OWN // 128, norm_rows, 0)


def greet(partners):
    barrier = pltpu.get_barrier_semaphore()
    for partner in partners:
        pl.semaphore_signal(barrier, inc=1, device_id=partner, device_id_type=MESH)
    pl.semaphore_wait(barrier, len(partners))


def along_tensor(step):
    core, rep, part = place()
    return (core, rep, lax.bitwise_xor(part, step))


def along_dp(step):
    core, rep, part = place()
    return (core, lax.bitwise_xor(rep, step), part)


def sibling():
    core, rep, part = place()
    return (1 - core, rep, part)


def all_partners():
    return [along_tensor(step) for step in (1, 2, 3)] + [along_dp(step) for step in (1, 2, 3)] + [sibling()]


def remote(source, target, send, receive, device):
    return pltpu.make_async_remote_copy(src_ref=source, dst_ref=target, send_sem=send, recv_sem=receive, device_id=device, device_id_type=MESH)


def fill_masks(lens_ref, bias_ref, turned):
    core, rep, part = place()
    slots, keys = task_plan(core)
    bounds, bound = [], 0
    for index in range(lens_ref.shape[1]):
        bound = bound + lens_ref[part, index]
        bounds.append(bound)
    for task in range(TASKS):
        block = jnp.where(slots[task] == 0, core, 3 - core)
        shape = (1, BLOCK) if turned else (BLOCK, 1)
        query = block * BLOCK + lax.broadcasted_iota(jnp.int32, shape, 1 if turned else 0)
        start = jnp.zeros(shape, jnp.int32)
        for bound in bounds:
            start = jnp.where(query >= bound, bound, start)
        key = keys[task] * BLOCK + lax.broadcasted_iota(jnp.int32, (BLOCK, BLOCK), 0 if turned else 1)
        bias_ref[task] = jnp.where((key >= start) & (key <= query), 0.0, NEGATIVE)


def rows_view(array, rows, index):
    return array.at[:, rows] if index == QKV else array.at[rows]


def quarter_rows(array, which):
    count = array.shape[-2] // PARTS
    return tile_rows(which * count, count)


SAVED = (
    ((OWN, WIDTH), jnp.bfloat16),
    ((WIDTH, OWN), jnp.bfloat16),
    ((PAIRS, 2, OWN, 128), jnp.bfloat16),
    ((2, PAIRS, 1024, 128), jnp.bfloat16),
    ((PAIRS, OWN, 128), jnp.float32),
    ((PAIRS, 128, OWN), jnp.bfloat16),
    ((2, 8, BLOCK), jnp.float32),
    ((OWN, WIDTH), jnp.float32),
    ((WIDTH, OWN), jnp.bfloat16),
    ((PARTS, OWN, 512), jnp.bfloat16),
    ((PARTS, OWN, 512), jnp.bfloat16),
)
WEIGHTS = (
    ((PARTS, 3, 512, 128), jnp.bfloat16),
    ((PARTS, 128, 512), jnp.bfloat16),
    ((PARTS, 512, 512), jnp.bfloat16),
    ((PARTS, 512, 512), jnp.bfloat16),
    ((PARTS, 8, 512), jnp.float32),
)
QKV, OUT, UP, DOWN, VEC = range(5)


ALL = (1, 2, 3)
DIRECT = ((0, QKV),)
FORWARD_PLAN = (
    ("masks", None, 0, "near", ALL, (QKV,)),
    ("masks", None, 0, "own", None, (QKV, OUT, UP, DOWN)),
    ("vec", None, 0, "z", (1, 2), (OUT, UP, DOWN)),
    ("rows", None, 0, "z", (3,), (OUT, UP, DOWN)),
    ("norm0", None, 0, "sib", ALL, (QKV,)),
    ("norm0", None, 1, "own", None, (QKV, OUT, UP, DOWN)),
    ("project0", 0, 0, "near", (1,), (OUT, UP, DOWN)),
    ("project0", 2, 0, "near", (2,), (OUT, UP, DOWN)),
    ("attend0", 0, 0, "far", (1,), (OUT, UP, DOWN)),
    ("attend0", 1, 0, "near", (3,), (OUT, UP, DOWN)),
    ("attend0", 1, 0, "far", (2,), (OUT, UP, DOWN)),
    ("attend0", 2, 1, "z", ALL, (QKV,)),
    ("attend0", 2, 0, "sib", (1,), (OUT, UP, DOWN)),
    ("attend0", 3, 0, "far", (3,), (OUT, UP, DOWN)),
    ("attend0", 3, 0, "sib", (2,), (OUT, UP, DOWN)),
    ("attended0", None, 1, "z", (1, 2), (OUT, UP, DOWN)),
    ("second0", None, 1, "near", ALL, (QKV,)),
    ("attended0", None, 0, "sib", (3,), (OUT, UP, DOWN)),
    ("chunk0", 0, 1, "z", (3,), (OUT, UP, DOWN)),
    ("chunk0", 2, 1, "near", (1,), (OUT, UP, DOWN)),
    ("chunk0", 3, 1, "near", (2,), (OUT, UP, DOWN)),
    ("chunk0", 2, 1, "far", ALL, (QKV,)),
    ("chunk0", 2, None, "rows", None, ()),
    ("chunk0", 3, 1, "sib", ALL, (QKV,)),
    ("project1", 1, 1, "near", (3,), (OUT, UP, DOWN)),
    ("project1", 2, 1, "far", (1,), (OUT, UP, DOWN)),
    ("attend1", 0, 1, "far", (2,), (OUT, UP, DOWN)),
    ("attend1", 1, 1, "sib", (1,), (OUT, UP, DOWN)),
    ("attend1", 2, 1, "far", (3,), (OUT, UP, DOWN)),
    ("attend1", 3, 1, "sib", (2,), (OUT, UP, DOWN)),
    ("attended1", None, 1, "sib", (3,), (OUT, UP, DOWN)),
)


def forward_kernel(lens_ref, tokens, cotangent, *refs):
    shards, vectors, refs = refs[:4], refs[4:11], refs[11:]
    dy_out, y_out, saved_out, weights_out, refs = refs[0], refs[1], refs[2:13], refs[13:18], refs[18:]
    saved, weights, refs = refs[:11], refs[11:16], refs[16:]
    y_ref, bias_ref, normed, logit, factor, stat, wide, total, vec_own, refs = *refs[:9], refs[9:]
    row_send, row_recv, row_local, z_send, z_recv, xy_send, xy_recv, sib_send, sib_recv, local, kv_send, kv_recv, save_sem, keep_sem, pass_send, chunk_sem = refs
    core, rep, part = place()
    shards = (*shards, vec_own)
    vec_own[...] = jnp.zeros_like(vec_own)
    for row, vector in enumerate(vectors):
        vec_own[row : row + 1, :] = vector[...]
    greet(all_partners())

    steps = (1, 2, 3)

    def z_copy(index, step):
        slot = (index, step - 1)
        if index == VEC:
            return remote(shards[index], weights[index].at[core, part], z_send.at[slot], z_recv.at[slot], along_tensor(step))
        rows = quarter_rows(shards[index], rep)
        return remote(rows_view(shards[index], rows, index), rows_view(weights[index].at[core, part], rows, index), z_send.at[slot], z_recv.at[slot], along_tensor(step))

    def ends():
        return (part == 0) | (part == 3)

    def pass_copy(index):
        view = rows_view(weights[index].at[core, turn_part(2)], quarter_rows(shards[index], rep), index)
        return remote(view, view, pass_send.at[index], z_recv.at[index, 2], along_tensor(1))

    def own_copy(index):
        return pltpu.make_async_copy(shards[index], weights[index].at[core, part], local.at[index])

    def near_copy(index, step, far):
        slot = (index, far - 1, step - 1)
        view = rows_view(weights[index].at[core, turn_part(far)], quarter_rows(shards[index], rep), index)
        return remote(view, view, xy_send.at[slot], xy_recv.at[slot], along_dp(step))

    def far_copy(index, step, far):
        slot = (index, far - 1, step + 1)
        count = shards[index].shape[-2] // PARTS
        rows = tile_rows(lax.bitwise_xor(rep, 3 - step) * count + (2 - step) * (count // 2), count // 2)
        view = rows_view(weights[index].at[core, turn_part(far)], rows, index)
        return remote(view, view, xy_send.at[slot], xy_recv.at[slot], along_dp(step))

    def across_copy(index, far):
        slot = (index, far - 1, 2)
        view = rows_view(weights[index].at[core, turn_part(far)], quarter_rows(shards[index], rep), index)
        return remote(view, view, xy_send.at[slot], xy_recv.at[slot], along_dp(3))

    def sib_copy(index, far):
        target = weights[index].at[core, turn_part(far)]
        source = target if far else shards[index]
        return remote(source, target, sib_send.at[index, far], sib_recv.at[index, far], sibling())

    def vec_copy():
        view = weights[VEC].at[core]
        return remote(view, view, sib_send.at[VEC, 0], sib_recv.at[VEC, 0], sibling())

    def own_start(*which):
        for index in which:
            own_copy(index).start()
            sib_copy(index, 0).start()

    def z_start(far, *which):
        for index in which:
            if far < 3 or index == VEC:
                z_copy(index, far).start()
            else:
                pl.when(jnp.logical_not(ends()))(z_copy(index, far).start)

    def near_start(far, *which):
        for index in which:
            z_copy(index, far).wait_recv()
            if far == 2:
                pl.when(jnp.logical_not(ends()))(pass_copy(index).start)
            for step in (1, 2):
                near_copy(index, step, far).start()
            for layer in range(2):
                if (layer, index) in DIRECT:
                    pl.when(core == layer)(across_copy(index, far).start)

    def far_start(far, *which):
        for index in which:
            for step in (2, 1):
                near_copy(index, 3 - step, far).wait_recv()
                far_copy(index, step, far).start()

    def sib_direct(far, *which):
        for index in which:
            for step in (1, 2):
                near_copy(index, step, far).wait_recv()
            across_copy(index, far).wait_recv()
            sib_copy(index, far).start()

    def sib_passed(far, *which):
        for index in which:
            for step in (1, 2):
                far_copy(index, step, far).wait_recv()
            sib_copy(index, far).start()

    def sib_start(far, *which):
        for layer in range(2):
            pl.when(core == layer)(partial(sib_direct, far, *[index for index in which if (layer, index) in DIRECT]))
            pl.when(core == layer)(partial(sib_passed, far, *[index for index in which if (layer, index) not in DIRECT]))

    def need(layer, far, *which):
        @pl.when(core != layer)
        def _():
            for index in which:
                sib_copy(index, far).wait_recv()

        if far == 0:

            @pl.when(core == layer)
            def _():
                for index in which:
                    own_copy(index).wait()

    def need_turn(layer, turn, *which):
        for far in range(PARTS):
            pl.when(turn == far)(partial(need, layer, far, *which))

    def keep_copy(layer, index):
        return pltpu.make_async_copy(weights[index].at[layer], weights_out[index].at[layer], keep_sem.at[layer, index])

    def keep(layer, *which):
        for index in which:
            keep_copy(layer, index).start()

    def on(layer, action, *which):
        pl.when(core == layer)(partial(action, *which))

    def at(layer, turn, when, action, *which):
        pl.when((core == layer) & (turn == when))(partial(action, *which))

    owner = jnp.where((part == 0) | (part == 3), 0, 1)
    place_here = jnp.where(part < 2, 0, 1)
    row_pairs = ((tokens, saved[0].at[0]), (cotangent, dy_out))

    def row_targets(array, batch):
        source, target = row_pairs[array]
        rows = target.at[tile_rows(place_here * BLOCK, BLOCK)]
        there = remote(source.at[batch], rows, row_send.at[array, batch], row_recv.at[array, place_here], (core, rep, batch))
        here = pltpu.make_async_copy(source.at[batch], rows, row_local.at[array])
        return there, here

    def rows_each(array, act):
        for batch in range(PARTS):
            there, here = row_targets(array, batch)

            @pl.when((core == owner) & (part != batch))
            def _():
                there.start() if act == "start" else there.wait_send()

            @pl.when((core == owner) & (part == batch))
            def _():
                here.start() if act == "start" else here.wait()

    def rows_arrived(array):
        for slot, block in enumerate(blocks_of(core)):

            @pl.when(block != part)
            def _():
                source, target = row_pairs[array]
                rows = target.at[slot * BLOCK : (slot + 1) * BLOCK]
                remote(source.at[0], rows, row_send.at[array, 0], row_recv.at[array, slot], sibling()).wait_recv()

    def save(layer, *which):
        for index in which:
            pltpu.make_async_copy(saved[index].at[layer], saved_out[index].at[layer], save_sem.at[layer, index]).start()

    def chunk_copies(layer, turn):
        chunk = turn_part(turn)
        return [
            pltpu.make_async_copy(saved[index].at[layer, chunk], saved_out[index].at[layer, chunk], chunk_sem.at[layer, index - 9, turn])
            for index in (9, 10)
        ]

    def kv_copies(layer, pair, receiving):
        copies = []
        for slot, block in enumerate(blocks_of(1 - core if receiving else core)):
            view = saved[3].at[layer, :, pair, tile_rows(block * BLOCK, BLOCK), :]
            copies.append(remote(view, view, kv_send.at[layer, pair, slot], kv_recv.at[layer, pair, slot], sibling()))
        return copies

    actions = {"own": own_start, "z": z_start, "near": near_start, "far": far_start, "sib": sib_start}

    def run(point, turn=None):
        for where, when, owner_core, name, fars, which in FORWARD_PLAN:
            if where != point:
                continue

            def act():
                if name == "own":
                    own_start(*which)
                elif name == "rows":
                    rows_each(1, "start")
                else:
                    for far in fars:
                        actions[name](far, *[index for index in which if name != "far" or (owner_core, index) not in DIRECT])

            here = core == owner_core if owner_core is not None else None
            if turn is not None:
                here = turn == when if here is None else here & (turn == when)
            act() if here is None else pl.when(here)(act)

    for far in steps:
        on(0, z_start, far, QKV)
        z_start(far, VEC)
    own_copy(VEC).start()
    rows_each(0, "start")
    fill_masks(lens_ref, bias_ref, False)
    run("masks")
    own_copy(VEC).wait()
    for step in steps:
        z_copy(VEC, step).wait_recv()
    vec_copy().start()
    run("vec")
    rows_each(0, "wait")
    rows_arrived(0)
    vec_copy().wait_recv()
    run("rows")
    for layer in range(2):
        signed = layer == 0
        held = [item.at[layer] for item in saved]
        qkv, out, up, down, vec = [item.at[layer] for item in weights]
        x_ref, normed_one_t, queries, kv, attended, attended_t, logs, hidden, normed_two_t, act, slope = held

        def after_norm():
            run(f"norm{layer}")

        def before_project(turn):
            run(f"project{layer}", turn)
            need_turn(layer, turn, QKV)

        def push_kv(turn, pair):
            for copy in kv_copies(layer, pair, False):
                copy.start()

        def before_attend(turn, pair):
            run(f"attend{layer}", turn)
            for copy in kv_copies(layer, pair, True):
                copy.wait_recv()

        def before_out(turn):
            need_turn(layer, turn, OUT)

        def before_feed():
            save(layer, 7, 8)
            run(f"second{layer}")

        def before_chunk(turn):
            need_turn(layer, turn, UP, DOWN)
            if layer == 1:
                pl.when(turn == PARTS - 1)(partial(keep, 1, OUT, UP, DOWN))

        def during_chunk(turn):
            for copy in chunk_copies(layer, turn):
                copy.start()
            run(f"chunk{layer}", turn)

        project(x_ref, vec, qkv, normed_one_t, queries, kv, normed, after_norm, before_project, push_kv)
        save(layer, 0, 1, 2)
        keep(layer, QKV, VEC)
        attend_rows(signed, queries, kv, bias_ref, attended, attended_t, logs, logit, factor, stat, before_attend)
        save(layer, 3, 4, 5, 6)
        run(f"attended{layer}")
        target = saved[0].at[1] if layer == 0 else y_ref
        feed(x_ref, attended, vec, out, up, down, hidden, normed_two_t, act, slope, target, normed, wide, total, before_out, before_feed, before_chunk, during_chunk)
        if layer == 0:
            keep(0, OUT, UP, DOWN)
    y_copy = pltpu.make_async_copy(y_ref, y_out, row_local.at[0])
    y_copy.start()
    rows_each(1, "wait")
    rows_arrived(1)
    for index in range(5):
        for step in steps:
            if step < 3 or index == VEC:
                z_copy(index, step).wait_send()
            else:
                pl.when(jnp.logical_not(ends()))(z_copy(index, step).wait_send)
                pl.when(jnp.logical_not(ends()))(pass_copy(index).wait_send)
            if index != VEC:
                for way in (1, 2):
                    near_copy(index, way, step).wait_send()
                    for layer in range(2):
                        if (layer, index) not in DIRECT:
                            pl.when(core == layer)(far_copy(index, way, step).wait_send)
                for layer in range(2):
                    if (layer, index) in DIRECT:
                        pl.when(core == layer)(across_copy(index, step).wait_send)
                sib_copy(index, step).wait_send()
        sib_copy(index, 0).wait_send() if index != VEC else vec_copy().wait_send()
    for layer in range(2):
        for pair in range(PAIRS):
            for copy in kv_copies(layer, pair, False):
                copy.wait_send()
        for index in range(9):
            pltpu.make_async_copy(saved[index].at[layer], saved_out[index].at[layer], save_sem.at[layer, index]).wait()
        for turn in range(PARTS):
            for copy in chunk_copies(layer, turn):
                copy.wait()
    y_copy.wait()
    for layer in range(2):
        for index in range(5):
            keep_copy(layer, index).wait()


FEED, ATTEND = 0, 1
GROUPS = ((0, 1024), (1024, 1536))


def backward_kernel(lens_ref, dy_in, y_in, *refs):
    saved_in, weights_in, refs = refs[:11], refs[11:16], refs[16:]
    down_out, up_out, out_out, qkv_out, vec_out, bias_out, blocks_out, rows_out, refs = *refs[:8], refs[8:]
    held, weights, refs = refs[:11], refs[11:16], refs[16:]
    dy_low, dy_ref, bias_ref, grads_ref, vec_grad, low, low_t, chunk, total, grad_hidden, grad_att, centres, grad_query, grad_kv, kv_out, kv_got, grad_low, refs = *refs[:17], refs[17:]
    got_core, got_first, got_second, part_sum, got_part, final, vec_core, vec_chip, vec_dp, vec_rep, vec_part, grads_out, vec_total, refs = *refs[:13], refs[13:]
    load_sem, weight_sem, dy_sem, y_send, y_recv, row_send, row_recv, kv_send, kv_recv, core_send, core_recv, first_send, first_recv, second_send, second_recv, part_send, part_recv, vec_send, vec_recv, last_send, last_recv = refs
    core, rep, part = place()
    steps = (1, 2, 3)
    mine, theirs = tile_rows(core * 64, 64), tile_rows((1 - core) * 64, 64)

    def load(layer, which=(), matrices=()):
        copies = [pltpu.make_async_copy(saved_in[index].at[layer], held[index], load_sem.at[index]) for index in which]
        return copies + [pltpu.make_async_copy(weights_in[index].at[layer], weights[index], weight_sem.at[index]) for index in matrices]

    def start(copies):
        for copy in copies:
            copy.start()

    def wait(copies):
        for copy in copies:
            copy.wait()

    chunk_set = ((10, 9, 8), (DOWN, UP))
    norm_set = ((7, 5, 4), (VEC, OUT))
    attend_set = ((2, 3, 6), ())
    project_set = ((0, 1), (QKV,))
    dy_copy = pltpu.make_async_copy(dy_in, dy_low, dy_sem.at[0])
    dy_copy.start()
    for group in (chunk_set, norm_set, attend_set, project_set):
        start(load(1, *group))
    greet(all_partners() + [(1 - core, rep, lax.bitwise_xor(part, step)) for step in steps])

    owner = jnp.where((part == 0) | (part == 3), 0, 1)

    def deliver(source, layer, target, send, receive, act):
        for slot, block in enumerate(blocks_of(core)):
            rows = source.at[slot * BLOCK : (slot + 1) * BLOCK]
            stays = (core == layer) & (block == part)

            @pl.when(stays)
            def _():
                copy = pltpu.make_async_copy(rows, target.at[part], send.at[layer, slot])
                copy.start() if act == "start" else copy.wait()

            @pl.when(jnp.logical_not(stays))
            def _():
                copy = remote(rows, target.at[part], send.at[layer, slot], receive.at[part], (layer, rep, block))
                copy.start() if act == "start" else copy.wait_send()

    def delivered(target, source, send, receive):
        for batch in range(PARTS):

            @pl.when((core != owner) | (part != batch))
            def _():
                remote(source.at[:BLOCK], target.at[batch], send.at[0, 0], receive.at[batch], sibling()).wait_recv()

    deliver(saved_in[0].at[1], 0, blocks_out, y_send, y_recv, "start")
    deliver(y_in, 1, blocks_out, y_send, y_recv, "start")

    def core_copy(layer, group, turn):
        first, last = GROUPS[group]
        other, slot = turn_part(turn + 1), (layer, group, turn)
        return remote(grads_ref.at[:, other, theirs, first:last], got_core.at[layer, :, other, :, first:last], core_send.at[slot], core_recv.at[slot], sibling())

    def halves(way):
        return pl.ds(0, 32) if way == 1 else pl.ds(32, 32)

    def first_copy(layer, group, turn, way, piece):
        first, last = GROUPS[group]
        other, slot = turn_part(turn + 1), (layer, group, turn, way - 1, piece)
        source = got_core.at[layer, lax.bitwise_xor(rep, 3 if piece else way), other, halves(way), first:last]
        return remote(source, got_first.at[layer, way - 1, piece, other, :, first:last], first_send.at[slot], first_recv.at[slot], along_dp(way))

    def second_copy(layer, group, turn, way):
        first, last = GROUPS[group]
        other, slot = turn_part(turn + 1), (layer, group, turn, way - 1)
        source = got_core.at[layer, lax.bitwise_xor(rep, 3 - way), other, halves(way), first:last]
        return remote(source, got_second.at[layer, way - 1, other, :, first:last], second_send.at[slot], second_recv.at[slot], along_dp(3 - way))

    def part_copy(layer, group, turn):
        first, last = GROUPS[group]
        slot = (layer, group, turn)
        return remote(part_sum.at[layer, turn, :, first:last], got_part.at[layer, turn, :, first:last], part_send.at[slot], part_recv.at[slot], along_tensor(turn + 1))

    def dp_start(layer, group, turn):
        first, last = GROUPS[group]
        core_copy(layer, group, turn).wait()
        other = turn_part(turn + 1)

        def add(major, carry):
            own = grads_ref[major, other, mine, first:last]
            got_core[layer, major, other, :, first:last] = own + got_core[layer, major, other, :, first:last]
            return carry

        lax.fori_loop(0, PARTS, add, 0)
        start(first_copy(layer, group, turn, way, piece) for way in (1, 2) for piece in range(2))

    def dp_next(layer, group, turn):
        first, last = GROUPS[group]
        other = turn_part(turn + 1)
        for way in (1, 2):
            for piece in (1, 0):
                first_copy(layer, group, turn, way, piece).wait()
                major = lax.bitwise_xor(rep, 3 - way) if piece else rep
                own = got_core[layer, major, other, halves(way), first:last]
                got_core[layer, major, other, halves(way), first:last] = own + got_first[layer, way - 1, piece, other, :, first:last]
                if piece:
                    second_copy(layer, group, turn, way).start()

    def part_start(layer, group, turn):
        first, last = GROUPS[group]
        other = turn_part(turn + 1)
        for way in (1, 2):
            second_copy(layer, group, turn, way).wait()
            own = got_core[layer, rep, other, halves(way), first:last]
            part_sum[layer, turn, halves(way), first:last] = own + got_second[layer, way - 1, other, :, first:last]
        if turn < PARTS - 1:
            part_copy(layer, group, turn).start()

    def finish(layer, group):
        first, last = GROUPS[group]
        sum_here = part_sum[layer, PARTS - 1, :, first:last].astype(jnp.float32)
        for turn in range(PARTS - 1):
            part_copy(layer, group, turn).wait()
            sum_here = sum_here + got_part[layer, turn, :, first:last].astype(jnp.float32)
        final[layer, :, first:last] = sum_here

    def last_copy(layer):
        return remote(final.at[layer], grads_out.at[mine], last_send.at[0], last_recv.at[0], sibling())

    def hand_over(layer):
        @pl.when(core == layer)
        def _():
            grads_out[mine, :] = final[layer]

        @pl.when(core != layer)
        def _():
            last_copy(layer).start()

    def kv_copy(layer, pair):
        return remote(kv_out.at[:, pair], kv_got.at[layer, :, pair], kv_send.at[layer, pair], kv_recv.at[layer, pair], sibling())

    fill_masks(lens_ref, bias_ref, True)
    for layer in (1, 0):
        signed = layer == 0
        x_ref, normed_one_t, queries, kv, attended, attended_t, logs, hidden, normed_two_t, act, slope = held
        qkv, out, up, down, vec = weights
        if layer == 1:
            dy_copy.wait()
            dy_ref[...] = dy_low[...].astype(jnp.float32)
        wait(load(layer, *chunk_set))

        def at(turn, when, action, *which):
            pl.when(turn == when)(partial(action, *which))

        def during_chunk(turn):
            pl.when(turn > 0)(lambda: dp_start(layer, FEED, turn - 1))
            if layer == 0:
                at(turn, 0, dp_next, 1, ATTEND, 1)
                at(turn, 0, dp_next, 1, ATTEND, 2)
                at(turn, 1, dp_next, 1, ATTEND, 3)
                at(turn, 1, part_start, 1, ATTEND, 0)
                at(turn, 2, part_start, 1, ATTEND, 1)
                at(turn, 2, part_start, 1, ATTEND, 2)
                at(turn, 3, part_start, 1, ATTEND, 3)

        def after_chunk(turn, chunk):
            core_copy(layer, FEED, turn).start()

        def before_norm():
            wait(load(layer, *norm_set))

        def after_norm():
            dp_start(layer, FEED, 3)

        feed_back(dy_ref, act, slope, down, up, hidden, normed_two_t, vec, out, attended, attended_t, grad_hidden, grad_att, centres, grads_ref, vec_grad.at[layer], low, low_t, chunk, total, during_chunk, after_chunk, before_norm, after_norm)
        if layer == 1:
            start(load(0, (9, 10, 7, 8, 4, 5), (DOWN, UP, OUT)))
        wait(load(layer, *attend_set))

        def before_attend(turn):
            for index in range(4):
                at(turn, index, dp_next, layer, FEED, index)
            at(turn, 2, part_start, layer, FEED, 0)
            at(turn, 3, part_start, layer, FEED, 1)
            if layer == 0:
                at(turn, 3, finish, 1, FEED)
                at(turn, 3, finish, 1, ATTEND)
                at(turn, 3, hand_over, 1)

        def project_turn(turn):
            pair = turn_part(turn + 1)
            kv_copy(layer, pair).wait()
            project_back_pair(pair, lax.rem(turn, 2), grad_query, grad_kv, kv_got.at[layer], normed_one_t, qkv, grads_ref, total, core_copy(layer, ATTEND, turn).start)

        def after_attend(turn, pair):
            kv_copy(layer, pair).start()
            at(turn, 2, dp_start, layer, ATTEND, 0)
            at(turn, 3, dp_start, layer, ATTEND, 1)
            at(turn, 3, dp_next, layer, ATTEND, 0)
            pl.when(turn > 0)(lambda: project_turn(turn - 1))

        wait(load(layer, *project_set))
        total[...] = jnp.zeros_like(total)
        attend_rows_back(signed, queries, kv, grad_att, bias_ref, logs, centres, grad_query, grad_kv, kv_out, before_attend, after_attend)
        if layer == 1:
            start(load(0, *attend_set))
        dp_start(layer, ATTEND, 2)
        part_start(layer, FEED, 2)
        project_turn(PAIRS - 1)
        part_start(layer, FEED, 3)
        project_back_norm(x_ref, grad_hidden, vec, dy_ref, grad_low.at[layer], vec_grad.at[layer], total)
        if layer == 1:
            start(load(0, (0, 1), (QKV, VEC)))
        deliver(grad_low.at[layer], layer, rows_out, row_send, row_recv, "start")
        dp_start(layer, ATTEND, 3)
    vec_copy = remote(vec_grad.at[1 - core], vec_core, vec_send.at[0], vec_recv.at[0], sibling())
    vec_copy.start()
    dp_next(0, ATTEND, 1)
    dp_next(0, ATTEND, 2)
    finish(0, FEED)
    vec_copy.wait()
    vec_chip[...] = vec_grad[core] + vec_core[...]
    vec_copies = [remote(vec_chip, vec_dp.at[step - 1], vec_send.at[step], vec_recv.at[step], along_dp(step)) for step in steps]
    start(vec_copies)
    dp_next(0, ATTEND, 3)
    for turn in range(PARTS):
        part_start(0, ATTEND, turn)
    wait(vec_copies)
    vec_rep[...] = vec_chip[...] + vec_dp[0] + vec_dp[1] + vec_dp[2]
    vec_copies = [remote(vec_rep, vec_part.at[step - 1], vec_send.at[3 + step], vec_recv.at[3 + step], along_tensor(step)) for step in steps]
    start(vec_copies)
    finish(0, ATTEND)
    hand_over(0)
    wait(vec_copies)
    vec_total[...] = vec_rep[...] + vec_part[0] + vec_part[1] + vec_part[2]
    own = rep * PARTS + part
    vec_out[...] = pltpu.roll(vec_total[:8, :], 512 - own * 32, 1)[:, :128]
    columns = vec_total[:, tile_rows(rep * 128, 128)]
    row = lax.broadcasted_iota(jnp.int32, columns.shape, 0)
    bias_out[...] = column_sum(jnp.where(row == 6 + part, columns, 0.0))
    deliver(saved_in[0].at[1], 0, blocks_out, y_send, y_recv, "wait")
    deliver(y_in, 1, blocks_out, y_send, y_recv, "wait")
    delivered(blocks_out, y_in, y_send, y_recv)
    for layer in range(2):
        deliver(grad_low.at[layer], layer, rows_out, row_send, row_recv, "wait")
    delivered(rows_out, grad_low.at[0], row_send, row_recv)
    last_copy(0).wait_recv()
    last_copy(0).wait_send()
    down_out[...] = grads_out[:, :512].T
    up_out[...] = grads_out[:, 512:1024]
    out_out[...] = grads_out[:, 1024:1152]
    for kind in range(3):
        qkv_out[kind] = grads_out[:, 1152 + kind * 128 : 1280 + kind * 128]


def specs(space, count):
    return [pl.BlockSpec(memory_space=space)] * count


def kernel_call(body, name, ins, in_specs, outs, out_specs, scratch, collective):
    dma = pltpu.SemaphoreType.DMA
    return pl.pallas_call(
        body,
        out_shape=[jax.ShapeDtypeStruct(shape, kind) for shape, kind in outs],
        in_specs=in_specs,
        out_specs=out_specs,
        scratch_shapes=[pltpu.VMEM(*item) if len(item) == 2 and isinstance(item[0], tuple) else dma(item) for item in scratch],
        compiler_params=pltpu.CompilerParams(collective_id=collective, has_side_effects=True, vmem_limit_bytes=60 * 2**20),
        name=name,
    )(*ins)


def twice(items):
    return tuple(((2, *shape), kind) for shape, kind in items)


def on_device_whole(
    tokens,
    lengths,
    cotangent,
    ln_one_gain,
    ln_one_bias,
    qkv_weight,
    out_weight,
    out_bias,
    ln_two_gain,
    ln_two_bias,
    up_weight,
    up_bias,
    down_weight,
    down_bias,
):
    f32, low = jnp.float32, jnp.bfloat16
    core, rep, part = place()
    vectors = (ln_one_gain, ln_one_bias, out_bias, ln_two_gain, ln_two_bias, down_bias, up_bias)
    rows, rows_low = ((OWN, WIDTH), f32), ((OWN, WIDTH), low)
    square = ((BLOCK, BLOCK), f32)
    results = kernel_call(
        forward_kernel,
        "forward",
        (lengths, tokens, cotangent, qkv_weight[0].transpose(1, 0, 2), out_weight[0], up_weight[0], down_weight[0], *vectors),
        specs(pltpu.SMEM, 1) + specs(pl.ANY, 6) + specs(pltpu.VMEM, 7),
        (rows_low, rows_low, *twice(SAVED), *twice(WEIGHTS)),
        specs(pl.ANY, 18),
        (
            *twice(SAVED),
            *twice(WEIGHTS),
            rows_low,
            ((TASKS, BLOCK, BLOCK), f32),
            rows_low,
            ((TASKS, 2 * BLOCK, BLOCK), f32),
            ((TASKS, 2 * BLOCK, BLOCK), f32),
            ((2, BLOCK, 128), f32),
            rows,
            rows,
            ((8, 512), f32),
            (2, 4),
            (2, 2),
            (2,),
            (5, 3),
            (5, 3),
            (4, 3, 4),
            (4, 3, 4),
            (5, PARTS),
            (5, PARTS),
            (5,),
            (2, PAIRS, 2),
            (2, PAIRS, 2),
            (2, 11),
            (2, 5),
            (4,),
            (2, 2, PARTS),
        ),
        0,
    )
    down_grad, up_grad, out_grad, qkv_grad, spread, up_bias_grad, block_outputs, grad_rows = kernel_call(
        backward_kernel,
        "backward",
        (lengths, *results),
        specs(pltpu.SMEM, 1) + specs(pl.ANY, 18),
        (
            ((512, 128), f32),
            ((128, 512), f32),
            ((128, 128), f32),
            ((3, 128, 128), f32),
            ((8, 128), f32),
            ((1, 128), f32),
            ((PARTS, BLOCK, WIDTH), low),
            ((PARTS, BLOCK, WIDTH), low),
        ),
        specs(pltpu.VMEM, 6) + specs(pl.ANY, 2),
        (
            *SAVED,
            *WEIGHTS,
            rows_low,
            rows,
            ((TASKS, BLOCK, BLOCK), f32),
            ((PARTS, PARTS, 128, 1536), low),
            ((2, 16, 512), f32),
            rows_low,
            ((WIDTH, OWN), low),
            ((OWN, 512), low),
            rows,
            rows,
            ((PAIRS, 2, OWN, 128), low),
            ((PAIRS, 8, OWN), f32),
            ((PAIRS, OWN, 128), low),
            ((2, 2, 1024, 128), f32),
            ((2, PAIRS, OWN, 128), low),
            ((2, 2, PAIRS, OWN, 128), low),
            ((2, OWN, WIDTH), low),
            ((2, PARTS, PARTS, 64, 1536), low),
            ((2, 2, 2, PARTS, 32, 1536), low),
            ((2, 2, PARTS, 32, 1536), low),
            ((2, PARTS, 64, 1536), low),
            ((2, 3, 64, 1536), low),
            ((2, 64, 1536), f32),
            ((16, 512), f32),
            ((16, 512), f32),
            ((3, 16, 512), f32),
            ((16, 512), f32),
            ((3, 16, 512), f32),
            ((128, 1536), f32),
            ((16, 512), f32),
            (11,),
            (5,),
            (1,),
            (2, 2),
            (PARTS,),
            (2, 2),
            (PARTS,),
            (2, PAIRS),
            (2, PAIRS),
            (2, 2, PARTS),
            (2, 2, PARTS),
            (2, 2, PARTS, 2, 2),
            (2, 2, PARTS, 2, 2),
            (2, 2, PARTS, 2),
            (2, 2, PARTS, 2),
            (2, 2, PARTS),
            (2, 2, PARTS),
            (7,),
            (7,),
            (1,),
            (1,),
        ),
        1,
    )
    vector_grads = [spread[row : row + 1, :32] for row in range(6)]
    return (
        block_outputs[None],
        grad_rows.astype(f32)[None],
        vector_grads[0],
        vector_grads[1],
        qkv_grad.transpose(1, 0, 2)[None],
        out_grad[None],
        vector_grads[2],
        vector_grads[3],
        vector_grads[4],
        up_grad[None],
        up_bias_grad[None],
        down_grad[None],
        vector_grads[5],
    )


def solution(mesh):
    return jax.shard_map(
        on_device_whole if whole_batch_fits(mesh) else on_device,
        mesh=mesh,
        in_specs=(
            P("dp", "tensor", None),
            P("dp", None),
            P("dp", "tensor", None),
            P("section", None),
            P("section", None),
            P("section", None, None, "tensor"),
            P("section", "tensor", None),
            P("section", None),
            P("section", None),
            P("section", None),
            P("section", None, "tensor"),
            P("section", "tensor"),
            P("section", "tensor", None),
            P("section", None),
        ),
        out_specs=(
            P("section", "dp", "tensor", None),
            P("section", "dp", "tensor", None),
            P("section", ("dp", "tensor")),
            P("section", ("dp", "tensor")),
            P("section", "dp", None, "tensor"),
            P("section", "tensor", "dp"),
            P("section", ("dp", "tensor")),
            P("section", ("dp", "tensor")),
            P("section", ("dp", "tensor")),
            P("section", "dp", "tensor"),
            P("section", "tensor", "dp"),
            P("section", "tensor", "dp"),
            P("section", ("dp", "tensor")),
        ),
        check_vma=False,
    )
```

```python
from functools import partial
import math

import jax
import jax.numpy as jnp
from jax import lax
from jax.experimental import pallas as pl
from jax.experimental.pallas import tpu as pltpu
from jax.sharding import PartitionSpec as P

HEAD = 64
FF = 2048


def passed_along(block, axis, distance):
    devices = range(lax.axis_size(axis))
    route = [(i - distance, i) for i in devices if i - distance in devices]
    return lax.ppermute(block, axis, route)


def normalize(values, gain_vec, bias_vec):
    centre = values - jnp.mean(values, axis=-1, keepdims=True)
    spread = jnp.mean(centre * centre, axis=-1, keepdims=True)
    return centre * lax.rsqrt(spread + 1e-05) * gain_vec + bias_vec


def document_ids(seq_lens, row_count):
    bounds = jnp.cumsum(seq_lens)
    places = jnp.arange(row_count, dtype=jnp.int32)
    return jnp.sum((places[:, None] >= bounds[None, :]).astype(jnp.int32), axis=1)


def first_key_block(doc_number, seq_lens, block):
    starts = jnp.cumsum(seq_lens) - seq_lens
    numbers = jnp.arange(seq_lens.shape[0], dtype=jnp.int32)
    return jnp.sum(jnp.where(numbers == doc_number, starts, 0)) // block


def grouped_sum(left, right, groups):
    row_count, inner = left.shape
    terms = jnp.einsum(
        "rgc,gcd->grd",
        left.reshape(row_count, groups, inner // groups),
        right.reshape(groups, inner // groups, right.shape[-1]),
        preferred_element_type=jnp.float32,
    )
    return jnp.sum(lax.optimization_barrier(terms.astype(jnp.bfloat16)).astype(jnp.float32), axis=0)


def branch_total(left, right):
    return grouped_sum(left, right, lax.axis_size("tensor"))


def key_scores(query_rows, key_part, query_docs, key_docs, query_first, key_first, signed):
    scale = 1.0 / math.sqrt(query_rows.shape[-1])
    scores = (
        jnp.einsum("qhe,khe->hqk", query_rows, key_part, preferred_element_type=jnp.float32) * scale
    )
    query_places = query_first + jnp.arange(query_rows.shape[0], dtype=jnp.int32)
    key_places = key_first + jnp.arange(key_part.shape[0], dtype=jnp.int32)
    allowed = (query_docs[:, None] == key_docs[None, :]) & (
        query_places[:, None] >= key_places[None, :]
    )
    modulus = jnp.sqrt(scores * scores + 1.0)
    logits = jnp.where(signed, modulus, scores)
    factor = jnp.where(signed, scores / modulus, 1.0)
    return (modulus, logits, factor, allowed[None])


def attend(queries, key_rows, values, doc_rows, seq_lens, signed, offset):
    query_count, heads_here, head_size = queries.shape
    key_count = key_rows.shape[0]
    query_block = min(512, query_count)
    key_block = min(512, key_count)
    query_first = offset + 0
    query_docs = lax.dynamic_slice_in_dim(doc_rows, query_first, query_block, 0)
    lowest = first_key_block(query_docs[0], seq_lens, key_block)
    upper = (query_first + query_block - 1) // key_block + 1

    def block_scores(key_index):
        key_first = key_index * key_block
        return key_scores(
            queries,
            lax.dynamic_slice_in_dim(key_rows, key_first, key_block, 0),
            query_docs,
            lax.dynamic_slice_in_dim(doc_rows, key_first, key_block, 0),
            query_first,
            key_first,
            signed,
        )

    def measure(key_index, carry):
        running_max, running_sum = carry
        modulus, logits, factor, allowed = block_scores(key_index)
        masked = jnp.where(allowed, logits, -1e30)
        new_max = jnp.maximum(running_max, jnp.max(masked, axis=-1))
        added = jnp.sum(jnp.where(allowed, jnp.exp(masked - new_max[:, :, None]), 0.0), axis=-1)
        return (new_max, running_sum * jnp.exp(running_max - new_max) + added)

    start_max = jnp.full((heads_here, query_block), -1e30, jnp.float32)
    start_sum = jnp.zeros((heads_here, query_block), jnp.float32)
    row_max, row_sum = lax.fori_loop(lowest, upper, measure, (start_max, start_sum))
    log_total = row_max + jnp.log(row_sum)

    def accumulate(key_index, partial_out):
        modulus, logits, factor, allowed = block_scores(key_index)
        probs = jnp.where(allowed, jnp.exp(logits - log_total[:, :, None]), 0.0)
        weights = (factor * probs).astype(jnp.bfloat16)
        value_rows = lax.dynamic_slice_in_dim(values, key_index * key_block, key_block, 0)
        return partial_out + jnp.einsum(
            "hqk,khe->qhe", weights, value_rows, preferred_element_type=jnp.float32
        )

    outputs_list = lax.fori_loop(
        lowest, upper, accumulate, jnp.zeros((query_block, heads_here, head_size), jnp.float32)
    )
    return (outputs_list, log_total)


def attend_back(
    queries,
    key_rows,
    values,
    doc_rows,
    seq_lens,
    signed,
    attended,
    log_totals,
    grad_attended,
    offset,
):
    query_count, heads_here, head_size = queries.shape
    key_count = key_rows.shape[0]
    query_block = min(512, query_count)
    key_block = min(512, key_count)
    scale = 1.0 / math.sqrt(head_size)
    centre_terms = jnp.sum(grad_attended.astype(jnp.float32) * attended, axis=-1).T
    grad_keys = jnp.zeros(key_rows.shape, jnp.float32)
    grad_values = jnp.zeros(key_rows.shape, jnp.float32)
    query_first = offset + 0
    query_docs = lax.dynamic_slice_in_dim(doc_rows, query_first, query_block, 0)
    lowest = first_key_block(query_docs[0], seq_lens, key_block)
    upper = (query_first + query_block - 1) // key_block + 1

    def backward_step(key_index, carry):
        grad_query, keys_total, values_total = carry
        key_first = key_index * key_block
        key_part = lax.dynamic_slice_in_dim(key_rows, key_first, key_block, 0)
        value_rows = lax.dynamic_slice_in_dim(values, key_first, key_block, 0)
        modulus, logits, factor, allowed = key_scores(
            queries,
            key_part,
            query_docs,
            lax.dynamic_slice_in_dim(doc_rows, key_first, key_block, 0),
            query_first,
            key_first,
            signed,
        )
        probs = jnp.where(allowed, jnp.exp(logits - log_totals[:, :, None]), 0.0)
        weights = (factor * probs).astype(jnp.bfloat16)
        grad_weights = jnp.einsum(
            "qhe,khe->hqk", grad_attended, value_rows, preferred_element_type=jnp.float32
        )
        grad_scores = factor * probs * (factor * grad_weights - centre_terms[:, :, None])
        grad_scores = grad_scores + jnp.where(
            signed, probs * grad_weights / (modulus * modulus * modulus), 0.0
        )
        grad_low = grad_scores.astype(jnp.bfloat16)
        grad_query = (
            grad_query
            + jnp.einsum("hqk,khe->qhe", grad_low, key_part, preferred_element_type=jnp.float32)
            * scale
        )
        key_term = (
            jnp.einsum("hqk,qhe->khe", grad_low, queries, preferred_element_type=jnp.float32)
            * scale
        )
        value_term = jnp.einsum(
            "hqk,qhe->khe", weights, grad_attended, preferred_element_type=jnp.float32
        )
        keys_total = lax.dynamic_update_slice_in_dim(
            keys_total,
            lax.dynamic_slice_in_dim(keys_total, key_first, key_block, 0) + key_term,
            key_first,
            0,
        )
        values_total = lax.dynamic_update_slice_in_dim(
            values_total,
            lax.dynamic_slice_in_dim(values_total, key_first, key_block, 0) + value_term,
            key_first,
            0,
        )
        return (grad_query, keys_total, values_total)

    start_query = jnp.zeros((query_block, heads_here, head_size), jnp.float32)
    grad_query, grad_keys, grad_values = lax.fori_loop(
        lowest, upper, backward_step, (start_query, grad_keys, grad_values)
    )
    return (grad_query, grad_keys, grad_values)


def forward_layer(inputs, seq_lens, params, signed, finish):
    (
        gain_one,
        bias_one,
        qkv_weight,
        out_weight,
        out_bias,
        gain_two,
        bias_two,
        up_weight,
        up_bias,
        down_weight,
        down_bias,
    ) = params
    normed_one = normalize(inputs, gain_one, bias_one).astype(jnp.bfloat16)
    offset = lax.axis_index("tensor") * normed_one.shape[0]
    row_count = normed_one.shape[0]
    width = qkv_weight.shape[-1]
    projected = jnp.dot(
        normed_one,
        qkv_weight.reshape(qkv_weight.shape[0], 3 * width),
        preferred_element_type=jnp.float32,
    ).astype(jnp.bfloat16)
    head_shape = (row_count, width // HEAD, HEAD)
    queries = projected[:, :width].reshape(head_shape)
    key_rows = projected[:, width : 2 * width].reshape(head_shape)
    values = projected[:, 2 * width :].reshape(head_shape)
    key_all, value_all = (
        lax.all_gather(key_rows, "tensor", axis=0, tiled=True),
        lax.all_gather(values, "tensor", axis=0, tiled=True),
    )
    doc_rows = document_ids(seq_lens, key_all.shape[0])
    attended, log_totals = attend(queries, key_all, value_all, doc_rows, seq_lens, signed, offset)
    attended_low = attended.reshape(row_count, width).astype(jnp.bfloat16)
    hidden_one = inputs + branch_total(attended_low, out_weight) + out_bias
    normed_two = normalize(hidden_one, gain_two, bias_two).astype(jnp.bfloat16)
    up_values = jnp.dot(normed_two, up_weight, preferred_element_type=jnp.float32) + up_bias
    activated = jax.nn.gelu(up_values, approximate=False).astype(jnp.bfloat16)
    if finish:
        outputs = hidden_one + branch_total(activated, down_weight) + down_bias
    else:
        outputs = hidden_one
    saved = (
        normed_one,
        queries,
        key_all,
        value_all,
        doc_rows,
        attended,
        attended_low,
        log_totals,
        hidden_one,
        normed_two,
        up_values,
        activated,
        offset,
    )
    return (outputs, saved)


def backward_layer(inputs, seq_lens, params, signed, grad_outputs):
    (
        gain_one,
        bias_one,
        qkv_weight,
        out_weight,
        out_bias,
        gain_two,
        bias_two,
        up_weight,
        up_bias,
        down_weight,
        down_bias,
    ) = params
    unused_out, saved = forward_layer(inputs, seq_lens, params, signed, False)
    (
        rows_one,
        queries,
        key_all,
        value_all,
        doc_rows,
        attended,
        attended_low,
        log_totals,
        hidden_one,
        rows_two,
        up_values,
        activated,
        offset,
    ) = saved
    row_count, width = attended_low.shape
    grad_low = grad_outputs.astype(jnp.bfloat16)
    grad_down = jnp.einsum("rf,rd->fd", activated, grad_low, preferred_element_type=jnp.float32)
    grad_act = jnp.einsum("rd,fd->rf", grad_low, down_weight, preferred_element_type=jnp.float32)
    gelu_value, gelu_back = jax.vjp(partial(jax.nn.gelu, approximate=False), up_values)
    grad_up_values = gelu_back(grad_act)[0].astype(jnp.bfloat16)
    grad_up_bias = jnp.sum(grad_up_values.astype(jnp.float32), axis=0)
    grad_up = jnp.einsum("rd,rf->df", rows_two, grad_up_values, preferred_element_type=jnp.float32)
    normed_two_terms = jnp.einsum(
        "rf,df->rd", grad_up_values, up_weight, preferred_element_type=jnp.float32
    )
    norm_value, norm_back = jax.vjp(normalize, hidden_one, gain_two, bias_two)
    grad_hidden, grad_gain_two, grad_bias_two = norm_back(normed_two_terms)
    grad_hidden = grad_hidden + grad_outputs
    hidden_low = grad_hidden.astype(jnp.bfloat16)
    grad_out = jnp.einsum("rc,rd->cd", attended_low, hidden_low, preferred_element_type=jnp.float32)
    grad_attended = (
        jnp.einsum("rd,cd->rc", hidden_low, out_weight, preferred_element_type=jnp.float32)
        .astype(jnp.bfloat16)
        .reshape(queries.shape)
    )
    grad_queries, grad_keys, grad_values = attend_back(
        queries,
        key_all,
        value_all,
        doc_rows,
        seq_lens,
        signed,
        attended,
        log_totals,
        grad_attended,
        offset,
    )
    grad_keys, grad_values = (
        lax.psum_scatter(
            grad_keys.astype(jnp.bfloat16), "tensor", scatter_dimension=0, tiled=True
        ).astype(jnp.float32),
        lax.psum_scatter(
            grad_values.astype(jnp.bfloat16), "tensor", scatter_dimension=0, tiled=True
        ).astype(jnp.float32),
    )
    grad_projected = jnp.concatenate(
        [
            grad_queries.reshape(row_count, width),
            grad_keys.reshape(row_count, width),
            grad_values.reshape(row_count, width),
        ],
        axis=1,
    ).astype(jnp.bfloat16)
    grad_qkv = jnp.einsum(
        "rd,rc->dc", rows_one, grad_projected, preferred_element_type=jnp.float32
    ).reshape(qkv_weight.shape)
    normed_one_terms = jnp.einsum(
        "rc,dc->rd",
        grad_projected,
        qkv_weight.reshape(qkv_weight.shape[0], 3 * width),
        preferred_element_type=jnp.float32,
    )
    norm_value_one, norm_back_one = jax.vjp(normalize, inputs, gain_one, bias_one)
    grad_inputs, grad_gain_one, grad_bias_one = norm_back_one(normed_one_terms)
    grad_inputs = grad_inputs + grad_hidden
    matrices = (
        grad_qkv[None],
        grad_out[None],
        grad_up[None],
        grad_up_bias.reshape(1, -1, FF // lax.axis_size("tensor")),
        grad_down[None],
    )
    vectors = (
        grad_gain_one[None],
        grad_bias_one[None],
        jnp.sum(grad_hidden, axis=0)[None],
        grad_gain_two[None],
        grad_bias_two[None],
        jnp.sum(grad_outputs, axis=0)[None],
    )
    return (grad_inputs, matrices, vectors)


def on_device(
    tokens,
    lengths,
    cotangent,
    ln_one_gain,
    ln_one_bias,
    qkv_weight,
    out_weight,
    out_bias,
    ln_two_gain,
    ln_two_bias,
    up_weight,
    up_bias,
    down_weight,
    down_bias,
):
    signed = lax.axis_index("section") == 0
    params = tuple(
        (
            array_item[0]
            for array_item in (
                ln_one_gain,
                ln_one_bias,
                qkv_weight,
                out_weight,
                out_bias,
                ln_two_gain,
                ln_two_bias,
                up_weight,
                up_bias,
                down_weight,
                down_bias,
            )
        )
    )
    whole = (
        lax.all_gather(qkv_weight, "tensor", axis=3, tiled=True),
        lax.all_gather(out_weight, "tensor", axis=1, tiled=True),
        lax.all_gather(up_weight, "tensor", axis=2, tiled=True),
        lax.all_gather(down_weight, "tensor", axis=1, tiled=True),
    )
    bias_whole = lax.all_gather(up_bias, "tensor", axis=1, tiled=True)
    params = (
        params[0],
        params[1],
        whole[0][0],
        whole[1][0],
        params[4],
        params[5],
        params[6],
        whole[2][0],
        bias_whole[0],
        whole[3][0],
        params[10],
    )
    batches = tokens.shape[0]
    arrived = jnp.zeros(tokens.shape[1:], jnp.bfloat16)
    produced_all = jnp.zeros(tokens.shape, jnp.bfloat16)
    received_all = jnp.zeros(tokens.shape, jnp.bfloat16)
    for tick in range(batches + 1):
        own_index = min(tick, batches - 1)
        prior_index = max(tick - 1, 0)
        inputs_now = jnp.where(signed, tokens[own_index], arrived).astype(jnp.float32)
        lens_now = jnp.where(signed, lengths[own_index], lengths[prior_index])
        produced = forward_layer(inputs_now, lens_now, params, signed, True)[0].astype(jnp.bfloat16)
        if tick < batches:
            produced_all = produced_all.at[tick].set(
                jnp.where(signed, produced, produced_all[tick])
            )
        if tick > 0:
            produced_all = produced_all.at[tick - 1].set(
                jnp.where(signed, produced_all[tick - 1], produced)
            )
            received_all = received_all.at[tick - 1].set(arrived)
        if tick < batches:
            arrived = passed_along(produced, "section", 1)
    block_inputs = jnp.where(signed, tokens, received_all)
    returned = jnp.zeros(tokens.shape[1:], jnp.float32)
    grad_inputs_all = jnp.zeros(tokens.shape, jnp.float32)
    matrix_total = None
    vector_total = None
    for tick in range(batches + 1):
        later_index = batches - 1 - tick if tick < batches else 0
        earlier_index = batches - tick if tick > 0 else 0
        index_now = jnp.where(signed, earlier_index, later_index)
        live_now = jnp.where(signed, tick > 0, tick < batches)
        grad_now = jnp.where(signed, returned, cotangent[later_index].astype(jnp.float32))
        grad_now = jnp.where(live_now, grad_now, 0.0)
        inputs_now = block_inputs[index_now].astype(jnp.float32)
        grad_back, matrices, vectors = backward_layer(
            inputs_now, lengths[index_now], params, signed, grad_now
        )
        if tick == 0:
            matrix_total = tuple(matrices)
            vector_total = tuple(vectors)
        else:
            matrix_total = tuple(
                (
                    jnp.add(total_item, new_item)
                    for total_item, new_item in zip(matrix_total, matrices)
                )
            )
            vector_total = tuple(
                (
                    jnp.add(total_item, new_item)
                    for total_item, new_item in zip(vector_total, vectors)
                )
            )
        if tick > 0:
            grad_inputs_all = grad_inputs_all.at[earlier_index].set(
                jnp.where(signed, grad_back, grad_inputs_all[earlier_index])
            )
        if tick < batches:
            grad_inputs_all = grad_inputs_all.at[later_index].set(
                jnp.where(signed, grad_inputs_all[later_index], grad_back)
            )
            returned = passed_along(grad_back.astype(jnp.bfloat16), "section", -1).astype(
                grad_back.dtype
            )
    matrix_final = (
        lax.psum_scatter(
            matrix_total[0].astype(jnp.bfloat16), "dp", scatter_dimension=1, tiled=True
        ).astype(jnp.float32),
        lax.psum_scatter(
            matrix_total[1].astype(jnp.bfloat16), "dp", scatter_dimension=2, tiled=True
        ).astype(jnp.float32),
        lax.psum_scatter(
            matrix_total[2].astype(jnp.bfloat16), "dp", scatter_dimension=1, tiled=True
        ).astype(jnp.float32),
        lax.psum_scatter(
            matrix_total[3].astype(jnp.bfloat16), "dp", scatter_dimension=2, tiled=True
        ).astype(jnp.float32),
        lax.psum_scatter(
            matrix_total[4].astype(jnp.bfloat16), "dp", scatter_dimension=2, tiled=True
        ).astype(jnp.float32),
    )
    vector_final = (
        lax.psum_scatter(vector_total[0], ("dp", "tensor"), scatter_dimension=1, tiled=True),
        lax.psum_scatter(vector_total[1], ("dp", "tensor"), scatter_dimension=1, tiled=True),
        lax.psum_scatter(vector_total[2], ("dp", "tensor"), scatter_dimension=1, tiled=True),
        lax.psum_scatter(vector_total[3], ("dp", "tensor"), scatter_dimension=1, tiled=True),
        lax.psum_scatter(vector_total[4], ("dp", "tensor"), scatter_dimension=1, tiled=True),
        lax.psum_scatter(vector_total[5], ("dp", "tensor"), scatter_dimension=1, tiled=True),
    )
    matrix_final = (
        lax.psum_scatter(
            matrix_final[0].astype(jnp.bfloat16), "tensor", scatter_dimension=3, tiled=True
        ).astype(jnp.float32),
        lax.psum_scatter(
            matrix_final[1].astype(jnp.bfloat16), "tensor", scatter_dimension=1, tiled=True
        ).astype(jnp.float32),
        lax.psum_scatter(
            matrix_final[2].astype(jnp.bfloat16), "tensor", scatter_dimension=2, tiled=True
        ).astype(jnp.float32),
        lax.psum_scatter(
            matrix_final[3].astype(jnp.bfloat16), "tensor", scatter_dimension=1, tiled=True
        ).astype(jnp.float32),
        lax.psum_scatter(
            matrix_final[4].astype(jnp.bfloat16), "tensor", scatter_dimension=1, tiled=True
        ).astype(jnp.float32),
    )
    grad_qkv, grad_out, grad_up, grad_up_bias, grad_down = matrix_final
    grad_gain_one, grad_bias_one, grad_out_bias, grad_gain_two, grad_bias_two, grad_down_bias = (
        vector_final
    )
    return (
        produced_all[None],
        grad_inputs_all[None],
        grad_gain_one,
        grad_bias_one,
        grad_qkv,
        grad_out,
        grad_out_bias,
        grad_gain_two,
        grad_bias_two,
        grad_up,
        grad_up_bias,
        grad_down,
        grad_down_bias,
    )


MESH = pl.DeviceIdType.MESH
PARTS = 4
BLOCK = 256
OWN = 512
WIDTH = 512
PAIRS = 4
TASKS = 5
NEGATIVE = -1e30
LEFT = (((1,), (0,)), ((), ()))
BOTH_LAST = (((1,), (1,)), ((), ()))
BOTH_FIRST = (((0,), (0,)), ((), ()))


def whole_batch_fits(mesh):
    shape = dict(mesh.shape)
    return shape["tensor"] == PARTS and shape["dp"] == PARTS and shape["section"] == 2


def dot(left, right, dims=LEFT):
    return lax.dot_general(left, right, dims, preferred_element_type=jnp.float32)


def place():
    return lax.axis_index("section"), lax.axis_index("dp"), lax.axis_index("tensor")


def blocks_of(core):
    return (core, 3 - core)


def turn_part(turn):
    return lax.bitwise_xor(lax.axis_index("tensor"), lax.rem(turn, PARTS))


def tile_rows(start, count):
    return pl.ds(pl.multiple_of(start, count), count)


def standard(values):
    centre = values - jnp.mean(values, axis=-1, keepdims=True)
    spread = jnp.mean(centre * centre, axis=-1, keepdims=True)
    inverse = lax.rsqrt(spread + 1e-05)
    return centre * inverse, inverse


def standard_back(grads, gain, units, inverse):
    scaled = grads * gain
    inner = jnp.mean(scaled * units, axis=-1, keepdims=True)
    return inverse * (scaled - jnp.mean(scaled, axis=-1, keepdims=True) - units * inner)


def column_sum(values):
    return jnp.sum(values, axis=0, keepdims=True)


def keep_head(values, parity):
    lane = lax.broadcasted_iota(jnp.int32, values.shape, 1)
    return jnp.where((lane < HEAD) == (parity == 0), values, 0.0)


def side_by_side(weight_ref, pair):
    return jnp.concatenate([weight_ref[pair, kind] for kind in range(3)], axis=1)


def project(x_ref, vec_ref, weight_ref, normed_t_ref, query_ref, kv_ref, normed_ref, between, before_pair, after_pair):
    core = lax.axis_index("section")
    gain, bias = vec_ref[0, 0:1, :], vec_ref[0, 1:2, :]

    def norm_rows(index, carry):
        rows = tile_rows(index * 128, 128)
        units, _ = standard(x_ref[rows, :].astype(jnp.float32))
        normed_ref[rows, :] = (units * gain + bias).astype(jnp.bfloat16)
        return carry

    lax.fori_loop(0, OWN // 128, norm_rows, 0)
    normed_t_ref[...] = normed_ref[...].T
    between()

    def pair_step(turn, carry):
        pair = turn_part(turn)
        before_pair(turn)
        out = dot(normed_ref[...], side_by_side(weight_ref, pair))
        queries = out[:, :128] * 0.125
        for parity in range(2):
            query_ref[pair, parity] = keep_head(queries, parity).astype(jnp.bfloat16)
        for slot, block in enumerate(blocks_of(core)):
            part = out[slot * BLOCK : (slot + 1) * BLOCK, :]
            kv_ref[0, pair, tile_rows(block * BLOCK, BLOCK), :] = part[:, 128:256].astype(jnp.bfloat16)
            kv_ref[1, pair, tile_rows(block * BLOCK, BLOCK), :] = part[:, 256:].astype(jnp.bfloat16)
        after_pair(turn, pair)
        return carry

    lax.fori_loop(0, PAIRS, pair_step, 0)


def task_plan(core):
    first = core == 0
    slots = (0, jnp.where(first, 1, 0), 1, 1, 1)
    keys = (0, jnp.where(first, 0, 1), jnp.where(first, 1, 0), jnp.where(first, 2, 1), jnp.where(first, 3, 2))
    return slots, keys


def attend_rows(signed, query_ref, kv_ref, bias_ref, attended_ref, attended_t_ref, log_ref, logit_ref, factor_ref, stat_ref, before_pair):
    core = lax.axis_index("section")
    slots, keys = task_plan(core)
    middle_late = core == 0
    lane = lax.broadcasted_iota(jnp.int32, (BLOCK, 128), 1)

    def pair_step(turn, carry):
        pair = turn_part(turn)
        before_pair(turn, pair)
        tops = []
        for task in range(TASKS):
            rows = tile_rows(slots[task] * BLOCK, BLOCK)
            key_rows = tile_rows(keys[task] * BLOCK, BLOCK)
            queries = query_ref[pair, :, rows, :].reshape(2 * BLOCK, 128)
            scores = dot(queries, kv_ref[0, pair, key_rows, :], BOTH_LAST)
            if signed:
                raised = scores * scores + 1.0
                inverse = lax.rsqrt(raised)
                factor_ref[task] = scores * inverse
                scores = raised * inverse
            logits = scores + jnp.concatenate([bias_ref[task]] * 2, axis=0)
            logit_ref[task] = logits
            tops.append(jnp.maximum(logits[:, :128], logits[:, 128:]))
        low = jnp.full((2 * BLOCK, 128), NEGATIVE, jnp.float32)
        top_early = jnp.maximum(tops[0], jnp.where(middle_late, low, tops[1]))
        top_late = jnp.maximum(jnp.maximum(tops[2], tops[3]), jnp.maximum(tops[4], jnp.where(middle_late, tops[1], low)))
        max_early = jnp.max(top_early, axis=-1, keepdims=True)
        max_late = jnp.max(top_late, axis=-1, keepdims=True)
        max_middle = jnp.where(middle_late, max_late, max_early)
        shifts = (max_early, max_middle, max_late, max_late, max_late)
        sums, terms = [], []
        for task in range(TASKS):
            key_rows = tile_rows(keys[task] * BLOCK, BLOCK)
            powers = jnp.exp(logit_ref[task] - shifts[task])
            sums.append(powers[:, :128] + powers[:, 128:])
            if signed:
                powers = powers * factor_ref[task]
            terms.append(dot(powers.astype(jnp.bfloat16), kv_ref[1, pair, key_rows, :]))
        early = jnp.where(middle_late, 0.0, 1.0)
        late = 1.0 - early
        totals = (sums[0] + sums[1] * early, sums[2] + sums[3] + sums[4] + sums[1] * late)
        values = (terms[0] + terms[1] * early, terms[2] + terms[3] + terms[4] + terms[1] * late)
        for slot, top in enumerate((max_early, max_late)):
            total = jnp.sum(totals[slot], axis=-1, keepdims=True)
            outs = values[slot] / total
            logs = top + jnp.log(total)
            for parity in range(2):
                stat_ref[slot] = jnp.where(lane == pair * 2 + parity, logs[parity * BLOCK : (parity + 1) * BLOCK], stat_ref[slot])
            merged = jnp.where(lane < HEAD, outs[:BLOCK], outs[BLOCK:])
            attended_ref[pair, slot * BLOCK : (slot + 1) * BLOCK, :] = merged
            attended_t_ref[pair, :, slot * BLOCK : (slot + 1) * BLOCK] = merged.T.astype(jnp.bfloat16)
        return carry

    stat_ref[...] = jnp.zeros_like(stat_ref)
    lax.fori_loop(0, PAIRS, pair_step, 0)
    for slot in range(2):
        log_ref[slot] = stat_ref[slot].T[:8, :]


def gelu_both(values):
    lower = 0.5 * (1.0 + lax.erf(values * math.sqrt(0.5)))
    density = jnp.exp(-0.5 * values * values) * (1.0 / math.sqrt(2.0 * math.pi))
    return values * lower, lower + values * density


def feed(x_ref, attended_ref, vec_ref, out_ref, up_ref, down_ref, hidden_ref, normed_t_ref, act_ref, slope_ref, y_ref, normed_ref, wide_ref, sum_ref, before_out, between, before_chunk, during_chunk):
    out_bias = vec_ref[0, 2:3, :]
    gain, bias = vec_ref[0, 3:4, :], vec_ref[0, 4:5, :]
    down_bias = vec_ref[0, 5:6, :]
    sum_ref[...] = jnp.zeros_like(sum_ref)

    def out_step(turn, carry):
        pair = turn_part(turn)
        before_out(turn)
        sum_ref[...] += dot(attended_ref[pair].astype(jnp.bfloat16), out_ref[pair])
        return carry

    lax.fori_loop(0, PAIRS, out_step, 0)

    def norm_rows(index, carry):
        rows = tile_rows(index * 128, 128)
        hidden = x_ref[rows, :].astype(jnp.float32) + sum_ref[rows, :] + out_bias
        hidden_ref[rows, :] = hidden
        units, _ = standard(hidden)
        normed_ref[rows, :] = (units * gain + bias).astype(jnp.bfloat16)
        sum_ref[rows, :] = hidden + down_bias
        return carry

    lax.fori_loop(0, OWN // 128, norm_rows, 0)
    normed_t_ref[...] = normed_ref[...].T
    between()

    def chunk_step(turn, carry):
        chunk = turn_part(turn)
        before_chunk(turn)
        wide_ref[...] = dot(normed_ref[...], up_ref[chunk])
        up_bias = vec_ref[chunk, 6:7, :]

        def gelu_rows(index, inner):
            rows = tile_rows(index * 32, 32)
            act, slope = gelu_both(wide_ref[rows, :] + up_bias)
            act_ref[chunk, rows, :] = act.astype(jnp.bfloat16)
            slope_ref[chunk, rows, :] = slope.astype(jnp.bfloat16)
            return inner

        lax.fori_loop(0, OWN // 32, gelu_rows, 0)
        during_chunk(turn)
        sum_ref[...] += dot(act_ref[chunk], down_ref[chunk])
        return carry

    lax.fori_loop(0, PARTS, chunk_step, 0)
    y_ref[...] = sum_ref[...].astype(jnp.bfloat16)


def feed_back(dy_ref, act_ref, slope_ref, down_ref, up_ref, hidden_ref, normed_t_ref, vec_ref, out_ref, attended_ref, attended_t_ref, grad_hidden_ref, grad_att_ref, centre_ref, grads_ref, vec_grad_ref, low_ref, low_t_ref, chunk_ref, sum_ref, during_chunk, after_chunk, before_norm, between):
    low_ref[...] = dy_ref[...].astype(jnp.bfloat16)
    low_t_ref[...] = low_ref[...].T
    vec_grad_ref[...] = jnp.zeros_like(vec_grad_ref)
    sum_ref[...] = jnp.zeros_like(sum_ref)

    def chunk_step(turn, carry):
        chunk = turn_part(turn + 1)
        grad_act = dot(low_ref[...], down_ref[chunk], BOTH_LAST)
        grad_up = (grad_act * slope_ref[chunk].astype(jnp.float32)).astype(jnp.bfloat16)
        chunk_ref[...] = grad_up
        vec_grad_ref[pl.ds(6 + chunk, 1), :] = column_sum(grad_up.astype(jnp.float32))
        down_term = dot(low_t_ref[...], act_ref[chunk]).astype(jnp.bfloat16)
        up_term = dot(normed_t_ref[...], chunk_ref[...]).astype(jnp.bfloat16)
        for part in range(PARTS):
            grads_ref[part, chunk, :, 0:512] = down_term[part * 128 : (part + 1) * 128, :]
            grads_ref[part, chunk, :, 512:1024] = up_term[part * 128 : (part + 1) * 128, :]
        after_chunk(turn, chunk)
        sum_ref[...] += dot(chunk_ref[...], up_ref[chunk], BOTH_LAST)
        during_chunk(turn)
        return carry

    lax.fori_loop(0, PARTS, chunk_step, 0)
    before_norm()
    gain = vec_ref[0, 3:4, :]

    def norm_rows(index, carry):
        rows = tile_rows(index * 128, 128)
        grads, dy = sum_ref[rows, :], dy_ref[rows, :]
        units, inverse = standard(hidden_ref[rows, :])
        grad_hidden = dy + standard_back(grads, gain, units, inverse)
        grad_hidden_ref[rows, :] = grad_hidden
        low_ref[rows, :] = grad_hidden.astype(jnp.bfloat16)
        vec_grad_ref[2:3, :] += column_sum(grad_hidden)
        vec_grad_ref[3:4, :] += column_sum(grads * units)
        vec_grad_ref[4:5, :] += column_sum(grads)
        vec_grad_ref[5:6, :] += column_sum(dy)
        return carry

    lax.fori_loop(0, OWN // 128, norm_rows, 0)
    between()
    row = lax.broadcasted_iota(jnp.int32, (8, 128), 0)
    lane = lax.broadcasted_iota(jnp.int32, (8, 128), 1)
    picks = jnp.where((row < 2) & ((lane < HEAD) == (row == 0)), 1.0, 0.0).astype(jnp.bfloat16)

    def pair_step(pair, carry):
        out_term = dot(attended_t_ref[pair], low_ref[...]).astype(jnp.bfloat16)
        for part in range(PARTS):
            grads_ref[part, pair, :, 1024:1152] = out_term[:, part * 128 : (part + 1) * 128]
        grad_att = dot(low_ref[...], out_ref[pair], BOTH_LAST).astype(jnp.bfloat16)
        wide = grad_att.astype(jnp.float32)
        for parity in range(2):
            grad_att_ref[pair, parity] = keep_head(wide, parity).astype(jnp.bfloat16)
        products = wide * attended_ref[pair]
        upper = products.astype(jnp.bfloat16)
        lower = (products - upper.astype(jnp.float32)).astype(jnp.bfloat16)
        centre_ref[pair] = dot(picks, upper, BOTH_LAST) + dot(picks, lower, BOTH_LAST)
        return carry

    lax.fori_loop(0, PAIRS, pair_step, 0)


def attend_rows_back(signed, query_ref, kv_ref, grad_att_ref, bias_ref, log_ref, centre_ref, grad_query_ref, grad_kv_ref, send_ref, before_pair, after_pair):
    core = lax.axis_index("section")
    slots, keys = task_plan(core)
    early = jnp.where(core == 0, 0.0, 1.0)
    lane = lax.broadcasted_iota(jnp.int32, (BLOCK, 128), 1)

    def pair_step(turn, carry):
        pair = turn_part(turn + 1)
        held = lax.rem(turn, 2)
        before_pair(turn)
        grad_kv_ref[held] = jnp.zeros(grad_kv_ref.shape[1:], jnp.float32)
        merged = []
        for task in range(TASKS):
            rows = tile_rows(slots[task] * BLOCK, BLOCK)
            key_rows = tile_rows(keys[task] * BLOCK, BLOCK)
            key_part, value_part = kv_ref[0, pair, key_rows, :], kv_ref[1, pair, key_rows, :]
            queries = query_ref[pair, :, rows, :].reshape(2 * BLOCK, 128)
            grad_att = grad_att_ref[pair, :, rows, :].reshape(2 * BLOCK, 128)
            scores = dot(key_part, queries, BOTH_LAST)
            grad_weights = dot(value_part, grad_att, BOTH_LAST)
            log_row = jnp.concatenate([log_ref[slots[task], pl.ds(pair * 2 + parity, 1), :] for parity in range(2)], axis=1)
            centre = jnp.concatenate([centre_ref[pair, parity : parity + 1, rows] for parity in range(2)], axis=1)
            bias = jnp.concatenate([bias_ref[task]] * 2, axis=1)
            if signed:
                raised = scores * scores + 1.0
                inverse = lax.rsqrt(raised)
                factor = scores * inverse
                probs = jnp.exp(raised * inverse + bias - log_row)
                weights = factor * probs
                grad_scores = weights * (factor * grad_weights - centre)
                grad_scores = grad_scores + probs * grad_weights * (inverse * inverse * inverse)
            else:
                weights = jnp.exp(scores + bias - log_row)
                grad_scores = weights * (grad_weights - centre)
            grad_low = grad_scores.astype(jnp.bfloat16)
            grad_kv_ref[held, 0, key_rows, :] += dot(grad_low, queries)
            grad_kv_ref[held, 1, key_rows, :] += dot(weights.astype(jnp.bfloat16), grad_att)
            grad_query = dot(grad_low, key_part, BOTH_FIRST)
            merged.append(jnp.where(lane < HEAD, grad_query[:BLOCK], grad_query[BLOCK:]))
        grad_query_ref[pair, :BLOCK, :] = ((merged[0] + merged[1] * early) * 0.125).astype(jnp.bfloat16)
        grad_query_ref[pair, BLOCK:, :] = ((merged[1] * (1.0 - early) + merged[2] + merged[3] + merged[4]) * 0.125).astype(jnp.bfloat16)
        for slot, block in enumerate(blocks_of(1 - core)):
            for kind in range(2):
                rows = grad_kv_ref[held, kind, tile_rows(block * BLOCK, BLOCK), :]
                send_ref[kind, pair, slot * BLOCK : (slot + 1) * BLOCK, :] = rows.astype(jnp.bfloat16)
        after_pair(turn, pair)
        return carry

    lax.fori_loop(0, PAIRS, pair_step, 0)


def project_back_pair(pair, held, grad_query_ref, grad_kv_ref, other_ref, normed_t_ref, weight_ref, grads_ref, sum_ref, send):
    parts = [grad_query_ref[pair]]
    for kind in range(2):
        halves = []
        for slot, block in enumerate(blocks_of(lax.axis_index("section"))):
            own = grad_kv_ref[held, kind, tile_rows(block * BLOCK, BLOCK), :]
            halves.append(own + other_ref[kind, pair, slot * BLOCK : (slot + 1) * BLOCK, :].astype(jnp.float32))
        parts.append(jnp.concatenate(halves, axis=0).astype(jnp.bfloat16))
    grads = jnp.concatenate(parts, axis=1)
    term = dot(normed_t_ref[...], grads).astype(jnp.bfloat16)
    for part in range(PARTS):
        grads_ref[part, pair, :, 1152:1536] = term[part * 128 : (part + 1) * 128, :]
    send()
    sum_ref[...] += dot(grads, side_by_side(weight_ref, pair), BOTH_LAST)


def project_back_norm(x_ref, grad_hidden_ref, vec_ref, grad_x_ref, grad_x_low_ref, vec_grad_ref, sum_ref):
    gain = vec_ref[0, 0:1, :]

    def norm_rows(index, carry):
        rows = tile_rows(index * 128, 128)
        grads = sum_ref[rows, :]
        units, inverse = standard(x_ref[rows, :].astype(jnp.float32))
        grad_x = grad_hidden_ref[rows, :] + standard_back(grads, gain, units, inverse)
        grad_x_ref[rows, :] = grad_x
        grad_x_low_ref[rows, :] = grad_x.astype(jnp.bfloat16)
        vec_grad_ref[0:1, :] += column_sum(grads * units)
        vec_grad_ref[1:2, :] += column_sum(grads)
        return carry

    lax.fori_loop(0, OWN // 128, norm_rows, 0)


def greet(partners, meanwhile=None):
    barrier = pltpu.get_barrier_semaphore()
    for partner in partners:
        pl.semaphore_signal(barrier, inc=1, device_id=partner, device_id_type=MESH)
    if meanwhile is not None:
        meanwhile()
    pl.semaphore_wait(barrier, len(partners))


def along_tensor(step):
    core, rep, part = place()
    return (core, rep, lax.bitwise_xor(part, step))


def along_dp(step):
    core, rep, part = place()
    return (core, lax.bitwise_xor(rep, step), part)


def sibling():
    core, rep, part = place()
    return (1 - core, rep, part)


def all_partners():
    return [along_tensor(step) for step in (1, 2, 3)] + [along_dp(step) for step in (1, 2, 3)] + [sibling()]


def remote(source, target, send, receive, device):
    return pltpu.make_async_remote_copy(src_ref=source, dst_ref=target, send_sem=send, recv_sem=receive, device_id=device, device_id_type=MESH)


def fill_masks(lens_ref, bias_ref, turned):
    core, rep, part = place()
    slots, keys = task_plan(core)
    bounds, bound = [], 0
    for index in range(lens_ref.shape[1]):
        bound = bound + lens_ref[part, index]
        bounds.append(bound)
    for task in range(TASKS):
        block = jnp.where(slots[task] == 0, core, 3 - core)
        shape = (1, BLOCK) if turned else (BLOCK, 1)
        query = block * BLOCK + lax.broadcasted_iota(jnp.int32, shape, 1 if turned else 0)
        start = jnp.zeros(shape, jnp.int32)
        for bound in bounds:
            start = jnp.where(query >= bound, bound, start)
        key = keys[task] * BLOCK + lax.broadcasted_iota(jnp.int32, (BLOCK, BLOCK), 0 if turned else 1)
        bias_ref[task] = jnp.where((key >= start) & (key <= query), 0.0, NEGATIVE)


def rows_view(array, rows, index):
    return array.at[:, rows] if index == QKV else array.at[rows]


def quarter_rows(array, which):
    count = array.shape[-2] // PARTS
    return tile_rows(which * count, count)


SAVED = (
    ((OWN, WIDTH), jnp.bfloat16),
    ((WIDTH, OWN), jnp.bfloat16),
    ((PAIRS, 2, OWN, 128), jnp.bfloat16),
    ((2, PAIRS, 1024, 128), jnp.bfloat16),
    ((PAIRS, OWN, 128), jnp.float32),
    ((PAIRS, 128, OWN), jnp.bfloat16),
    ((2, 8, BLOCK), jnp.float32),
    ((OWN, WIDTH), jnp.float32),
    ((WIDTH, OWN), jnp.bfloat16),
    ((PARTS, OWN, 512), jnp.bfloat16),
    ((PARTS, OWN, 512), jnp.bfloat16),
)
WEIGHTS = (
    ((PARTS, 3, 512, 128), jnp.bfloat16),
    ((PARTS, 128, 512), jnp.bfloat16),
    ((PARTS, 512, 512), jnp.bfloat16),
    ((PARTS, 512, 512), jnp.bfloat16),
    ((PARTS, 8, 512), jnp.float32),
)
QKV, OUT, UP, DOWN, VEC = range(5)


ALL = (1, 2, 3)
DIRECT = ((0, QKV),)
FORWARD_PLAN = (
    ("masks", None, 0, "near", ALL, (QKV,)),
    ("masks", None, 0, "own", None, (QKV, OUT, UP, DOWN)),
    ("vec", None, 0, "z", (1, 2), (OUT, UP, DOWN)),
    ("rows", None, 0, "z", (3,), (OUT, UP, DOWN)),
    ("norm0", None, 0, "sib", ALL, (QKV,)),
    ("norm0", None, 1, "own", None, (QKV, OUT, UP, DOWN)),
    ("project0", 0, 0, "near", (1,), (OUT, UP, DOWN)),
    ("project0", 2, 0, "near", (2,), (OUT, UP, DOWN)),
    ("attend0", 0, 0, "far", (1,), (OUT, UP, DOWN)),
    ("attend0", 1, 0, "near", (3,), (OUT, UP, DOWN)),
    ("attend0", 1, 0, "far", (2,), (OUT, UP, DOWN)),
    ("attend0", 2, 1, "z", ALL, (QKV,)),
    ("attend0", 2, 0, "sib", (1,), (OUT, UP, DOWN)),
    ("attend0", 3, 0, "far", (3,), (OUT, UP, DOWN)),
    ("attend0", 3, 0, "sib", (2,), (OUT, UP, DOWN)),
    ("attended0", None, 1, "z", (1, 2), (OUT, UP, DOWN)),
    ("second0", None, 1, "near", ALL, (QKV,)),
    ("attended0", None, 0, "sib", (3,), (OUT, UP, DOWN)),
    ("chunk0", 0, 1, "z", (3,), (OUT, UP, DOWN)),
    ("chunk0", 2, 1, "near", (1,), (OUT, UP, DOWN)),
    ("chunk0", 3, 1, "near", (2,), (OUT, UP, DOWN)),
    ("chunk0", 2, 1, "far", ALL, (QKV,)),
    ("chunk0", 2, None, "rows", None, ()),
    ("chunk0", 3, 1, "sib", ALL, (QKV,)),
    ("project1", 1, 1, "near", (3,), (OUT, UP, DOWN)),
    ("project1", 2, 1, "far", (1,), (OUT, UP, DOWN)),
    ("attend1", 0, 1, "far", (2,), (OUT, UP, DOWN)),
    ("attend1", 1, 1, "sib", (1,), (OUT, UP, DOWN)),
    ("attend1", 2, 1, "far", (3,), (OUT, UP, DOWN)),
    ("attend1", 3, 1, "sib", (2,), (OUT, UP, DOWN)),
    ("attended1", None, 1, "sib", (3,), (OUT, UP, DOWN)),
)


def forward_kernel(lens_ref, tokens, cotangent, *refs):
    shards, vectors, refs = refs[:4], refs[4:11], refs[11:]
    dy_out, y_out, saved_out, weights_out, refs = refs[0], refs[1], refs[2:13], refs[13:18], refs[18:]
    saved, weights, refs = refs[:11], refs[11:16], refs[16:]
    y_ref, bias_ref, normed, logit, factor, stat, wide, total, vec_own, refs = *refs[:9], refs[9:]
    row_send, row_recv, row_local, z_send, z_recv, xy_send, xy_recv, sib_send, sib_recv, local, kv_send, kv_recv, save_sem, keep_sem, pass_send, chunk_sem = refs
    core, rep, part = place()
    shards = (*shards, vec_own)
    vec_own[...] = jnp.zeros_like(vec_own)
    for row, vector in enumerate(vectors):
        vec_own[row : row + 1, :] = vector[...]
    greet(all_partners(), partial(fill_masks, lens_ref, bias_ref, False))

    steps = (1, 2, 3)

    def z_copy(index, step):
        slot = (index, step - 1)
        if index == VEC:
            return remote(shards[index], weights[index].at[core, part], z_send.at[slot], z_recv.at[slot], along_tensor(step))
        rows = quarter_rows(shards[index], rep)
        return remote(rows_view(shards[index], rows, index), rows_view(weights[index].at[core, part], rows, index), z_send.at[slot], z_recv.at[slot], along_tensor(step))

    def ends():
        return (part == 0) | (part == 3)

    def pass_copy(index):
        view = rows_view(weights[index].at[core, turn_part(2)], quarter_rows(shards[index], rep), index)
        return remote(view, view, pass_send.at[index], z_recv.at[index, 2], along_tensor(1))

    def own_copy(index):
        return pltpu.make_async_copy(shards[index], weights[index].at[core, part], local.at[index])

    def near_copy(index, step, far):
        slot = (index, far - 1, step - 1)
        view = rows_view(weights[index].at[core, turn_part(far)], quarter_rows(shards[index], rep), index)
        return remote(view, view, xy_send.at[slot], xy_recv.at[slot], along_dp(step))

    def far_copy(index, step, far):
        slot = (index, far - 1, step + 1)
        count = shards[index].shape[-2] // PARTS
        rows = tile_rows(lax.bitwise_xor(rep, 3 - step) * count + (2 - step) * (count // 2), count // 2)
        view = rows_view(weights[index].at[core, turn_part(far)], rows, index)
        return remote(view, view, xy_send.at[slot], xy_recv.at[slot], along_dp(step))

    def across_copy(index, far):
        slot = (index, far - 1, 2)
        view = rows_view(weights[index].at[core, turn_part(far)], quarter_rows(shards[index], rep), index)
        return remote(view, view, xy_send.at[slot], xy_recv.at[slot], along_dp(3))

    def sib_copy(index, far):
        target = weights[index].at[core, turn_part(far)]
        source = target if far else shards[index]
        return remote(source, target, sib_send.at[index, far], sib_recv.at[index, far], sibling())

    def vec_copy():
        view = weights[VEC].at[core]
        return remote(view, view, sib_send.at[VEC, 0], sib_recv.at[VEC, 0], sibling())

    def own_start(*which):
        for index in which:
            own_copy(index).start()
            sib_copy(index, 0).start()

    def z_start(far, *which):
        for index in which:
            if far < 3 or index == VEC:
                z_copy(index, far).start()
            else:
                pl.when(jnp.logical_not(ends()))(z_copy(index, far).start)

    def near_start(far, *which):
        for index in which:
            z_copy(index, far).wait_recv()
            if far == 2:
                pl.when(jnp.logical_not(ends()))(pass_copy(index).start)
            for step in (1, 2):
                near_copy(index, step, far).start()
            for layer in range(2):
                if (layer, index) in DIRECT:
                    pl.when(core == layer)(across_copy(index, far).start)

    def far_start(far, *which):
        for index in which:
            for step in (2, 1):
                near_copy(index, 3 - step, far).wait_recv()
                far_copy(index, step, far).start()

    def sib_direct(far, *which):
        for index in which:
            for step in (1, 2):
                near_copy(index, step, far).wait_recv()
            across_copy(index, far).wait_recv()
            sib_copy(index, far).start()

    def sib_passed(far, *which):
        for index in which:
            for step in (1, 2):
                far_copy(index, step, far).wait_recv()
            sib_copy(index, far).start()

    def sib_start(far, *which):
        for layer in range(2):
            pl.when(core == layer)(partial(sib_direct, far, *[index for index in which if (layer, index) in DIRECT]))
            pl.when(core == layer)(partial(sib_passed, far, *[index for index in which if (layer, index) not in DIRECT]))

    def need(layer, far, *which):
        @pl.when(core != layer)
        def _():
            for index in which:
                sib_copy(index, far).wait_recv()

        if far == 0:

            @pl.when(core == layer)
            def _():
                for index in which:
                    own_copy(index).wait()

    def need_turn(layer, turn, *which):
        for far in range(PARTS):
            pl.when(turn == far)(partial(need, layer, far, *which))

    def keep_copy(layer, index):
        return pltpu.make_async_copy(weights[index].at[layer], weights_out[index].at[layer], keep_sem.at[layer, index])

    def keep(layer, *which):
        for index in which:
            keep_copy(layer, index).start()

    def on(layer, action, *which):
        pl.when(core == layer)(partial(action, *which))

    def at(layer, turn, when, action, *which):
        pl.when((core == layer) & (turn == when))(partial(action, *which))

    owner = jnp.where((part == 0) | (part == 3), 0, 1)
    place_here = jnp.where(part < 2, 0, 1)
    row_pairs = ((tokens, saved[0].at[0]), (cotangent, dy_out))

    def row_targets(array, batch):
        source, target = row_pairs[array]
        rows = target.at[tile_rows(place_here * BLOCK, BLOCK)]
        there = remote(source.at[batch], rows, row_send.at[array, batch], row_recv.at[array, place_here], (core, rep, batch))
        here = pltpu.make_async_copy(source.at[batch], rows, row_local.at[array])
        return there, here

    def rows_each(array, act):
        for batch in range(PARTS):
            there, here = row_targets(array, batch)

            @pl.when((core == owner) & (part != batch))
            def _():
                there.start() if act == "start" else there.wait_send()

            @pl.when((core == owner) & (part == batch))
            def _():
                here.start() if act == "start" else here.wait()

    def rows_arrived(array):
        for slot, block in enumerate(blocks_of(core)):

            @pl.when(block != part)
            def _():
                source, target = row_pairs[array]
                rows = target.at[slot * BLOCK : (slot + 1) * BLOCK]
                remote(source.at[0], rows, row_send.at[array, 0], row_recv.at[array, slot], sibling()).wait_recv()

    def save(layer, *which):
        for index in which:
            pltpu.make_async_copy(saved[index].at[layer], saved_out[index].at[layer], save_sem.at[layer, index]).start()

    def chunk_copies(layer, turn):
        chunk = turn_part(turn)
        return [
            pltpu.make_async_copy(saved[index].at[layer, chunk], saved_out[index].at[layer, chunk], chunk_sem.at[layer, index - 9, turn])
            for index in (9, 10)
        ]

    def kv_copies(layer, pair, receiving):
        copies = []
        for slot, block in enumerate(blocks_of(1 - core if receiving else core)):
            view = saved[3].at[layer, :, pair, tile_rows(block * BLOCK, BLOCK), :]
            copies.append(remote(view, view, kv_send.at[layer, pair, slot], kv_recv.at[layer, pair, slot], sibling()))
        return copies

    actions = {"own": own_start, "z": z_start, "near": near_start, "far": far_start, "sib": sib_start}

    def run(point, turn=None):
        for where, when, owner_core, name, fars, which in FORWARD_PLAN:
            if where != point:
                continue

            def act():
                if name == "own":
                    own_start(*which)
                elif name == "rows":
                    rows_each(1, "start")
                else:
                    for far in fars:
                        actions[name](far, *[index for index in which if name != "far" or (owner_core, index) not in DIRECT])

            here = core == owner_core if owner_core is not None else None
            if turn is not None:
                here = turn == when if here is None else here & (turn == when)
            act() if here is None else pl.when(here)(act)

    for far in steps:
        on(0, z_start, far, QKV)
        z_start(far, VEC)
    own_copy(VEC).start()
    rows_each(0, "start")
    run("masks")
    own_copy(VEC).wait()
    for step in steps:
        z_copy(VEC, step).wait_recv()
    vec_copy().start()
    run("vec")
    rows_each(0, "wait")
    rows_arrived(0)
    vec_copy().wait_recv()
    run("rows")
    for layer in range(2):
        signed = layer == 0
        held = [item.at[layer] for item in saved]
        qkv, out, up, down, vec = [item.at[layer] for item in weights]
        x_ref, normed_one_t, queries, kv, attended, attended_t, logs, hidden, normed_two_t, act, slope = held

        def after_norm():
            run(f"norm{layer}")

        def before_project(turn):
            run(f"project{layer}", turn)
            need_turn(layer, turn, QKV)

        def push_kv(turn, pair):
            for copy in kv_copies(layer, pair, False):
                copy.start()

        def before_attend(turn, pair):
            run(f"attend{layer}", turn)
            for copy in kv_copies(layer, pair, True):
                copy.wait_recv()

        def before_out(turn):
            need_turn(layer, turn, OUT)

        def before_feed():
            save(layer, 7, 8)
            run(f"second{layer}")

        def before_chunk(turn):
            need_turn(layer, turn, UP, DOWN)
            if layer == 1:
                pl.when(turn == PARTS - 1)(partial(keep, 1, OUT, UP, DOWN))

        def during_chunk(turn):
            for copy in chunk_copies(layer, turn):
                copy.start()
            run(f"chunk{layer}", turn)

        project(x_ref, vec, qkv, normed_one_t, queries, kv, normed, after_norm, before_project, push_kv)
        save(layer, 0, 1, 2)
        keep(layer, QKV, VEC)
        attend_rows(signed, queries, kv, bias_ref, attended, attended_t, logs, logit, factor, stat, before_attend)
        save(layer, 3, 4, 5, 6)
        run(f"attended{layer}")
        target = saved[0].at[1] if layer == 0 else y_ref
        feed(x_ref, attended, vec, out, up, down, hidden, normed_two_t, act, slope, target, normed, wide, total, before_out, before_feed, before_chunk, during_chunk)
        if layer == 0:
            keep(0, OUT, UP, DOWN)
    y_copy = pltpu.make_async_copy(y_ref, y_out, row_local.at[0])
    y_copy.start()
    rows_each(1, "wait")
    rows_arrived(1)
    for index in range(5):
        for step in steps:
            if step < 3 or index == VEC:
                z_copy(index, step).wait_send()
            else:
                pl.when(jnp.logical_not(ends()))(z_copy(index, step).wait_send)
                pl.when(jnp.logical_not(ends()))(pass_copy(index).wait_send)
            if index != VEC:
                for way in (1, 2):
                    near_copy(index, way, step).wait_send()
                    for layer in range(2):
                        if (layer, index) not in DIRECT:
                            pl.when(core == layer)(far_copy(index, way, step).wait_send)
                for layer in range(2):
                    if (layer, index) in DIRECT:
                        pl.when(core == layer)(across_copy(index, step).wait_send)
                sib_copy(index, step).wait_send()
        sib_copy(index, 0).wait_send() if index != VEC else vec_copy().wait_send()
    for layer in range(2):
        for pair in range(PAIRS):
            for copy in kv_copies(layer, pair, False):
                copy.wait_send()
        for index in range(9):
            pltpu.make_async_copy(saved[index].at[layer], saved_out[index].at[layer], save_sem.at[layer, index]).wait()
        for turn in range(PARTS):
            for copy in chunk_copies(layer, turn):
                copy.wait()
    y_copy.wait()
    for layer in range(2):
        for index in range(5):
            keep_copy(layer, index).wait()


FEED, ATTEND = 0, 1
GROUPS = ((0, 1024), (1024, 1536))


def backward_kernel(lens_ref, dy_in, y_in, *refs):
    saved_in, weights_in, refs = refs[:11], refs[11:16], refs[16:]
    down_out, up_out, out_out, qkv_out, vec_out, bias_out, blocks_out, rows_out, refs = *refs[:8], refs[8:]
    held, weights, refs = refs[:11], refs[11:16], refs[16:]
    dy_low, dy_ref, bias_ref, grads_ref, vec_grad, low, low_t, chunk, total, grad_hidden, grad_att, centres, grad_query, grad_kv, kv_out, kv_got, grad_low, refs = *refs[:17], refs[17:]
    got_core, got_first, got_second, part_sum, got_part, final, vec_core, vec_chip, vec_dp, vec_rep, vec_part, grads_out, vec_total, refs = *refs[:13], refs[13:]
    load_sem, weight_sem, dy_sem, y_send, y_recv, row_send, row_recv, kv_send, kv_recv, core_send, core_recv, first_send, first_recv, second_send, second_recv, part_send, part_recv, vec_send, vec_recv, last_send, last_recv = refs
    core, rep, part = place()
    steps = (1, 2, 3)
    mine, theirs = tile_rows(core * 64, 64), tile_rows((1 - core) * 64, 64)

    def load(layer, which=(), matrices=()):
        copies = [pltpu.make_async_copy(saved_in[index].at[layer], held[index], load_sem.at[index]) for index in which]
        return copies + [pltpu.make_async_copy(weights_in[index].at[layer], weights[index], weight_sem.at[index]) for index in matrices]

    def start(copies):
        for copy in copies:
            copy.start()

    def wait(copies):
        for copy in copies:
            copy.wait()

    chunk_set = ((10, 9, 8), (DOWN, UP))
    norm_set = ((7, 5, 4), (VEC, OUT))
    attend_set = ((2, 3, 6), ())
    project_set = ((0, 1), (QKV,))
    dy_copy = pltpu.make_async_copy(dy_in, dy_low, dy_sem.at[0])
    dy_copy.start()
    for group in (chunk_set, norm_set, attend_set, project_set):
        start(load(1, *group))
    greet(all_partners() + [(1 - core, rep, lax.bitwise_xor(part, step)) for step in steps], partial(fill_masks, lens_ref, bias_ref, True))

    owner = jnp.where((part == 0) | (part == 3), 0, 1)

    def deliver(source, layer, target, send, receive, act):
        for slot, block in enumerate(blocks_of(core)):
            rows = source.at[slot * BLOCK : (slot + 1) * BLOCK]
            stays = (core == layer) & (block == part)

            @pl.when(stays)
            def _():
                copy = pltpu.make_async_copy(rows, target.at[part], send.at[layer, slot])
                copy.start() if act == "start" else copy.wait()

            @pl.when(jnp.logical_not(stays))
            def _():
                copy = remote(rows, target.at[part], send.at[layer, slot], receive.at[part], (layer, rep, block))
                copy.start() if act == "start" else copy.wait_send()

    def delivered(target, source, send, receive):
        for batch in range(PARTS):

            @pl.when((core != owner) | (part != batch))
            def _():
                remote(source.at[:BLOCK], target.at[batch], send.at[0, 0], receive.at[batch], sibling()).wait_recv()

    deliver(saved_in[0].at[1], 0, blocks_out, y_send, y_recv, "start")
    deliver(y_in, 1, blocks_out, y_send, y_recv, "start")

    def core_copy(layer, group, turn):
        first, last = GROUPS[group]
        other, slot = turn_part(turn + 1), (layer, group, turn)
        return remote(grads_ref.at[:, other, theirs, first:last], got_core.at[layer, :, other, :, first:last], core_send.at[slot], core_recv.at[slot], sibling())

    def halves(way):
        return pl.ds(0, 32) if way == 1 else pl.ds(32, 32)

    def first_copy(layer, group, turn, way, piece):
        first, last = GROUPS[group]
        other, slot = turn_part(turn + 1), (layer, group, turn, way - 1, piece)
        source = got_core.at[layer, lax.bitwise_xor(rep, 3 if piece else way), other, halves(way), first:last]
        return remote(source, got_first.at[layer, way - 1, piece, other, :, first:last], first_send.at[slot], first_recv.at[slot], along_dp(way))

    def second_copy(layer, group, turn, way):
        first, last = GROUPS[group]
        other, slot = turn_part(turn + 1), (layer, group, turn, way - 1)
        source = got_core.at[layer, lax.bitwise_xor(rep, 3 - way), other, halves(way), first:last]
        return remote(source, got_second.at[layer, way - 1, other, :, first:last], second_send.at[slot], second_recv.at[slot], along_dp(3 - way))

    def part_copy(layer, group, turn):
        first, last = GROUPS[group]
        slot = (layer, group, turn)
        return remote(part_sum.at[layer, turn, :, first:last], got_part.at[layer, turn, :, first:last], part_send.at[slot], part_recv.at[slot], along_tensor(turn + 1))

    def dp_start(layer, group, turn):
        first, last = GROUPS[group]
        core_copy(layer, group, turn).wait()
        other = turn_part(turn + 1)

        def add(major, carry):
            own = grads_ref[major, other, mine, first:last]
            got_core[layer, major, other, :, first:last] = own + got_core[layer, major, other, :, first:last]
            return carry

        lax.fori_loop(0, PARTS, add, 0)
        start(first_copy(layer, group, turn, way, piece) for way in (1, 2) for piece in range(2))

    def dp_next(layer, group, turn):
        first, last = GROUPS[group]
        other = turn_part(turn + 1)
        for way in (1, 2):
            for piece in (1, 0):
                first_copy(layer, group, turn, way, piece).wait()
                major = lax.bitwise_xor(rep, 3 - way) if piece else rep
                own = got_core[layer, major, other, halves(way), first:last]
                got_core[layer, major, other, halves(way), first:last] = own + got_first[layer, way - 1, piece, other, :, first:last]
                if piece:
                    second_copy(layer, group, turn, way).start()

    def part_start(layer, group, turn):
        first, last = GROUPS[group]
        other = turn_part(turn + 1)
        for way in (1, 2):
            second_copy(layer, group, turn, way).wait()
            own = got_core[layer, rep, other, halves(way), first:last]
            part_sum[layer, turn, halves(way), first:last] = own + got_second[layer, way - 1, other, :, first:last]
        if turn < PARTS - 1:
            part_copy(layer, group, turn).start()

    def finish(layer, group):
        first, last = GROUPS[group]
        sum_here = part_sum[layer, PARTS - 1, :, first:last].astype(jnp.float32)
        for turn in range(PARTS - 1):
            part_copy(layer, group, turn).wait()
            sum_here = sum_here + got_part[layer, turn, :, first:last].astype(jnp.float32)
        final[layer, :, first:last] = sum_here

    def last_copy(layer):
        return remote(final.at[layer], grads_out.at[mine], last_send.at[0], last_recv.at[0], sibling())

    def hand_over(layer):
        @pl.when(core == layer)
        def _():
            grads_out[mine, :] = final[layer]

        @pl.when(core != layer)
        def _():
            last_copy(layer).start()

    def kv_copy(layer, pair):
        return remote(kv_out.at[:, pair], kv_got.at[layer, :, pair], kv_send.at[layer, pair], kv_recv.at[layer, pair], sibling())

    for layer in (1, 0):
        signed = layer == 0
        x_ref, normed_one_t, queries, kv, attended, attended_t, logs, hidden, normed_two_t, act, slope = held
        qkv, out, up, down, vec = weights
        if layer == 1:
            dy_copy.wait()
            dy_ref[...] = dy_low[...].astype(jnp.float32)
        wait(load(layer, *chunk_set))

        def at(turn, when, action, *which):
            pl.when(turn == when)(partial(action, *which))

        def during_chunk(turn):
            pl.when(turn > 0)(lambda: dp_start(layer, FEED, turn - 1))
            if layer == 0:
                at(turn, 0, dp_next, 1, ATTEND, 1)
                at(turn, 0, dp_next, 1, ATTEND, 2)
                at(turn, 1, dp_next, 1, ATTEND, 3)
                at(turn, 1, part_start, 1, ATTEND, 0)
                at(turn, 2, part_start, 1, ATTEND, 1)
                at(turn, 2, part_start, 1, ATTEND, 2)
                at(turn, 3, part_start, 1, ATTEND, 3)

        def after_chunk(turn, chunk):
            core_copy(layer, FEED, turn).start()

        def before_norm():
            wait(load(layer, *norm_set))

        def after_norm():
            dp_start(layer, FEED, 3)

        feed_back(dy_ref, act, slope, down, up, hidden, normed_two_t, vec, out, attended, attended_t, grad_hidden, grad_att, centres, grads_ref, vec_grad.at[layer], low, low_t, chunk, total, during_chunk, after_chunk, before_norm, after_norm)
        if layer == 1:
            start(load(0, (9, 10, 7, 8, 4, 5), (DOWN, UP, OUT)))
        wait(load(layer, *attend_set))

        def before_attend(turn):
            for index in range(4):
                at(turn, index, dp_next, layer, FEED, index)
            at(turn, 2, part_start, layer, FEED, 0)
            at(turn, 3, part_start, layer, FEED, 1)
            if layer == 0:
                at(turn, 2, finish, 1, FEED)

        def project_turn(turn):
            pair = turn_part(turn + 1)
            kv_copy(layer, pair).wait()
            project_back_pair(pair, lax.rem(turn, 2), grad_query, grad_kv, kv_got.at[layer], normed_one_t, qkv, grads_ref, total, core_copy(layer, ATTEND, turn).start)

        def after_attend(turn, pair):
            kv_copy(layer, pair).start()
            at(turn, 2, dp_start, layer, ATTEND, 0)
            at(turn, 3, dp_start, layer, ATTEND, 1)
            at(turn, 3, dp_next, layer, ATTEND, 0)
            pl.when(turn > 0)(lambda: project_turn(turn - 1))

        wait(load(layer, *project_set))
        total[...] = jnp.zeros_like(total)
        attend_rows_back(signed, queries, kv, grad_att, bias_ref, logs, centres, grad_query, grad_kv, kv_out, before_attend, after_attend)
        if layer == 1:
            start(load(0, *attend_set))
        dp_start(layer, ATTEND, 2)
        part_start(layer, FEED, 2)
        project_turn(PAIRS - 1)
        part_start(layer, FEED, 3)
        if layer == 0:
            finish(1, ATTEND)
            hand_over(1)
        project_back_norm(x_ref, grad_hidden, vec, dy_ref, grad_low.at[layer], vec_grad.at[layer], total)
        if layer == 1:
            start(load(0, (0, 1), (QKV, VEC)))
        deliver(grad_low.at[layer], layer, rows_out, row_send, row_recv, "start")
        dp_start(layer, ATTEND, 3)
    vec_copy = remote(vec_grad.at[1 - core], vec_core, vec_send.at[0], vec_recv.at[0], sibling())
    vec_copy.start()
    dp_next(0, ATTEND, 1)
    dp_next(0, ATTEND, 2)
    finish(0, FEED)
    vec_copy.wait()
    vec_chip[...] = vec_grad[core] + vec_core[...]
    vec_copies = [remote(vec_chip, vec_dp.at[step - 1], vec_send.at[step], vec_recv.at[step], along_dp(step)) for step in steps]
    start(vec_copies)
    dp_next(0, ATTEND, 3)
    for turn in range(PARTS):
        part_start(0, ATTEND, turn)
    wait(vec_copies)
    vec_rep[...] = vec_chip[...] + vec_dp[0] + vec_dp[1] + vec_dp[2]
    vec_copies = [remote(vec_rep, vec_part.at[step - 1], vec_send.at[3 + step], vec_recv.at[3 + step], along_tensor(step)) for step in steps]
    start(vec_copies)
    finish(0, ATTEND)
    hand_over(0)
    wait(vec_copies)
    vec_total[...] = vec_rep[...] + vec_part[0] + vec_part[1] + vec_part[2]
    own = rep * PARTS + part
    vec_out[...] = pltpu.roll(vec_total[:8, :], 512 - own * 32, 1)[:, :128]
    columns = vec_total[:, tile_rows(rep * 128, 128)]
    row = lax.broadcasted_iota(jnp.int32, columns.shape, 0)
    bias_out[...] = column_sum(jnp.where(row == 6 + part, columns, 0.0))
    deliver(saved_in[0].at[1], 0, blocks_out, y_send, y_recv, "wait")
    deliver(y_in, 1, blocks_out, y_send, y_recv, "wait")
    delivered(blocks_out, y_in, y_send, y_recv)
    for layer in range(2):
        deliver(grad_low.at[layer], layer, rows_out, row_send, row_recv, "wait")
    delivered(rows_out, grad_low.at[0], row_send, row_recv)
    last_copy(0).wait_recv()
    last_copy(0).wait_send()
    down_out[...] = grads_out[:, :512].T
    up_out[...] = grads_out[:, 512:1024]
    out_out[...] = grads_out[:, 1024:1152]
    for kind in range(3):
        qkv_out[kind] = grads_out[:, 1152 + kind * 128 : 1280 + kind * 128]


def specs(space, count):
    return [pl.BlockSpec(memory_space=space)] * count


def kernel_call(body, name, ins, in_specs, outs, out_specs, scratch, collective):
    dma = pltpu.SemaphoreType.DMA
    return pl.pallas_call(
        body,
        out_shape=[jax.ShapeDtypeStruct(shape, kind) for shape, kind in outs],
        in_specs=in_specs,
        out_specs=out_specs,
        scratch_shapes=[pltpu.VMEM(*item) if len(item) == 2 and isinstance(item[0], tuple) else dma(item) for item in scratch],
        compiler_params=pltpu.CompilerParams(collective_id=collective, has_side_effects=True, vmem_limit_bytes=60 * 2**20),
        name=name,
    )(*ins)


def twice(items):
    return tuple(((2, *shape), kind) for shape, kind in items)


def on_device_whole(
    tokens,
    lengths,
    cotangent,
    ln_one_gain,
    ln_one_bias,
    qkv_weight,
    out_weight,
    out_bias,
    ln_two_gain,
    ln_two_bias,
    up_weight,
    up_bias,
    down_weight,
    down_bias,
):
    f32, low = jnp.float32, jnp.bfloat16
    core, rep, part = place()
    vectors = (ln_one_gain, ln_one_bias, out_bias, ln_two_gain, ln_two_bias, down_bias, up_bias)
    rows, rows_low = ((OWN, WIDTH), f32), ((OWN, WIDTH), low)
    square = ((BLOCK, BLOCK), f32)
    results = kernel_call(
        forward_kernel,
        "forward",
        (lengths, tokens, cotangent, qkv_weight[0].transpose(1, 0, 2), out_weight[0], up_weight[0], down_weight[0], *vectors),
        specs(pltpu.SMEM, 1) + specs(pl.ANY, 6) + specs(pltpu.VMEM, 7),
        (rows_low, rows_low, *twice(SAVED), *twice(WEIGHTS)),
        specs(pl.ANY, 18),
        (
            *twice(SAVED),
            *twice(WEIGHTS),
            rows_low,
            ((TASKS, BLOCK, BLOCK), f32),
            rows_low,
            ((TASKS, 2 * BLOCK, BLOCK), f32),
            ((TASKS, 2 * BLOCK, BLOCK), f32),
            ((2, BLOCK, 128), f32),
            rows,
            rows,
            ((8, 512), f32),
            (2, 4),
            (2, 2),
            (2,),
            (5, 3),
            (5, 3),
            (4, 3, 4),
            (4, 3, 4),
            (5, PARTS),
            (5, PARTS),
            (5,),
            (2, PAIRS, 2),
            (2, PAIRS, 2),
            (2, 11),
            (2, 5),
            (4,),
            (2, 2, PARTS),
        ),
        0,
    )
    down_grad, up_grad, out_grad, qkv_grad, spread, up_bias_grad, block_outputs, grad_rows = kernel_call(
        backward_kernel,
        "backward",
        (lengths, *results),
        specs(pltpu.SMEM, 1) + specs(pl.ANY, 18),
        (
            ((512, 128), f32),
            ((128, 512), f32),
            ((128, 128), f32),
            ((3, 128, 128), f32),
            ((8, 128), f32),
            ((1, 128), f32),
            ((PARTS, BLOCK, WIDTH), low),
            ((PARTS, BLOCK, WIDTH), low),
        ),
        specs(pltpu.VMEM, 6) + specs(pl.ANY, 2),
        (
            *SAVED,
            *WEIGHTS,
            rows_low,
            rows,
            ((TASKS, BLOCK, BLOCK), f32),
            ((PARTS, PARTS, 128, 1536), low),
            ((2, 16, 512), f32),
            rows_low,
            ((WIDTH, OWN), low),
            ((OWN, 512), low),
            rows,
            rows,
            ((PAIRS, 2, OWN, 128), low),
            ((PAIRS, 8, OWN), f32),
            ((PAIRS, OWN, 128), low),
            ((2, 2, 1024, 128), f32),
            ((2, PAIRS, OWN, 128), low),
            ((2, 2, PAIRS, OWN, 128), low),
            ((2, OWN, WIDTH), low),
            ((2, PARTS, PARTS, 64, 1536), low),
            ((2, 2, 2, PARTS, 32, 1536), low),
            ((2, 2, PARTS, 32, 1536), low),
            ((2, PARTS, 64, 1536), low),
            ((2, 3, 64, 1536), low),
            ((2, 64, 1536), f32),
            ((16, 512), f32),
            ((16, 512), f32),
            ((3, 16, 512), f32),
            ((16, 512), f32),
            ((3, 16, 512), f32),
            ((128, 1536), f32),
            ((16, 512), f32),
            (11,),
            (5,),
            (1,),
            (2, 2),
            (PARTS,),
            (2, 2),
            (PARTS,),
            (2, PAIRS),
            (2, PAIRS),
            (2, 2, PARTS),
            (2, 2, PARTS),
            (2, 2, PARTS, 2, 2),
            (2, 2, PARTS, 2, 2),
            (2, 2, PARTS, 2),
            (2, 2, PARTS, 2),
            (2, 2, PARTS),
            (2, 2, PARTS),
            (7,),
            (7,),
            (1,),
            (1,),
        ),
        1,
    )
    vector_grads = [spread[row : row + 1, :32] for row in range(6)]
    return (
        block_outputs[None],
        grad_rows.astype(f32)[None],
        vector_grads[0],
        vector_grads[1],
        qkv_grad.transpose(1, 0, 2)[None],
        out_grad[None],
        vector_grads[2],
        vector_grads[3],
        vector_grads[4],
        up_grad[None],
        up_bias_grad[None],
        down_grad[None],
        vector_grads[5],
    )


def solution(mesh):
    return jax.shard_map(
        on_device_whole if whole_batch_fits(mesh) else on_device,
        mesh=mesh,
        in_specs=(
            P("dp", "tensor", None),
            P("dp", None),
            P("dp", "tensor", None),
            P("section", None),
            P("section", None),
            P("section", None, None, "tensor"),
            P("section", "tensor", None),
            P("section", None),
            P("section", None),
            P("section", None),
            P("section", None, "tensor"),
            P("section", "tensor"),
            P("section", "tensor", None),
            P("section", None),
        ),
        out_specs=(
            P("section", "dp", "tensor", None),
            P("section", "dp", "tensor", None),
            P("section", ("dp", "tensor")),
            P("section", ("dp", "tensor")),
            P("section", "dp", None, "tensor"),
            P("section", "tensor", "dp"),
            P("section", ("dp", "tensor")),
            P("section", ("dp", "tensor")),
            P("section", ("dp", "tensor")),
            P("section", "dp", "tensor"),
            P("section", "tensor", "dp"),
            P("section", "tensor", "dp"),
            P("section", ("dp", "tensor")),
        ),
        check_vma=False,
    )
```
